32 devices in a mesh: rep: 4 (over z), grp: 8 (over y, x, core).
Axes of the slice: x: 2, y: 2, z: 4, core: 2. Of those that a mesh axis runs over, the one named last changes fastest.
Arguments:
- tokens: bfloat16 [32256, 768], P(('rep', 'grp')), may hold values from -6 to 6
- cotangent: bfloat16 [32256, 768], P(('rep', 'grp')), may hold values from -6 to 6
- window_fill: int32 [224], P(('rep', 'grp')), may hold values from 48 to 144, as said below
- qkv_weight: float32 [768, 2304], P('grp'), may hold values from -0.21875 to 0.21875
- proj_weight: float32 [768, 768], P('grp'), may hold values from -0.625 to 0.625
- fc1_weight: float32 [768, 3072], P('grp'), may hold values from -0.21875 to 0.21875
- fc2_weight: float32 [3072, 768], P('grp'), may hold values from -0.109375 to 0.109375
- vectors: float32 [12, 768], replicated
- vector_moments: float32 [12, 768], replicated, may hold values from -112 to 112
- bias_table: float32 [529, 24], replicated, may hold values from -4 to 4
- table_moments: float32 [529, 24], replicated, may hold values from -16 to 16
- stats_model: float32 [5, 768, 768], P(None, 'grp'), as said below
- stats_qkv: float32 [2304, 2304], P('grp'), as said below
- stats_hidden: float32 [2, 3072, 3072], P(None, 'grp'), as said below
- roots_model: float32 [5, 768, 768], P(None, 'grp'), as said below
- roots_qkv: float32 [2304, 2304], P('grp'), as said below
- roots_hidden: float32 [2, 3072, 3072], P(None, 'grp'), as said below
Outputs:
- layer_output: bfloat16 [32256, 768], P(('rep', 'grp'))
- input_gradient: bfloat16 [32256, 768], P(('rep', 'grp'))
- qkv_gradient: float32 [768, 2304], P('grp')
- proj_gradient: float32 [768, 768], P('grp')
- fc1_gradient: float32 [768, 3072], P('grp')
- fc2_gradient: float32 [3072, 768], P('grp')
- qkv_new: float32 [768, 2304], P('grp')
- proj_new: float32 [768, 768], P('grp')
- fc1_new: float32 [768, 3072], P('grp')
- fc2_new: float32 [3072, 768], P('grp')
- qkv_copy: bfloat16 [768, 2304], P('grp')
- proj_copy: bfloat16 [768, 768], P('grp')
- fc1_copy: bfloat16 [768, 3072], P('grp')
- fc2_copy: bfloat16 [3072, 768], P('grp')
- new_stats_model: float32 [5, 768, 768], P(None, 'grp')
- new_stats_qkv: float32 [2304, 2304], P('grp')
- new_stats_hidden: float32 [2, 3072, 3072], P(None, 'grp')
- new_vectors: float32 [12, 768], replicated
- new_vector_moments: float32 [12, 768], replicated
- new_table: float32 [529, 24], replicated
- new_table_moments: float32 [529, 24], replicated
The draws below stay inside these ranges and needn't reach their ends.
Inputs may be any that keep to these rules, and one draw needn't show every extreme that they name: `window_fill`: some window is full. `roots_model`: each matrix is symmetric. `roots_qkv`: the matrix is symmetric. `roots_hidden`: each matrix is symmetric. `stats_model`: each matrix is symmetric. `stats_qkv`: the matrix is symmetric. `stats_hidden`: each matrix is symmetric.
All inputs are finite; a program needn't handle non-finite values.
Results may differ from the reference program's by a relative error of at most 0.012.
Values may be sent and summed in bfloat16 or wider, within the bound.
A program may use at most 320 MiB of HBM per device.

```python
import math
import jax
import jax.numpy as jnp
from jax import lax

D = 768
HEADS = 24
HD = 32
FF = 3072
WT = 144
TABLE_ROWS = 529
WIN_DEV = 7
WINDOWS = 224
TOKENS = 32256
N_REP = 4
N_GRP = 8


def symmetric_stack(source, amount, degree, scales):
    first_key, second_key = jax.random.split(source)
    diagonal = jax.random.uniform(first_key, (amount, degree), jnp.float32, 1.0, 4.0) * scales[:, None]
    jitter = jax.random.normal(second_key, (amount, degree, degree), jnp.float32)
    mirror = (jitter + jnp.swapaxes(jitter, 1, 2)) * (0.45 / math.sqrt(degree))
    on_diagonal = jnp.arange(degree)[:, None] == jnp.arange(degree)[None, :]
    return jnp.where(on_diagonal[None], diagonal[:, :, None], mirror * scales[:, None, None])


def square_scale():
    return 0.16 * WINDOWS * WT


def root_scales(factors):
    return 0.7 * (factors * square_scale()) ** (-0.25)


def draw_window_fill(key, part):
    key = jax.random.fold_in(key, 1)
    first_key, second_key = jax.random.split(key)
    counts = jax.random.randint(first_key, (WINDOWS,), WT // 3, WT + 1)
    full_window = jax.random.randint(second_key, (), 0, WINDOWS)
    return jnp.where(jnp.arange(WINDOWS) == full_window, WT, counts).astype(jnp.int32)


def draw_vectors(key, part):
    key = jax.random.fold_in(key, 2)
    first_key, second_key = jax.random.split(key)
    row_ids = jnp.arange(12)[:, None]
    gains = 1.0 + 0.3 * jax.random.uniform(first_key, (12, D), jnp.float32, -1.0, 1.0)
    shifts = 0.4 * jax.random.normal(second_key, (12, D), jnp.float32)
    is_gain = (row_ids == 0) | (row_ids == 5)
    return jnp.where(is_gain, gains, shifts).astype(jnp.float32)


def draw_stats_model(key, part):
    key = jax.random.fold_in(key, 11)
    factors = jnp.array([3 * D, D, D, FF, FF], jnp.float32)
    return symmetric_stack(key, 5, D, factors * square_scale())


def draw_stats_qkv(key, part):
    key = jax.random.fold_in(key, 12)
    factors = jnp.array([D], jnp.float32)
    return symmetric_stack(key, 1, 3 * D, factors * square_scale())[0]


def draw_stats_hidden(key, part):
    key = jax.random.fold_in(key, 13)
    factors = jnp.array([D, D], jnp.float32)
    return symmetric_stack(key, 2, FF, factors * square_scale())


def draw_roots_model(key, part):
    key = jax.random.fold_in(key, 21)
    factors = jnp.array([3 * D, D, D, FF, FF], jnp.float32)
    return symmetric_stack(key, 5, D, root_scales(factors))


def draw_roots_qkv(key, part):
    key = jax.random.fold_in(key, 22)
    factors = jnp.array([D], jnp.float32)
    return symmetric_stack(key, 1, 3 * D, root_scales(factors))[0]


def draw_roots_hidden(key, part):
    key = jax.random.fold_in(key, 23)
    factors = jnp.array([D, D], jnp.float32)
    return symmetric_stack(key, 2, FF, root_scales(factors))


def steps_of(key, extent, shards, least, high):
    gain, own = 1.0, jax.random.fold_in(key, 6)
    for dim, shards_of in shards:
        steps = jnp.exp(jax.random.uniform(jax.random.fold_in(own, dim), (shards_of,), jnp.float32, least / len(shards), high / len(shards)))
        gain = gain * jnp.repeat(steps, extent[dim] // shards_of).reshape([-1 if axis == dim else 1 for axis in range(len(extent))])
    return gain


def bell_draw(own_key, shape, spread, bound, cuts=(), held_as=jnp.bfloat16):
    values = jax.random.normal(own_key, shape, jnp.float32) * spread
    if len(cuts) > 0:
        values = steps_of(own_key, shape, cuts, -0.22, 0.18) * values
    return jnp.clip(values, min=-bound, max=bound).astype(held_as)


def setup_inputs(seed: int = 0) -> dict:
    streams_of = jax.random.split(jax.random.key(seed), 18)
    tokens = bell_draw(streams_of[0], (TOKENS, D), 1.0, 6.0, ((0, 32),))
    cotangent = bell_draw(streams_of[1], (TOKENS, D), 1.0, 6.0, ((0, 32),))
    window_fill = draw_window_fill(jax.random.fold_in(streams_of[17], 71), 0)
    qkv_weight = bell_draw(streams_of[3], (D, 3 * D), D ** -0.5, 0.21875, ((0, 8),), jnp.float32)
    proj_weight = bell_draw(streams_of[4], (D, D), (D // 8) ** -0.5, 0.625, ((0, 8),), jnp.float32)
    fc1_weight = bell_draw(streams_of[5], (D, FF), D ** -0.5, 0.21875, ((0, 8),), jnp.float32)
    fc2_weight = bell_draw(streams_of[6], (FF, D), FF ** -0.5, 0.109375, ((0, 8),), jnp.float32)
    vectors = draw_vectors(jax.random.fold_in(streams_of[17], 71), 0)
    vector_moments = bell_draw(streams_of[8], (12, D), (0.1 * (WINDOWS * WT) ** 0.5), 112.0, (), jnp.float32)
    bias_table = bell_draw(streams_of[9], (TABLE_ROWS, HEADS), 1.0, 4.0, (), jnp.float32)
    table_moments = bell_draw(streams_of[10], (TABLE_ROWS, HEADS), (0.015 * (WINDOWS * WT) ** 0.5), 16.0, (), jnp.float32)
    stats_model = draw_stats_model(jax.random.fold_in(streams_of[17], 71), 0)
    stats_qkv = draw_stats_qkv(jax.random.fold_in(streams_of[17], 71), 0)
    stats_hidden = draw_stats_hidden(jax.random.fold_in(streams_of[17], 71), 0)
    roots_model = draw_roots_model(jax.random.fold_in(streams_of[17], 71), 0)
    roots_qkv = draw_roots_qkv(jax.random.fold_in(streams_of[17], 71), 0)
    roots_hidden = draw_roots_hidden(jax.random.fold_in(streams_of[17], 71), 0)
    return dict(tokens=tokens, cotangent=cotangent, window_fill=window_fill, qkv_weight=qkv_weight, proj_weight=proj_weight, fc1_weight=fc1_weight, fc2_weight=fc2_weight, vectors=vectors, vector_moments=vector_moments, bias_table=bias_table, table_moments=table_moments, stats_model=stats_model, stats_qkv=stats_qkv, stats_hidden=stats_hidden, roots_model=roots_model, roots_qkv=roots_qkv, roots_hidden=roots_hidden)


highest = lax.Precision.HIGHEST

@jax.custom_vjp
def low(v):
    return lax.optimization_barrier(v.astype(jnp.bfloat16)).astype(jnp.float32)

@jax.custom_vjp
def low_back(v):
    return v

def low_keep(v):
    return (low(v), None)

def low_pass(kept, grad):
    return (grad,)

def back_keep(v):
    return (v, None)

def back_low(kept, grad):
    return (low(grad),)
low.defvjp(low_keep, low_pass)
low_back.defvjp(back_keep, back_low)

def norm_rows(values, norm_gain, norm_shift):
    average = lax.optimization_barrier(jnp.mean(values, axis=-1, keepdims=True))
    centred = values - average
    variance = lax.optimization_barrier(jnp.mean(centred * centred, axis=-1, keepdims=True))
    return centred * lax.rsqrt(variance + 1e-05) * norm_gain + norm_shift

def exact_gelu(values):
    return jax.nn.gelu(values, approximate=False)

def window_masks(window_ids, window_fill):
    slot_ids = jnp.arange(WT, dtype=jnp.int32)
    placed = window_ids % 4
    image_row = (placed // 2)[:, None] * 12 + (slot_ids // 12)[None, :]
    image_col = (placed % 2)[:, None] * 12 + (slot_ids % 12)[None, :]
    region_row = (image_row >= 12).astype(jnp.int32) + (image_row >= 18).astype(jnp.int32)
    region_col = (image_col >= 12).astype(jnp.int32) + (image_col >= 18).astype(jnp.int32)
    region = region_row * 3 + region_col
    same_region = region[:, :, None] == region[:, None, :]
    live_key = slot_ids[None, None, :] < window_fill[:, None, None]
    shifted = jnp.where(same_region, jnp.float32(0.0), jnp.float32(-100.0))
    return jnp.where(live_key, shifted, jnp.float32(-1e+30))

def relative_index():
    slot_ids = jnp.arange(WT, dtype=jnp.int32)
    slot_row = slot_ids // 12
    slot_col = slot_ids % 12
    return (slot_row[:, None] - slot_row[None, :] + 11) * 23 + slot_col[:, None] - slot_col[None, :] + 11

def block_forward(inputs, qkv_master, proj_master, fc1_master, fc2_master, vector_set, table_set, additive, index_table):
    model_width = vector_set.shape[1]
    window_count = inputs.shape[0] // WT
    score_scale = HD ** (-0.5)
    relative = jnp.transpose(table_set[index_table], (2, 0, 1))
    normed_one = low(norm_rows(inputs, vector_set[0], vector_set[1]))
    qkv_shift = jnp.concatenate([vector_set[2], jnp.zeros_like(vector_set[2]), vector_set[3]])
    mixed = jnp.dot(normed_one, low(qkv_master), precision=highest) + qkv_shift
    mixed = low(low_back(mixed))
    shaped = mixed.reshape(window_count, WT, 3, HEADS, HD)
    queries = shaped[:, :, 0]
    keyset = shaped[:, :, 1]
    valueset = shaped[:, :, 2]
    scores = jnp.einsum('wihd,wjhd->whij', queries, keyset, precision=highest) * score_scale
    scores = low_back(scores + relative[None] + additive[:, None])
    largest = lax.optimization_barrier(jnp.max(scores, axis=-1, keepdims=True))
    exponent = jnp.exp(scores - largest)
    attention = low(exponent / lax.optimization_barrier(jnp.sum(exponent, axis=-1, keepdims=True)))
    context = jnp.einsum('whij,wjhd->wihd', attention, valueset, precision=highest).reshape(-1, model_width)
    context = low(low_back(context))
    branch = low_back(jnp.dot(context, low(proj_master), precision=highest) + vector_set[4])
    middle = inputs + branch
    normed_two = low(norm_rows(middle, vector_set[5], vector_set[6]))
    hidden = low_back(jnp.dot(normed_two, low(fc1_master), precision=highest) + vector_set[8:12].reshape(-1))
    active = low(exact_gelu(hidden))
    output = low_back(jnp.dot(active, low(fc2_master), precision=highest) + vector_set[7])
    return middle + output

def precondition(gradient, master, left_matrix, right_matrix, left_root, right_root):
    left_new = 0.5 * left_matrix + 0.5 * jnp.dot(gradient, gradient.T, precision=highest)
    right_new = 0.5 * right_matrix + 0.5 * jnp.dot(gradient.T, gradient, precision=highest)
    direction = jnp.dot(jnp.dot(left_root, gradient, precision=highest), right_root, precision=highest)
    return (left_new, right_new, master - 1.0 * direction)

def reference(tokens, cotangent, window_fill, qkv_weight, proj_weight, fc1_weight, fc2_weight, vectors, vector_moments, bias_table, table_moments, stats_model, stats_qkv, stats_hidden, roots_model, roots_qkv, roots_hidden):
    block_count = N_REP * N_GRP
    token_blocks = tokens.reshape(block_count, WIN_DEV * WT, D)
    back_blocks = cotangent.reshape(block_count, WIN_DEV * WT, D)
    fill_blocks = window_fill.reshape(block_count, WIN_DEV)
    id_blocks = jnp.arange(WINDOWS, dtype=jnp.int32).reshape(block_count, WIN_DEV)
    index_table = relative_index()

    def one_block(totals, pieces):
        token_block, back_block, fill_block, id_block = pieces
        additive = window_masks(id_block, fill_block)

        def bound_forward(inputs, qkv_master, proj_master, fc1_master, fc2_master, vector_set, table_set):
            return block_forward(inputs, qkv_master, proj_master, fc1_master, fc2_master, vector_set, table_set, additive, index_table)
        outputs, pullback = jax.vjp(bound_forward, token_block.astype(jnp.float32), qkv_weight, proj_weight, fc1_weight, fc2_weight, vectors, bias_table)
        gradients = pullback(back_block.astype(jnp.float32))
        totals = jax.tree.map(jnp.add, totals, tuple(gradients[1:]))
        return (totals, (outputs.astype(jnp.bfloat16), gradients[0].astype(jnp.bfloat16)))
    initial = (jnp.zeros_like(qkv_weight), jnp.zeros_like(proj_weight), jnp.zeros_like(fc1_weight), jnp.zeros_like(fc2_weight), jnp.zeros_like(vectors), jnp.zeros_like(bias_table))
    totals, stacked = lax.scan(one_block, initial, (token_blocks, back_blocks, fill_blocks, id_blocks))
    qkv_gradient, proj_gradient, fc1_gradient, fc2_gradient, vector_gradient, table_gradient = totals
    layer_output = stacked[0].reshape(TOKENS, D)
    input_gradient = stacked[1].reshape(TOKENS, D)
    qkv_left, qkv_right, qkv_new = precondition(qkv_gradient, qkv_weight, stats_model[0], stats_qkv, roots_model[0], roots_qkv)
    proj_left, proj_right, proj_new = precondition(proj_gradient, proj_weight, stats_model[1], stats_model[2], roots_model[1], roots_model[2])
    fc1_left, fc1_right, fc1_new = precondition(fc1_gradient, fc1_weight, stats_model[3], stats_hidden[0], roots_model[3], roots_hidden[0])
    fc2_left, fc2_right, fc2_new = precondition(fc2_gradient, fc2_weight, stats_hidden[1], stats_model[4], roots_hidden[1], roots_model[4])
    new_stats_model = jnp.stack([qkv_left, proj_left, proj_right, fc1_left, fc2_right])
    new_stats_hidden = jnp.stack([fc1_right, fc2_left])
    rate_base = (WINDOWS * WT) ** (-0.5)
    new_vector_moments = 0.9 * vector_moments + 0.1 * vector_gradient
    new_vectors = vectors - 2.0 * rate_base * new_vector_moments
    new_table_moments = 0.9 * table_moments + 0.1 * table_gradient
    new_table = bias_table - 8.0 * rate_base * new_table_moments
    return (layer_output, input_gradient, qkv_gradient, proj_gradient, fc1_gradient, fc2_gradient, qkv_new, proj_new, fc1_new, fc2_new, qkv_new.astype(jnp.bfloat16), proj_new.astype(jnp.bfloat16), fc1_new.astype(jnp.bfloat16), fc2_new.astype(jnp.bfloat16), new_stats_model, qkv_right, new_stats_hidden, new_vectors, new_vector_moments, new_table, new_table_moments)
```

```python
import jax
import jax.numpy as jnp
from jax import lax
from jax.sharding import PartitionSpec as P

WT = 144


highest = lax.Precision.HIGHEST


def norm_rows(values, norm_gain, norm_shift):
    average = jnp.mean(values, axis=-1, keepdims=True)
    centred = values - average
    variance = jnp.mean(centred * centred, axis=-1, keepdims=True)
    return centred * lax.rsqrt(variance + 1e-05) * norm_gain + norm_shift


def exact_gelu(values):
    return jax.nn.gelu(values, approximate=False)


def window_masks(window_ids, window_fill):
    slot_ids = jnp.arange(WT, dtype=jnp.int32)
    placed = window_ids % 4
    image_row = (placed // 2)[:, None] * 12 + (slot_ids // 12)[None, :]
    image_col = (placed % 2)[:, None] * 12 + (slot_ids % 12)[None, :]
    region_row = (image_row >= 12).astype(jnp.int32) + (image_row >= 18).astype(jnp.int32)
    region_col = (image_col >= 12).astype(jnp.int32) + (image_col >= 18).astype(jnp.int32)
    region = region_row * 3 + region_col
    same_region = region[:, :, None] == region[:, None, :]
    live_key = slot_ids[None, None, :] < window_fill[:, None, None]
    shifted = jnp.where(same_region, jnp.float32(0.0), jnp.float32(-100.0))
    return jnp.where(live_key, shifted, jnp.float32(-1e30))


def relative_bias(bias_table):
    head_count = bias_table.shape[1]
    pair_ids = jnp.arange(144, dtype=jnp.int32)
    offset = pair_ids // 12 - pair_ids % 12 + 11
    one_hot = (offset[:, None] == jnp.arange(23, dtype=jnp.int32)[None, :]).astype(jnp.float32)
    table_grid = bias_table.reshape(23, 23 * head_count)
    by_rows = jnp.dot(one_hot, table_grid, precision=highest).reshape(144, 23, head_count)
    combined = jnp.einsum("qx,pxh->pqh", one_hot, by_rows, precision=highest)
    shaped = combined.reshape(12, 12, 12, 12, head_count)
    return jnp.transpose(shaped, (4, 0, 2, 1, 3)).reshape(head_count, WT, WT)


def contract_rows(left_matrix, right_matrix):
    return lax.dot_general(
        left_matrix, right_matrix, (((0,), (0,)), ((), ())), preferred_element_type=jnp.float32
    )


def contract_cols(left_matrix, right_matrix):
    return lax.dot_general(
        left_matrix, right_matrix, (((1,), (1,)), ((), ())), preferred_element_type=jnp.float32
    )


def shards(
    tokens,
    cotangent,
    window_fill,
    qkv_weight,
    proj_weight,
    fc1_weight,
    fc2_weight,
    vectors,
    vector_moments,
    bias_table,
    table_moments,
    stats_model,
    stats_qkv,
    stats_hidden,
    roots_model,
    roots_qkv,
    roots_hidden,
):
    model_width = vectors.shape[1]
    local_windows = window_fill.shape[0]
    head_count = bias_table.shape[1]
    head_size = model_width // head_count
    score_scale = head_size ** (-0.5)
    window_ids = lax.axis_index(("rep", "grp")) * local_windows + jnp.arange(
        local_windows, dtype=jnp.int32
    )
    additive = window_masks(window_ids, window_fill)
    relative, bias_pullback = jax.vjp(relative_bias, bias_table)
    qkv_full, proj_full, fc1_full, fc2_full = (
        lax.all_gather(qkv_weight.astype(jnp.bfloat16), "grp", axis=0, tiled=True),
        lax.all_gather(proj_weight.astype(jnp.bfloat16), "grp", axis=0, tiled=True),
        lax.all_gather(fc1_weight.astype(jnp.bfloat16), "grp", axis=0, tiled=True),
        lax.all_gather(fc2_weight.astype(jnp.bfloat16), "grp", axis=0, tiled=True),
    )
    inputs = tokens.astype(jnp.float32)
    normed_one, norm_one_pullback = jax.vjp(norm_rows, inputs, vectors[0], vectors[1])
    normed_one_low = normed_one.astype(jnp.bfloat16)
    qkv_shift = jnp.concatenate([vectors[2], jnp.zeros_like(vectors[2]), vectors[3]])
    mixed_low = (
        jnp.dot(normed_one_low, qkv_full, preferred_element_type=jnp.float32) + qkv_shift
    ).astype(jnp.bfloat16)
    shaped = mixed_low.reshape(local_windows, WT, 3, head_count, head_size)
    queries = shaped[:, :, 0]
    keyset = shaped[:, :, 1]
    valueset = shaped[:, :, 2]
    scores = (
        jnp.einsum("wihd,wjhd->whij", queries, keyset, preferred_element_type=jnp.float32)
        * score_scale
    )
    scores = scores + relative[None] + additive[:, None]
    largest = jnp.max(scores, axis=-1, keepdims=True)
    exponent = jnp.exp(scores - largest)
    softmax_rows = exponent / jnp.sum(exponent, axis=-1, keepdims=True)
    attention = softmax_rows.astype(jnp.bfloat16)
    context = (
        jnp.einsum("whij,wjhd->wihd", attention, valueset, preferred_element_type=jnp.float32)
        .reshape(-1, model_width)
        .astype(jnp.bfloat16)
    )
    middle = inputs + jnp.dot(context, proj_full, preferred_element_type=jnp.float32) + vectors[4]
    normed_two, norm_two_pullback = jax.vjp(norm_rows, middle, vectors[5], vectors[6])
    normed_two_low = normed_two.astype(jnp.bfloat16)
    hidden = jnp.dot(normed_two_low, fc1_full, preferred_element_type=jnp.float32) + vectors[
        8:12
    ].reshape(-1)
    active, gelu_pullback = jax.vjp(exact_gelu, hidden)
    active_low = active.astype(jnp.bfloat16)
    layer_output = (
        middle + jnp.dot(active_low, fc2_full, preferred_element_type=jnp.float32) + vectors[7]
    ).astype(jnp.bfloat16)
    fc2_term = contract_rows(active_low, cotangent)
    fc2_bias_grad = jnp.sum(cotangent, axis=0, dtype=jnp.float32)
    active_back = contract_cols(cotangent, fc2_full)
    hidden_back = gelu_pullback(active_back)[0].astype(jnp.bfloat16)
    fc1_term = contract_rows(normed_two_low, hidden_back)
    fc1_bias_grad = jnp.sum(hidden_back, axis=0, dtype=jnp.float32)
    normed_two_back = contract_cols(hidden_back, fc1_full)
    middle_part, gain_two_grad, shift_two_grad = norm_two_pullback(normed_two_back)
    middle_back = cotangent.astype(jnp.float32) + middle_part
    branch_back = middle_back.astype(jnp.bfloat16)
    proj_term = contract_rows(context, branch_back)
    proj_bias_grad = jnp.sum(branch_back, axis=0, dtype=jnp.float32)
    context_back = (
        contract_cols(branch_back, proj_full)
        .astype(jnp.bfloat16)
        .reshape(local_windows, WT, head_count, head_size)
    )
    value_back = jnp.einsum(
        "whij,wihd->wjhd", attention, context_back, preferred_element_type=jnp.float32
    )
    probs_back = jnp.einsum(
        "wihd,wjhd->whij", context_back, valueset, preferred_element_type=jnp.float32
    )
    scores_back = (
        softmax_rows * (probs_back - jnp.sum(softmax_rows * probs_back, axis=-1, keepdims=True))
    ).astype(jnp.bfloat16)
    relative_back = jnp.sum(scores_back, axis=0, dtype=jnp.float32)
    table_grad = bias_pullback(relative_back)[0]
    query_back = (
        jnp.einsum("whij,wjhd->wihd", scores_back, keyset, preferred_element_type=jnp.float32)
        * score_scale
    )
    key_back = (
        jnp.einsum("whij,wihd->wjhd", scores_back, queries, preferred_element_type=jnp.float32)
        * score_scale
    )
    mixed_back = (
        jnp.stack([query_back, key_back, value_back], axis=2)
        .reshape(-1, 3 * model_width)
        .astype(jnp.bfloat16)
    )
    qkv_term = contract_rows(normed_one_low, mixed_back)
    query_bias_grad = jnp.sum(mixed_back[:, :model_width], axis=0, dtype=jnp.float32)
    value_bias_grad = jnp.sum(mixed_back[:, 2 * model_width :], axis=0, dtype=jnp.float32)
    normed_one_back = contract_cols(mixed_back, qkv_full)
    input_part, gain_one_grad, shift_one_grad = norm_one_pullback(normed_one_back)
    input_gradient = (middle_back + input_part).astype(jnp.bfloat16)
    vector_grad = jnp.concatenate(
        [
            jnp.stack(
                [
                    gain_one_grad,
                    shift_one_grad,
                    query_bias_grad,
                    value_bias_grad,
                    proj_bias_grad,
                    gain_two_grad,
                    shift_two_grad,
                    fc2_bias_grad,
                ]
            ),
            fc1_bias_grad.reshape(4, model_width),
        ]
    )
    low = jnp.bfloat16
    head_rows = table_grad.shape[0]
    small = jnp.concatenate([vector_grad.reshape(-1), table_grad.reshape(-1)])
    vector_size = vector_grad.size
    small_rows = -(-small.size // 1024) * 8
    small = jnp.pad(small, (0, small_rows * 128 - small.size)).reshape(small_rows, 128)
    small = lax.psum(small, ("rep", "grp")).reshape(-1)
    vector_total = small[:vector_size].reshape(vector_grad.shape)
    table_total = small[vector_size : vector_size + table_grad.size].reshape(head_rows, head_count)
    qkv_low, proj_low, fc1_low, fc2_low = (
        lax.psum(lax.psum_scatter(term.astype(low), "grp", scatter_dimension=0, tiled=True), "rep")
        for term in (qkv_term, proj_term, fc1_term, fc2_term)
    )
    qkv_gradient, proj_gradient, fc1_gradient, fc2_gradient = (
        part.astype(jnp.float32) for part in (qkv_low, proj_low, fc1_low, fc2_low)
    )
    qkv_whole, proj_whole, fc1_whole, fc2_whole = (
        lax.all_gather(part, "grp", axis=0, tiled=True)
        for part in (qkv_low, proj_low, fc1_low, fc2_low)
    )
    member = lax.axis_index("grp")
    small_roots = jnp.stack([roots_model[i] for i in (0, 2, 3, 4)]).astype(low)
    small_roots = lax.all_gather(small_roots, "grp", axis=1, tiled=True)

    def statistic_update(grad_rows, grad_whole, left_rows, right_rows):
        left_new = 0.5 * left_rows + 0.5 * contract_cols(grad_rows, grad_whole)
        row_span = right_rows.shape[0]
        columns = lax.dynamic_slice_in_dim(grad_whole, member * row_span, row_span, 1)
        right_new = 0.5 * right_rows + 0.5 * contract_rows(columns, grad_whole)
        return (left_new, right_new)

    def row_step(left_root_rows, grad_whole, right_root):
        product = jnp.dot(left_root_rows.astype(low), grad_whole, preferred_element_type=jnp.float32)
        return jnp.dot(product.astype(low), right_root, preferred_element_type=jnp.float32)

    def column_step(left_root, grad_whole, right_root_rows):
        product = contract_cols(grad_whole, right_root_rows.astype(low)).astype(low)
        columns = jnp.dot(left_root, product, preferred_element_type=jnp.float32).astype(low)
        return lax.all_to_all(columns, "grp", 0, 1, tiled=True).astype(jnp.float32)

    qkv_left, qkv_right = statistic_update(qkv_low, qkv_whole, stats_model[0], stats_qkv)
    proj_left, proj_right = statistic_update(proj_low, proj_whole, stats_model[1], stats_model[2])
    fc1_left, fc1_right = statistic_update(fc1_low, fc1_whole, stats_model[3], stats_hidden[0])
    fc2_left, fc2_right = statistic_update(fc2_low, fc2_whole, stats_hidden[1], stats_model[4])
    qkv_new = qkv_weight - column_step(small_roots[0], qkv_whole, roots_qkv)
    fc1_new = fc1_weight - column_step(small_roots[2], fc1_whole, roots_hidden[0])
    proj_new = proj_weight - row_step(roots_model[1], proj_whole, small_roots[1])
    fc2_new = fc2_weight - row_step(roots_hidden[1], fc2_whole, small_roots[3])
    new_stats_model = jnp.stack([qkv_left, proj_left, proj_right, fc1_left, fc2_right])
    new_stats_hidden = jnp.stack([fc1_right, fc2_left])
    total_tokens = tokens.shape[0] * lax.axis_size("rep") * lax.axis_size("grp")
    rate_base = total_tokens ** (-0.5)
    new_vector_moments = 0.9 * vector_moments + 0.1 * vector_total
    new_vectors = vectors - 2.0 * rate_base * new_vector_moments
    new_table_moments = 0.9 * table_moments + 0.1 * table_total
    new_table = bias_table - 8.0 * rate_base * new_table_moments
    return (
        layer_output,
        input_gradient,
        qkv_gradient,
        proj_gradient,
        fc1_gradient,
        fc2_gradient,
        qkv_new,
        proj_new,
        fc1_new,
        fc2_new,
        qkv_new.astype(jnp.bfloat16),
        proj_new.astype(jnp.bfloat16),
        fc1_new.astype(jnp.bfloat16),
        fc2_new.astype(jnp.bfloat16),
        new_stats_model,
        qkv_right,
        new_stats_hidden,
        new_vectors,
        new_vector_moments,
        new_table,
        new_table_moments,
    )


def solution(mesh):
    return jax.shard_map(
        shards,
        mesh=mesh,
        in_specs=(
            P(("rep", "grp"), None),
            P(("rep", "grp"), None),
            P(("rep", "grp")),
            P("grp", None),
            P("grp", None),
            P("grp", None),
            P("grp", None),
            P(),
            P(),
            P(),
            P(),
            P(None, "grp", None),
            P("grp", None),
            P(None, "grp", None),
            P(None, "grp", None),
            P("grp", None),
            P(None, "grp", None),
        ),
        out_specs=(
            P(("rep", "grp"), None),
            P(("rep", "grp"), None),
            P("grp", None),
            P("grp", None),
            P("grp", None),
            P("grp", None),
            P("grp", None),
            P("grp", None),
            P("grp", None),
            P("grp", None),
            P("grp", None),
            P("grp", None),
            P("grp", None),
            P("grp", None),
            P(None, "grp", None),
            P("grp", None),
            P(None, "grp", None),
            P(),
            P(),
            P(),
            P(),
        ),
        check_vma=False,
    )
```

```python
import functools

import jax
import jax.numpy as jnp
import numpy as np
from jax import lax
from jax.experimental import pallas as pl
from jax.experimental.pallas import tpu as pltpu
from jax.sharding import PartitionSpec as P

WT = 144
SIDE = 12
SPAN = 2 * SIDE - 1
LANES = 256
DIAG = 384
ROW_TILE = 144
MIB = 1024 * 1024
low = jnp.bfloat16
f32 = jnp.float32

ROWS_BY_COLS = (((1,), (0,)), ((), ()))
COLS_BY_COLS = (((1,), (1,)), ((), ()))
ROWS_BY_ROWS = (((0,), (0,)), ((), ()))


def dot(left_matrix, right_matrix, dims=ROWS_BY_COLS):
    return lax.dot_general(left_matrix, right_matrix, dims, preferred_element_type=f32)


def standardize(values):
    centred = values - jnp.mean(values, axis=-1, keepdims=True)
    inverse = lax.rsqrt(jnp.mean(centred * centred, axis=-1, keepdims=True) + 1e-05)
    return centred * inverse, inverse


def norm_back(grad, gain, xhat, inverse):
    scaled = grad * gain
    mean_scaled = jnp.mean(scaled, axis=-1, keepdims=True)
    mean_product = jnp.mean(scaled * xhat, axis=-1, keepdims=True)
    return inverse * (scaled - mean_scaled - xhat * mean_product)


def column_sum(values):
    return jnp.sum(values, axis=0, keepdims=True)


def diagonal_tables():
    pair = np.arange(DIAG) - WT
    quotient, rest = pair // SIDE, pair % SIDE
    near = (quotient + SIDE - 1) * SPAN + rest + SIDE - 1
    far = (quotient + SIDE) * SPAN + rest - 1
    near_live = (np.abs(pair) < WT) & (quotient >= 1 - SIDE)
    far_live = (np.abs(pair) < WT) & (rest >= 1) & (quotient < SIDE - 1)
    hot = np.zeros((2, DIAG, SPAN * SPAN), np.float32)
    hot[0, np.arange(DIAG)[near_live], near[near_live]] = 1.0
    hot[1, np.arange(DIAG)[far_live], far[far_live]] = 1.0
    return hot.reshape(2 * DIAG, SPAN * SPAN)


def near_mask(shape, mirrored=False):
    column = lax.rem(lax.broadcasted_iota(jnp.int32, shape, 0), SIDE)
    if mirrored:
        column = SIDE - 1 - column
    rest = lax.rem(lax.broadcasted_iota(jnp.int32, shape, 1), SIDE)
    return column + rest < SIDE


def additive_types(heads):
    slot = np.arange(WT)
    row_high, col_high = slot // SIDE >= SIDE // 2, slot % SIDE >= SIDE // 2
    row_differs = row_high[:, None] != row_high[None, :]
    col_differs = col_high[:, None] != col_high[None, :]
    types = [
        np.where((row_differs & bool(kind // 2)) | (col_differs & bool(kind % 2)), -100.0, 0.0)
        for kind in range(4)
    ]
    return np.tile(np.stack(types), (1, 1, heads)).astype(np.float32)


def stack_mask(heads, head_size):
    lane_head = np.arange(heads * head_size) // head_size
    hot = lane_head[None, None, :] == np.arange(heads)[:, None, None]
    return np.broadcast_to(hot, (heads, WT, heads * head_size)).reshape(heads * WT, -1).astype(low)


def relative_kernel(heads, diag_ref, rel_ref):
    mask = near_mask((WT, DIAG))
    for head in range(heads * rel_ref.shape[0]):
        group, place = head // heads, head % heads
        near = diag_ref[head : head + 1, :DIAG]
        far = diag_ref[head : head + 1, DIAG:]
        rows = jnp.where(mask, near, far)
        rolled = pltpu.roll(rows, DIAG - WT, 1, stride=1, stride_axis=0)
        rel_ref[group, :, place * WT : (place + 1) * WT] = rolled[:, :WT]


def relative_bias(diagonals, heads):
    head_count = diagonals.shape[0]
    return pl.pallas_call(
        functools.partial(relative_kernel, heads),
        out_shape=jax.ShapeDtypeStruct((head_count // heads, WT, heads * WT), f32),
        compiler_params=pltpu.CompilerParams(vmem_limit_bytes=32 * MIB),
        name="relative_bias",
    )(diagonals)


def stacked(block, mask_ref, heads):
    return jnp.concatenate([block] * heads, axis=0) * mask_ref[...]


def diagonal_blocks(full, heads, head_size):
    lane_head = lax.broadcasted_iota(jnp.int32, (WT, full.shape[1]), 1) // head_size
    picked = jnp.zeros((WT, full.shape[1]), f32)
    for head in range(heads):
        picked = jnp.where(lane_head == head, full[head * WT : (head + 1) * WT], picked)
    return picked


def forward_kernel(
    heads, head_size, fill_ref, base_ref, tokens_ref, qkv_ref, proj_ref, vec_ref, rel_ref, add_ref, mask_ref,
    probs_ref, mixed_out_ref, normed_t_ref, context_ref, middle_ref, normed_two_ref, normed_two_t_ref,
    mixed_ref, normed_ref, added_ref,
):
    window = pl.program_id(0)
    width = tokens_ref.shape[1]
    count = tokens_ref.shape[0]
    groups = width // LANES
    score_scale = head_size ** (-0.5)

    @pl.when(window == 0)
    def _():
        def norm_step(step, carry):
            rows = pl.ds(pl.multiple_of(step * ROW_TILE, ROW_TILE), ROW_TILE)
            xhat, _ = standardize(tokens_ref[rows, :].astype(f32))
            normed_ref[rows, :] = (xhat * vec_ref[0:1, :] + vec_ref[1:2, :]).astype(low)
            return carry

        lax.fori_loop(0, count // ROW_TILE, norm_step, 0)
        for part in range(3):
            for tile in range(groups):
                start = part * width + tile * LANES
                sums = dot(normed_ref[...], qkv_ref[:, start : start + LANES])
                if part != 1:
                    shift_row = 2 if part == 0 else 3
                    sums = sums + vec_ref[shift_row : shift_row + 1, tile * LANES : (tile + 1) * LANES]
                mixed_ref[:, start : start + LANES] = sums.astype(low)
        for tile in range(groups):
            span = slice(tile * LANES, (tile + 1) * LANES)
            normed_t_ref[span, :] = normed_ref[:, span].T

    rows = pl.ds(pl.multiple_of(window * WT, WT), WT)
    mixed_out_ref[...] = mixed_ref[rows, :]
    kind = lax.rem(base_ref[0] + window, 4)
    slot = lax.broadcasted_iota(jnp.int32, added_ref.shape, 0)
    added_ref[...] = jnp.where(slot < fill_ref[window], add_ref[kind], -1e30)
    for group in range(groups):
        span = slice(group * LANES, (group + 1) * LANES)
        query = mixed_ref[rows, span]
        key = mixed_ref[rows, width + group * LANES : width + (group + 1) * LANES]
        value = mixed_ref[rows, 2 * width + group * LANES : 2 * width + (group + 1) * LANES]
        scores = dot(key, stacked(query, mask_ref, heads), COLS_BY_COLS) * score_scale
        scores = scores + rel_ref[group] + added_ref[...]
        exponent = jnp.exp(scores - jnp.max(scores, axis=0, keepdims=True))
        probs = (exponent * (1.0 / jnp.sum(exponent, axis=0, keepdims=True))).astype(low)
        probs_ref[group] = probs
        full = dot(probs, value, ROWS_BY_ROWS)
        context_ref[rows, span] = diagonal_blocks(full, heads, head_size).astype(low)

    @pl.when(window == pl.num_programs(0) - 1)
    def _():
        for tile in range(groups):
            span = slice(tile * LANES, (tile + 1) * LANES)
            middle_ref[:, span] = (
                tokens_ref[:, span].astype(f32) + dot(context_ref[...], proj_ref[:, span]) + vec_ref[4:5, span]
            )

        def norm_step(step, carry):
            part = pl.ds(pl.multiple_of(step * ROW_TILE, ROW_TILE), ROW_TILE)
            xhat, _ = standardize(middle_ref[part, :])
            normed_two_ref[part, :] = (xhat * vec_ref[5:6, :] + vec_ref[6:7, :]).astype(low)
            return carry

        lax.fori_loop(0, count // ROW_TILE, norm_step, 0)
        for tile in range(groups):
            span = slice(tile * LANES, (tile + 1) * LANES)
            normed_two_t_ref[span, :] = normed_two_ref[:, span].T


def whole(shape):
    return pl.BlockSpec(shape, lambda *_: (0,) * len(shape), pipeline_mode=pl.Buffered(1))


def struct(shape, dtype):
    return jax.ShapeDtypeStruct(shape, dtype)


def attention_forward(fill, base, tokens, qkv_full, proj_full, vectors, relative, head_count):
    count, width = tokens.shape
    windows = fill.shape[0]
    head_size = width // head_count
    heads = LANES // head_size
    groups = width // LANES
    additive = jnp.asarray(additive_types(heads))
    mask = jnp.asarray(stack_mask(heads, head_size))
    smem = pl.BlockSpec(memory_space=pltpu.SMEM)
    return pl.pallas_call(
        functools.partial(forward_kernel, heads, head_size),
        grid=(windows,),
        in_specs=[smem, smem] + [whole(x.shape) for x in (tokens, qkv_full, proj_full, vectors, relative, additive, mask)],
        out_specs=[
            pl.BlockSpec((groups, WT, heads * WT), lambda w: (w, 0, 0)),
            pl.BlockSpec((WT, 3 * width), lambda w: (w, 0)),
            whole((width, count)),
            whole((count, width)),
            whole((count, width)),
            whole((count, width)),
            whole((width, count)),
        ],
        out_shape=[
            struct((windows * groups, WT, heads * WT), low),
            struct((count, 3 * width), low),
            struct((width, count), low),
            struct((count, width), low),
            struct((count, width), f32),
            struct((count, width), low),
            struct((width, count), low),
        ],
        scratch_shapes=[
            pltpu.VMEM((count, 3 * width), low),
            pltpu.VMEM((count, width), low),
            pltpu.VMEM((WT, heads * WT), f32),
        ],
        compiler_params=pltpu.CompilerParams(vmem_limit_bytes=56 * MIB),
        name="attention_forward",
    )(fill, base, tokens, qkv_full, proj_full, vectors, relative, additive, mask)


def feed_forward_kernel(
    normed_ref, normed_t_ref, cot_ref, middle_ref, fc1_ref, fc2_ref, bias_ref, vec_ref,
    out_ref, middle_back_ref, branch_back_ref, fc1_grad_ref, fc2_grad_ref, bias_grad_ref, vec_grad_ref,
    out_sum, back_sum,
):
    step = pl.program_id(0)
    count, width = cot_ref.shape
    hidden = dot(normed_ref[...], fc1_ref[...]) + bias_ref[...]
    bell = jnp.exp(hidden * hidden * -0.5)
    below = 0.5 * (1.0 + lax.erf(hidden * (0.5 ** 0.5)))
    active = (hidden * below).astype(low)
    slope = below + hidden * bell * ((2.0 * np.pi) ** -0.5)
    hidden_back = dot(cot_ref[...], fc2_ref[...], COLS_BY_COLS) * slope
    hidden_back = hidden_back.astype(low)
    bias_grad_ref[...] = column_sum(hidden_back.astype(f32))
    fc2_grad_ref[...] = dot(active, cot_ref[...], ROWS_BY_ROWS).astype(low)
    fc1_grad_ref[...] = dot(normed_t_ref[...], hidden_back).astype(low)
    out_term = dot(active, fc2_ref[...])
    back_term = dot(hidden_back, fc1_ref[...], COLS_BY_COLS)

    @pl.when(step == 0)
    def _():
        out_sum[...] = out_term
        back_sum[...] = back_term

    @pl.when(step > 0)
    def _():
        out_sum[...] += out_term
        back_sum[...] += back_term

    @pl.when(step == pl.num_programs(0) - 1)
    def _():
        vec_grad_ref[...] = jnp.zeros_like(vec_grad_ref)

        def finish(part, carry):
            rows = pl.ds(pl.multiple_of(part * ROW_TILE, ROW_TILE), ROW_TILE)
            middle = middle_ref[rows, :]
            cot = cot_ref[rows, :].astype(f32)
            out_ref[rows, :] = (middle + out_sum[rows, :] + vec_ref[7:8, :]).astype(low)
            xhat, inverse = standardize(middle)
            grad = back_sum[rows, :]
            middle_back = cot + norm_back(grad, vec_ref[5:6, :], xhat, inverse)
            middle_back_ref[rows, :] = middle_back
            branch_back = middle_back.astype(low)
            branch_back_ref[rows, :] = branch_back
            vec_grad_ref[0:1, :] += column_sum(branch_back.astype(f32))
            vec_grad_ref[1:2, :] += column_sum(grad * xhat)
            vec_grad_ref[2:3, :] += column_sum(grad)
            vec_grad_ref[3:4, :] += column_sum(cot)
            return carry

        lax.fori_loop(0, count // ROW_TILE, finish, 0)


def feed_forward(normed, normed_t, cotangent, middle, fc1_full, fc2_full, vectors):
    count, width = cotangent.shape
    hidden_width = fc1_full.shape[1]
    tile = LANES
    bias = vectors[8:].reshape(1, hidden_width)
    return pl.pallas_call(
        feed_forward_kernel,
        grid=(hidden_width // tile,),
        in_specs=[whole(x.shape) for x in (normed, normed_t, cotangent, middle)]
        + [
            pl.BlockSpec((width, tile), lambda f: (0, f)),
            pl.BlockSpec((tile, width), lambda f: (f, 0)),
            pl.BlockSpec((1, tile), lambda f: (0, f)),
            whole(vectors.shape),
        ],
        out_specs=[
            whole((count, width)),
            whole((count, width)),
            whole((count, width)),
            pl.BlockSpec((width, tile), lambda f: (0, f)),
            pl.BlockSpec((tile, width), lambda f: (f, 0)),
            pl.BlockSpec((1, tile), lambda f: (0, f)),
            whole((8, width)),
        ],
        out_shape=[
            struct((count, width), low),
            struct((count, width), f32),
            struct((count, width), low),
            struct((width, hidden_width), low),
            struct((hidden_width, width), low),
            struct((1, hidden_width), f32),
            struct((8, width), f32),
        ],
        scratch_shapes=[pltpu.VMEM((count, width), f32), pltpu.VMEM((count, width), f32)],
        compiler_params=pltpu.CompilerParams(vmem_limit_bytes=56 * MIB),
        name="feed_forward",
    )(normed, normed_t, cotangent, middle, fc1_full, fc2_full, bias, vectors)


def backward_kernel(
    heads, head_size, probs_ref, mixed_ref, branch_back_ref, middle_back_ref, proj_ref, context_ref, normed_t_ref,
    tokens_ref, qkv_ref, vec_ref, mask_ref,
    input_grad_ref, qkv_grad_ref, proj_grad_ref, vec_grad_ref, diag_ref,
    context_back_ref, mixed_back_ref, pairs_ref, normed_back_ref,
):
    window = pl.program_id(0)
    count, width = tokens_ref.shape
    groups = width // LANES
    score_scale = head_size ** (-0.5)

    @pl.when(window == 0)
    def _():
        pairs_ref[...] = jnp.zeros_like(pairs_ref)
        for tile in range(groups):
            span = slice(tile * LANES, (tile + 1) * LANES)
            context_back_ref[:, span] = dot(branch_back_ref[...], proj_ref[span, :], COLS_BY_COLS).astype(low)
            proj_grad_ref[span, :] = dot(context_ref[:, span], branch_back_ref[...], ROWS_BY_ROWS).astype(low)

    rows = pl.ds(pl.multiple_of(window * WT, WT), WT)
    for group in range(groups):
        spans = [slice(part * width + group * LANES, part * width + (group + 1) * LANES) for part in range(3)]
        query, key, value = (mixed_ref[:, span] for span in spans)
        probs_low = probs_ref[group]
        probs = probs_low.astype(f32)
        back_stack = stacked(context_back_ref[rows, spans[0]], mask_ref, heads)
        value_back = dot(probs_low, back_stack)
        product = probs * dot(value, back_stack, COLS_BY_COLS)
        scores_back = (product - probs * jnp.sum(product, axis=0, keepdims=True)).astype(low)
        pairs_ref[group] += scores_back.astype(f32)
        key_back = dot(scores_back, stacked(query, mask_ref, heads)) * score_scale
        full = dot(scores_back, key, ROWS_BY_ROWS)
        query_back = diagonal_blocks(full, heads, head_size) * score_scale
        mixed_back_ref[rows, spans[0]] = query_back.astype(low)
        mixed_back_ref[rows, spans[1]] = key_back.astype(low)
        mixed_back_ref[rows, spans[2]] = value_back.astype(low)

    @pl.when(window == pl.num_programs(0) - 1)
    def _():
        vec_grad_ref[...] = jnp.zeros_like(vec_grad_ref)
        for part in range(3):
            for tile in range(groups):
                start = part * width + tile * LANES
                block = mixed_back_ref[:, start : start + LANES]
                qkv_grad_ref[:, start : start + LANES] = dot(normed_t_ref[...], block).astype(low)
                if part != 1:
                    row = 2 if part == 0 else 3
                    span = slice(tile * LANES, (tile + 1) * LANES)
                    vec_grad_ref[row : row + 1, span] = column_sum(block.astype(f32))
        for tile in range(groups):
            span = slice(tile * LANES, (tile + 1) * LANES)
            normed_back_ref[:, span] = dot(mixed_back_ref[...], qkv_ref[span, :], COLS_BY_COLS)

        def finish(part, carry):
            rows = pl.ds(pl.multiple_of(part * ROW_TILE, ROW_TILE), ROW_TILE)
            xhat, inverse = standardize(tokens_ref[rows, :].astype(f32))
            grad = normed_back_ref[rows, :]
            back = middle_back_ref[rows, :] + norm_back(grad, vec_ref[0:1, :], xhat, inverse)
            input_grad_ref[rows, :] = back.astype(low)
            vec_grad_ref[0:1, :] += column_sum(grad * xhat)
            vec_grad_ref[1:2, :] += column_sum(grad)
            return carry

        lax.fori_loop(0, count // ROW_TILE, finish, 0)
        mask = near_mask((WT, DIAG), mirrored=True)
        order = [lax.broadcasted_iota(jnp.int32, (WT, WT), axis) for axis in range(2)]
        mirror = jnp.where(order[0] + order[1] == WT - 1, 1.0, 0.0).astype(f32)
        for group in range(groups):
            pairs_ref[group] = lax.dot_general(
                mirror, pairs_ref[group], ROWS_BY_COLS, precision=lax.Precision.HIGHEST, preferred_element_type=f32
            )
        for head in range(groups * heads):
            group, place = head // heads, head % heads
            block = pairs_ref[group, :, place * WT : (place + 1) * WT]
            block = jnp.concatenate([block, jnp.zeros((WT, DIAG - WT), f32)], axis=1)
            rolled = pltpu.roll(block, 1, 1, stride=1, stride_axis=0)
            near = column_sum(jnp.where(mask, rolled, 0.0))
            far = column_sum(jnp.where(mask, 0.0, rolled))
            diag_ref[head : head + 1, :DIAG] = near
            diag_ref[head : head + 1, DIAG:] = far


def attention_backward(
    probs, mixed, branch_back, middle_back, proj_full, context, normed_t, tokens, qkv_full, vectors, head_count
):
    count, width = tokens.shape
    windows = count // WT
    head_size = width // head_count
    heads = LANES // head_size
    groups = width // LANES
    mask = jnp.asarray(stack_mask(heads, head_size))
    return pl.pallas_call(
        functools.partial(backward_kernel, heads, head_size),
        grid=(windows,),
        in_specs=[
            pl.BlockSpec((groups, WT, heads * WT), lambda w: (w, 0, 0)),
            pl.BlockSpec((WT, 3 * width), lambda w: (w, 0)),
        ]
        + [
            whole(x.shape)
            for x in (branch_back, middle_back, proj_full, context, normed_t, tokens, qkv_full, vectors, mask)
        ],
        out_specs=[
            whole((count, width)),
            whole((width, 3 * width)),
            whole((width, width)),
            whole((8, width)),
            whole((head_count, 2 * DIAG)),
        ],
        out_shape=[
            struct((count, width), low),
            struct((width, 3 * width), low),
            struct((width, width), low),
            struct((8, width), f32),
            struct((head_count, 2 * DIAG), f32),
        ],
        scratch_shapes=[
            pltpu.VMEM((count, width), low),
            pltpu.VMEM((count, 3 * width), low),
            pltpu.VMEM((groups, WT, heads * WT), f32),
            pltpu.VMEM((count, width), f32),
        ],
        compiler_params=pltpu.CompilerParams(vmem_limit_bytes=60 * MIB),
        name="attention_backward",
    )(probs, mixed, branch_back, middle_back, proj_full, context, normed_t, tokens, qkv_full, vectors, mask)


def shards(
    tokens, cotangent, window_fill, qkv_weight, proj_weight, fc1_weight, fc2_weight, vectors, vector_moments,
    bias_table, table_moments, stats_model, stats_qkv, stats_hidden, roots_model, roots_qkv, roots_hidden,
):
    width = vectors.shape[1]
    head_count = bias_table.shape[1]
    heads = LANES // (width // head_count)
    local_windows = window_fill.shape[0]
    base = (lax.axis_index(("rep", "grp")) * local_windows).astype(jnp.int32).reshape(1)
    gather = functools.partial(lax.all_gather, axis_name="grp", tiled=True)
    qkv_full, proj_full, fc1_full, fc2_full = (
        gather(weight.astype(low)) for weight in (qkv_weight, proj_weight, fc1_weight, fc2_weight)
    )
    hot = jnp.asarray(diagonal_tables())
    diagonals = lax.dot_general(bias_table, hot, (((0,), (1,)), ((), ())), precision=lax.Precision.HIGHEST)
    relative = relative_bias(diagonals, heads)
    probs, mixed, normed_t, context, middle, normed_two, normed_two_t = attention_forward(
        window_fill, base, tokens, qkv_full, proj_full, vectors, relative, head_count
    )
    layer_output, middle_back, branch_back, fc1_term, fc2_term, fc1_bias_grad, ffn_vec = feed_forward(
        normed_two, normed_two_t, cotangent, middle, fc1_full, fc2_full, vectors
    )
    input_gradient, qkv_term, proj_term, att_vec, diag_grad = attention_backward(
        probs, mixed, branch_back, middle_back, proj_full, context, normed_t, tokens, qkv_full, vectors, head_count
    )
    small = jnp.concatenate([part.reshape(-1, 128) for part in (att_vec[:4], ffn_vec[:4], fc1_bias_grad, diag_grad)])
    small = lax.psum(small, ("rep", "grp"))
    vector_total = small[: vectors.size // 128].reshape(vectors.shape)
    table_total = lax.dot_general(
        hot, small[vectors.size // 128 :].reshape(diag_grad.shape), (((0,), (1,)), ((), ())), precision=lax.Precision.HIGHEST
    )
    qkv_low, proj_low, fc1_low, fc2_low = (
        lax.psum(lax.psum_scatter(term, "grp", scatter_dimension=0, tiled=True), "rep")
        for term in (qkv_term, proj_term, fc1_term, fc2_term)
    )
    qkv_whole, proj_whole, fc1_whole, fc2_whole = (gather(part) for part in (qkv_low, proj_low, fc1_low, fc2_low))
    member = lax.axis_index("grp")
    small_roots = jnp.stack([roots_model[i] for i in (0, 2, 3, 4)]).astype(low)
    small_roots = gather(small_roots, axis=1)

    def statistic_update(grad_rows, grad_whole, left_rows, right_rows):
        left_new = 0.5 * left_rows + 0.5 * dot(grad_rows, grad_whole, COLS_BY_COLS)
        row_span = right_rows.shape[0]
        columns = lax.dynamic_slice_in_dim(grad_whole, member * row_span, row_span, 1)
        right_new = 0.5 * right_rows + 0.5 * dot(columns, grad_whole, ROWS_BY_ROWS)
        return (left_new, right_new)

    def row_step(left_root_rows, grad_whole, right_root):
        product = dot(left_root_rows.astype(low), grad_whole)
        return dot(product.astype(low), right_root)

    def column_step(left_root, grad_whole, right_root_rows):
        product = dot(grad_whole, right_root_rows.astype(low), COLS_BY_COLS).astype(low)
        columns = dot(left_root, product).astype(low)
        return lax.all_to_all(columns, "grp", 0, 1, tiled=True).astype(f32)

    qkv_left, qkv_right = statistic_update(qkv_low, qkv_whole, stats_model[0], stats_qkv)
    proj_left, proj_right = statistic_update(proj_low, proj_whole, stats_model[1], stats_model[2])
    fc1_left, fc1_right = statistic_update(fc1_low, fc1_whole, stats_model[3], stats_hidden[0])
    fc2_left, fc2_right = statistic_update(fc2_low, fc2_whole, stats_hidden[1], stats_model[4])
    qkv_new = qkv_weight - column_step(small_roots[0], qkv_whole, roots_qkv)
    fc1_new = fc1_weight - column_step(small_roots[2], fc1_whole, roots_hidden[0])
    proj_new = proj_weight - row_step(roots_model[1], proj_whole, small_roots[1])
    fc2_new = fc2_weight - row_step(roots_hidden[1], fc2_whole, small_roots[3])
    new_stats_model = jnp.stack([qkv_left, proj_left, proj_right, fc1_left, fc2_right])
    new_stats_hidden = jnp.stack([fc1_right, fc2_left])
    total_tokens = tokens.shape[0] * lax.axis_size("rep") * lax.axis_size("grp")
    rate_base = total_tokens ** (-0.5)
    new_vector_moments = 0.9 * vector_moments + 0.1 * vector_total
    new_vectors = vectors - 2.0 * rate_base * new_vector_moments
    new_table_moments = 0.9 * table_moments + 0.1 * table_total
    new_table = bias_table - 8.0 * rate_base * new_table_moments
    masters = (qkv_new, proj_new, fc1_new, fc2_new)
    return (
        (layer_output, input_gradient)
        + tuple(part.astype(f32) for part in (qkv_low, proj_low, fc1_low, fc2_low))
        + masters
        + tuple(master.astype(low) for master in masters)
        + (new_stats_model, qkv_right, new_stats_hidden, new_vectors, new_vector_moments, new_table, new_table_moments)
    )


def solution(mesh):
    tokens, rows, blocks, copied = P(("rep", "grp"), None), P("grp", None), P(None, "grp", None), P()
    return jax.shard_map(
        shards,
        mesh=mesh,
        in_specs=(tokens, tokens, P(("rep", "grp")))
        + (rows,) * 4
        + (copied,) * 4
        + (blocks, rows, blocks) * 2,
        out_specs=(tokens,) * 2 + (rows,) * 12 + (blocks, rows, blocks) + (copied,) * 4,
        check_vma=False,
    )
```

```python
import functools

import jax
import jax.numpy as jnp
import numpy as np
from jax import lax
from jax.experimental import pallas as pl
from jax.experimental.pallas import tpu as pltpu
from jax.sharding import PartitionSpec as P

WT = 144
SIDE = 12
SPAN = 2 * SIDE - 1
LANES = 256
DIAG = 384
ROW_TILE = 144
MIB = 1024 * 1024
low = jnp.bfloat16
f32 = jnp.float32

ROWS_BY_COLS = (((1,), (0,)), ((), ()))
COLS_BY_COLS = (((1,), (1,)), ((), ()))
ROWS_BY_ROWS = (((0,), (0,)), ((), ()))


def dot(left_matrix, right_matrix, dims=ROWS_BY_COLS):
    return lax.dot_general(left_matrix, right_matrix, dims, preferred_element_type=f32)


def standardize(values):
    centred = values - jnp.mean(values, axis=-1, keepdims=True)
    inverse = lax.rsqrt(jnp.mean(centred * centred, axis=-1, keepdims=True) + 1e-05)
    return centred * inverse, inverse


def norm_back(grad, gain, xhat, inverse):
    scaled = grad * gain
    mean_scaled = jnp.mean(scaled, axis=-1, keepdims=True)
    mean_product = jnp.mean(scaled * xhat, axis=-1, keepdims=True)
    return inverse * (scaled - mean_scaled - xhat * mean_product)


def column_sum(values):
    return jnp.sum(values, axis=0, keepdims=True)


def diagonal_tables():
    pair = np.arange(DIAG) - WT
    quotient, rest = pair // SIDE, pair % SIDE
    near = (quotient + SIDE - 1) * SPAN + rest + SIDE - 1
    far = (quotient + SIDE) * SPAN + rest - 1
    near_live = (np.abs(pair) < WT) & (quotient >= 1 - SIDE)
    far_live = (np.abs(pair) < WT) & (rest >= 1) & (quotient < SIDE - 1)
    hot = np.zeros((2, DIAG, SPAN * SPAN), np.float32)
    hot[0, np.arange(DIAG)[near_live], near[near_live]] = 1.0
    hot[1, np.arange(DIAG)[far_live], far[far_live]] = 1.0
    return hot.reshape(2 * DIAG, SPAN * SPAN)


def near_mask(shape, mirrored=False):
    column = lax.rem(lax.broadcasted_iota(jnp.int32, shape, 0), SIDE)
    if mirrored:
        column = SIDE - 1 - column
    rest = lax.rem(lax.broadcasted_iota(jnp.int32, shape, 1), SIDE)
    return column + rest < SIDE


def additive_types(heads):
    slot = np.arange(WT)
    row_high, col_high = slot // SIDE >= SIDE // 2, slot % SIDE >= SIDE // 2
    row_differs = row_high[:, None] != row_high[None, :]
    col_differs = col_high[:, None] != col_high[None, :]
    types = [
        np.where((row_differs & bool(kind // 2)) | (col_differs & bool(kind % 2)), -100.0, 0.0)
        for kind in range(4)
    ]
    return np.tile(np.stack(types), (1, 1, heads)).astype(np.float32)


def stack_mask(heads, head_size):
    lane_head = np.arange(heads * head_size) // head_size
    hot = lane_head[None, None, :] == np.arange(heads)[:, None, None]
    return np.broadcast_to(hot, (heads, WT, heads * head_size)).reshape(heads * WT, -1).astype(low)


def relative_kernel(heads, diag_ref, rel_ref):
    mask = near_mask((WT, DIAG))
    for head in range(heads * rel_ref.shape[0]):
        group, place = head // heads, head % heads
        near = diag_ref[head : head + 1, :DIAG]
        far = diag_ref[head : head + 1, DIAG:]
        rows = jnp.where(mask, near, far)
        rolled = pltpu.roll(rows, DIAG - WT, 1, stride=1, stride_axis=0)
        rel_ref[group, :, place * WT : (place + 1) * WT] = rolled[:, :WT]


def relative_bias(diagonals, heads):
    head_count = diagonals.shape[0]
    return pl.pallas_call(
        functools.partial(relative_kernel, heads),
        out_shape=jax.ShapeDtypeStruct((head_count // heads, WT, heads * WT), f32),
        compiler_params=pltpu.CompilerParams(vmem_limit_bytes=32 * MIB),
        name="relative_bias",
    )(diagonals)


def stacked(block, mask_ref, heads):
    return jnp.concatenate([block] * heads, axis=0) * mask_ref[...]


def diagonal_blocks(full, heads, head_size):
    lane_head = lax.broadcasted_iota(jnp.int32, (WT, full.shape[1]), 1) // head_size
    picked = jnp.zeros((WT, full.shape[1]), f32)
    for head in range(heads):
        picked = jnp.where(lane_head == head, full[head * WT : (head + 1) * WT], picked)
    return picked


def forward_kernel(
    heads, head_size, fill_ref, base_ref, tokens_ref, qkv_ref, proj_ref, vec_ref, rel_ref, add_ref, mask_ref,
    probs_ref, mixed_out_ref, normed_ref, context_ref, middle_ref, normedwo_ref,
    mixed_ref, added_ref,
):
    window = pl.program_id(0)
    width = tokens_ref.shape[1]
    count = tokens_ref.shape[0]
    groups = width // LANES
    score_scale = head_size ** (-0.5)

    @pl.when(window == 0)
    def _():
        def norm_step(step, carry):
            rows = pl.ds(pl.multiple_of(step * ROW_TILE, ROW_TILE), ROW_TILE)
            xhat, _ = standardize(tokens_ref[rows, :].astype(f32))
            normed_ref[rows, :] = (xhat * vec_ref[0:1, :] + vec_ref[1:2, :]).astype(low)
            return carry

        lax.fori_loop(0, count // ROW_TILE, norm_step, 0)
        for part in range(3):
            for tile in range(groups):
                start = part * width + tile * LANES
                sums = dot(normed_ref[...], qkv_ref[:, start : start + LANES])
                if part != 1:
                    shift_row = 2 if part == 0 else 3
                    sums = sums + vec_ref[shift_row : shift_row + 1, tile * LANES : (tile + 1) * LANES]
                mixed_ref[:, start : start + LANES] = sums.astype(low)

    rows = pl.ds(pl.multiple_of(window * WT, WT), WT)
    mixed_out_ref[...] = mixed_ref[rows, :]
    kind = lax.rem(base_ref[0] + window, 4)
    slot = lax.broadcasted_iota(jnp.int32, added_ref.shape, 0)
    added_ref[...] = jnp.where(slot < fill_ref[window], add_ref[kind], -1e30)
    for group in range(groups):
        span = slice(group * LANES, (group + 1) * LANES)
        query = mixed_ref[rows, span]
        key = mixed_ref[rows, width + group * LANES : width + (group + 1) * LANES]
        value = mixed_ref[rows, 2 * width + group * LANES : 2 * width + (group + 1) * LANES]
        scores = dot(key, stacked(query, mask_ref, heads), COLS_BY_COLS) * score_scale
        scores = scores + rel_ref[group] + added_ref[...]
        exponent = jnp.exp(scores - jnp.max(scores, axis=0, keepdims=True))
        probs = (exponent * (1.0 / jnp.sum(exponent, axis=0, keepdims=True))).astype(low)
        probs_ref[group] = probs
        full = dot(probs, value, ROWS_BY_ROWS)
        context_ref[rows, span] = diagonal_blocks(full, heads, head_size).astype(low)

    @pl.when(window == pl.num_programs(0) - 1)
    def _():
        for tile in range(groups):
            span = slice(tile * LANES, (tile + 1) * LANES)
            middle_ref[:, span] = (
                tokens_ref[:, span].astype(f32) + dot(context_ref[...], proj_ref[:, span]) + vec_ref[4:5, span]
            )

        def norm_step(step, carry):
            part = pl.ds(pl.multiple_of(step * ROW_TILE, ROW_TILE), ROW_TILE)
            xhat, _ = standardize(middle_ref[part, :])
            normedwo_ref[part, :] = (xhat * vec_ref[5:6, :] + vec_ref[6:7, :]).astype(low)
            return carry

        lax.fori_loop(0, count // ROW_TILE, norm_step, 0)


def whole(shape):
    return pl.BlockSpec(shape, lambda *_: (0,) * len(shape), pipeline_mode=pl.Buffered(1))


def struct(shape, dtype):
    return jax.ShapeDtypeStruct(shape, dtype)


def attention_forward(fill, base, tokens, qkv_full, proj_full, vectors, relative, head_count):
    count, width = tokens.shape
    windows = fill.shape[0]
    head_size = width // head_count
    heads = LANES // head_size
    groups = width // LANES
    additive = jnp.asarray(additive_types(heads))
    mask = jnp.asarray(stack_mask(heads, head_size))
    smem = pl.BlockSpec(memory_space=pltpu.SMEM)
    return pl.pallas_call(
        functools.partial(forward_kernel, heads, head_size),
        grid=(windows,),
        in_specs=[smem, smem] + [whole(x.shape) for x in (tokens, qkv_full, proj_full, vectors, relative, additive, mask)],
        out_specs=[
            pl.BlockSpec((groups, WT, heads * WT), lambda w: (w, 0, 0)),
            pl.BlockSpec((WT, 3 * width), lambda w: (w, 0)),
            whole((count, width)),
            whole((count, width)),
            whole((count, width)),
            whole((count, width)),
        ],
        out_shape=[
            struct((windows * groups, WT, heads * WT), low),
            struct((count, 3 * width), low),
            struct((count, width), low),
            struct((count, width), low),
            struct((count, width), f32),
            struct((count, width), low),
        ],
        scratch_shapes=[
            pltpu.VMEM((count, 3 * width), low),
            pltpu.VMEM((WT, heads * WT), f32),
        ],
        compiler_params=pltpu.CompilerParams(vmem_limit_bytes=56 * MIB),
        name="attention_forward",
    )(fill, base, tokens, qkv_full, proj_full, vectors, relative, additive, mask)


def feed_forward_kernel(
    normed_ref, cot_ref, middle_ref, fc1_ref, fc2_ref, bias_ref, vec_ref,
    out_ref, middle_back_ref, branch_back_ref, fc1_grad_ref, fc2_grad_ref, bias_grad_ref, vec_grad_ref,
    out_sum, back_sum,
):
    step = pl.program_id(0)
    count, width = cot_ref.shape
    hidden = dot(normed_ref[...], fc1_ref[...]) + bias_ref[...]
    bell = jnp.exp(hidden * hidden * -0.5)
    below = 0.5 * (1.0 + lax.erf(hidden * (0.5 ** 0.5)))
    active = (hidden * below).astype(low)
    slope = below + hidden * bell * ((2.0 * np.pi) ** -0.5)
    hidden_back = dot(cot_ref[...], fc2_ref[...], COLS_BY_COLS) * slope
    hidden_back = hidden_back.astype(low)
    bias_grad_ref[...] = column_sum(hidden_back.astype(f32))
    fc2_grad_ref[...] = dot(active, cot_ref[...], ROWS_BY_ROWS).astype(low)
    fc1_grad_ref[...] = dot(hidden_back, normed_ref[...], ROWS_BY_ROWS).astype(low)
    out_term = dot(active, fc2_ref[...])
    back_term = dot(hidden_back, fc1_ref[...], COLS_BY_COLS)

    @pl.when(step == 0)
    def _():
        out_sum[...] = out_term
        back_sum[...] = back_term

    @pl.when(step > 0)
    def _():
        out_sum[...] += out_term
        back_sum[...] += back_term

    @pl.when(step == pl.num_programs(0) - 1)
    def _():
        vec_grad_ref[...] = jnp.zeros_like(vec_grad_ref)

        def finish(part, carry):
            rows = pl.ds(pl.multiple_of(part * ROW_TILE, ROW_TILE), ROW_TILE)
            middle = middle_ref[rows, :]
            cot = cot_ref[rows, :].astype(f32)
            out_ref[rows, :] = (middle + out_sum[rows, :] + vec_ref[7:8, :]).astype(low)
            xhat, inverse = standardize(middle)
            grad = back_sum[rows, :]
            middle_back = cot + norm_back(grad, vec_ref[5:6, :], xhat, inverse)
            middle_back_ref[rows, :] = middle_back
            branch_back = middle_back.astype(low)
            branch_back_ref[rows, :] = branch_back
            vec_grad_ref[0:1, :] += column_sum(branch_back.astype(f32))
            vec_grad_ref[1:2, :] += column_sum(grad * xhat)
            vec_grad_ref[2:3, :] += column_sum(grad)
            vec_grad_ref[3:4, :] += column_sum(cot)
            return carry

        lax.fori_loop(0, count // ROW_TILE, finish, 0)


def feed_forward(normed, cotangent, middle, fc1_full, fc2_full, vectors):
    count, width = cotangent.shape
    hidden_width = fc1_full.shape[1]
    tile = LANES
    bias = vectors[8:].reshape(1, hidden_width)
    return pl.pallas_call(
        feed_forward_kernel,
        grid=(hidden_width // tile,),
        in_specs=[whole(x.shape) for x in (normed, cotangent, middle)]
        + [
            pl.BlockSpec((width, tile), lambda f: (0, f)),
            pl.BlockSpec((tile, width), lambda f: (f, 0)),
            pl.BlockSpec((1, tile), lambda f: (0, f)),
            whole(vectors.shape),
        ],
        out_specs=[
            whole((count, width)),
            whole((count, width)),
            whole((count, width)),
            pl.BlockSpec((tile, width), lambda f: (f, 0)),
            pl.BlockSpec((tile, width), lambda f: (f, 0)),
            pl.BlockSpec((1, tile), lambda f: (0, f)),
            whole((8, width)),
        ],
        out_shape=[
            struct((count, width), low),
            struct((count, width), f32),
            struct((count, width), low),
            struct((hidden_width, width), low),
            struct((hidden_width, width), low),
            struct((1, hidden_width), f32),
            struct((8, width), f32),
        ],
        scratch_shapes=[pltpu.VMEM((count, width), f32), pltpu.VMEM((count, width), f32)],
        compiler_params=pltpu.CompilerParams(vmem_limit_bytes=56 * MIB),
        name="feed_forward",
    )(normed, cotangent, middle, fc1_full, fc2_full, bias, vectors)


def backward_kernel(
    heads, head_size, probs_ref, mixed_ref, branch_back_ref, middle_back_ref, proj_ref, context_ref, normed_ref,
    tokens_ref, qkv_ref, vec_ref, mask_ref,
    input_grad_ref, weight_grad_ref, vec_grad_ref, diag_ref,
    context_back_ref, mixed_back_ref, pairs_ref, normed_back_ref,
):
    window = pl.program_id(0)
    count, width = tokens_ref.shape
    groups = width // LANES
    score_scale = head_size ** (-0.5)

    @pl.when(window == 0)
    def _():
        pairs_ref[...] = jnp.zeros_like(pairs_ref)
        for tile in range(groups):
            span = slice(tile * LANES, (tile + 1) * LANES)
            context_back_ref[:, span] = dot(branch_back_ref[...], proj_ref[span, :], COLS_BY_COLS).astype(low)
            weight_grad_ref[3 * width + tile * LANES : 3 * width + (tile + 1) * LANES, :] = dot(
                context_ref[:, span], branch_back_ref[...], ROWS_BY_ROWS
            ).astype(low)

    rows = pl.ds(pl.multiple_of(window * WT, WT), WT)
    for group in range(groups):
        spans = [slice(part * width + group * LANES, part * width + (group + 1) * LANES) for part in range(3)]
        query, key, value = (mixed_ref[:, span] for span in spans)
        probs_low = probs_ref[group]
        probs = probs_low.astype(f32)
        back_stack = stacked(context_back_ref[rows, spans[0]], mask_ref, heads)
        value_back = dot(probs_low, back_stack)
        product = probs * dot(value, back_stack, COLS_BY_COLS)
        scores_back = (product - probs * jnp.sum(product, axis=0, keepdims=True)).astype(low)
        pairs_ref[group] += scores_back.astype(f32)
        key_back = dot(scores_back, stacked(query, mask_ref, heads)) * score_scale
        full = dot(scores_back, key, ROWS_BY_ROWS)
        query_back = diagonal_blocks(full, heads, head_size) * score_scale
        mixed_back_ref[rows, spans[0]] = query_back.astype(low)
        mixed_back_ref[rows, spans[1]] = key_back.astype(low)
        mixed_back_ref[rows, spans[2]] = value_back.astype(low)

    @pl.when(window == pl.num_programs(0) - 1)
    def _():
        vec_grad_ref[...] = jnp.zeros_like(vec_grad_ref)
        for part in range(3):
            for tile in range(groups):
                start = part * width + tile * LANES
                block = mixed_back_ref[:, start : start + LANES]
                weight_grad_ref[start : start + LANES, :] = dot(block, normed_ref[...], ROWS_BY_ROWS).astype(low)
                if part != 1:
                    row = 2 if part == 0 else 3
                    span = slice(tile * LANES, (tile + 1) * LANES)
                    vec_grad_ref[row : row + 1, span] = column_sum(block.astype(f32))
        for tile in range(groups):
            span = slice(tile * LANES, (tile + 1) * LANES)
            normed_back_ref[:, span] = dot(mixed_back_ref[...], qkv_ref[span, :], COLS_BY_COLS)

        def finish(part, carry):
            rows = pl.ds(pl.multiple_of(part * ROW_TILE, ROW_TILE), ROW_TILE)
            xhat, inverse = standardize(tokens_ref[rows, :].astype(f32))
            grad = normed_back_ref[rows, :]
            back = middle_back_ref[rows, :] + norm_back(grad, vec_ref[0:1, :], xhat, inverse)
            input_grad_ref[rows, :] = back.astype(low)
            vec_grad_ref[0:1, :] += column_sum(grad * xhat)
            vec_grad_ref[1:2, :] += column_sum(grad)
            return carry

        lax.fori_loop(0, count // ROW_TILE, finish, 0)
        mask = near_mask((WT, DIAG), mirrored=True)
        order = [lax.broadcasted_iota(jnp.int32, (WT, WT), axis) for axis in range(2)]
        mirror = jnp.where(order[0] + order[1] == WT - 1, 1.0, 0.0).astype(f32)
        for group in range(groups):
            pairs_ref[group] = lax.dot_general(
                mirror, pairs_ref[group], ROWS_BY_COLS, precision=lax.Precision.HIGHEST, preferred_element_type=f32
            )
        for head in range(groups * heads):
            group, place = head // heads, head % heads
            block = pairs_ref[group, :, place * WT : (place + 1) * WT]
            block = jnp.concatenate([block, jnp.zeros((WT, DIAG - WT), f32)], axis=1)
            rolled = pltpu.roll(block, 1, 1, stride=1, stride_axis=0)
            near = column_sum(jnp.where(mask, rolled, 0.0))
            far = column_sum(jnp.where(mask, 0.0, rolled))
            diag_ref[head : head + 1, :DIAG] = near
            diag_ref[head : head + 1, DIAG:] = far


def attention_backward(
    probs, mixed, branch_back, middle_back, proj_full, context, normed, tokens, qkv_full, vectors, head_count
):
    count, width = tokens.shape
    windows = count // WT
    head_size = width // head_count
    heads = LANES // head_size
    groups = width // LANES
    mask = jnp.asarray(stack_mask(heads, head_size))
    return pl.pallas_call(
        functools.partial(backward_kernel, heads, head_size),
        grid=(windows,),
        in_specs=[
            pl.BlockSpec((groups, WT, heads * WT), lambda w: (w, 0, 0)),
            pl.BlockSpec((WT, 3 * width), lambda w: (w, 0)),
        ]
        + [
            whole(x.shape)
            for x in (branch_back, middle_back, proj_full, context, normed, tokens, qkv_full, vectors, mask)
        ],
        out_specs=[
            whole((count, width)),
            whole((4 * width, width)),
            whole((8, width)),
            whole((head_count, 2 * DIAG)),
        ],
        out_shape=[
            struct((count, width), low),
            struct((4 * width, width), low),
            struct((8, width), f32),
            struct((head_count, 2 * DIAG), f32),
        ],
        scratch_shapes=[
            pltpu.VMEM((count, width), low),
            pltpu.VMEM((count, 3 * width), low),
            pltpu.VMEM((groups, WT, heads * WT), f32),
            pltpu.VMEM((count, width), f32),
        ],
        compiler_params=pltpu.CompilerParams(vmem_limit_bytes=60 * MIB),
        name="attention_backward",
    )(probs, mixed, branch_back, middle_back, proj_full, context, normed, tokens, qkv_full, vectors, mask)


MESH = pl.DeviceIdType.MESH


class Peers:
    def __init__(self):
        self.z = lax.axis_index("rep")
        place = lax.axis_index("grp")
        self.c = lax.rem(place, 2)
        self.x = lax.rem(place // 2, 2)
        self.y = place // 4
        self.core_peer = (self.z, place + 1 - 2 * self.c)
        self.x_peer = (self.z, place + 2 - 4 * self.x)
        self.y_peer = (self.z, place + 4 - 8 * self.y)
        self.z_places = [lax.rem(self.z + step, 4) for step in range(1, 4)]
        self.z_peers = [(there, place) for there in self.z_places]

    def plane(self):
        return [self.core_peer, self.x_peer, self.y_peer]

    def everyone(self):
        return self.plane() + self.z_peers


def meet(peers):
    barrier = pltpu.get_barrier_semaphore()
    for peer in peers:
        pl.semaphore_signal(barrier, inc=1, device_id=peer, device_id_type=MESH)
    pl.semaphore_wait(barrier, len(peers))


class Copies:
    def __init__(self, send_sems, recv_sems):
        self.send_sems, self.recv_sems, self.made = send_sems, recv_sems, 0
        self.started = []

    def make(self, source, target, peer):
        copy = pltpu.make_async_remote_copy(
            src_ref=source,
            dst_ref=target,
            send_sem=self.send_sems.at[self.made],
            recv_sem=self.recv_sems.at[self.made],
            device_id=peer,
            device_id_type=MESH,
        )
        self.made += 1
        self.started.append(copy)
        copy.start()
        return copy

    def drain(self):
        for copy in self.started:
            copy.wait_send()


def gather_kernel(amount, *refs):
    shards, outs = refs[:amount], refs[amount : 2 * amount]
    send_sems, recv_sems, local_sems = refs[2 * amount :]
    me = Peers()
    meet(me.plane())
    copies = Copies(send_sems, recv_sems)
    own = (me.y, me.x, me.c)
    locals_, first, second, across = [], [], [], []
    for index, (shard, out) in enumerate(zip(shards, outs)):
        local = pltpu.make_async_copy(shard, out.at[own], local_sems.at[index])
        local.start()
        locals_.append(local)
        by_x = copies.make(shard, out.at[own], me.x_peer)
        by_y = copies.make(shard, out.at[own], me.y_peer)
        by_core = copies.make(shard, out.at[own], me.core_peer)
        first.append((by_x, by_y))
        across.append(by_core)
    for out, (by_x, by_y) in zip(outs, first):
        half = out.shape[3] // 2
        from_x, from_y = (me.y, 1 - me.x, me.c), (1 - me.y, me.x, me.c)
        by_x.wait_recv()
        part = out.at[from_x].at[pl.ds(0, half)]
        second.append(copies.make(part, part, me.y_peer))
        by_y.wait_recv()
        part = out.at[from_y].at[pl.ds(half, half)]
        second.append(copies.make(part, part, me.x_peer))
        for place in (from_x, from_y):
            across.append(copies.make(out.at[place], out.at[place], me.core_peer))
    for index, out in enumerate(outs):
        second[2 * index].wait_recv()
        second[2 * index + 1].wait_recv()
        place = (1 - me.y, 1 - me.x, me.c)
        across.append(copies.make(out.at[place], out.at[place], me.core_peer))
    for copy in across:
        copy.wait_recv()
    for local in locals_:
        local.wait()
    copies.drain()


def gather_over_plane(shards, collective_id):
    amount = len(shards)
    count = 8 * amount
    hbm = pl.BlockSpec(memory_space=pl.ANY)
    wholes = pl.pallas_call(
        functools.partial(gather_kernel, amount),
        in_specs=[hbm] * amount,
        out_specs=[hbm] * amount,
        out_shape=[struct((2, 2, 2) + shard.shape, shard.dtype) for shard in shards],
        scratch_shapes=[
            pltpu.SemaphoreType.DMA((count,)),
            pltpu.SemaphoreType.DMA((count,)),
            pltpu.SemaphoreType.DMA((amount,)),
        ],
        compiler_params=pltpu.CompilerParams(collective_id=collective_id, has_side_effects=True),
        name="gather_over_plane",
    )(*shards)
    return [out.reshape((8 * shard.shape[0],) + shard.shape[1:]) for out, shard in zip(wholes, shards)]


PIECE = 48


def reduce_kernel(amount, *refs):
    terms, small, outs, small_out = refs[:amount], refs[amount], refs[amount + 1 : 2 * amount + 1], refs[2 * amount + 1]
    mine, core_in, first_in, second_in, z_in, final, small_in, send_sems, recv_sems, local_sems = refs[2 * amount + 2 :]
    me = Peers()
    meet(me.everyone())
    copies = Copies(send_sems, recv_sems)
    c, x, y, z = me.c, me.x, me.y, me.z
    parts = range(amount)
    core, first, second, over_z, last_z, spread, relay, across = ([None] * amount for _ in range(8))
    loads, stores = [None] * amount, [None] * amount

    def start(k):
        core[k] = copies.make(terms[k].at[1 - c], core_in.at[k], me.core_peer)
        loads[k] = pltpu.make_async_copy(terms[k].at[c], mine.at[k], local_sems.at[2 * k])
        loads[k].start()

    def finish_core(k):
        loads[k].wait()
        core[k].wait_recv()

        def add(step, carry):
            at = (k, step // 16, lax.rem(step // 8, 2), lax.rem(step // 2, 4), lax.rem(step, 2))
            mine[at] = mine[at] + core_in[at]
            return carry

        lax.fori_loop(0, 32, add, 0)
        first[k] = (
            copies.make(mine.at[k, 1 - x, :, :, 0], first_in.at[k, 0], me.x_peer),
            copies.make(mine.at[k, :, 1 - y, :, 1], first_in.at[k, 1], me.y_peer),
        )

    def finish_first(k):
        first[k][0].wait_recv()
        first[k][1].wait_recv()

        def add(step, carry):
            other, place = step // 4, lax.rem(step, 4)
            at = (k, x, other, place, 0)
            mine[at] = mine[at] + first_in[k, 0, other, place]
            at = (k, other, y, place, 1)
            mine[at] = mine[at] + first_in[k, 1, other, place]
            return carry

        lax.fori_loop(0, 8, add, 0)
        second[k] = (
            copies.make(mine.at[k, x, 1 - y, :, 0], second_in.at[k, 0], me.y_peer),
            copies.make(mine.at[k, 1 - x, y, :, 1], second_in.at[k, 1], me.x_peer),
        )

    def finish_second(k):
        second[k][0].wait_recv()
        second[k][1].wait_recv()

        def add(place, carry):
            for side in range(2):
                at = (k, x, y, place, side)
                mine[at] = mine[at] + second_in[k, side, place]
            return carry

        lax.fori_loop(0, 4, add, 0)
        over_z[k] = [
            copies.make(mine.at[k, x, y, there], z_in.at[k, z], peer) for there, peer in zip(me.z_places, me.z_peers)
        ]
        z_in[k, z] = mine[k, x, y, z]

    def finish_z(k):
        for copy in over_z[k]:
            copy.wait_recv()
        for side in range(2):
            total = z_in[k, 0, side].astype(f32)
            for place in range(1, 4):
                total = total + z_in[k, place, side].astype(f32)
            final[k, side] = total.astype(low)
        target = outs[k].at[c, x, y, z]
        last_z[k] = [copies.make(final.at[k], target, peer) for peer in me.z_peers]
        stores[k] = pltpu.make_async_copy(final.at[k], target, local_sems.at[2 * k + 1])
        stores[k].start()

    def finish_last_z(k):
        for copy in last_z[k]:
            copy.wait_recv()
        stores[k].wait()
        own = outs[k].at[c, x, y]
        spread[k] = [copies.make(own, own, peer) for peer in (me.x_peer, me.y_peer)]
        across[k] = [copies.make(own, own, me.core_peer)]

    def finish_spread(k):
        by_x, by_y = spread[k]
        by_y.wait_recv()
        part = outs[k].at[c, x, 1 - y, :, 0]
        to_x = copies.make(part, part, me.x_peer)
        by_x.wait_recv()
        part = outs[k].at[c, 1 - x, y, :, 1]
        to_y = copies.make(part, part, me.y_peer)
        relay[k] = (to_x, to_y)
        for part in (outs[k].at[c, 1 - x, y], outs[k].at[c, x, 1 - y]):
            across[k].append(copies.make(part, part, me.core_peer))

    def finish_relay(k):
        for copy in relay[k]:
            copy.wait_recv()
        part = outs[k].at[c, 1 - x, 1 - y]
        across[k].append(copies.make(part, part, me.core_peer))

    small_peers = [me.core_peer, me.x_peer, me.y_peer]
    small_copies = []

    def small_step(step):
        if step > 0:
            small_copies[step - 1].wait_recv()
            small_out[...] += small_in[step - 1]
        else:
            small_out[...] = small[...]
        if step < 3:
            small_in[step + 6] = small_out[...]
            small_copies.append(copies.make(small_in.at[step + 6], small_in.at[step], small_peers[step]))
        elif step == 3:
            small_in[9 + z] = small_out[...]
            for peer in me.z_peers:
                small_copies.append(copies.make(small_in.at[9 + z], small_in.at[9 + z], peer))

    def small_end():
        for copy in small_copies[3:]:
            copy.wait_recv()
        small_out[...] = (small_in[9] + small_in[10]) + (small_in[11] + small_in[12])

    for k in parts:
        start(k)
    stages = [finish_core, finish_first, finish_second, finish_z, finish_last_z, finish_spread, finish_relay]
    small_step(0)
    for wave in range(amount + len(stages) - 1):
        for k in reversed(parts):
            if 0 <= wave - k < len(stages):
                stages[wave - k](k)
        if 1 <= wave <= 3:
            small_step(wave)
        elif wave == 4:
            small_end()
    for k in parts:
        for copy in across[k]:
            copy.wait_recv()
    copies.drain()


def all_reduce(terms, small, collective_id):
    amount = len(terms)
    width = terms[0].shape[1]
    shape = (2, 2, 2, 4, 2, PIECE, width)
    count = 19 * amount + 8
    hbm = pl.BlockSpec(memory_space=pl.ANY)
    vmem = pl.BlockSpec(memory_space=pltpu.VMEM)
    results = pl.pallas_call(
        functools.partial(reduce_kernel, amount),
        in_specs=[hbm] * amount + [vmem],
        out_specs=[hbm] * amount + [vmem],
        out_shape=[struct(shape, low)] * amount + [struct(small.shape, f32)],
        scratch_shapes=[
            pltpu.VMEM((amount,) + shape[1:], low),
            pltpu.VMEM((amount,) + shape[1:], low),
            pltpu.VMEM((amount, 2, 2, 4, PIECE, width), low),
            pltpu.VMEM((amount, 2, 4, PIECE, width), low),
            pltpu.VMEM((amount, 4, 2, PIECE, width), low),
            pltpu.VMEM((amount, 2, PIECE, width), low),
            pltpu.VMEM((13,) + small.shape, f32),
            pltpu.SemaphoreType.DMA((count,)),
            pltpu.SemaphoreType.DMA((count,)),
            pltpu.SemaphoreType.DMA((2 * amount,)),
        ],
        compiler_params=pltpu.CompilerParams(
            collective_id=collective_id, has_side_effects=True, vmem_limit_bytes=48 * MIB
        ),
        name="all_reduce",
    )(*[term.reshape(shape) for term in terms], small)
    return [out.reshape(terms[0].shape) for out in results[:amount]], results[amount]


def shards(
    plain, tokens, cotangent, window_fill, qkv_weight, proj_weight, fc1_weight, fc2_weight, vectors, vector_moments,
    bias_table, table_moments, stats_model, stats_qkv, stats_hidden, roots_model, roots_qkv, roots_hidden,
):
    width = vectors.shape[1]
    head_count = bias_table.shape[1]
    heads = LANES // (width // head_count)
    local_windows = window_fill.shape[0]
    base = (lax.axis_index(("rep", "grp")) * local_windows).astype(jnp.int32).reshape(1)
    gather = functools.partial(lax.all_gather, axis_name="grp", tiled=True)
    weights_low = [weight.astype(low) for weight in (qkv_weight, proj_weight, fc1_weight, fc2_weight)]
    if plain:
        qkv_full, proj_full, fc1_full, fc2_full = (gather(weight) for weight in weights_low)
    else:
        qkv_full, proj_full, fc1_full, fc2_full = gather_over_plane(weights_low, 0)
    hot = jnp.asarray(diagonal_tables())
    diagonals = lax.dot_general(bias_table, hot, (((0,), (1,)), ((), ())), precision=lax.Precision.HIGHEST)
    relative = relative_bias(diagonals, heads)
    probs, mixed, normed, context, middle, normed_two = attention_forward(
        window_fill, base, tokens, qkv_full, proj_full, vectors, relative, head_count
    )
    small_roots = gather(jnp.stack([roots_model[i] for i in (0, 2, 3, 4)]).astype(low), axis=1)
    layer_output, middle_back, branch_back, fc1_term, fc2_term, fc1_bias_grad, ffn_vec = feed_forward(
        normed_two, cotangent, middle, fc1_full, fc2_full, vectors
    )
    small_roots, branch_back = lax.optimization_barrier((small_roots, branch_back))
    input_gradient, att_term, att_vec, diag_grad = attention_backward(
        probs, mixed, branch_back, middle_back, proj_full, context, normed, tokens, qkv_full, vectors, head_count
    )
    small = jnp.concatenate([part.reshape(-1, 128) for part in (att_vec[:4], ffn_vec[:4], fc1_bias_grad, diag_grad)])
    terms = (fc2_term, fc1_term, att_term)
    if plain:
        small = lax.psum(small, ("rep", "grp"))
        parts = [lax.psum(lax.psum_scatter(term, "grp", scatter_dimension=0, tiled=True), "rep") for term in terms]
        wholes = [gather(part) for part in parts]
    else:
        wholes, small = all_reduce(terms, small, 1)
    fc2_whole, fc1_whole, att_whole = wholes
    qkv_whole, proj_whole = att_whole[: 3 * width], att_whole[3 * width :]
    vector_total = small[: vectors.size // 128].reshape(vectors.shape)
    table_total = lax.dot_general(
        hot, small[vectors.size // 128 :].reshape(diag_grad.shape), (((0,), (1,)), ((), ())), precision=lax.Precision.HIGHEST
    )
    member = lax.axis_index("grp")
    model_rows = qkv_weight.shape[0]
    picked = member * model_rows + jnp.arange(model_rows, dtype=jnp.int32)
    pick = (picked[:, None] == jnp.arange(width, dtype=jnp.int32)[None, :]).astype(low)

    def statistic_update(tall, small_rows, big_rows):
        columns = dot(pick, tall, COLS_BY_COLS)
        small_new = 0.5 * small_rows + 0.5 * dot(columns.astype(low), tall)
        rows = lax.dynamic_slice_in_dim(tall, member * big_rows.shape[0], big_rows.shape[0], 0)
        big_new = 0.5 * big_rows + 0.5 * dot(rows, tall, COLS_BY_COLS)
        return small_new, big_new, columns, rows.astype(f32)

    def row_step(big_root_rows, tall, small_root):
        return dot(dot(big_root_rows.astype(low), tall).astype(low), small_root)

    def column_step(big_root_rows, tall, small_root):
        product = dot(big_root_rows.astype(low), tall).astype(low)
        columns = dot(small_root, product, COLS_BY_COLS).astype(low)
        return lax.all_to_all(columns, "grp", 0, 1, tiled=True).astype(f32)

    qkv_left, qkv_right, qkv_gradient, _ = statistic_update(qkv_whole, stats_model[0], stats_qkv)
    proj_right, proj_left, _, proj_gradient = statistic_update(proj_whole, stats_model[2], stats_model[1])
    fc1_left, fc1_right, fc1_gradient, _ = statistic_update(fc1_whole, stats_model[3], stats_hidden[0])
    fc2_right, fc2_left, _, fc2_gradient = statistic_update(fc2_whole, stats_model[4], stats_hidden[1])
    qkv_new = qkv_weight - column_step(roots_qkv, qkv_whole, small_roots[0])
    fc1_new = fc1_weight - column_step(roots_hidden[0], fc1_whole, small_roots[2])
    proj_new = proj_weight - row_step(roots_model[1], proj_whole, small_roots[1])
    fc2_new = fc2_weight - row_step(roots_hidden[1], fc2_whole, small_roots[3])
    new_stats_model = jnp.stack([qkv_left, proj_left, proj_right, fc1_left, fc2_right])
    new_stats_hidden = jnp.stack([fc1_right, fc2_left])
    total_tokens = tokens.shape[0] * lax.axis_size("rep") * lax.axis_size("grp")
    rate_base = total_tokens ** (-0.5)
    new_vector_moments = 0.9 * vector_moments + 0.1 * vector_total
    new_vectors = vectors - 2.0 * rate_base * new_vector_moments
    new_table_moments = 0.9 * table_moments + 0.1 * table_total
    new_table = bias_table - 8.0 * rate_base * new_table_moments
    masters = (qkv_new, proj_new, fc1_new, fc2_new)
    return (
        (layer_output, input_gradient, qkv_gradient, proj_gradient, fc1_gradient, fc2_gradient)
        + masters
        + tuple(master.astype(low) for master in masters)
        + (new_stats_model, qkv_right, new_stats_hidden, new_vectors, new_vector_moments, new_table, new_table_moments)
    )


def solution(mesh):
    tokens, rows, blocks, copied = P(("rep", "grp"), None), P("grp", None), P(None, "grp", None), P()
    plain = (mesh.shape["rep"], mesh.shape["grp"]) != (4, 8)
    return jax.shard_map(
        functools.partial(shards, plain),
        mesh=mesh,
        in_specs=(tokens, tokens, P(("rep", "grp")))
        + (rows,) * 4
        + (copied,) * 4
        + (blocks, rows, blocks) * 2,
        out_specs=(tokens,) * 2 + (rows,) * 12 + (blocks, rows, blocks) + (copied,) * 4,
        check_vma=False,
    )
```

```python
import functools

import jax
import jax.numpy as jnp
import numpy as np
from jax import lax
from jax.experimental import pallas as pl
from jax.experimental.pallas import tpu as pltpu
from jax.sharding import PartitionSpec as P

WT = 144
SIDE = 12
SPAN = 2 * SIDE - 1
LANES = 256
DIAG = 384
ROW_TILE = 144
MIB = 1024 * 1024
low = jnp.bfloat16
f32 = jnp.float32

ROWS_BY_COLS = (((1,), (0,)), ((), ()))
COLS_BY_COLS = (((1,), (1,)), ((), ()))
ROWS_BY_ROWS = (((0,), (0,)), ((), ()))


def dot(left_matrix, right_matrix, dims=ROWS_BY_COLS):
    return lax.dot_general(left_matrix, right_matrix, dims, preferred_element_type=f32)


def standardize(values):
    centred = values - jnp.mean(values, axis=-1, keepdims=True)
    inverse = lax.rsqrt(jnp.mean(centred * centred, axis=-1, keepdims=True) + 1e-05)
    return centred * inverse, inverse


def norm_back(grad, gain, xhat, inverse):
    scaled = grad * gain
    mean_scaled = jnp.mean(scaled, axis=-1, keepdims=True)
    mean_product = jnp.mean(scaled * xhat, axis=-1, keepdims=True)
    return inverse * (scaled - mean_scaled - xhat * mean_product)


def column_sum(values):
    return jnp.sum(values, axis=0, keepdims=True)


def diagonal_tables():
    pair = np.arange(DIAG) - WT
    quotient, rest = pair // SIDE, pair % SIDE
    near = (quotient + SIDE - 1) * SPAN + rest + SIDE - 1
    far = (quotient + SIDE) * SPAN + rest - 1
    near_live = (np.abs(pair) < WT) & (quotient >= 1 - SIDE)
    far_live = (np.abs(pair) < WT) & (rest >= 1) & (quotient < SIDE - 1)
    hot = np.zeros((2, DIAG, SPAN * SPAN), np.float32)
    hot[0, np.arange(DIAG)[near_live], near[near_live]] = 1.0
    hot[1, np.arange(DIAG)[far_live], far[far_live]] = 1.0
    return hot.reshape(2 * DIAG, SPAN * SPAN)


def near_mask(shape, mirrored=False):
    column = lax.rem(lax.broadcasted_iota(jnp.int32, shape, 0), SIDE)
    if mirrored:
        column = SIDE - 1 - column
    rest = lax.rem(lax.broadcasted_iota(jnp.int32, shape, 1), SIDE)
    return column + rest < SIDE


def additive_types(heads):
    slot = np.arange(WT)
    row_high, col_high = slot // SIDE >= SIDE // 2, slot % SIDE >= SIDE // 2
    row_differs = row_high[:, None] != row_high[None, :]
    col_differs = col_high[:, None] != col_high[None, :]
    types = [
        np.where((row_differs & bool(kind // 2)) | (col_differs & bool(kind % 2)), -100.0, 0.0)
        for kind in range(4)
    ]
    return np.tile(np.stack(types), (1, 1, heads)).astype(np.float32)


def stack_mask(heads, head_size):
    lane_head = np.arange(heads * head_size) // head_size
    hot = lane_head[None, None, :] == np.arange(heads)[:, None, None]
    return np.broadcast_to(hot, (heads, WT, heads * head_size)).reshape(heads * WT, -1).astype(low)


def relative_kernel(heads, diag_ref, rel_ref):
    mask = near_mask((WT, DIAG))
    for head in range(heads * rel_ref.shape[0]):
        group, place = head // heads, head % heads
        near = diag_ref[head : head + 1, :DIAG]
        far = diag_ref[head : head + 1, DIAG:]
        rows = jnp.where(mask, near, far)
        rolled = pltpu.roll(rows, DIAG - WT, 1, stride=1, stride_axis=0)
        rel_ref[group, :, place * WT : (place + 1) * WT] = rolled[:, :WT]


def relative_bias(diagonals, heads):
    head_count = diagonals.shape[0]
    return pl.pallas_call(
        functools.partial(relative_kernel, heads),
        out_shape=jax.ShapeDtypeStruct((head_count // heads, WT, heads * WT), f32),
        compiler_params=pltpu.CompilerParams(vmem_limit_bytes=32 * MIB),
        name="relative_bias",
    )(diagonals)


def stacked(block, mask_ref, heads):
    return jnp.concatenate([block] * heads, axis=0) * mask_ref[...]


def diagonal_blocks(full, heads, head_size):
    lane_head = lax.broadcasted_iota(jnp.int32, (WT, full.shape[1]), 1) // head_size
    picked = jnp.zeros((WT, full.shape[1]), f32)
    for head in range(heads):
        picked = jnp.where(lane_head == head, full[head * WT : (head + 1) * WT], picked)
    return picked


def forward_kernel(
    heads, head_size, fill_ref, base_ref, tokens_ref, qkv_ref, proj_ref, vec_ref, rel_ref, add_ref, mask_ref,
    probs_ref, mixed_out_ref, normed_ref, context_ref, middle_ref, normedwo_ref,
    mixed_ref, added_ref,
):
    window = pl.program_id(0)
    width = tokens_ref.shape[1]
    count = tokens_ref.shape[0]
    groups = width // LANES
    score_scale = head_size ** (-0.5)

    @pl.when(window == 0)
    def _():
        def norm_step(step, carry):
            rows = pl.ds(pl.multiple_of(step * ROW_TILE, ROW_TILE), ROW_TILE)
            xhat, _ = standardize(tokens_ref[rows, :].astype(f32))
            normed_ref[rows, :] = (xhat * vec_ref[0:1, :] + vec_ref[1:2, :]).astype(low)
            return carry

        lax.fori_loop(0, count // ROW_TILE, norm_step, 0)
        for part in range(3):
            for tile in range(groups):
                start = part * width + tile * LANES
                sums = dot(normed_ref[...], qkv_ref[:, start : start + LANES])
                if part != 1:
                    shift_row = 2 if part == 0 else 3
                    sums = sums + vec_ref[shift_row : shift_row + 1, tile * LANES : (tile + 1) * LANES]
                mixed_ref[:, start : start + LANES] = sums.astype(low)

    rows = pl.ds(pl.multiple_of(window * WT, WT), WT)
    mixed_out_ref[...] = mixed_ref[rows, :]
    kind = lax.rem(base_ref[0] + window, 4)
    slot = lax.broadcasted_iota(jnp.int32, added_ref.shape, 0)
    added_ref[...] = jnp.where(slot < fill_ref[window], add_ref[kind], -1e30)
    for group in range(groups):
        span = slice(group * LANES, (group + 1) * LANES)
        query = mixed_ref[rows, span]
        key = mixed_ref[rows, width + group * LANES : width + (group + 1) * LANES]
        value = mixed_ref[rows, 2 * width + group * LANES : 2 * width + (group + 1) * LANES]
        scores = dot(key, stacked(query, mask_ref, heads), COLS_BY_COLS) * score_scale
        scores = scores + rel_ref[group] + added_ref[...]
        exponent = jnp.exp(scores - jnp.max(scores, axis=0, keepdims=True))
        probs = (exponent * (1.0 / jnp.sum(exponent, axis=0, keepdims=True))).astype(low)
        probs_ref[group] = probs
        full = dot(probs, value, ROWS_BY_ROWS)
        context_ref[rows, span] = diagonal_blocks(full, heads, head_size).astype(low)

    @pl.when(window == pl.num_programs(0) - 1)
    def _():
        for tile in range(groups):
            span = slice(tile * LANES, (tile + 1) * LANES)
            middle_ref[:, span] = (
                tokens_ref[:, span].astype(f32) + dot(context_ref[...], proj_ref[:, span]) + vec_ref[4:5, span]
            )

        def norm_step(step, carry):
            part = pl.ds(pl.multiple_of(step * ROW_TILE, ROW_TILE), ROW_TILE)
            xhat, _ = standardize(middle_ref[part, :])
            normedwo_ref[part, :] = (xhat * vec_ref[5:6, :] + vec_ref[6:7, :]).astype(low)
            return carry

        lax.fori_loop(0, count // ROW_TILE, norm_step, 0)


def whole(shape):
    return pl.BlockSpec(shape, lambda *_: (0,) * len(shape), pipeline_mode=pl.Buffered(1))


def struct(shape, dtype):
    return jax.ShapeDtypeStruct(shape, dtype)


def attention_forward(fill, base, tokens, qkv_full, proj_full, vectors, relative, head_count):
    count, width = tokens.shape
    windows = fill.shape[0]
    head_size = width // head_count
    heads = LANES // head_size
    groups = width // LANES
    additive = jnp.asarray(additive_types(heads))
    mask = jnp.asarray(stack_mask(heads, head_size))
    smem = pl.BlockSpec(memory_space=pltpu.SMEM)
    return pl.pallas_call(
        functools.partial(forward_kernel, heads, head_size),
        grid=(windows,),
        in_specs=[smem, smem] + [whole(x.shape) for x in (tokens, qkv_full, proj_full, vectors, relative, additive, mask)],
        out_specs=[
            pl.BlockSpec((groups, WT, heads * WT), lambda w: (w, 0, 0)),
            pl.BlockSpec((WT, 3 * width), lambda w: (w, 0)),
            whole((count, width)),
            whole((count, width)),
            whole((count, width)),
            whole((count, width)),
        ],
        out_shape=[
            struct((windows * groups, WT, heads * WT), low),
            struct((count, 3 * width), low),
            struct((count, width), low),
            struct((count, width), low),
            struct((count, width), f32),
            struct((count, width), low),
        ],
        scratch_shapes=[
            pltpu.VMEM((count, 3 * width), low),
            pltpu.VMEM((WT, heads * WT), f32),
        ],
        compiler_params=pltpu.CompilerParams(vmem_limit_bytes=56 * MIB),
        name="attention_forward",
    )(fill, base, tokens, qkv_full, proj_full, vectors, relative, additive, mask)


def feed_forward_kernel(
    normed_ref, cot_ref, middle_ref, fc1_ref, fc2_ref, bias_ref, vec_ref,
    out_ref, middle_back_ref, branch_back_ref, fc1_grad_ref, fc2_grad_ref, bias_grad_ref, vec_grad_ref,
    out_sum, back_sum,
):
    step = pl.program_id(0)
    count, width = cot_ref.shape
    hidden = dot(normed_ref[...], fc1_ref[...]) + bias_ref[...]
    bell = jnp.exp(hidden * hidden * -0.5)
    below = 0.5 * (1.0 + lax.erf(hidden * (0.5 ** 0.5)))
    active = (hidden * below).astype(low)
    slope = below + hidden * bell * ((2.0 * np.pi) ** -0.5)
    hidden_back = dot(cot_ref[...], fc2_ref[...], COLS_BY_COLS) * slope
    hidden_back = hidden_back.astype(low)
    bias_grad_ref[...] = column_sum(hidden_back.astype(f32))
    fc2_grad_ref[...] = dot(active, cot_ref[...], ROWS_BY_ROWS).astype(low)
    fc1_grad_ref[...] = dot(hidden_back, normed_ref[...], ROWS_BY_ROWS).astype(low)
    out_term = dot(active, fc2_ref[...])
    back_term = dot(hidden_back, fc1_ref[...], COLS_BY_COLS)

    @pl.when(step == 0)
    def _():
        out_sum[...] = out_term
        back_sum[...] = back_term

    @pl.when(step > 0)
    def _():
        out_sum[...] += out_term
        back_sum[...] += back_term

    @pl.when(step == pl.num_programs(0) - 1)
    def _():
        vec_grad_ref[...] = jnp.zeros_like(vec_grad_ref)

        def finish(part, carry):
            rows = pl.ds(pl.multiple_of(part * ROW_TILE, ROW_TILE), ROW_TILE)
            middle = middle_ref[rows, :]
            cot = cot_ref[rows, :].astype(f32)
            out_ref[rows, :] = (middle + out_sum[rows, :] + vec_ref[7:8, :]).astype(low)
            xhat, inverse = standardize(middle)
            grad = back_sum[rows, :]
            middle_back = cot + norm_back(grad, vec_ref[5:6, :], xhat, inverse)
            middle_back_ref[rows, :] = middle_back
            branch_back = middle_back.astype(low)
            branch_back_ref[rows, :] = branch_back
            vec_grad_ref[0:1, :] += column_sum(branch_back.astype(f32))
            vec_grad_ref[1:2, :] += column_sum(grad * xhat)
            vec_grad_ref[2:3, :] += column_sum(grad)
            vec_grad_ref[3:4, :] += column_sum(cot)
            return carry

        lax.fori_loop(0, count // ROW_TILE, finish, 0)


def feed_forward(normed, cotangent, middle, fc1_full, fc2_full, vectors):
    count, width = cotangent.shape
    hidden_width = fc1_full.shape[1]
    tile = LANES
    bias = vectors[8:].reshape(1, hidden_width)
    return pl.pallas_call(
        feed_forward_kernel,
        grid=(hidden_width // tile,),
        in_specs=[whole(x.shape) for x in (normed, cotangent, middle)]
        + [
            pl.BlockSpec((width, tile), lambda f: (0, f)),
            pl.BlockSpec((tile, width), lambda f: (f, 0)),
            pl.BlockSpec((1, tile), lambda f: (0, f)),
            whole(vectors.shape),
        ],
        out_specs=[
            whole((count, width)),
            whole((count, width)),
            whole((count, width)),
            pl.BlockSpec((tile, width), lambda f: (f, 0)),
            pl.BlockSpec((tile, width), lambda f: (f, 0)),
            pl.BlockSpec((1, tile), lambda f: (0, f)),
            whole((8, width)),
        ],
        out_shape=[
            struct((count, width), low),
            struct((count, width), f32),
            struct((count, width), low),
            struct((hidden_width, width), low),
            struct((hidden_width, width), low),
            struct((1, hidden_width), f32),
            struct((8, width), f32),
        ],
        scratch_shapes=[pltpu.VMEM((count, width), f32), pltpu.VMEM((count, width), f32)],
        compiler_params=pltpu.CompilerParams(vmem_limit_bytes=56 * MIB),
        name="feed_forward",
    )(normed, cotangent, middle, fc1_full, fc2_full, bias, vectors)


def backward_kernel(
    heads, head_size, probs_ref, mixed_ref, branch_back_ref, middle_back_ref, proj_ref, context_ref, normed_ref,
    tokens_ref, qkv_ref, vec_ref, mask_ref,
    input_grad_ref, weight_grad_ref, vec_grad_ref, diag_ref,
    context_back_ref, mixed_back_ref, pairs_ref, normed_back_ref,
):
    window = pl.program_id(0)
    count, width = tokens_ref.shape
    groups = width // LANES
    score_scale = head_size ** (-0.5)

    @pl.when(window == 0)
    def _():
        pairs_ref[...] = jnp.zeros_like(pairs_ref)
        for tile in range(groups):
            span = slice(tile * LANES, (tile + 1) * LANES)
            context_back_ref[:, span] = dot(branch_back_ref[...], proj_ref[span, :], COLS_BY_COLS).astype(low)
            weight_grad_ref[3 * width + tile * LANES : 3 * width + (tile + 1) * LANES, :] = dot(
                context_ref[:, span], branch_back_ref[...], ROWS_BY_ROWS
            ).astype(low)

    rows = pl.ds(pl.multiple_of(window * WT, WT), WT)
    for group in range(groups):
        spans = [slice(part * width + group * LANES, part * width + (group + 1) * LANES) for part in range(3)]
        query, key, value = (mixed_ref[:, span] for span in spans)
        probs_low = probs_ref[group]
        probs = probs_low.astype(f32)
        back_stack = stacked(context_back_ref[rows, spans[0]], mask_ref, heads)
        value_back = dot(probs_low, back_stack)
        product = probs * dot(value, back_stack, COLS_BY_COLS)
        scores_back = (product - probs * jnp.sum(product, axis=0, keepdims=True)).astype(low)
        pairs_ref[group] += scores_back.astype(f32)
        key_back = dot(scores_back, stacked(query, mask_ref, heads)) * score_scale
        full = dot(scores_back, key, ROWS_BY_ROWS)
        query_back = diagonal_blocks(full, heads, head_size) * score_scale
        mixed_back_ref[rows, spans[0]] = query_back.astype(low)
        mixed_back_ref[rows, spans[1]] = key_back.astype(low)
        mixed_back_ref[rows, spans[2]] = value_back.astype(low)

    @pl.when(window == pl.num_programs(0) - 1)
    def _():
        vec_grad_ref[...] = jnp.zeros_like(vec_grad_ref)
        for part in range(3):
            for tile in range(groups):
                start = part * width + tile * LANES
                block = mixed_back_ref[:, start : start + LANES]
                weight_grad_ref[start : start + LANES, :] = dot(block, normed_ref[...], ROWS_BY_ROWS).astype(low)
                if part != 1:
                    row = 2 if part == 0 else 3
                    span = slice(tile * LANES, (tile + 1) * LANES)
                    vec_grad_ref[row : row + 1, span] = column_sum(block.astype(f32))
        for tile in range(groups):
            span = slice(tile * LANES, (tile + 1) * LANES)
            normed_back_ref[:, span] = dot(mixed_back_ref[...], qkv_ref[span, :], COLS_BY_COLS)

        def finish(part, carry):
            rows = pl.ds(pl.multiple_of(part * ROW_TILE, ROW_TILE), ROW_TILE)
            xhat, inverse = standardize(tokens_ref[rows, :].astype(f32))
            grad = normed_back_ref[rows, :]
            back = middle_back_ref[rows, :] + norm_back(grad, vec_ref[0:1, :], xhat, inverse)
            input_grad_ref[rows, :] = back.astype(low)
            vec_grad_ref[0:1, :] += column_sum(grad * xhat)
            vec_grad_ref[1:2, :] += column_sum(grad)
            return carry

        lax.fori_loop(0, count // ROW_TILE, finish, 0)
        mask = near_mask((WT, DIAG), mirrored=True)
        order = [lax.broadcasted_iota(jnp.int32, (WT, WT), axis) for axis in range(2)]
        mirror = jnp.where(order[0] + order[1] == WT - 1, 1.0, 0.0).astype(f32)
        for group in range(groups):
            pairs_ref[group] = lax.dot_general(
                mirror, pairs_ref[group], ROWS_BY_COLS, precision=lax.Precision.HIGHEST, preferred_element_type=f32
            )
        for head in range(groups * heads):
            group, place = head // heads, head % heads
            block = pairs_ref[group, :, place * WT : (place + 1) * WT]
            block = jnp.concatenate([block, jnp.zeros((WT, DIAG - WT), f32)], axis=1)
            rolled = pltpu.roll(block, 1, 1, stride=1, stride_axis=0)
            near = column_sum(jnp.where(mask, rolled, 0.0))
            far = column_sum(jnp.where(mask, 0.0, rolled))
            diag_ref[head : head + 1, :DIAG] = near
            diag_ref[head : head + 1, DIAG:] = far


def attention_backward(
    probs, mixed, branch_back, middle_back, proj_full, context, normed, tokens, qkv_full, vectors, head_count
):
    count, width = tokens.shape
    windows = count // WT
    head_size = width // head_count
    heads = LANES // head_size
    groups = width // LANES
    mask = jnp.asarray(stack_mask(heads, head_size))
    return pl.pallas_call(
        functools.partial(backward_kernel, heads, head_size),
        grid=(windows,),
        in_specs=[
            pl.BlockSpec((groups, WT, heads * WT), lambda w: (w, 0, 0)),
            pl.BlockSpec((WT, 3 * width), lambda w: (w, 0)),
        ]
        + [
            whole(x.shape)
            for x in (branch_back, middle_back, proj_full, context, normed, tokens, qkv_full, vectors, mask)
        ],
        out_specs=[
            whole((count, width)),
            whole((4 * width, width)),
            whole((8, width)),
            whole((head_count, 2 * DIAG)),
        ],
        out_shape=[
            struct((count, width), low),
            struct((4 * width, width), low),
            struct((8, width), f32),
            struct((head_count, 2 * DIAG), f32),
        ],
        scratch_shapes=[
            pltpu.VMEM((count, width), low),
            pltpu.VMEM((count, 3 * width), low),
            pltpu.VMEM((groups, WT, heads * WT), f32),
            pltpu.VMEM((count, width), f32),
        ],
        compiler_params=pltpu.CompilerParams(vmem_limit_bytes=60 * MIB),
        name="attention_backward",
    )(probs, mixed, branch_back, middle_back, proj_full, context, normed, tokens, qkv_full, vectors, mask)


MESH = pl.DeviceIdType.MESH


class Peers:
    def __init__(self):
        self.z = lax.axis_index("rep")
        place = lax.axis_index("grp")
        self.c = lax.rem(place, 2)
        self.x = lax.rem(place // 2, 2)
        self.y = place // 4
        self.core_peer = (self.z, place + 1 - 2 * self.c)
        self.x_peer = (self.z, place + 2 - 4 * self.x)
        self.y_peer = (self.z, place + 4 - 8 * self.y)
        self.z_places = [lax.rem(self.z + step, 4) for step in range(1, 4)]
        self.z_peers = [(there, place) for there in self.z_places]

    def plane(self):
        return [self.core_peer, self.x_peer, self.y_peer]

    def everyone(self):
        return self.plane() + self.z_peers


def meet(peers):
    barrier = pltpu.get_barrier_semaphore()
    for peer in peers:
        pl.semaphore_signal(barrier, inc=1, device_id=peer, device_id_type=MESH)
    pl.semaphore_wait(barrier, len(peers))


class Copies:
    def __init__(self, send_sems, recv_sems):
        self.send_sems, self.recv_sems, self.made = send_sems, recv_sems, 0
        self.started = []

    def make(self, source, target, peer):
        copy = pltpu.make_async_remote_copy(
            src_ref=source,
            dst_ref=target,
            send_sem=self.send_sems.at[self.made],
            recv_sem=self.recv_sems.at[self.made],
            device_id=peer,
            device_id_type=MESH,
        )
        self.made += 1
        self.started.append(copy)
        copy.start()
        return copy

    def drain(self):
        for copy in self.started:
            copy.wait_send()


def gather_kernel(amount, *refs):
    shards, outs = refs[:amount], refs[amount : 2 * amount]
    send_sems, recv_sems, local_sems = refs[2 * amount :]
    me = Peers()
    meet(me.plane())
    copies = Copies(send_sems, recv_sems)
    own = (me.y, me.x, me.c)
    locals_, first, second, across = [], [], [], []
    for index, (shard, out) in enumerate(zip(shards, outs)):
        local = pltpu.make_async_copy(shard, out.at[own], local_sems.at[index])
        local.start()
        locals_.append(local)
        by_x = copies.make(shard, out.at[own], me.x_peer)
        by_y = copies.make(shard, out.at[own], me.y_peer)
        by_core = copies.make(shard, out.at[own], me.core_peer)
        first.append((by_x, by_y))
        across.append(by_core)
    for out, (by_x, by_y) in zip(outs, first):
        half = out.shape[3] // 2
        from_x, from_y = (me.y, 1 - me.x, me.c), (1 - me.y, me.x, me.c)
        by_x.wait_recv()
        part = out.at[from_x].at[pl.ds(0, half)]
        second.append(copies.make(part, part, me.y_peer))
        by_y.wait_recv()
        part = out.at[from_y].at[pl.ds(half, half)]
        second.append(copies.make(part, part, me.x_peer))
        for place in (from_x, from_y):
            across.append(copies.make(out.at[place], out.at[place], me.core_peer))
    for index, out in enumerate(outs):
        second[2 * index].wait_recv()
        second[2 * index + 1].wait_recv()
        place = (1 - me.y, 1 - me.x, me.c)
        across.append(copies.make(out.at[place], out.at[place], me.core_peer))
    for copy in across:
        copy.wait_recv()
    for local in locals_:
        local.wait()
    copies.drain()


def gather_over_plane(shards, collective_id):
    amount = len(shards)
    count = 8 * amount
    hbm = pl.BlockSpec(memory_space=pl.ANY)
    wholes = pl.pallas_call(
        functools.partial(gather_kernel, amount),
        in_specs=[hbm] * amount,
        out_specs=[hbm] * amount,
        out_shape=[struct((2, 2, 2) + shard.shape, shard.dtype) for shard in shards],
        scratch_shapes=[
            pltpu.SemaphoreType.DMA((count,)),
            pltpu.SemaphoreType.DMA((count,)),
            pltpu.SemaphoreType.DMA((amount,)),
        ],
        compiler_params=pltpu.CompilerParams(collective_id=collective_id, has_side_effects=True),
        name="gather_over_plane",
    )(*shards)
    return [out.reshape((8 * shard.shape[0],) + shard.shape[1:]) for out, shard in zip(wholes, shards)]


PIECE = 48
BLOCK = 32 * PIECE


def reduce_kernel(where, amount, *refs):
    inputs = 1 + max(source for source, _ in where)
    terms, small, out, small_out = refs[:inputs], refs[inputs], refs[inputs + 1], refs[inputs + 2]
    mine, core_in, first_in, second_in, z_in, final, small_in, send_sems, recv_sems, local_sems = refs[inputs + 3 :]
    me = Peers()
    meet(me.everyone())
    copies = Copies(send_sems, recv_sems)
    c, x, y, z = me.c, me.x, me.y, me.z
    parts = range(amount)
    core, first, second, over_z, last_z, spread, relay, across = ([None] * amount for _ in range(8))
    loads, stores = [None] * amount, [None] * amount
    half = out.shape[-1] // 2
    by_x_first, by_y_first = pl.ds(0, half), pl.ds(half, half)

    def start(k):
        source, place = where[k]
        core[k] = copies.make(terms[source].at[place, 1 - c], core_in.at[k], me.core_peer)
        loads[k] = pltpu.make_async_copy(terms[source].at[place, c], mine.at[k], local_sems.at[2 * k])
        loads[k].start()

    def finish_core(k):
        loads[k].wait()
        core[k].wait_recv()

        def add(step, carry):
            at = (k, step // 8, lax.rem(step // 4, 2), lax.rem(step, 4))
            mine[at] = mine[at] + core_in[at]
            return carry

        lax.fori_loop(0, 16, add, 0)
        first[k] = (
            copies.make(mine.at[k, 1 - x, :, :, :, by_x_first], first_in.at[k, 0], me.x_peer),
            copies.make(mine.at[k, :, 1 - y, :, :, by_y_first], first_in.at[k, 1], me.y_peer),
        )

    def finish_first(k):
        first[k][0].wait_recv()
        first[k][1].wait_recv()

        def add(step, carry):
            other, place = step // 4, lax.rem(step, 4)
            mine[k, x, other, place, :, :half] += first_in[k, 0, other, place]
            mine[k, other, y, place, :, half:] += first_in[k, 1, other, place]
            return carry

        lax.fori_loop(0, 8, add, 0)
        second[k] = (
            copies.make(mine.at[k, x, 1 - y, :, :, by_x_first], second_in.at[k, 0], me.y_peer),
            copies.make(mine.at[k, 1 - x, y, :, :, by_y_first], second_in.at[k, 1], me.x_peer),
        )

    def finish_second(k):
        second[k][0].wait_recv()
        second[k][1].wait_recv()

        def add(place, carry):
            mine[k, x, y, place, :, :half] += second_in[k, 0, place]
            mine[k, x, y, place, :, half:] += second_in[k, 1, place]
            return carry

        lax.fori_loop(0, 4, add, 0)
        over_z[k] = [
            copies.make(mine.at[k, x, y, there], z_in.at[k, z], peer) for there, peer in zip(me.z_places, me.z_peers)
        ]
        z_in[k, z] = mine[k, x, y, z]

    def finish_z(k):
        for copy in over_z[k]:
            copy.wait_recv()
        total = z_in[k, 0].astype(f32)
        for place in range(1, 4):
            total = total + z_in[k, place].astype(f32)
        final[k] = total.astype(low)
        target = out.at[k, c, x, y, z]
        last_z[k] = [copies.make(final.at[k], target, peer) for peer in me.z_peers]
        stores[k] = pltpu.make_async_copy(final.at[k], target, local_sems.at[2 * k + 1])
        stores[k].start()

    def finish_last_z(k):
        for copy in last_z[k]:
            copy.wait_recv()
        stores[k].wait()
        own = out.at[k, c, x, y]
        spread[k] = [copies.make(own, own, peer) for peer in (me.x_peer, me.y_peer)]
        across[k] = [copies.make(own, own, me.core_peer)]

    def finish_spread(k):
        by_x, by_y = spread[k]
        by_y.wait_recv()
        part = out.at[k, c, x, 1 - y, :, :, by_x_first]
        to_x = copies.make(part, part, me.x_peer)
        by_x.wait_recv()
        part = out.at[k, c, 1 - x, y, :, :, by_y_first]
        to_y = copies.make(part, part, me.y_peer)
        relay[k] = (to_x, to_y)
        for part in (out.at[k, c, 1 - x, y], out.at[k, c, x, 1 - y]):
            across[k].append(copies.make(part, part, me.core_peer))

    def finish_relay(k):
        for copy in relay[k]:
            copy.wait_recv()
        part = out.at[k, c, 1 - x, 1 - y]
        across[k].append(copies.make(part, part, me.core_peer))

    small_peers = [me.core_peer, me.x_peer, me.y_peer]
    small_copies = []

    def small_step(step):
        if step > 0:
            small_copies[step - 1].wait_recv()
            small_out[...] += small_in[step - 1]
        else:
            small_out[...] = small[...]
        if step < 3:
            small_in[step + 6] = small_out[...]
            small_copies.append(copies.make(small_in.at[step + 6], small_in.at[step], small_peers[step]))
        else:
            small_in[9 + z] = small_out[...]
            for peer in me.z_peers:
                small_copies.append(copies.make(small_in.at[9 + z], small_in.at[9 + z], peer))

    def small_end():
        for copy in small_copies[3:]:
            copy.wait_recv()
        small_out[...] = (small_in[9] + small_in[10]) + (small_in[11] + small_in[12])

    for k in parts:
        start(k)
    stages = [finish_core, finish_first, finish_second, finish_z, finish_last_z, finish_spread, finish_relay]
    small_step(0)
    for wave in range(amount + len(stages) - 1):
        for k in reversed(parts):
            if 0 <= wave - k < len(stages):
                stages[wave - k](k)
        if 1 <= wave <= 3:
            small_step(wave)
        elif wave == 4:
            small_end()
    for k in parts:
        for copy in across[k]:
            copy.wait_recv()
    copies.drain()


def all_reduce(terms, small, collective_id):
    width = terms[0].shape[1]
    where = [(source, place) for source, term in enumerate(terms) for place in range(term.shape[0] // BLOCK)]
    amount = len(where)
    shape = (2, 2, 2, 4, PIECE, width)
    count = 19 * amount + 8
    hbm = pl.BlockSpec(memory_space=pl.ANY)
    vmem = pl.BlockSpec(memory_space=pltpu.VMEM)
    whole_sum, small_sum = pl.pallas_call(
        functools.partial(reduce_kernel, where, amount),
        in_specs=[hbm] * len(terms) + [vmem],
        out_specs=[hbm, vmem],
        out_shape=[struct((amount,) + shape, low), struct(small.shape, f32)],
        scratch_shapes=[
            pltpu.VMEM((amount,) + shape[1:], low),
            pltpu.VMEM((amount,) + shape[1:], low),
            pltpu.VMEM((amount, 2, 2, 4, PIECE, width // 2), low),
            pltpu.VMEM((amount, 2, 4, PIECE, width // 2), low),
            pltpu.VMEM((amount, 4, PIECE, width), low),
            pltpu.VMEM((amount, PIECE, width), low),
            pltpu.VMEM((13,) + small.shape, f32),
            pltpu.SemaphoreType.DMA((count,)),
            pltpu.SemaphoreType.DMA((count,)),
            pltpu.SemaphoreType.DMA((2 * amount,)),
        ],
        compiler_params=pltpu.CompilerParams(
            collective_id=collective_id, has_side_effects=True, vmem_limit_bytes=48 * MIB
        ),
        name="all_reduce",
    )(*[term.reshape((-1,) + shape) for term in terms], small)
    return whole_sum.reshape(-1, width), small_sum


def tile_update(tall, rows, big, root, pick, product_ref, small_ref, fresh):
    columns = dot(pick, tall, COLS_BY_COLS)
    product = dot(root.astype(low), tall)
    small = dot(columns.astype(low), tall)

    @pl.when(fresh)
    def _():
        product_ref[...] = product
        small_ref[...] = small

    @pl.when(jnp.logical_not(fresh))
    def _():
        product_ref[...] += product
        small_ref[...] += small

    return 0.5 * big + 0.5 * dot(rows, tall, COLS_BY_COLS), columns


def column_pick(member, shape):
    row, column = (lax.broadcasted_iota(jnp.int32, shape, axis) for axis in range(2))
    return jnp.where(column == row + member * shape[0], 1.0, 0.0).astype(low)


def hidden_kernel(
    member_ref, tall_ref, rows_ref, big_ref, root_ref, small_ref, small_root_ref, fc2_ref,
    big_out_ref, small_out_ref, fc1_grad_ref, fc1_step_ref, fc2_grad_ref, fc2_new_ref, fc2_copy_ref,
    product_sum, small_sum,
):
    matrix, tile = pl.program_id(0), pl.program_id(1)
    pick = column_pick(member_ref[0], small_sum.shape)
    big_new, columns = tile_update(
        tall_ref[...], rows_ref[...], big_ref[0], root_ref[0], pick, product_sum, small_sum, tile == 0
    )
    big_out_ref[0] = big_new

    @pl.when(matrix == 0)
    def _():
        fc1_grad_ref[...] = columns

    @pl.when(tile == pl.num_programs(1) - 1)
    def _():
        small_out_ref[0] = 0.5 * small_ref[0] + 0.5 * small_sum[...]
        product = product_sum[...].astype(low)

        @pl.when(matrix == 0)
        def _():
            fc1_step_ref[...] = dot(small_root_ref[0], product, COLS_BY_COLS).astype(low)

        @pl.when(matrix == 1)
        def _():
            new = fc2_ref[...] - dot(product, small_root_ref[0])
            fc2_new_ref[...] = new
            fc2_copy_ref[...] = new.astype(low)
            fc2_grad_ref[...] = rows_ref[...].astype(f32)


def hidden_update(member, gradients, stats_hidden, roots_hidden, stats_model, small_roots, fc2_weight):
    width = gradients.shape[1]
    _, span, hidden_width = stats_hidden.shape
    model_rows = stats_model.shape[1]
    tiles = hidden_width // width
    skip = 4 * width // width
    last = tiles - 1
    return pl.pallas_call(
        hidden_kernel,
        grid_spec=pltpu.PrefetchScalarGridSpec(
            num_scalar_prefetch=1,
            grid=(2, tiles),
            in_specs=[
                pl.BlockSpec((width, width), lambda i, j, m: (skip + i * tiles + j, 0)),
                pl.BlockSpec((span, width), lambda i, j, m: ((4 * width + i * hidden_width) // span + m[0], 0)),
                pl.BlockSpec((1, span, width), lambda i, j, m: (i, 0, j)),
                pl.BlockSpec((1, span, width), lambda i, j, m: (i, 0, j)),
                pl.BlockSpec((1, model_rows, width), lambda i, j, m: (3 + i, 0, 0)),
                pl.BlockSpec((1, width, width), lambda i, j, m: (2 + i, 0, 0)),
                pl.BlockSpec((span, width), lambda i, j, m: (0, 0)),
            ],
            out_specs=[
                pl.BlockSpec((1, span, width), lambda i, j, m: (i, 0, j)),
                pl.BlockSpec((1, model_rows, width), lambda i, j, m: (i, 0, 0)),
                pl.BlockSpec((model_rows, width), lambda i, j, m: (0, jnp.where(i == 0, j, last))),
                pl.BlockSpec((width, span), lambda i, j, m: (0, 0)),
                pl.BlockSpec((span, width), lambda i, j, m: (0, 0)),
                pl.BlockSpec((span, width), lambda i, j, m: (0, 0)),
                pl.BlockSpec((span, width), lambda i, j, m: (0, 0)),
            ],
            scratch_shapes=[pltpu.VMEM((span, width), f32), pltpu.VMEM((model_rows, width), f32)],
        ),
        out_shape=[
            struct(stats_hidden.shape, f32),
            struct((2, model_rows, width), f32),
            struct((model_rows, hidden_width), f32),
            struct((width, span), low),
            struct((span, width), f32),
            struct((span, width), f32),
            struct((span, width), low),
        ],
        compiler_params=pltpu.CompilerParams(vmem_limit_bytes=48 * MIB),
        name="hidden_update",
    )(member, gradients, gradients, stats_hidden, roots_hidden, stats_model, small_roots, fc2_weight)


def model_kernel(
    member_ref, tall_ref, qkv_rows_ref, proj_rows_ref, big_ref, root_ref, stats_ref, hidden_small_ref, proj_root_ref,
    small_root_ref, proj_ref,
    big_out_ref, stats_out_ref, qkv_grad_ref, qkv_step_ref, proj_grad_ref, proj_new_ref, proj_copy_ref,
    product_sum, proj_product, small_sum,
):
    tile = pl.program_id(0)
    last = pl.num_programs(0) - 1
    pick = column_pick(member_ref[0], small_sum.shape)

    @pl.when(tile < last)
    def _():
        big_new, columns = tile_update(
            tall_ref[...], qkv_rows_ref[...], big_ref[...], root_ref[...], pick, product_sum, small_sum, tile == 0
        )
        big_out_ref[...] = big_new
        qkv_grad_ref[...] = columns

    @pl.when(tile == last)
    def _():
        qkv_step_ref[...] = dot(small_root_ref[0], product_sum[...].astype(low), COLS_BY_COLS).astype(low)
        stats_out_ref[0] = 0.5 * stats_ref[0] + 0.5 * small_sum[...]
        rows = proj_rows_ref[...]
        proj_left, _ = tile_update(
            tall_ref[...], rows, stats_ref[1], proj_root_ref[0], pick, proj_product, small_sum, tile == last
        )
        stats_out_ref[1] = proj_left
        stats_out_ref[2] = 0.5 * stats_ref[2] + 0.5 * small_sum[...]
        stats_out_ref[3] = hidden_small_ref[0]
        stats_out_ref[4] = hidden_small_ref[1]
        new = proj_ref[...] - dot(proj_product[...].astype(low), small_root_ref[1])
        proj_new_ref[...] = new
        proj_copy_ref[...] = new.astype(low)
        proj_grad_ref[...] = rows.astype(f32)


def model_update(
    member, gradients, stats_qkv, roots_qkv, stats_model, hidden_small, roots_model, small_roots, proj_weight
):
    width = gradients.shape[1]
    span, qkv_width = stats_qkv.shape
    model_rows = stats_model.shape[1]
    tiles = qkv_width // width

    def fixed(shape):
        return pl.BlockSpec(shape, lambda j, m: (0,) * len(shape))

    clamped = pl.BlockSpec((span, width), lambda j, m: (0, jnp.minimum(j, tiles - 1)))
    return pl.pallas_call(
        model_kernel,
        grid_spec=pltpu.PrefetchScalarGridSpec(
            num_scalar_prefetch=1,
            grid=(tiles + 1,),
            in_specs=[
                pl.BlockSpec((width, width), lambda j, m: (j, 0)),
                pl.BlockSpec((span, width), lambda j, m: (m[0], 0)),
                pl.BlockSpec((model_rows, width), lambda j, m: (qkv_width // model_rows + m[0], 0)),
                clamped,
                clamped,
                fixed(stats_model.shape),
                fixed(hidden_small.shape),
                pl.BlockSpec((1, model_rows, width), lambda j, m: (1, 0, 0)),
                pl.BlockSpec((2, width, width), lambda j, m: (0, 0, 0)),
                fixed(proj_weight.shape),
            ],
            out_specs=[
                clamped,
                fixed(stats_model.shape),
                pl.BlockSpec((model_rows, width), lambda j, m: (0, jnp.minimum(j, tiles - 1))),
                fixed((width, span)),
                fixed((model_rows, width)),
                fixed((model_rows, width)),
                fixed((model_rows, width)),
            ],
            scratch_shapes=[
                pltpu.VMEM((span, width), f32),
                pltpu.VMEM((model_rows, width), f32),
                pltpu.VMEM((model_rows, width), f32),
            ],
        ),
        out_shape=[
            struct(stats_qkv.shape, f32),
            struct(stats_model.shape, f32),
            struct((model_rows, qkv_width), f32),
            struct((width, span), low),
            struct((model_rows, width), f32),
            struct((model_rows, width), f32),
            struct((model_rows, width), low),
        ],
        compiler_params=pltpu.CompilerParams(vmem_limit_bytes=48 * MIB),
        name="model_update",
    )(
        member, gradients, gradients, gradients, stats_qkv, roots_qkv, stats_model, hidden_small, roots_model,
        small_roots, proj_weight,
    )


def plain_update(
    gradients, stats_model, stats_qkv, stats_hidden, roots_model, roots_qkv, roots_hidden, small_roots, proj_weight,
    fc2_weight,
):
    width = gradients.shape[1]
    member = lax.axis_index("grp")
    model_rows = stats_model.shape[1]
    picked = member * model_rows + jnp.arange(model_rows, dtype=jnp.int32)
    pick = (picked[:, None] == jnp.arange(width, dtype=jnp.int32)[None, :]).astype(low)

    def statistic_update(tall, small_rows, big_rows):
        columns = dot(pick, tall, COLS_BY_COLS)
        small_new = 0.5 * small_rows + 0.5 * dot(columns.astype(low), tall)
        rows = lax.dynamic_slice_in_dim(tall, member * big_rows.shape[0], big_rows.shape[0], 0)
        big_new = 0.5 * big_rows + 0.5 * dot(rows, tall, COLS_BY_COLS)
        return small_new, big_new, columns, rows.astype(f32)

    def product_of(big_root_rows, tall):
        return dot(big_root_rows.astype(low), tall).astype(low)

    qkv, proj, fc1, fc2 = jnp.split(gradients, [3 * width, 4 * width, 4 * width + stats_hidden.shape[2]])
    qkv_left, qkv_right, qkv_gradient, _ = statistic_update(qkv, stats_model[0], stats_qkv)
    proj_right, proj_left, _, proj_gradient = statistic_update(proj, stats_model[2], stats_model[1])
    fc1_left, fc1_right, fc1_gradient, _ = statistic_update(fc1, stats_model[3], stats_hidden[0])
    fc2_right, fc2_left, _, fc2_gradient = statistic_update(fc2, stats_model[4], stats_hidden[1])
    qkv_step = dot(small_roots[0], product_of(roots_qkv, qkv), COLS_BY_COLS).astype(low)
    fc1_step = dot(small_roots[2], product_of(roots_hidden[0], fc1), COLS_BY_COLS).astype(low)
    proj_new = proj_weight - dot(product_of(roots_model[1], proj), small_roots[1])
    fc2_new = fc2_weight - dot(product_of(roots_hidden[1], fc2), small_roots[3])
    new_stats_model = jnp.stack([qkv_left, proj_left, proj_right, fc1_left, fc2_right])
    return (
        (new_stats_model, qkv_right, jnp.stack([fc1_right, fc2_left]), qkv_step, fc1_step)
        + (qkv_gradient, proj_gradient, fc1_gradient, fc2_gradient, proj_new, fc2_new)
    )


def shards(
    plain, tokens, cotangent, window_fill, qkv_weight, proj_weight, fc1_weight, fc2_weight, vectors, vector_moments,
    bias_table, table_moments, stats_model, stats_qkv, stats_hidden, roots_model, roots_qkv, roots_hidden,
):
    width = vectors.shape[1]
    head_count = bias_table.shape[1]
    heads = LANES // (width // head_count)
    local_windows = window_fill.shape[0]
    base = (lax.axis_index(("rep", "grp")) * local_windows).astype(jnp.int32).reshape(1)
    gather = functools.partial(lax.all_gather, axis_name="grp", tiled=True)
    weights_low = [weight.astype(low) for weight in (qkv_weight, proj_weight, fc1_weight, fc2_weight)]
    if plain:
        qkv_full, proj_full, fc1_full, fc2_full = (gather(weight) for weight in weights_low)
    else:
        qkv_full, proj_full, fc1_full, fc2_full = gather_over_plane(weights_low, 0)
    hot = jnp.asarray(diagonal_tables())
    diagonals = lax.dot_general(bias_table, hot, (((0,), (1,)), ((), ())), precision=lax.Precision.HIGHEST)
    relative = relative_bias(diagonals, heads)
    probs, mixed, normed, context, middle, normed_two = attention_forward(
        window_fill, base, tokens, qkv_full, proj_full, vectors, relative, head_count
    )
    roots_low = jnp.stack([roots_model[i] for i in (0, 2, 3, 4)]).astype(low)
    roots_low, normed_two = lax.optimization_barrier((roots_low, normed_two))
    small_roots = gather(roots_low, axis=1)
    layer_output, middle_back, branch_back, fc1_term, fc2_term, fc1_bias_grad, ffn_vec = feed_forward(
        normed_two, cotangent, middle, fc1_full, fc2_full, vectors
    )
    small_roots, branch_back = lax.optimization_barrier((small_roots, branch_back))
    input_gradient, att_term, att_vec, diag_grad = attention_backward(
        probs, mixed, branch_back, middle_back, proj_full, context, normed, tokens, qkv_full, vectors, head_count
    )
    small = jnp.concatenate([part.reshape(-1, 128) for part in (att_vec[:4], ffn_vec[:4], fc1_bias_grad, diag_grad)])
    terms = (att_term, fc1_term, fc2_term)
    if plain:
        small = lax.psum(small, ("rep", "grp"))
        parts = [lax.psum(lax.psum_scatter(term, "grp", scatter_dimension=0, tiled=True), "rep") for term in terms]
        gradients = jnp.concatenate([gather(part) for part in parts])
    else:
        gradients, small = all_reduce(terms, small, 1)
    vector_total = small[: vectors.size // 128].reshape(vectors.shape)
    table_total = lax.dot_general(
        hot, small[vectors.size // 128 :].reshape(diag_grad.shape), (((0,), (1,)), ((), ())), precision=lax.Precision.HIGHEST
    )
    if plain:
        updates = plain_update(
            gradients, stats_model, stats_qkv, stats_hidden, roots_model, roots_qkv, roots_hidden, small_roots,
            proj_weight, fc2_weight,
        )
    else:
        member = lax.axis_index("grp").astype(jnp.int32).reshape(1)
        new_stats_hidden, hidden_small, fc1_gradient, fc1_step, fc2_gradient, fc2_new, fc2_copy = hidden_update(
            member, gradients, stats_hidden, roots_hidden, stats_model, small_roots, fc2_weight
        )
        qkv_right, new_stats_model, qkv_gradient, qkv_step, proj_gradient, proj_new, proj_copy = model_update(
            member, gradients, stats_qkv, roots_qkv, stats_model, hidden_small, roots_model, small_roots, proj_weight
        )
        updates = (
            (new_stats_model, qkv_right, new_stats_hidden, qkv_step, fc1_step)
            + (qkv_gradient, proj_gradient, fc1_gradient, fc2_gradient, proj_new, fc2_new)
        )
    new_stats_model, qkv_right, new_stats_hidden, qkv_step, fc1_step = updates[:5]
    qkv_gradient, proj_gradient, fc1_gradient, fc2_gradient, proj_new, fc2_new = updates[5:]
    qkv_new = qkv_weight - lax.all_to_all(qkv_step, "grp", 0, 1, tiled=True).astype(f32)
    fc1_new = fc1_weight - lax.all_to_all(fc1_step, "grp", 0, 1, tiled=True).astype(f32)
    total_tokens = tokens.shape[0] * lax.axis_size("rep") * lax.axis_size("grp")
    rate_base = total_tokens ** (-0.5)
    new_vector_moments = 0.9 * vector_moments + 0.1 * vector_total
    new_vectors = vectors - 2.0 * rate_base * new_vector_moments
    new_table_moments = 0.9 * table_moments + 0.1 * table_total
    new_table = bias_table - 8.0 * rate_base * new_table_moments
    masters = (qkv_new, proj_new, fc1_new, fc2_new)
    copies = [master.astype(low) for master in masters]
    if not plain:
        copies[1], copies[3] = proj_copy, fc2_copy
    return (
        (layer_output, input_gradient, qkv_gradient, proj_gradient, fc1_gradient, fc2_gradient)
        + masters
        + tuple(copies)
        + (new_stats_model, qkv_right, new_stats_hidden, new_vectors, new_vector_moments, new_table, new_table_moments)
    )


def solution(mesh):
    tokens, rows, blocks, copied = P(("rep", "grp"), None), P("grp", None), P(None, "grp", None), P()
    plain = (mesh.shape["rep"], mesh.shape["grp"]) != (4, 8)
    return jax.shard_map(
        functools.partial(shards, plain),
        mesh=mesh,
        in_specs=(tokens, tokens, P(("rep", "grp")))
        + (rows,) * 4
        + (copied,) * 4
        + (blocks, rows, blocks) * 2,
        out_specs=(tokens,) * 2 + (rows,) * 12 + (blocks, rows, blocks) + (copied,) * 4,
        check_vma=False,
    )
```

```python
import functools

import jax
import jax.numpy as jnp
import numpy as np
from jax import lax
from jax.experimental import pallas as pl
from jax.experimental.pallas import tpu as pltpu
from jax.sharding import PartitionSpec as P

WT = 144
SIDE = 12
SPAN = 2 * SIDE - 1
LANES = 256
DIAG = 384
ROW_TILE = 144
MIB = 1024 * 1024
low = jnp.bfloat16
f32 = jnp.float32

ROWS_BY_COLS = (((1,), (0,)), ((), ()))
COLS_BY_COLS = (((1,), (1,)), ((), ()))
ROWS_BY_ROWS = (((0,), (0,)), ((), ()))


def dot(left_matrix, right_matrix, dims=ROWS_BY_COLS):
    return lax.dot_general(left_matrix, right_matrix, dims, preferred_element_type=f32)


def standardize(values):
    centred = values - jnp.mean(values, axis=-1, keepdims=True)
    inverse = lax.rsqrt(jnp.mean(centred * centred, axis=-1, keepdims=True) + 1e-05)
    return centred * inverse, inverse


def norm_back(grad, gain, xhat, inverse):
    scaled = grad * gain
    mean_scaled = jnp.mean(scaled, axis=-1, keepdims=True)
    mean_product = jnp.mean(scaled * xhat, axis=-1, keepdims=True)
    return inverse * (scaled - mean_scaled - xhat * mean_product)


def column_sum(values):
    return jnp.sum(values, axis=0, keepdims=True)


def diagonal_tables():
    pair = np.arange(DIAG) - WT
    quotient, rest = pair // SIDE, pair % SIDE
    near = (quotient + SIDE - 1) * SPAN + rest + SIDE - 1
    far = (quotient + SIDE) * SPAN + rest - 1
    near_live = (np.abs(pair) < WT) & (quotient >= 1 - SIDE)
    far_live = (np.abs(pair) < WT) & (rest >= 1) & (quotient < SIDE - 1)
    hot = np.zeros((2, DIAG, SPAN * SPAN), np.float32)
    hot[0, np.arange(DIAG)[near_live], near[near_live]] = 1.0
    hot[1, np.arange(DIAG)[far_live], far[far_live]] = 1.0
    return hot.reshape(2 * DIAG, SPAN * SPAN)


def near_mask(shape, mirrored=False):
    column = lax.rem(lax.broadcasted_iota(jnp.int32, shape, 0), SIDE)
    if mirrored:
        column = SIDE - 1 - column
    rest = lax.rem(lax.broadcasted_iota(jnp.int32, shape, 1), SIDE)
    return column + rest < SIDE


def additive_types(heads):
    slot = np.arange(WT)
    row_high, col_high = slot // SIDE >= SIDE // 2, slot % SIDE >= SIDE // 2
    row_differs = row_high[:, None] != row_high[None, :]
    col_differs = col_high[:, None] != col_high[None, :]
    types = [
        np.where((row_differs & bool(kind // 2)) | (col_differs & bool(kind % 2)), -100.0, 0.0)
        for kind in range(4)
    ]
    return np.tile(np.stack(types), (1, 1, heads)).astype(np.float32)


def stack_mask(heads, head_size):
    lane_head = np.arange(heads * head_size) // head_size
    hot = lane_head[None, None, :] == np.arange(heads)[:, None, None]
    return np.broadcast_to(hot, (heads, WT, heads * head_size)).reshape(heads * WT, -1).astype(low)


def relative_rows(heads, diag_ref, rel_ref):
    mask = near_mask((WT, DIAG))
    for head in range(heads * rel_ref.shape[0]):
        group, place = head // heads, head % heads
        near = diag_ref[head : head + 1, :DIAG]
        far = diag_ref[head : head + 1, DIAG:]
        rolled = pltpu.roll(jnp.where(mask, near, far), DIAG - WT, 1, stride=1, stride_axis=0)
        rel_ref[group, :, place * WT : (place + 1) * WT] = rolled[:, :WT]


def stacked(block, mask_ref, heads):
    return jnp.concatenate([block] * heads, axis=0) * mask_ref[...]


def diagonal_blocks(full, heads, head_size):
    lane_head = lax.broadcasted_iota(jnp.int32, (WT, full.shape[1]), 1) // head_size
    picked = jnp.zeros((WT, full.shape[1]), f32)
    for head in range(heads):
        picked = jnp.where(lane_head == head, full[head * WT : (head + 1) * WT], picked)
    return picked


def for_row_tiles(count, body):
    def step(index, carry):
        body(pl.ds(pl.multiple_of(index * ROW_TILE, ROW_TILE), ROW_TILE))
        return carry

    lax.fori_loop(0, count // ROW_TILE, step, 0)


class Forward:
    def __init__(self, heads, head_size, refs):
        self.heads, self.head_size = heads, head_size
        self.fill, self.tokens, self.vec, self.diag, self.add, self.mask = refs[:6]
        self.probs, self.mixed_out, self.normed, self.context, self.middle, self.normed_two = refs[6:12]
        self.mixed, self.added, self.rel = refs[12:15]
        self.count, self.width = self.tokens.shape
        self.groups = self.width // LANES

    def norm_one(self):
        def body(rows):
            xhat, _ = standardize(self.tokens[rows, :].astype(f32))
            self.normed[rows, :] = (xhat * self.vec[0:1, :] + self.vec[1:2, :]).astype(low)

        for_row_tiles(self.count, body)

    def mix(self, weight_tile):
        for part in range(3):
            for tile in range(self.groups):
                start = part * self.width + tile * LANES
                sums = dot(self.normed[...], weight_tile(start))
                if part != 1:
                    row = 2 if part == 0 else 3
                    sums = sums + self.vec[row : row + 1, tile * LANES : (tile + 1) * LANES]
                self.mixed[:, start : start + LANES] = sums.astype(low)

    def attend(self, window, first_window):
        width, heads = self.width, self.heads
        rows = pl.ds(pl.multiple_of(window * WT, WT), WT)
        self.mixed_out[...] = self.mixed[rows, :]
        kind = lax.rem(first_window + window, 4)
        slot = lax.broadcasted_iota(jnp.int32, self.added.shape, 0)
        self.added[...] = jnp.where(slot < self.fill[window], self.add[kind], -1e30)
        for group in range(self.groups):
            query, key, value = (
                self.mixed[rows, part * width + group * LANES : part * width + (group + 1) * LANES]
                for part in range(3)
            )
            scores = dot(key, stacked(query, self.mask, heads), COLS_BY_COLS) * self.head_size ** (-0.5)
            scores = scores + self.rel[group] + self.added[...]
            exponent = jnp.exp(scores - jnp.max(scores, axis=0, keepdims=True))
            probs = (exponent * (1.0 / jnp.sum(exponent, axis=0, keepdims=True))).astype(low)
            self.probs[group] = probs
            full = dot(probs, value, ROWS_BY_ROWS)
            self.context[rows, group * LANES : (group + 1) * LANES] = diagonal_blocks(
                full, heads, self.head_size
            ).astype(low)

    def finish(self, weight_tile):
        for tile in range(self.groups):
            span = slice(tile * LANES, (tile + 1) * LANES)
            self.middle[:, span] = (
                self.tokens[:, span].astype(f32) + dot(self.context[...], weight_tile(tile * LANES)) + self.vec[4:5, span]
            )

        def body(rows):
            xhat, _ = standardize(self.middle[rows, :])
            self.normed_two[rows, :] = (xhat * self.vec[5:6, :] + self.vec[6:7, :]).astype(low)

        for_row_tiles(self.count, body)


def plain_forward_kernel(heads, head_size, base_ref, qkv_ref, proj_ref, *refs):
    work = Forward(heads, head_size, refs)
    window = pl.program_id(0)

    @pl.when(window == 0)
    def _():
        relative_rows(heads, work.diag, work.rel)
        work.norm_one()
        work.mix(lambda start: qkv_ref[:, start : start + LANES])

    work.attend(window, base_ref[0])

    @pl.when(window == pl.num_programs(0) - 1)
    def _():
        work.finish(lambda start: proj_ref[:, start : start + LANES])


def whole(shape):
    return pl.BlockSpec(shape, lambda *_: (0,) * len(shape), pipeline_mode=pl.Buffered(1))


def struct(shape, dtype):
    return jax.ShapeDtypeStruct(shape, dtype)


HBM = pl.BlockSpec(memory_space=pl.ANY)
SMEM = pl.BlockSpec(memory_space=pltpu.SMEM)


def forward_parts(fill, tokens, vectors, diagonals, head_count):
    count, width = tokens.shape
    windows = fill.shape[0]
    head_size = width // head_count
    heads = LANES // head_size
    groups = width // LANES
    operands = [tokens, vectors, diagonals, jnp.asarray(additive_types(heads)), jnp.asarray(stack_mask(heads, head_size))]
    in_specs = [SMEM] + [whole(operand.shape) for operand in operands]
    out_specs = [
        pl.BlockSpec((groups, WT, heads * WT), lambda w: (w, 0, 0)),
        pl.BlockSpec((WT, 3 * width), lambda w: (w, 0)),
    ] + [whole((count, width))] * 4
    out_shape = [
        struct((windows * groups, WT, heads * WT), low),
        struct((count, 3 * width), low),
        struct((count, width), low),
        struct((count, width), low),
        struct((count, width), f32),
        struct((count, width), low),
    ]
    scratch = [
        pltpu.VMEM((count, 3 * width), low),
        pltpu.VMEM((WT, heads * WT), f32),
        pltpu.VMEM((groups, WT, heads * WT), f32),
    ]
    return (heads, head_size), [fill] + operands, in_specs, out_specs, out_shape, scratch


def attention_forward(fill, base, tokens, qkv_full, proj_full, vectors, diagonals, head_count):
    sizes, operands, in_specs, out_specs, out_shape, scratch = forward_parts(
        fill, tokens, vectors, diagonals, head_count
    )
    return pl.pallas_call(
        functools.partial(plain_forward_kernel, *sizes),
        grid=(fill.shape[0],),
        in_specs=[SMEM, whole(qkv_full.shape), whole(proj_full.shape)] + in_specs,
        out_specs=out_specs,
        out_shape=out_shape,
        scratch_shapes=scratch,
        compiler_params=pltpu.CompilerParams(vmem_limit_bytes=56 * MIB),
        name="attention_forward",
    )(base, qkv_full, proj_full, *operands)


def feed_forward_kernel(
    normed_ref, cot_ref, middle_ref, fc1_ref, fc2_ref, bias_ref, vec_ref,
    out_ref, middle_back_ref, branch_back_ref, fc1_grad_ref, fc2_grad_ref, bias_grad_ref, vec_grad_ref,
    out_sum, back_sum,
):
    step = pl.program_id(0)
    count, width = cot_ref.shape
    hidden = dot(normed_ref[...], fc1_ref[...]) + bias_ref[...]
    bell = jnp.exp(hidden * hidden * -0.5)
    below = 0.5 * (1.0 + lax.erf(hidden * (0.5 ** 0.5)))
    active = (hidden * below).astype(low)
    slope = below + hidden * bell * ((2.0 * np.pi) ** -0.5)
    hidden_back = dot(cot_ref[...], fc2_ref[...], COLS_BY_COLS) * slope
    hidden_back = hidden_back.astype(low)
    bias_grad_ref[...] = column_sum(hidden_back.astype(f32))
    fc2_grad_ref[...] = dot(active, cot_ref[...], ROWS_BY_ROWS).astype(low)
    fc1_grad_ref[...] = dot(hidden_back, normed_ref[...], ROWS_BY_ROWS).astype(low)
    out_term = dot(active, fc2_ref[...])
    back_term = dot(hidden_back, fc1_ref[...], COLS_BY_COLS)

    @pl.when(step == 0)
    def _():
        out_sum[...] = out_term
        back_sum[...] = back_term

    @pl.when(step > 0)
    def _():
        out_sum[...] += out_term
        back_sum[...] += back_term

    @pl.when(step == pl.num_programs(0) - 1)
    def _():
        vec_grad_ref[...] = jnp.zeros_like(vec_grad_ref)

        def finish(part, carry):
            rows = pl.ds(pl.multiple_of(part * ROW_TILE, ROW_TILE), ROW_TILE)
            middle = middle_ref[rows, :]
            cot = cot_ref[rows, :].astype(f32)
            out_ref[rows, :] = (middle + out_sum[rows, :] + vec_ref[7:8, :]).astype(low)
            xhat, inverse = standardize(middle)
            grad = back_sum[rows, :]
            middle_back = cot + norm_back(grad, vec_ref[5:6, :], xhat, inverse)
            middle_back_ref[rows, :] = middle_back
            branch_back = middle_back.astype(low)
            branch_back_ref[rows, :] = branch_back
            vec_grad_ref[0:1, :] += column_sum(branch_back.astype(f32))
            vec_grad_ref[1:2, :] += column_sum(grad * xhat)
            vec_grad_ref[2:3, :] += column_sum(grad)
            vec_grad_ref[3:4, :] += column_sum(cot)
            return carry

        lax.fori_loop(0, count // ROW_TILE, finish, 0)


def feed_forward(normed, cotangent, middle, fc1_full, fc2_full, vectors):
    count, width = cotangent.shape
    hidden_width = fc1_full.shape[1]
    tile = LANES
    bias = vectors[8:].reshape(1, hidden_width)
    return pl.pallas_call(
        feed_forward_kernel,
        grid=(hidden_width // tile,),
        in_specs=[whole(x.shape) for x in (normed, cotangent, middle)]
        + [
            pl.BlockSpec((width, tile), lambda f: (0, f)),
            pl.BlockSpec((tile, width), lambda f: (f, 0)),
            pl.BlockSpec((1, tile), lambda f: (0, f)),
            whole(vectors.shape),
        ],
        out_specs=[
            whole((count, width)),
            whole((count, width)),
            whole((count, width)),
            pl.BlockSpec((tile, width), lambda f: (f, 0)),
            pl.BlockSpec((tile, width), lambda f: (f, 0)),
            pl.BlockSpec((1, tile), lambda f: (0, f)),
            whole((8, width)),
        ],
        out_shape=[
            struct((count, width), low),
            struct((count, width), f32),
            struct((count, width), low),
            struct((hidden_width, width), low),
            struct((hidden_width, width), low),
            struct((1, hidden_width), f32),
            struct((8, width), f32),
        ],
        scratch_shapes=[pltpu.VMEM((count, width), f32), pltpu.VMEM((count, width), f32)],
        compiler_params=pltpu.CompilerParams(vmem_limit_bytes=56 * MIB),
        name="feed_forward",
    )(normed, cotangent, middle, fc1_full, fc2_full, bias, vectors)


def backward_kernel(
    heads, head_size, probs_ref, mixed_ref, branch_back_ref, middle_back_ref, proj_ref, context_ref, normed_ref,
    tokens_ref, qkv_ref, vec_ref, mask_ref,
    input_grad_ref, weight_grad_ref, vec_grad_ref, diag_ref,
    context_back_ref, mixed_back_ref, pairs_ref, normed_back_ref,
):
    window = pl.program_id(0)
    count, width = tokens_ref.shape
    groups = width // LANES
    score_scale = head_size ** (-0.5)

    @pl.when(window == 0)
    def _():
        pairs_ref[...] = jnp.zeros_like(pairs_ref)
        for tile in range(groups):
            span = slice(tile * LANES, (tile + 1) * LANES)
            context_back_ref[:, span] = dot(branch_back_ref[...], proj_ref[span, :], COLS_BY_COLS).astype(low)
            weight_grad_ref[3 * width + tile * LANES : 3 * width + (tile + 1) * LANES, :] = dot(
                context_ref[:, span], branch_back_ref[...], ROWS_BY_ROWS
            ).astype(low)

    rows = pl.ds(pl.multiple_of(window * WT, WT), WT)
    for group in range(groups):
        spans = [slice(part * width + group * LANES, part * width + (group + 1) * LANES) for part in range(3)]
        query, key, value = (mixed_ref[:, span] for span in spans)
        probs_low = probs_ref[group]
        probs = probs_low.astype(f32)
        back_stack = stacked(context_back_ref[rows, spans[0]], mask_ref, heads)
        value_back = dot(probs_low, back_stack)
        product = probs * dot(value, back_stack, COLS_BY_COLS)
        scores_back = (product - probs * jnp.sum(product, axis=0, keepdims=True)).astype(low)
        pairs_ref[group] += scores_back.astype(f32)
        key_back = dot(scores_back, stacked(query, mask_ref, heads)) * score_scale
        full = dot(scores_back, key, ROWS_BY_ROWS)
        query_back = diagonal_blocks(full, heads, head_size) * score_scale
        mixed_back_ref[rows, spans[0]] = query_back.astype(low)
        mixed_back_ref[rows, spans[1]] = key_back.astype(low)
        mixed_back_ref[rows, spans[2]] = value_back.astype(low)

    @pl.when(window == pl.num_programs(0) - 1)
    def _():
        vec_grad_ref[...] = jnp.zeros_like(vec_grad_ref)
        for part in range(3):
            for tile in range(groups):
                start = part * width + tile * LANES
                block = mixed_back_ref[:, start : start + LANES]
                weight_grad_ref[start : start + LANES, :] = dot(block, normed_ref[...], ROWS_BY_ROWS).astype(low)
                if part != 1:
                    row = 2 if part == 0 else 3
                    span = slice(tile * LANES, (tile + 1) * LANES)
                    vec_grad_ref[row : row + 1, span] = column_sum(block.astype(f32))
        for tile in range(groups):
            span = slice(tile * LANES, (tile + 1) * LANES)
            normed_back_ref[:, span] = dot(mixed_back_ref[...], qkv_ref[span, :], COLS_BY_COLS)

        def finish(part, carry):
            rows = pl.ds(pl.multiple_of(part * ROW_TILE, ROW_TILE), ROW_TILE)
            xhat, inverse = standardize(tokens_ref[rows, :].astype(f32))
            grad = normed_back_ref[rows, :]
            back = middle_back_ref[rows, :] + norm_back(grad, vec_ref[0:1, :], xhat, inverse)
            input_grad_ref[rows, :] = back.astype(low)
            vec_grad_ref[0:1, :] += column_sum(grad * xhat)
            vec_grad_ref[1:2, :] += column_sum(grad)
            return carry

        lax.fori_loop(0, count // ROW_TILE, finish, 0)
        mask = near_mask((WT, DIAG), mirrored=True)
        order = [lax.broadcasted_iota(jnp.int32, (WT, WT), axis) for axis in range(2)]
        mirror = jnp.where(order[0] + order[1] == WT - 1, 1.0, 0.0).astype(f32)
        for group in range(groups):
            pairs_ref[group] = lax.dot_general(
                mirror, pairs_ref[group], ROWS_BY_COLS, precision=lax.Precision.HIGHEST, preferred_element_type=f32
            )
        for head in range(groups * heads):
            group, place = head // heads, head % heads
            block = pairs_ref[group, :, place * WT : (place + 1) * WT]
            block = jnp.concatenate([block, jnp.zeros((WT, DIAG - WT), f32)], axis=1)
            rolled = pltpu.roll(block, 1, 1, stride=1, stride_axis=0)
            near = column_sum(jnp.where(mask, rolled, 0.0))
            far = column_sum(jnp.where(mask, 0.0, rolled))
            diag_ref[head : head + 1, :DIAG] = near
            diag_ref[head : head + 1, DIAG:] = far


def attention_backward(
    probs, mixed, branch_back, middle_back, proj_full, context, normed, tokens, qkv_full, vectors, head_count
):
    count, width = tokens.shape
    windows = count // WT
    head_size = width // head_count
    heads = LANES // head_size
    groups = width // LANES
    mask = jnp.asarray(stack_mask(heads, head_size))
    return pl.pallas_call(
        functools.partial(backward_kernel, heads, head_size),
        grid=(windows,),
        in_specs=[
            pl.BlockSpec((groups, WT, heads * WT), lambda w: (w, 0, 0)),
            pl.BlockSpec((WT, 3 * width), lambda w: (w, 0)),
        ]
        + [
            whole(x.shape)
            for x in (branch_back, middle_back, proj_full, context, normed, tokens, qkv_full, vectors, mask)
        ],
        out_specs=[
            whole((count, width)),
            whole((4 * width, width)),
            whole((8, width)),
            whole((head_count, 2 * DIAG)),
        ],
        out_shape=[
            struct((count, width), low),
            struct((4 * width, width), low),
            struct((8, width), f32),
            struct((head_count, 2 * DIAG), f32),
        ],
        scratch_shapes=[
            pltpu.VMEM((count, width), low),
            pltpu.VMEM((count, 3 * width), low),
            pltpu.VMEM((groups, WT, heads * WT), f32),
            pltpu.VMEM((count, width), f32),
        ],
        compiler_params=pltpu.CompilerParams(vmem_limit_bytes=60 * MIB),
        name="attention_backward",
    )(probs, mixed, branch_back, middle_back, proj_full, context, normed, tokens, qkv_full, vectors, mask)


MESH = pl.DeviceIdType.MESH


class Peers:
    def __init__(self):
        self.z = lax.axis_index("rep")
        place = lax.axis_index("grp")
        self.c = lax.rem(place, 2)
        self.x = lax.rem(place // 2, 2)
        self.y = place // 4
        self.core_peer = (self.z, place + 1 - 2 * self.c)
        self.x_peer = (self.z, place + 2 - 4 * self.x)
        self.y_peer = (self.z, place + 4 - 8 * self.y)
        self.z_places = [lax.rem(self.z + step, 4) for step in range(1, 4)]
        self.z_peers = [(there, place) for there in self.z_places]

    def plane(self):
        return [self.core_peer, self.x_peer, self.y_peer]

    def everyone(self):
        return self.plane() + self.z_peers


def meet(peers):
    barrier = pltpu.get_barrier_semaphore()
    for peer in peers:
        pl.semaphore_signal(barrier, inc=1, device_id=peer, device_id_type=MESH)
    pl.semaphore_wait(barrier, len(peers))


class Copies:
    def __init__(self, send_sems, recv_sems):
        self.send_sems, self.recv_sems = send_sems, recv_sems
        self.made = []

    def make(self, ends, peer):
        copy = Copy(self, len(self.made), ends, peer)
        self.made.append(copy)
        copy.build().start()
        return copy

    def drain(self):
        for copy in self.made:
            copy.build().wait_send()


class Copy:
    def __init__(self, owner, number, ends, peer):
        self.owner, self.number, self.ends, self.peer = owner, number, ends, peer

    def build(self):
        source, target = self.ends()
        return pltpu.make_async_remote_copy(
            src_ref=source,
            dst_ref=target,
            send_sem=self.owner.send_sems.at[self.number],
            recv_sem=self.owner.recv_sems.at[self.number],
            device_id=self.peer,
            device_id_type=MESH,
        )

    def wait_recv(self):
        self.build().wait_recv()


def same(place):
    return lambda: (place(), place())


class Gather:
    def __init__(self, me, copies, source, out):
        self.me, self.copies, self.source, self.out = me, copies, source, out
        self.half = out.shape[3] // 2
        self.across = []

    def block(self, flip_y, flip_x):
        me = self.me
        return self.out.at[1 - me.y if flip_y else me.y, 1 - me.x if flip_x else me.x, me.c]

    def start(self):
        me = self.me

        def ends():
            return self.source(), self.block(False, False)

        self.by_x = self.copies.make(ends, me.x_peer)
        self.by_y = self.copies.make(ends, me.y_peer)
        self.across.append(self.copies.make(ends, me.core_peer))

    def relay(self):
        me = self.me
        self.by_x.wait_recv()
        to_y = self.copies.make(same(lambda: self.block(False, True).at[pl.ds(0, self.half)]), me.y_peer)
        self.by_y.wait_recv()
        to_x = self.copies.make(same(lambda: self.block(True, False).at[pl.ds(self.half, self.half)]), me.x_peer)
        self.relayed = (to_x, to_y)
        self.across.append(self.copies.make(same(lambda: self.block(False, True)), me.core_peer))
        self.across.append(self.copies.make(same(lambda: self.block(True, False)), me.core_peer))

    def cross(self):
        for copy in self.relayed:
            copy.wait_recv()
        self.across.append(self.copies.make(same(lambda: self.block(True, True)), self.me.core_peer))

    def wait(self):
        for copy in self.across:
            copy.wait_recv()


def gathered_forward_kernel(heads, head_size, *refs):
    qkv_shard, proj_shard, fc1_shard, fc2_shard = refs[:4]
    outs = refs[10:20]
    qkv_out, proj_out, fc1_out, fc2_out = outs[6:]
    scratch = refs[20:]
    work = Forward(heads, head_size, refs[4:10] + outs[:6] + scratch[:3])
    qkv_full, proj_full, fc1_low, fc2_low, send_sems, recv_sems, local_sems = scratch[3:]
    me = Peers()
    copies = Copies(send_sems, recv_sems)
    own = (me.y, me.x, me.c)
    qkv = Gather(me, copies, lambda: qkv_full.at[own], qkv_full)
    proj = Gather(me, copies, lambda: proj_full.at[own], proj_full)
    fc1 = Gather(me, copies, lambda: fc1_low, fc1_out)
    fc2 = Gather(me, copies, lambda: fc2_low, fc2_out)

    def local(index):
        source = (fc1_low, fc2_low, qkv_full, proj_full)[index]
        target = (fc1_out, fc2_out, qkv_out, proj_out)[index]
        return pltpu.make_async_copy(source, target.at[own] if index < 2 else target, local_sems.at[index])

    window = pl.program_id(0)
    first_window = (me.z * 8 + me.y * 4 + me.x * 2 + me.c) * pl.num_programs(0)

    def weight_tile(full):
        def tile(start):
            return full[:, :, :, :, start : start + LANES].reshape(-1, LANES)

        return tile

    @pl.when(window == 0)
    def _():
        qkv_full[own] = qkv_shard[...].astype(low)
        proj_full[own] = proj_shard[...].astype(low)
        meet(me.plane())
        qkv.start()
        proj.start()
        fc1_low[...] = fc1_shard[...].astype(low)
        fc2_low[...] = fc2_shard[...].astype(low)
        work.norm_one()
        relative_rows(heads, work.diag, work.rel)
        qkv.relay()
        proj.relay()
        fc1.start()
        fc2.start()
        local(0).start()
        local(1).start()
        qkv.cross()
        qkv.wait()
        local(2).start()
        work.mix(weight_tile(qkv_full))

    @pl.when(window == 1)
    def _():
        proj.cross()

    @pl.when(window == 3)
    def _():
        fc1.relay()

    @pl.when(window == 6)
    def _():
        fc1.cross()
        fc2.relay()

    work.attend(window, first_window)

    @pl.when(window == pl.num_programs(0) - 1)
    def _():
        proj.wait()
        local(3).start()
        work.finish(weight_tile(proj_full))
        fc2.cross()
        fc1.wait()
        fc2.wait()
        for index in range(4):
            local(index).wait()
        copies.drain()


def gathered_forward(fill, tokens, weights, vectors, diagonals, head_count, collective_id):
    sizes, operands, in_specs, out_specs, out_shape, scratch = forward_parts(
        fill, tokens, vectors, diagonals, head_count
    )
    fulls = [(2, 2, 2) + weight.shape for weight in weights]
    results = pl.pallas_call(
        functools.partial(gathered_forward_kernel, *sizes),
        grid=(fill.shape[0],),
        in_specs=[whole(weight.shape) for weight in weights] + in_specs,
        out_specs=out_specs + [HBM] * 4,
        out_shape=out_shape + [struct(full, low) for full in fulls],
        scratch_shapes=scratch
        + [pltpu.VMEM(fulls[0], low), pltpu.VMEM(fulls[1], low)]
        + [pltpu.VMEM(weight.shape, low) for weight in weights[2:]]
        + [pltpu.SemaphoreType.DMA((32,)), pltpu.SemaphoreType.DMA((32,)), pltpu.SemaphoreType.DMA((4,))],
        compiler_params=pltpu.CompilerParams(
            collective_id=collective_id, has_side_effects=True, vmem_limit_bytes=58 * MIB
        ),
        name="gathered_forward",
    )(*weights, *operands)
    return results[:6], [full.reshape(-1, weight.shape[1]) for full, weight in zip(results[6:], weights)]


PIECE = 48
BLOCK = 32 * PIECE


def reduce_kernel(where, amount, *refs):
    inputs = 1 + max(source for source, _ in where)
    terms, small, out, small_out = refs[:inputs], refs[inputs], refs[inputs + 1], refs[inputs + 2]
    mine, core_in, first_in, second_in, z_in, final, small_in, send_sems, recv_sems, local_sems = refs[inputs + 3 :]
    me = Peers()
    meet(me.everyone())
    copies = Copies(send_sems, recv_sems)
    c, x, y, z = me.c, me.x, me.y, me.z
    parts = range(amount)
    core, first, second, over_z, last_z, spread, relay, across = ([None] * amount for _ in range(8))
    loads, stores = [None] * amount, [None] * amount
    half = out.shape[-1] // 2
    by_x_first, by_y_first = pl.ds(0, half), pl.ds(half, half)

    def start(k):
        source, place = where[k]
        core[k] = copies.make(lambda: (terms[source].at[place, 1 - c], core_in.at[k]), me.core_peer)
        loads[k] = pltpu.make_async_copy(terms[source].at[place, c], mine.at[k], local_sems.at[2 * k])
        loads[k].start()

    def finish_core(k):
        loads[k].wait()
        core[k].wait_recv()

        def add(step, carry):
            at = (k, step // 8, lax.rem(step // 4, 2), lax.rem(step, 4))
            mine[at] = mine[at] + core_in[at]
            return carry

        lax.fori_loop(0, 16, add, 0)
        first[k] = (
            copies.make(lambda: (mine.at[k, 1 - x, :, :, :, by_x_first], first_in.at[k, 0]), me.x_peer),
            copies.make(lambda: (mine.at[k, :, 1 - y, :, :, by_y_first], first_in.at[k, 1]), me.y_peer),
        )

    def finish_first(k):
        first[k][0].wait_recv()
        first[k][1].wait_recv()

        def add(step, carry):
            other, place = step // 4, lax.rem(step, 4)
            mine[k, x, other, place, :, :half] += first_in[k, 0, other, place]
            mine[k, other, y, place, :, half:] += first_in[k, 1, other, place]
            return carry

        lax.fori_loop(0, 8, add, 0)
        second[k] = (
            copies.make(lambda: (mine.at[k, x, 1 - y, :, :, by_x_first], second_in.at[k, 0]), me.y_peer),
            copies.make(lambda: (mine.at[k, 1 - x, y, :, :, by_y_first], second_in.at[k, 1]), me.x_peer),
        )

    def finish_second(k):
        second[k][0].wait_recv()
        second[k][1].wait_recv()

        def add(place, carry):
            mine[k, x, y, place, :, :half] += second_in[k, 0, place]
            mine[k, x, y, place, :, half:] += second_in[k, 1, place]
            return carry

        lax.fori_loop(0, 4, add, 0)
        over_z[k] = [
            copies.make(lambda there=there: (mine.at[k, x, y, there], z_in.at[k, z]), peer)
            for there, peer in zip(me.z_places, me.z_peers)
        ]
        z_in[k, z] = mine[k, x, y, z]

    def finish_z(k):
        for copy in over_z[k]:
            copy.wait_recv()
        total = z_in[k, 0].astype(f32)
        for place in range(1, 4):
            total = total + z_in[k, place].astype(f32)
        final[k] = total.astype(low)
        last_z[k] = [copies.make(lambda: (final.at[k], out.at[k, c, x, y, z]), peer) for peer in me.z_peers]
        stores[k] = pltpu.make_async_copy(final.at[k], out.at[k, c, x, y, z], local_sems.at[2 * k + 1])
        stores[k].start()

    def finish_last_z(k):
        for copy in last_z[k]:
            copy.wait_recv()
        stores[k].wait()
        own = same(lambda: out.at[k, c, x, y])
        spread[k] = [copies.make(own, peer) for peer in (me.x_peer, me.y_peer)]
        across[k] = [copies.make(own, me.core_peer)]

    def finish_spread(k):
        by_x, by_y = spread[k]
        by_y.wait_recv()
        to_x = copies.make(same(lambda: out.at[k, c, x, 1 - y, :, :, by_x_first]), me.x_peer)
        by_x.wait_recv()
        to_y = copies.make(same(lambda: out.at[k, c, 1 - x, y, :, :, by_y_first]), me.y_peer)
        relay[k] = (to_x, to_y)
        across[k].append(copies.make(same(lambda: out.at[k, c, 1 - x, y]), me.core_peer))
        across[k].append(copies.make(same(lambda: out.at[k, c, x, 1 - y]), me.core_peer))

    def finish_relay(k):
        for copy in relay[k]:
            copy.wait_recv()
        across[k].append(copies.make(same(lambda: out.at[k, c, 1 - x, 1 - y]), me.core_peer))

    small_peers = [me.core_peer, me.x_peer, me.y_peer]
    small_copies = []

    def small_step(step):
        if step > 0:
            small_copies[step - 1].wait_recv()
            small_out[...] += small_in[step - 1]
        else:
            small_out[...] = small[...]
        if step < 3:
            small_in[step + 6] = small_out[...]
            small_copies.append(
                copies.make(lambda: (small_in.at[step + 6], small_in.at[step]), small_peers[step])
            )
        else:
            small_in[9 + z] = small_out[...]
            for peer in me.z_peers:
                small_copies.append(copies.make(same(lambda: small_in.at[9 + z]), peer))

    def small_end():
        for copy in small_copies[3:]:
            copy.wait_recv()
        small_out[...] = (small_in[9] + small_in[10]) + (small_in[11] + small_in[12])

    for k in parts:
        start(k)
    stages = [finish_core, finish_first, finish_second, finish_z, finish_last_z, finish_spread, finish_relay]
    small_step(0)
    for wave in range(amount + len(stages) - 1):
        for k in reversed(parts):
            if 0 <= wave - k < len(stages):
                stages[wave - k](k)
        if 1 <= wave <= 3:
            small_step(wave)
        elif wave == 4:
            small_end()
    for k in parts:
        for copy in across[k]:
            copy.wait_recv()
    copies.drain()


def all_reduce(terms, small, collective_id):
    width = terms[0].shape[1]
    where = [(source, place) for source, term in enumerate(terms) for place in range(term.shape[0] // BLOCK)]
    amount = len(where)
    shape = (2, 2, 2, 4, PIECE, width)
    count = 19 * amount + 8
    vmem = pl.BlockSpec(memory_space=pltpu.VMEM)
    whole_sum, small_sum = pl.pallas_call(
        functools.partial(reduce_kernel, where, amount),
        in_specs=[HBM] * len(terms) + [vmem],
        out_specs=[HBM, vmem],
        out_shape=[struct((amount,) + shape, low), struct(small.shape, f32)],
        scratch_shapes=[
            pltpu.VMEM((amount,) + shape[1:], low),
            pltpu.VMEM((amount,) + shape[1:], low),
            pltpu.VMEM((amount, 2, 2, 4, PIECE, width // 2), low),
            pltpu.VMEM((amount, 2, 4, PIECE, width // 2), low),
            pltpu.VMEM((amount, 4, PIECE, width), low),
            pltpu.VMEM((amount, PIECE, width), low),
            pltpu.VMEM((13,) + small.shape, f32),
            pltpu.SemaphoreType.DMA((count,)),
            pltpu.SemaphoreType.DMA((count,)),
            pltpu.SemaphoreType.DMA((2 * amount,)),
        ],
        compiler_params=pltpu.CompilerParams(
            collective_id=collective_id, has_side_effects=True, vmem_limit_bytes=48 * MIB
        ),
        name="all_reduce",
    )(*[term.reshape((-1,) + shape) for term in terms], small)
    return whole_sum.reshape(-1, width), small_sum


def tile_update(tall, rows, big, root, pick, product_ref, small_ref, fresh):
    columns = dot(pick, tall, COLS_BY_COLS)
    product = dot(root.astype(low), tall)
    small = dot(columns.astype(low), tall)

    @pl.when(fresh)
    def _():
        product_ref[...] = product
        small_ref[...] = small

    @pl.when(jnp.logical_not(fresh))
    def _():
        product_ref[...] += product
        small_ref[...] += small

    return 0.5 * big + 0.5 * dot(rows, tall, COLS_BY_COLS), columns


def column_pick(member, shape):
    row, column = (lax.broadcasted_iota(jnp.int32, shape, axis) for axis in range(2))
    return jnp.where(column == row + member * shape[0], 1.0, 0.0).astype(low)


def hidden_kernel(
    member_ref, tall_ref, rows_ref, big_ref, root_ref, small_ref, small_root_ref, fc2_ref,
    big_out_ref, small_out_ref, fc1_grad_ref, fc1_step_ref, fc2_grad_ref, fc2_new_ref, fc2_copy_ref,
    product_sum, small_sum,
):
    matrix, tile = pl.program_id(0), pl.program_id(1)
    pick = column_pick(member_ref[0], small_sum.shape)
    big_new, columns = tile_update(
        tall_ref[...], rows_ref[...], big_ref[0], root_ref[0], pick, product_sum, small_sum, tile == 0
    )
    big_out_ref[0] = big_new

    @pl.when(matrix == 0)
    def _():
        fc1_grad_ref[...] = columns

    @pl.when(tile == pl.num_programs(1) - 1)
    def _():
        small_out_ref[0] = 0.5 * small_ref[0] + 0.5 * small_sum[...]
        product = product_sum[...].astype(low)

        @pl.when(matrix == 0)
        def _():
            fc1_step_ref[...] = dot(small_root_ref[0], product, COLS_BY_COLS).astype(low)

        @pl.when(matrix == 1)
        def _():
            new = fc2_ref[...] - dot(product, small_root_ref[0])
            fc2_new_ref[...] = new
            fc2_copy_ref[...] = new.astype(low)
            fc2_grad_ref[...] = rows_ref[...].astype(f32)


def hidden_update(member, gradients, stats_hidden, roots_hidden, stats_model, small_roots, fc2_weight):
    width = gradients.shape[1]
    _, span, hidden_width = stats_hidden.shape
    model_rows = stats_model.shape[1]
    tiles = hidden_width // width
    skip = 4 * width // width
    last = tiles - 1
    return pl.pallas_call(
        hidden_kernel,
        grid_spec=pltpu.PrefetchScalarGridSpec(
            num_scalar_prefetch=1,
            grid=(2, tiles),
            in_specs=[
                pl.BlockSpec((width, width), lambda i, j, m: (skip + i * tiles + j, 0)),
                pl.BlockSpec((span, width), lambda i, j, m: ((4 * width + i * hidden_width) // span + m[0], 0)),
                pl.BlockSpec((1, span, width), lambda i, j, m: (i, 0, j)),
                pl.BlockSpec((1, span, width), lambda i, j, m: (i, 0, j)),
                pl.BlockSpec((1, model_rows, width), lambda i, j, m: (3 + i, 0, 0)),
                pl.BlockSpec((1, width, width), lambda i, j, m: (2 + i, 0, 0)),
                pl.BlockSpec((span, width), lambda i, j, m: (0, 0)),
            ],
            out_specs=[
                pl.BlockSpec((1, span, width), lambda i, j, m: (i, 0, j)),
                pl.BlockSpec((1, model_rows, width), lambda i, j, m: (i, 0, 0)),
                pl.BlockSpec((model_rows, width), lambda i, j, m: (0, jnp.where(i == 0, j, last))),
                pl.BlockSpec((width, span), lambda i, j, m: (0, 0)),
                pl.BlockSpec((span, width), lambda i, j, m: (0, 0)),
                pl.BlockSpec((span, width), lambda i, j, m: (0, 0)),
                pl.BlockSpec((span, width), lambda i, j, m: (0, 0)),
            ],
            scratch_shapes=[pltpu.VMEM((span, width), f32), pltpu.VMEM((model_rows, width), f32)],
        ),
        out_shape=[
            struct(stats_hidden.shape, f32),
            struct((2, model_rows, width), f32),
            struct((model_rows, hidden_width), f32),
            struct((width, span), low),
            struct((span, width), f32),
            struct((span, width), f32),
            struct((span, width), low),
        ],
        compiler_params=pltpu.CompilerParams(vmem_limit_bytes=48 * MIB),
        name="hidden_update",
    )(member, gradients, gradients, stats_hidden, roots_hidden, stats_model, small_roots, fc2_weight)


def model_kernel(
    member_ref, tall_ref, qkv_rows_ref, proj_rows_ref, big_ref, root_ref, stats_ref, hidden_small_ref, proj_root_ref,
    small_root_ref, proj_ref,
    big_out_ref, stats_out_ref, qkv_grad_ref, qkv_step_ref, proj_grad_ref, proj_new_ref, proj_copy_ref,
    product_sum, proj_product, small_sum,
):
    tile = pl.program_id(0)
    last = pl.num_programs(0) - 1
    pick = column_pick(member_ref[0], small_sum.shape)

    @pl.when(tile < last)
    def _():
        big_new, columns = tile_update(
            tall_ref[...], qkv_rows_ref[...], big_ref[...], root_ref[...], pick, product_sum, small_sum, tile == 0
        )
        big_out_ref[...] = big_new
        qkv_grad_ref[...] = columns

    @pl.when(tile == last)
    def _():
        qkv_step_ref[...] = dot(small_root_ref[0], product_sum[...].astype(low), COLS_BY_COLS).astype(low)
        stats_out_ref[0] = 0.5 * stats_ref[0] + 0.5 * small_sum[...]
        rows = proj_rows_ref[...]
        proj_left, _ = tile_update(
            tall_ref[...], rows, stats_ref[1], proj_root_ref[0], pick, proj_product, small_sum, tile == last
        )
        stats_out_ref[1] = proj_left
        stats_out_ref[2] = 0.5 * stats_ref[2] + 0.5 * small_sum[...]
        stats_out_ref[3] = hidden_small_ref[0]
        stats_out_ref[4] = hidden_small_ref[1]
        new = proj_ref[...] - dot(proj_product[...].astype(low), small_root_ref[1])
        proj_new_ref[...] = new
        proj_copy_ref[...] = new.astype(low)
        proj_grad_ref[...] = rows.astype(f32)


def model_update(
    member, gradients, stats_qkv, roots_qkv, stats_model, hidden_small, roots_model, small_roots, proj_weight
):
    width = gradients.shape[1]
    span, qkv_width = stats_qkv.shape
    model_rows = stats_model.shape[1]
    tiles = qkv_width // width

    def fixed(shape):
        return pl.BlockSpec(shape, lambda j, m: (0,) * len(shape))

    clamped = pl.BlockSpec((span, width), lambda j, m: (0, jnp.minimum(j, tiles - 1)))
    return pl.pallas_call(
        model_kernel,
        grid_spec=pltpu.PrefetchScalarGridSpec(
            num_scalar_prefetch=1,
            grid=(tiles + 1,),
            in_specs=[
                pl.BlockSpec((width, width), lambda j, m: (j, 0)),
                pl.BlockSpec((span, width), lambda j, m: (m[0], 0)),
                pl.BlockSpec((model_rows, width), lambda j, m: (qkv_width // model_rows + m[0], 0)),
                clamped,
                clamped,
                fixed(stats_model.shape),
                fixed(hidden_small.shape),
                pl.BlockSpec((1, model_rows, width), lambda j, m: (1, 0, 0)),
                pl.BlockSpec((2, width, width), lambda j, m: (0, 0, 0)),
                fixed(proj_weight.shape),
            ],
            out_specs=[
                clamped,
                fixed(stats_model.shape),
                pl.BlockSpec((model_rows, width), lambda j, m: (0, jnp.minimum(j, tiles - 1))),
                fixed((width, span)),
                fixed((model_rows, width)),
                fixed((model_rows, width)),
                fixed((model_rows, width)),
            ],
            scratch_shapes=[
                pltpu.VMEM((span, width), f32),
                pltpu.VMEM((model_rows, width), f32),
                pltpu.VMEM((model_rows, width), f32),
            ],
        ),
        out_shape=[
            struct(stats_qkv.shape, f32),
            struct(stats_model.shape, f32),
            struct((model_rows, qkv_width), f32),
            struct((width, span), low),
            struct((model_rows, width), f32),
            struct((model_rows, width), f32),
            struct((model_rows, width), low),
        ],
        compiler_params=pltpu.CompilerParams(vmem_limit_bytes=48 * MIB),
        name="model_update",
    )(
        member, gradients, gradients, gradients, stats_qkv, roots_qkv, stats_model, hidden_small, roots_model,
        small_roots, proj_weight,
    )


def plain_update(
    gradients, stats_model, stats_qkv, stats_hidden, roots_model, roots_qkv, roots_hidden, small_roots, proj_weight,
    fc2_weight,
):
    width = gradients.shape[1]
    member = lax.axis_index("grp")
    model_rows = stats_model.shape[1]
    picked = member * model_rows + jnp.arange(model_rows, dtype=jnp.int32)
    pick = (picked[:, None] == jnp.arange(width, dtype=jnp.int32)[None, :]).astype(low)

    def statistic_update(tall, small_rows, big_rows):
        columns = dot(pick, tall, COLS_BY_COLS)
        small_new = 0.5 * small_rows + 0.5 * dot(columns.astype(low), tall)
        rows = lax.dynamic_slice_in_dim(tall, member * big_rows.shape[0], big_rows.shape[0], 0)
        big_new = 0.5 * big_rows + 0.5 * dot(rows, tall, COLS_BY_COLS)
        return small_new, big_new, columns, rows.astype(f32)

    def product_of(big_root_rows, tall):
        return dot(big_root_rows.astype(low), tall).astype(low)

    qkv, proj, fc1, fc2 = jnp.split(gradients, [3 * width, 4 * width, 4 * width + stats_hidden.shape[2]])
    qkv_left, qkv_right, qkv_gradient, _ = statistic_update(qkv, stats_model[0], stats_qkv)
    proj_right, proj_left, _, proj_gradient = statistic_update(proj, stats_model[2], stats_model[1])
    fc1_left, fc1_right, fc1_gradient, _ = statistic_update(fc1, stats_model[3], stats_hidden[0])
    fc2_right, fc2_left, _, fc2_gradient = statistic_update(fc2, stats_model[4], stats_hidden[1])
    qkv_step = dot(small_roots[0], product_of(roots_qkv, qkv), COLS_BY_COLS).astype(low)
    fc1_step = dot(small_roots[2], product_of(roots_hidden[0], fc1), COLS_BY_COLS).astype(low)
    proj_new = proj_weight - dot(product_of(roots_model[1], proj), small_roots[1])
    fc2_new = fc2_weight - dot(product_of(roots_hidden[1], fc2), small_roots[3])
    new_stats_model = jnp.stack([qkv_left, proj_left, proj_right, fc1_left, fc2_right])
    return (
        (new_stats_model, qkv_right, jnp.stack([fc1_right, fc2_left]), qkv_step, fc1_step)
        + (qkv_gradient, proj_gradient, fc1_gradient, fc2_gradient, proj_new, fc2_new)
    )


def shards(
    plain, tokens, cotangent, window_fill, qkv_weight, proj_weight, fc1_weight, fc2_weight, vectors, vector_moments,
    bias_table, table_moments, stats_model, stats_qkv, stats_hidden, roots_model, roots_qkv, roots_hidden,
):
    width = vectors.shape[1]
    head_count = bias_table.shape[1]
    gather = functools.partial(lax.all_gather, axis_name="grp", tiled=True)
    weights = (qkv_weight, proj_weight, fc1_weight, fc2_weight)
    hot = jnp.asarray(diagonal_tables())
    diagonals = lax.dot_general(bias_table, hot, (((0,), (1,)), ((), ())), precision=lax.Precision.HIGHEST)
    if plain:
        fulls = [gather(weight.astype(low)) for weight in weights]
        base = (lax.axis_index(("rep", "grp")) * window_fill.shape[0]).astype(jnp.int32).reshape(1)
        forward = attention_forward(window_fill, base, tokens, *fulls[:2], vectors, diagonals, head_count)
    else:
        forward, fulls = gathered_forward(window_fill, tokens, weights, vectors, diagonals, head_count, 0)
    probs, mixed, normed, context, middle, normed_two = forward
    qkv_full, proj_full, fc1_full, fc2_full = fulls
    roots_low = jnp.stack([roots_model[i] for i in (0, 2, 3, 4)]).astype(low)
    roots_low, normed_two = lax.optimization_barrier((roots_low, normed_two))
    small_roots = gather(roots_low, axis=1)
    layer_output, middle_back, branch_back, fc1_term, fc2_term, fc1_bias_grad, ffn_vec = feed_forward(
        normed_two, cotangent, middle, fc1_full, fc2_full, vectors
    )
    small_roots, branch_back = lax.optimization_barrier((small_roots, branch_back))
    input_gradient, att_term, att_vec, diag_grad = attention_backward(
        probs, mixed, branch_back, middle_back, proj_full, context, normed, tokens, qkv_full, vectors, head_count
    )
    small = jnp.concatenate([part.reshape(-1, 128) for part in (att_vec[:4], ffn_vec[:4], fc1_bias_grad, diag_grad)])
    terms = (att_term, fc1_term, fc2_term)
    if plain:
        small = lax.psum(small, ("rep", "grp"))
        parts = [lax.psum(lax.psum_scatter(term, "grp", scatter_dimension=0, tiled=True), "rep") for term in terms]
        gradients = jnp.concatenate([gather(part) for part in parts])
    else:
        gradients, small = all_reduce(terms, small, 1)
    vector_total = small[: vectors.size // 128].reshape(vectors.shape)
    table_total = lax.dot_general(
        hot, small[vectors.size // 128 :].reshape(diag_grad.shape), (((0,), (1,)), ((), ())), precision=lax.Precision.HIGHEST
    )
    if plain:
        updates = plain_update(
            gradients, stats_model, stats_qkv, stats_hidden, roots_model, roots_qkv, roots_hidden, small_roots,
            proj_weight, fc2_weight,
        )
    else:
        member = lax.axis_index("grp").astype(jnp.int32).reshape(1)
        new_stats_hidden, hidden_small, fc1_gradient, fc1_step, fc2_gradient, fc2_new, fc2_copy = hidden_update(
            member, gradients, stats_hidden, roots_hidden, stats_model, small_roots, fc2_weight
        )
        qkv_right, new_stats_model, qkv_gradient, qkv_step, proj_gradient, proj_new, proj_copy = model_update(
            member, gradients, stats_qkv, roots_qkv, stats_model, hidden_small, roots_model, small_roots, proj_weight
        )
        updates = (
            (new_stats_model, qkv_right, new_stats_hidden, qkv_step, fc1_step)
            + (qkv_gradient, proj_gradient, fc1_gradient, fc2_gradient, proj_new, fc2_new)
        )
    new_stats_model, qkv_right, new_stats_hidden, qkv_step, fc1_step = updates[:5]
    qkv_gradient, proj_gradient, fc1_gradient, fc2_gradient, proj_new, fc2_new = updates[5:]
    qkv_new = qkv_weight - lax.all_to_all(qkv_step, "grp", 0, 1, tiled=True).astype(f32)
    fc1_new = fc1_weight - lax.all_to_all(fc1_step, "grp", 0, 1, tiled=True).astype(f32)
    total_tokens = tokens.shape[0] * lax.axis_size("rep") * lax.axis_size("grp")
    rate_base = total_tokens ** (-0.5)
    new_vector_moments = 0.9 * vector_moments + 0.1 * vector_total
    new_vectors = vectors - 2.0 * rate_base * new_vector_moments
    new_table_moments = 0.9 * table_moments + 0.1 * table_total
    new_table = bias_table - 8.0 * rate_base * new_table_moments
    masters = (qkv_new, proj_new, fc1_new, fc2_new)
    copies = [master.astype(low) for master in masters]
    if not plain:
        copies[1], copies[3] = proj_copy, fc2_copy
    return (
        (layer_output, input_gradient, qkv_gradient, proj_gradient, fc1_gradient, fc2_gradient)
        + masters
        + tuple(copies)
        + (new_stats_model, qkv_right, new_stats_hidden, new_vectors, new_vector_moments, new_table, new_table_moments)
    )


def solution(mesh):
    tokens, rows, blocks, copied = P(("rep", "grp"), None), P("grp", None), P(None, "grp", None), P()
    plain = (mesh.shape["rep"], mesh.shape["grp"]) != (4, 8)
    return jax.shard_map(
        functools.partial(shards, plain),
        mesh=mesh,
        in_specs=(tokens, tokens, P(("rep", "grp")))
        + (rows,) * 4
        + (copied,) * 4
        + (blocks, rows, blocks) * 2,
        out_specs=(tokens,) * 2 + (rows,) * 12 + (blocks, rows, blocks) + (copied,) * 4,
        check_vma=False,
    )
```

```python
import functools

import jax
import jax.numpy as jnp
import numpy as np
from jax import lax
from jax.experimental import pallas as pl
from jax.experimental.pallas import tpu as pltpu
from jax.sharding import PartitionSpec as P

WT = 144
SIDE = 12
SPAN = 2 * SIDE - 1
LANES = 256
DIAG = 384
ROW_TILE = 144
MIB = 1024 * 1024
low = jnp.bfloat16
f32 = jnp.float32

ROWS_BY_COLS = (((1,), (0,)), ((), ()))
COLS_BY_COLS = (((1,), (1,)), ((), ()))
ROWS_BY_ROWS = (((0,), (0,)), ((), ()))


def dot(left_matrix, right_matrix, dims=ROWS_BY_COLS):
    return lax.dot_general(left_matrix, right_matrix, dims, preferred_element_type=f32)


def standardize(values):
    centred = values - jnp.mean(values, axis=-1, keepdims=True)
    inverse = lax.rsqrt(jnp.mean(centred * centred, axis=-1, keepdims=True) + 1e-05)
    return centred * inverse, inverse


def norm_back(grad, gain, xhat, inverse):
    scaled = grad * gain
    mean_scaled = jnp.mean(scaled, axis=-1, keepdims=True)
    mean_product = jnp.mean(scaled * xhat, axis=-1, keepdims=True)
    return inverse * (scaled - mean_scaled - xhat * mean_product)


def column_sum(values):
    return jnp.sum(values, axis=0, keepdims=True)


def diagonal_tables():
    pair = np.arange(DIAG) - WT
    quotient, rest = pair // SIDE, pair % SIDE
    near = (quotient + SIDE - 1) * SPAN + rest + SIDE - 1
    far = (quotient + SIDE) * SPAN + rest - 1
    near_live = (np.abs(pair) < WT) & (quotient >= 1 - SIDE)
    far_live = (np.abs(pair) < WT) & (rest >= 1) & (quotient < SIDE - 1)
    hot = np.zeros((2, DIAG, SPAN * SPAN), np.float32)
    hot[0, np.arange(DIAG)[near_live], near[near_live]] = 1.0
    hot[1, np.arange(DIAG)[far_live], far[far_live]] = 1.0
    return hot.reshape(2 * DIAG, SPAN * SPAN)


def near_mask(shape, mirrored=False):
    column = lax.rem(lax.broadcasted_iota(jnp.int32, shape, 0), SIDE)
    if mirrored:
        column = SIDE - 1 - column
    rest = lax.rem(lax.broadcasted_iota(jnp.int32, shape, 1), SIDE)
    return column + rest < SIDE


def additive_types(heads):
    slot = np.arange(WT)
    row_high, col_high = slot // SIDE >= SIDE // 2, slot % SIDE >= SIDE // 2
    row_differs = row_high[:, None] != row_high[None, :]
    col_differs = col_high[:, None] != col_high[None, :]
    types = [
        np.where((row_differs & bool(kind // 2)) | (col_differs & bool(kind % 2)), -100.0, 0.0)
        for kind in range(4)
    ]
    return np.tile(np.stack(types), (1, 1, heads)).astype(np.float32)


def stack_mask(heads, head_size):
    lane_head = np.arange(heads * head_size) // head_size
    hot = lane_head[None, None, :] == np.arange(heads)[:, None, None]
    return np.broadcast_to(hot, (heads, WT, heads * head_size)).reshape(heads * WT, -1).astype(low)


def relative_rows(heads, diag_ref, rel_ref):
    mask = near_mask((WT, DIAG))
    for head in range(heads * rel_ref.shape[0]):
        group, place = head // heads, head % heads
        near = diag_ref[head : head + 1, :DIAG]
        far = diag_ref[head : head + 1, DIAG:]
        rolled = pltpu.roll(jnp.where(mask, near, far), DIAG - WT, 1, stride=1, stride_axis=0)
        rel_ref[group, :, place * WT : (place + 1) * WT] = rolled[:, :WT]


def stacked(block, mask_ref, heads):
    return jnp.concatenate([block] * heads, axis=0) * mask_ref[...]


def diagonal_blocks(full, heads, head_size):
    lane_head = lax.broadcasted_iota(jnp.int32, (WT, full.shape[1]), 1) // head_size
    picked = jnp.zeros((WT, full.shape[1]), f32)
    for head in range(heads):
        picked = jnp.where(lane_head == head, full[head * WT : (head + 1) * WT], picked)
    return picked


def for_row_tiles(count, body):
    def step(index, carry):
        body(pl.ds(pl.multiple_of(index * ROW_TILE, ROW_TILE), ROW_TILE))
        return carry

    lax.fori_loop(0, count // ROW_TILE, step, 0)


class Forward:
    def __init__(self, heads, head_size, refs):
        self.heads, self.head_size = heads, head_size
        self.fill, self.tokens, self.vec, self.diag, self.add, self.mask = refs[:6]
        self.probs, self.mixed_out, self.normed, self.context, self.middle, self.normed_two = refs[6:12]
        self.mixed, self.added, self.rel = refs[12:15]
        self.count, self.width = self.tokens.shape
        self.groups = self.width // LANES

    def norm_one(self):
        def body(rows):
            xhat, _ = standardize(self.tokens[rows, :].astype(f32))
            self.normed[rows, :] = (xhat * self.vec[0:1, :] + self.vec[1:2, :]).astype(low)

        for_row_tiles(self.count, body)

    def mix(self, weight_tile):
        for part in range(3):
            for tile in range(self.groups):
                start = part * self.width + tile * LANES
                sums = dot(self.normed[...], weight_tile(start))
                if part != 1:
                    row = 2 if part == 0 else 3
                    sums = sums + self.vec[row : row + 1, tile * LANES : (tile + 1) * LANES]
                self.mixed[:, start : start + LANES] = sums.astype(low)

    def attend(self, window, first_window):
        width, heads = self.width, self.heads
        rows = pl.ds(pl.multiple_of(window * WT, WT), WT)
        self.mixed_out[...] = self.mixed[rows, :]
        kind = lax.rem(first_window + window, 4)
        slot = lax.broadcasted_iota(jnp.int32, self.added.shape, 0)
        self.added[...] = jnp.where(slot < self.fill[window], self.add[kind], -1e30)
        for group in range(self.groups):
            query, key, value = (
                self.mixed[rows, part * width + group * LANES : part * width + (group + 1) * LANES]
                for part in range(3)
            )
            scores = dot(key, stacked(query, self.mask, heads), COLS_BY_COLS) * self.head_size ** (-0.5)
            scores = scores + self.rel[group] + self.added[...]
            exponent = jnp.exp(scores - jnp.max(scores, axis=0, keepdims=True))
            probs = (exponent * (1.0 / jnp.sum(exponent, axis=0, keepdims=True))).astype(low)
            self.probs[group] = probs
            full = dot(probs, value, ROWS_BY_ROWS)
            self.context[rows, group * LANES : (group + 1) * LANES] = diagonal_blocks(
                full, heads, self.head_size
            ).astype(low)

    def finish(self, weight_tile):
        for tile in range(self.groups):
            span = slice(tile * LANES, (tile + 1) * LANES)
            self.middle[:, span] = (
                self.tokens[:, span].astype(f32) + dot(self.context[...], weight_tile(tile * LANES)) + self.vec[4:5, span]
            )

        def body(rows):
            xhat, _ = standardize(self.middle[rows, :])
            self.normed_two[rows, :] = (xhat * self.vec[5:6, :] + self.vec[6:7, :]).astype(low)

        for_row_tiles(self.count, body)


def plain_forward_kernel(heads, head_size, base_ref, qkv_ref, proj_ref, *refs):
    work = Forward(heads, head_size, refs)
    window = pl.program_id(0)

    @pl.when(window == 0)
    def _():
        relative_rows(heads, work.diag, work.rel)
        work.norm_one()
        work.mix(lambda start: qkv_ref[:, start : start + LANES])

    work.attend(window, base_ref[0])

    @pl.when(window == pl.num_programs(0) - 1)
    def _():
        work.finish(lambda start: proj_ref[:, start : start + LANES])


def whole(shape):
    return pl.BlockSpec(shape, lambda *_: (0,) * len(shape), pipeline_mode=pl.Buffered(1))


def struct(shape, dtype):
    return jax.ShapeDtypeStruct(shape, dtype)


HBM = pl.BlockSpec(memory_space=pl.ANY)
SMEM = pl.BlockSpec(memory_space=pltpu.SMEM)


def forward_parts(fill, tokens, vectors, diagonals, head_count):
    count, width = tokens.shape
    windows = fill.shape[0]
    head_size = width // head_count
    heads = LANES // head_size
    groups = width // LANES
    operands = [tokens, vectors, diagonals, jnp.asarray(additive_types(heads)), jnp.asarray(stack_mask(heads, head_size))]
    in_specs = [SMEM] + [whole(operand.shape) for operand in operands]
    out_specs = [
        pl.BlockSpec((groups, WT, heads * WT), lambda w: (w, 0, 0)),
        pl.BlockSpec((WT, 3 * width), lambda w: (w, 0)),
    ] + [whole((count, width))] * 4
    out_shape = [
        struct((windows * groups, WT, heads * WT), low),
        struct((count, 3 * width), low),
        struct((count, width), low),
        struct((count, width), low),
        struct((count, width), f32),
        struct((count, width), low),
    ]
    scratch = [
        pltpu.VMEM((count, 3 * width), low),
        pltpu.VMEM((WT, heads * WT), f32),
        pltpu.VMEM((groups, WT, heads * WT), f32),
    ]
    return (heads, head_size), [fill] + operands, in_specs, out_specs, out_shape, scratch


def attention_forward(fill, base, tokens, qkv_full, proj_full, vectors, diagonals, head_count):
    sizes, operands, in_specs, out_specs, out_shape, scratch = forward_parts(
        fill, tokens, vectors, diagonals, head_count
    )
    return pl.pallas_call(
        functools.partial(plain_forward_kernel, *sizes),
        grid=(fill.shape[0],),
        in_specs=[SMEM, whole(qkv_full.shape), whole(proj_full.shape)] + in_specs,
        out_specs=out_specs,
        out_shape=out_shape,
        scratch_shapes=scratch,
        compiler_params=pltpu.CompilerParams(vmem_limit_bytes=56 * MIB),
        name="attention_forward",
    )(base, qkv_full, proj_full, *operands)


def feed_forward_kernel(
    normed_ref, cot_ref, middle_ref, fc1_ref, fc2_ref, bias_ref, vec_ref,
    out_ref, middle_back_ref, branch_back_ref, fc1_grad_ref, fc2_grad_ref, bias_grad_ref, vec_grad_ref,
    out_sum, back_sum,
):
    step = pl.program_id(0)
    count, width = cot_ref.shape
    hidden = dot(normed_ref[...], fc1_ref[...]) + bias_ref[...]
    bell = jnp.exp(hidden * hidden * -0.5)
    below = 0.5 * (1.0 + lax.erf(hidden * (0.5 ** 0.5)))
    active = (hidden * below).astype(low)
    slope = below + hidden * bell * ((2.0 * np.pi) ** -0.5)
    hidden_back = dot(cot_ref[...], fc2_ref[...], COLS_BY_COLS) * slope
    hidden_back = hidden_back.astype(low)
    bias_grad_ref[...] = column_sum(hidden_back.astype(f32))
    fc2_grad_ref[...] = dot(active, cot_ref[...], ROWS_BY_ROWS).astype(low)
    fc1_grad_ref[...] = dot(hidden_back, normed_ref[...], ROWS_BY_ROWS).astype(low)
    out_term = dot(active, fc2_ref[...])
    back_term = dot(hidden_back, fc1_ref[...], COLS_BY_COLS)

    @pl.when(step == 0)
    def _():
        out_sum[...] = out_term
        back_sum[...] = back_term

    @pl.when(step > 0)
    def _():
        out_sum[...] += out_term
        back_sum[...] += back_term

    @pl.when(step == pl.num_programs(0) - 1)
    def _():
        vec_grad_ref[...] = jnp.zeros_like(vec_grad_ref)

        def finish(part, carry):
            rows = pl.ds(pl.multiple_of(part * ROW_TILE, ROW_TILE), ROW_TILE)
            middle = middle_ref[rows, :]
            cot = cot_ref[rows, :].astype(f32)
            out_ref[rows, :] = (middle + out_sum[rows, :] + vec_ref[7:8, :]).astype(low)
            xhat, inverse = standardize(middle)
            grad = back_sum[rows, :]
            middle_back = cot + norm_back(grad, vec_ref[5:6, :], xhat, inverse)
            middle_back_ref[rows, :] = middle_back
            branch_back = middle_back.astype(low)
            branch_back_ref[rows, :] = branch_back
            vec_grad_ref[0:1, :] += column_sum(branch_back.astype(f32))
            vec_grad_ref[1:2, :] += column_sum(grad * xhat)
            vec_grad_ref[2:3, :] += column_sum(grad)
            vec_grad_ref[3:4, :] += column_sum(cot)
            return carry

        lax.fori_loop(0, count // ROW_TILE, finish, 0)


def feed_forward(normed, cotangent, middle, fc1_full, fc2_full, vectors):
    count, width = cotangent.shape
    hidden_width = fc1_full.shape[1]
    tile = LANES
    bias = vectors[8:].reshape(1, hidden_width)
    return pl.pallas_call(
        feed_forward_kernel,
        grid=(hidden_width // tile,),
        in_specs=[whole(x.shape) for x in (normed, cotangent, middle)]
        + [
            pl.BlockSpec((width, tile), lambda f: (0, f)),
            pl.BlockSpec((tile, width), lambda f: (f, 0)),
            pl.BlockSpec((1, tile), lambda f: (0, f)),
            whole(vectors.shape),
        ],
        out_specs=[
            whole((count, width)),
            whole((count, width)),
            whole((count, width)),
            pl.BlockSpec((tile, width), lambda f: (f, 0)),
            pl.BlockSpec((tile, width), lambda f: (f, 0)),
            pl.BlockSpec((1, tile), lambda f: (0, f)),
            whole((8, width)),
        ],
        out_shape=[
            struct((count, width), low),
            struct((count, width), f32),
            struct((count, width), low),
            struct((hidden_width, width), low),
            struct((hidden_width, width), low),
            struct((1, hidden_width), f32),
            struct((8, width), f32),
        ],
        scratch_shapes=[pltpu.VMEM((count, width), f32), pltpu.VMEM((count, width), f32)],
        compiler_params=pltpu.CompilerParams(vmem_limit_bytes=56 * MIB),
        name="feed_forward",
    )(normed, cotangent, middle, fc1_full, fc2_full, bias, vectors)


class Backward:
    def __init__(self, heads, head_size, refs, proj_grad, qkv_grad):
        self.heads, self.head_size = heads, head_size
        self.probs, self.query, self.key, self.value = refs[:4]
        self.branch_back, self.middle_back, self.proj, self.context, self.normed, self.tokens, self.qkv = refs[4:11]
        self.vec, self.mask, self.ffn_grad, self.bias_grad = refs[11:15]
        self.input_grad = refs[15]
        self.context_back, self.mixed_back, self.pairs, self.normed_back, self.small = refs[16:]
        self.proj_grad, self.qkv_grad = proj_grad, qkv_grad
        self.count, self.width = self.tokens.shape
        self.groups = self.width // LANES
        self.windows = self.count // WT

    def begin(self):
        self.pairs[...] = jnp.zeros_like(self.pairs)
        self.small[...] = jnp.zeros_like(self.small)
        for tile in range(self.groups):
            span = slice(tile * LANES, (tile + 1) * LANES)
            self.context_back[:, span] = dot(self.branch_back[...], self.proj[span, :], COLS_BY_COLS).astype(low)

    def begin_grads(self):
        for tile in range(self.groups):
            span = slice(tile * LANES, (tile + 1) * LANES)
            self.proj_grad(tile, dot(self.context[:, span], self.branch_back[...], ROWS_BY_ROWS).astype(low))

    def columns(self, part, group):
        return pl.ds(pl.multiple_of(part * self.width + group * LANES, LANES), LANES)

    def attend(self, group, window):
        heads = self.heads
        score_scale = self.head_size ** (-0.5)
        rows = pl.ds(pl.multiple_of(window * WT, WT), WT)
        query, key, value = self.query[...], self.key[...], self.value[...]
        probs_low = self.probs[0]
        probs = probs_low.astype(f32)
        back_stack = stacked(self.context_back[rows, self.columns(0, group)], self.mask, heads)
        value_back = dot(probs_low, back_stack)
        product = probs * dot(value, back_stack, COLS_BY_COLS)
        scores_back = (product - probs * jnp.sum(product, axis=0, keepdims=True)).astype(low)
        self.pairs[group] += scores_back.astype(f32)
        key_back = dot(scores_back, stacked(query, self.mask, heads)) * score_scale
        full = dot(scores_back, key, ROWS_BY_ROWS)
        query_back = diagonal_blocks(full, heads, self.head_size) * score_scale
        for part, back in enumerate((query_back, key_back, value_back)):
            self.mixed_back[rows, self.columns(part, group)] = back.astype(low)

    def group_grads(self, group):
        for part in range(3):
            block = self.mixed_back[:, self.columns(part, group)]
            self.qkv_grad(part, group, dot(block, self.normed[...], ROWS_BY_ROWS).astype(low))

    def normed_back_step(self):
        for tile in range(self.groups):
            span = slice(tile * LANES, (tile + 1) * LANES)
            self.normed_back[:, span] = dot(self.mixed_back[...], self.qkv[span, :], COLS_BY_COLS)

    def finish(self):
        width = self.width
        for row, part in ((2, 0), (3, 2)):

            def body(rows, row=row, part=part):
                block = self.mixed_back[rows, part * width : (part + 1) * width]
                self.small[row : row + 1, :] += column_sum(block.astype(f32))

            for_row_tiles(self.count, body)

        def body(rows):
            xhat, inverse = standardize(self.tokens[rows, :].astype(f32))
            grad = self.normed_back[rows, :]
            back = self.middle_back[rows, :] + norm_back(grad, self.vec[0:1, :], xhat, inverse)
            self.input_grad[rows, :] = back.astype(low)
            self.small[0:1, :] += column_sum(grad * xhat)
            self.small[1:2, :] += column_sum(grad)

        for_row_tiles(self.count, body)
        self.small[4:8, :] = self.ffn_grad[0:4, :]
        for row in range(self.bias_grad.shape[1] // width):
            self.small[8 + row : 9 + row, :] = self.bias_grad[:, row * width : (row + 1) * width]

    def diagonals(self):
        mask = near_mask((WT, DIAG), mirrored=True)
        order = [lax.broadcasted_iota(jnp.int32, (WT, WT), axis) for axis in range(2)]
        mirror = jnp.where(order[0] + order[1] == WT - 1, 1.0, 0.0).astype(f32)
        for group in range(self.groups):
            self.pairs[group] = lax.dot_general(
                mirror, self.pairs[group], ROWS_BY_COLS, precision=lax.Precision.HIGHEST, preferred_element_type=f32
            )
        for head in range(self.groups * self.heads):
            group, place = head // self.heads, head % self.heads
            block = self.pairs[group, :, place * WT : (place + 1) * WT]
            block = jnp.concatenate([block, jnp.zeros((WT, DIAG - WT), f32)], axis=1)
            rolled = pltpu.roll(block, 1, 1, stride=1, stride_axis=0)
            row = SMALL_DIAG + head
            self.small[row : row + 1, :DIAG] = column_sum(jnp.where(mask, rolled, 0.0))
            self.small[row : row + 1, DIAG : 2 * DIAG] = column_sum(jnp.where(mask, 0.0, rolled))


SMALL_DIAG = 16


def plain_backward_kernel(heads, head_size, *refs):
    weight_grad = refs[16]
    width = weight_grad.shape[1]

    def proj_grad(tile, value):
        weight_grad[3 * width + tile * LANES : 3 * width + (tile + 1) * LANES, :] = value

    def qkv_grad(part, group, value):
        weight_grad[pl.ds(pl.multiple_of(part * width + group * LANES, LANES), LANES), :] = value

    work = Backward(heads, head_size, refs[:16] + refs[18:], proj_grad, qkv_grad)
    step = pl.program_id(0)
    windows = work.windows
    busy = windows * work.groups
    group, window = step // windows, lax.rem(step, windows)

    @pl.when(step == 0)
    def _():
        work.begin()
        work.begin_grads()

    @pl.when(step < busy)
    def _():
        work.attend(group, window)

    @pl.when((step < busy) & (window == windows - 1))
    def _():
        work.group_grads(group)

    @pl.when(step == busy)
    def _():
        work.normed_back_step()
        work.finish()
        work.diagonals()
        refs[17][...] = work.small[...]


def backward_parts(probs, mixed, operands, head_count):
    count, width = operands[0].shape
    windows = count // WT
    head_size = width // head_count
    heads = LANES // head_size
    groups = width // LANES
    last = windows * groups - 1
    mask = jnp.asarray(stack_mask(heads, head_size))
    operands = operands[:8] + [mask] + operands[8:]

    def place(step):
        step = jnp.minimum(step, last)
        return step // windows, lax.rem(step, windows)

    def probs_map(step):
        group, window = place(step)
        return window * groups + group, 0, 0

    def mixed_map(part):
        def index(step):
            group, window = place(step)
            return window, part * groups + group

        return index

    in_specs = (
        [pl.BlockSpec((1, WT, heads * WT), probs_map)]
        + [pl.BlockSpec((WT, LANES), mixed_map(part)) for part in range(3)]
        + [whole(operand.shape) for operand in operands]
    )
    scratch = [
        pltpu.VMEM((count, width), low),
        pltpu.VMEM((count, 3 * width), low),
        pltpu.VMEM((groups, WT, heads * WT), f32),
        pltpu.VMEM((count, width), f32),
        pltpu.VMEM((SMALL_DIAG + head_count, width), f32),
    ]
    return (heads, head_size), [probs, mixed, mixed, mixed] + operands, in_specs, scratch, last + 1


def attention_backward(probs, mixed, operands, head_count):
    sizes, operands, in_specs, scratch, busy = backward_parts(probs, mixed, operands, head_count)
    count, width = operands[4].shape
    small_shape = (SMALL_DIAG + head_count, width)
    return pl.pallas_call(
        functools.partial(plain_backward_kernel, *sizes),
        grid=(busy + 1,),
        in_specs=in_specs,
        out_specs=[whole((count, width)), whole((4 * width, width)), whole(small_shape)],
        out_shape=[struct((count, width), low), struct((4 * width, width), low), struct(small_shape, f32)],
        scratch_shapes=scratch,
        compiler_params=pltpu.CompilerParams(vmem_limit_bytes=60 * MIB),
        name="attention_backward",
    )(*operands)


MESH = pl.DeviceIdType.MESH


class Peers:
    def __init__(self):
        self.z = lax.axis_index("rep")
        place = lax.axis_index("grp")
        self.c = lax.rem(place, 2)
        self.x = lax.rem(place // 2, 2)
        self.y = place // 4
        self.core_peer = (self.z, place + 1 - 2 * self.c)
        self.x_peer = (self.z, place + 2 - 4 * self.x)
        self.y_peer = (self.z, place + 4 - 8 * self.y)
        self.z_places = [lax.rem(self.z + step, 4) for step in range(1, 4)]
        self.z_peers = [(there, place) for there in self.z_places]

    def plane(self):
        return [self.core_peer, self.x_peer, self.y_peer]

    def everyone(self):
        return self.plane() + self.z_peers


def meet(peers):
    barrier = pltpu.get_barrier_semaphore()
    for peer in peers:
        pl.semaphore_signal(barrier, inc=1, device_id=peer, device_id_type=MESH)
    pl.semaphore_wait(barrier, len(peers))


class Copies:
    def __init__(self, send_sems, recv_sems):
        self.send_sems, self.recv_sems = send_sems, recv_sems
        self.made = []

    def make(self, ends, peer):
        copy = Copy(self, len(self.made), ends, peer)
        self.made.append(copy)
        copy.build().start()
        return copy

    def drain(self):
        for copy in self.made:
            copy.build().wait_send()


class Copy:
    def __init__(self, owner, number, ends, peer):
        self.owner, self.number, self.ends, self.peer = owner, number, ends, peer

    def build(self):
        source, target = self.ends()
        return pltpu.make_async_remote_copy(
            src_ref=source,
            dst_ref=target,
            send_sem=self.owner.send_sems.at[self.number],
            recv_sem=self.owner.recv_sems.at[self.number],
            device_id=self.peer,
            device_id_type=MESH,
        )

    def wait_recv(self):
        self.build().wait_recv()


def same(place):
    return lambda: (place(), place())


class Gather:
    def __init__(self, me, copies, source, out):
        self.me, self.copies, self.source, self.out = me, copies, source, out
        self.half = out.shape[3] // 2
        self.across = []

    def block(self, flip_y, flip_x):
        me = self.me
        return self.out.at[1 - me.y if flip_y else me.y, 1 - me.x if flip_x else me.x, me.c]

    def start(self):
        me = self.me

        def ends():
            return self.source(), self.block(False, False)

        self.by_x = self.copies.make(ends, me.x_peer)
        self.by_y = self.copies.make(ends, me.y_peer)
        self.across.append(self.copies.make(ends, me.core_peer))

    def relay(self):
        me = self.me
        self.by_x.wait_recv()
        to_y = self.copies.make(same(lambda: self.block(False, True).at[pl.ds(0, self.half)]), me.y_peer)
        self.by_y.wait_recv()
        to_x = self.copies.make(same(lambda: self.block(True, False).at[pl.ds(self.half, self.half)]), me.x_peer)
        self.relayed = (to_x, to_y)
        self.across.append(self.copies.make(same(lambda: self.block(False, True)), me.core_peer))
        self.across.append(self.copies.make(same(lambda: self.block(True, False)), me.core_peer))

    def cross(self):
        for copy in self.relayed:
            copy.wait_recv()
        self.across.append(self.copies.make(same(lambda: self.block(True, True)), self.me.core_peer))

    def wait(self):
        for copy in self.across:
            copy.wait_recv()


def gathered_forward_kernel(heads, head_size, *refs):
    qkv_shard, proj_shard, fc1_shard, fc2_shard = refs[:4]
    outs = refs[10:20]
    qkv_out, proj_out, fc1_out, fc2_out = outs[6:]
    scratch = refs[20:]
    work = Forward(heads, head_size, refs[4:10] + outs[:6] + scratch[:3])
    qkv_full, proj_full, fc1_low, fc2_low, send_sems, recv_sems, local_sems = scratch[3:]
    me = Peers()
    copies = Copies(send_sems, recv_sems)
    own = (me.y, me.x, me.c)
    qkv = Gather(me, copies, lambda: qkv_full.at[own], qkv_full)
    proj = Gather(me, copies, lambda: proj_full.at[own], proj_full)
    fc1 = Gather(me, copies, lambda: fc1_low, fc1_out)
    fc2 = Gather(me, copies, lambda: fc2_low, fc2_out)

    def local(index):
        source = (fc1_low, fc2_low, qkv_full, proj_full)[index]
        target = (fc1_out, fc2_out, qkv_out, proj_out)[index]
        return pltpu.make_async_copy(source, target.at[own] if index < 2 else target, local_sems.at[index])

    window = pl.program_id(0)
    first_window = (me.z * 8 + me.y * 4 + me.x * 2 + me.c) * pl.num_programs(0)

    def weight_tile(full):
        def tile(start):
            return full[:, :, :, :, start : start + LANES].reshape(-1, LANES)

        return tile

    @pl.when(window == 0)
    def _():
        qkv_full[own] = qkv_shard[...].astype(low)
        proj_full[own] = proj_shard[...].astype(low)
        meet(me.plane())
        qkv.start()
        proj.start()
        fc1_low[...] = fc1_shard[...].astype(low)
        fc2_low[...] = fc2_shard[...].astype(low)
        work.norm_one()
        relative_rows(heads, work.diag, work.rel)
        qkv.relay()
        proj.relay()
        fc1.start()
        fc2.start()
        local(0).start()
        local(1).start()
        qkv.cross()
        qkv.wait()
        local(2).start()
        work.mix(weight_tile(qkv_full))

    @pl.when(window == 1)
    def _():
        proj.cross()

    @pl.when(window == 3)
    def _():
        fc1.relay()

    @pl.when(window == 6)
    def _():
        fc1.cross()
        fc2.relay()

    work.attend(window, first_window)

    @pl.when(window == pl.num_programs(0) - 1)
    def _():
        proj.wait()
        local(3).start()
        work.finish(weight_tile(proj_full))
        fc2.cross()
        fc1.wait()
        fc2.wait()
        for index in range(4):
            local(index).wait()
        copies.drain()


def gathered_forward(fill, tokens, weights, vectors, diagonals, head_count, collective_id):
    sizes, operands, in_specs, out_specs, out_shape, scratch = forward_parts(
        fill, tokens, vectors, diagonals, head_count
    )
    fulls = [(2, 2, 2) + weight.shape for weight in weights]
    results = pl.pallas_call(
        functools.partial(gathered_forward_kernel, *sizes),
        grid=(fill.shape[0],),
        in_specs=[whole(weight.shape) for weight in weights] + in_specs,
        out_specs=out_specs + [HBM] * 4,
        out_shape=out_shape + [struct(full, low) for full in fulls],
        scratch_shapes=scratch
        + [pltpu.VMEM(fulls[0], low), pltpu.VMEM(fulls[1], low)]
        + [pltpu.VMEM(weight.shape, low) for weight in weights[2:]]
        + [pltpu.SemaphoreType.DMA((32,)), pltpu.SemaphoreType.DMA((32,)), pltpu.SemaphoreType.DMA((4,))],
        compiler_params=pltpu.CompilerParams(
            collective_id=collective_id, has_side_effects=True, vmem_limit_bytes=58 * MIB
        ),
        name="gathered_forward",
    )(*weights, *operands)
    return results[:6], [full.reshape(-1, weight.shape[1]) for full, weight in zip(results[6:], weights)]


PIECE = 16


class Reduction:
    def __init__(self, me, copies, term, mine, out, buffers, load_sems, store_sems):
        self.me, self.copies, self.term, self.mine, self.out = me, copies, term, mine, out
        self.core_in, self.first_in, self.second_in, self.z_in, self.final = buffers
        self.load_sems, self.store_sems = load_sems, store_sems
        self.parts = self.core_in.shape[1]
        self.half = self.core_in.shape[-1] // 2
        self.core, self.first, self.second, self.over_z, self.last_z, self.spread, self.relayed, self.across = (
            {} for _ in range(8)
        )

    def sides(self):
        return pl.ds(0, self.half), pl.ds(self.half, self.half)

    def z_columns(self, z):
        return pl.ds(pl.multiple_of(lax.rem(z, 2) * self.half, self.half), self.half)

    def loop(self, amount, body):
        def step(index, carry):
            body(index)
            return carry

        lax.fori_loop(0, amount, step, 0)

    def load(self, k):
        ref, at = self.mine
        return pltpu.make_async_copy(self.term(k, self.me.c), ref.at[k], self.load_sems.at[k])

    def store(self, k):
        me = self.me
        return pltpu.make_async_copy(
            self.final.at[k], self.out(k, me.c, me.x, me.y, (me.z // 2, slice(None), self.z_columns(me.z))),
            self.store_sems.at[k],
        )

    def start(self, k):
        me = self.me
        self.core[k] = self.copies.make(lambda: (self.term(k, 1 - me.c), self.core_in.at[k]), me.core_peer)
        if self.load_sems is not None:
            self.load(k).start()

    def finish_core(self, k):
        me = self.me
        ref, at = self.mine
        if self.load_sems is not None:
            self.load(k).wait()
        self.core[k].wait_recv()

        def add(step):
            part, x, y, row = step // 8, lax.rem(step // 4, 2), lax.rem(step // 2, 2), lax.rem(step, 2)
            place = at(k, part, x, y, row)
            ref[place] = ref[place] + self.core_in[k, part, x, y, row]

        self.loop(8 * self.parts, add)
        every = slice(None)
        self.first[k] = (
            self.copies.make(
                lambda: (
                    ref.at[at(k, every, 1 - me.x, every, every) + (every, self.sides()[0])], self.first_in.at[k, 0],
                ),
                me.x_peer,
            ),
            self.copies.make(
                lambda: (
                    ref.at[at(k, every, every, 1 - me.y, every) + (every, self.sides()[1])], self.first_in.at[k, 1],
                ),
                me.y_peer,
            ),
        )

    def finish_first(self, k):
        me = self.me
        ref, at = self.mine
        for copy in self.first[k]:
            copy.wait_recv()
        half = self.half

        def add(step):
            part, other, row = step // 4, lax.rem(step // 2, 2), lax.rem(step, 2)
            place = at(k, part, me.x, other, row) + (slice(None), slice(0, half))
            ref[place] = ref[place] + self.first_in[k, 0, part, other, row]
            place = at(k, part, other, me.y, row) + (slice(None), slice(half, 2 * half))
            ref[place] = ref[place] + self.first_in[k, 1, part, other, row]

        self.loop(4 * self.parts, add)
        every = slice(None)
        self.second[k] = (
            self.copies.make(
                lambda: (
                    ref.at[at(k, every, me.x, 1 - me.y, every) + (every, self.sides()[0])], self.second_in.at[k, 0],
                ),
                me.y_peer,
            ),
            self.copies.make(
                lambda: (
                    ref.at[at(k, every, 1 - me.x, me.y, every) + (every, self.sides()[1])], self.second_in.at[k, 1],
                ),
                me.x_peer,
            ),
        )

    def finish_second(self, k):
        me = self.me
        ref, at = self.mine
        for copy in self.second[k]:
            copy.wait_recv()
        half = self.half

        def add(step):
            part, row = step // 2, lax.rem(step, 2)
            for side, span in enumerate((slice(0, half), slice(half, 2 * half))):
                place = at(k, part, me.x, me.y, row) + (slice(None), span)
                ref[place] = ref[place] + self.second_in[k, side, part, row]

        self.loop(2 * self.parts, add)

        def piece(part, z):
            return at(k, part, me.x, me.y, z // 2) + (slice(None), self.z_columns(z))

        self.over_z[k] = [
            self.copies.make(lambda there=there: (ref.at[piece(slice(None), there)], self.z_in.at[k, me.z]), peer)
            for there, peer in zip(me.z_places, me.z_peers)
        ]

        def keep(part):
            self.z_in[k, me.z, part] = ref[piece(part, me.z)]

        self.loop(self.parts, keep)

    def finish_z(self, k):
        me = self.me
        for copy in self.over_z[k]:
            copy.wait_recv()

        def add(part):
            total = self.z_in[k, 0, part].astype(f32)
            for place in range(1, 4):
                total = total + self.z_in[k, place, part].astype(f32)
            self.final[k, part] = total.astype(low)

        self.loop(self.parts, add)
        self.last_z[k] = [
            self.copies.make(
                lambda: (
                    self.final.at[k],
                    self.out(k, me.c, me.x, me.y, (me.z // 2, slice(None), self.z_columns(me.z))),
                ),
                peer,
            )
            for peer in me.z_peers
        ]
        self.store(k).start()

    def finish_last_z(self, k):
        me = self.me
        for copy in self.last_z[k]:
            copy.wait_recv()
        self.store(k).wait()
        own = same(lambda: self.out(k, me.c, me.x, me.y, ()))
        self.spread[k] = [self.copies.make(own, peer) for peer in (me.x_peer, me.y_peer)]
        self.across[k] = [self.copies.make(own, me.core_peer)]

    def finish_spread(self, k):
        me = self.me
        by_x, by_y = self.spread[k]
        every = slice(None)
        by_y.wait_recv()
        to_x = self.copies.make(
            same(lambda: self.out(k, me.c, me.x, 1 - me.y, (every, every, self.sides()[0]))), me.x_peer
        )
        by_x.wait_recv()
        to_y = self.copies.make(
            same(lambda: self.out(k, me.c, 1 - me.x, me.y, (every, every, self.sides()[1]))), me.y_peer
        )
        self.relayed[k] = (to_x, to_y)
        self.across[k].append(self.copies.make(same(lambda: self.out(k, me.c, 1 - me.x, me.y, ())), me.core_peer))
        self.across[k].append(self.copies.make(same(lambda: self.out(k, me.c, me.x, 1 - me.y, ())), me.core_peer))

    def finish_relay(self, k):
        me = self.me
        for copy in self.relayed[k]:
            copy.wait_recv()
        self.across[k].append(self.copies.make(same(lambda: self.out(k, me.c, 1 - me.x, 1 - me.y, ())), me.core_peer))

    def wait(self, k):
        for copy in self.across[k]:
            copy.wait_recv()

    def stage(self, number, k):
        stages = (
            self.finish_core, self.finish_first, self.finish_second, self.finish_z, self.finish_last_z,
            self.finish_spread, self.finish_relay,
        )
        stages[number](k)


STAGES = 7


def reduction_buffers(amount, parts, width):
    half = width // 2
    return [
        pltpu.VMEM((amount, parts, 2, 2, 2, PIECE, width), low),
        pltpu.VMEM((amount, 2, parts, 2, 2, PIECE, half), low),
        pltpu.VMEM((amount, 2, parts, 2, PIECE, half), low),
        pltpu.VMEM((amount, 4, parts, PIECE, half), low),
        pltpu.VMEM((amount, parts, PIECE, half), low),
    ]


class SmallSum:
    def __init__(self, me, copies, small, inbox):
        self.me, self.copies, self.small, self.inbox, self.made = me, copies, small, inbox, []

    def step(self, number):
        peers = self.me.plane()
        z = self.me.z
        if number > 0:
            self.made[number - 1].wait_recv()
            self.small[...] += self.inbox[number - 1]
        if number < 3:
            self.inbox[3 + number] = self.small[...]
            self.made.append(
                self.copies.make(lambda: (self.inbox.at[3 + number], self.inbox.at[number]), peers[number])
            )
        else:
            self.inbox[6 + z] = self.small[...]
            for peer in self.me.z_peers:
                self.made.append(self.copies.make(same(lambda: self.inbox.at[6 + z]), peer))

    def finish(self):
        for copy in self.made[3:]:
            copy.wait_recv()
        self.small[...] = (self.inbox[6] + self.inbox[7]) + (self.inbox[8] + self.inbox[9])


def reduced_backward_kernel(heads, head_size, *refs):
    fc1_term, fc2_term = refs[15:17]
    input_grad, fc_out, qkv_out, proj_out, small_out = refs[17:22]
    att, fc_mine = refs[27:29]
    fc_buffers, att_buffers = refs[29:34], refs[34:39]
    inbox, send_sems, recv_sems, load_sems, fc_store_sems, att_store_sems = refs[39:]
    groups = att.shape[0] - 1
    tile_shape = (2, 2, 2, 2, PIECE, att.shape[-1])

    def proj_grad(tile, value):
        att[groups, tile] = value.reshape(tile_shape)

    def qkv_grad(part, group, value):
        att[group, part] = value.reshape(tile_shape)

    work = Backward(heads, head_size, refs[:15] + (input_grad,) + refs[22:27], proj_grad, qkv_grad)
    me = Peers()
    copies = Copies(send_sems, recv_sems)
    chunks = fc1_term.shape[0]

    def fc_term(k, c):
        return (fc1_term, fc2_term)[k % 2].at[k // 2, :, c]

    def fc_place(k, c, x, y, rest):
        return fc_out.at[(k % 2, k // 2, slice(None), c, x, y) + rest]

    def att_place(k, c, x, y, rest):
        if k == groups:
            return proj_out.at[(slice(None), c, x, y) + rest]
        return qkv_out.at[(slice(None), k, c, x, y) + rest]

    fc = Reduction(
        me, copies, fc_term, (fc_mine, lambda *place: place), fc_place, fc_buffers, load_sems, fc_store_sems
    )
    att_sum = Reduction(
        me, copies, lambda k, c: att.at[k, :, c], (att, lambda k, part, *place: (k, part, me.c) + place), att_place,
        att_buffers, None, att_store_sems,
    )
    small = SmallSum(me, copies, work.small, inbox)
    order = [(fc, k) for k in range(2 * chunks)] + [(att_sum, groups)] + [(att_sum, k) for k in range(groups)]
    waves = len(order) + STAGES - 1
    done = [0]

    def wave():
        number = done[0]
        done[0] += 1
        for index in reversed(range(len(order))):
            if 0 <= number - index < STAGES:
                which, k = order[index]
                which.stage(number - index, k)

    step = pl.program_id(0)
    windows = work.windows
    busy = windows * groups
    group, window = step // windows, lax.rem(step, windows)

    @pl.when(step == 0)
    def _():
        meet(me.everyone())
        for k in range(2 * chunks):
            fc.start(k)
        work.begin_grads()
        att_sum.start(groups)
        work.begin()

    @pl.when(step < busy)
    def _():
        work.attend(group, window)

    for number in range(groups):

        @pl.when(step == (number + 1) * windows - 1)
        def _():
            work.group_grads(number)
            att_sum.start(number)

    for number in range(waves):
        at = 2 + 3 * number
        if at >= busy:
            break

        @pl.when(step == at)
        def _():
            wave()

    @pl.when(step == busy)
    def _():
        wave()
        work.normed_back_step()
        wave()
        work.finish()
        wave()
        work.diagonals()
        small.step(0)
        for number in range(1, 5):
            wave()
            if number < 4:
                small.step(number)
            else:
                small.finish()
        small_out[...] = work.small[...]
        while done[0] < waves:
            wave()
        for which, k in order:
            which.wait(k)
        copies.drain()


def reduced_backward(probs, mixed, operands, head_count, fc1_term, fc2_term, collective_id):
    sizes, operands, in_specs, scratch, busy = backward_parts(probs, mixed, operands, head_count)
    count, width = operands[4].shape
    hidden_width = fc1_term.shape[0]
    groups = width // LANES
    tile_shape = (2, 2, 2, 2, PIECE, width)
    chunks = 2
    parts = hidden_width // LANES // chunks
    small_shape = (SMALL_DIAG + head_count, width)
    fc_shape = (chunks, parts) + tile_shape
    copies = 19 * (2 * chunks + groups + 1) + 6
    input_grad, fc_sum, qkv_sum, proj_sum, small = pl.pallas_call(
        functools.partial(reduced_backward_kernel, *sizes),
        grid=(busy + 1,),
        in_specs=in_specs + [HBM] * 2,
        out_specs=[whole((count, width))] + [HBM] * 3 + [whole(small_shape)],
        out_shape=[
            struct((count, width), low),
            struct((2,) + fc_shape, low),
            struct((3, groups) + tile_shape, low),
            struct((groups,) + tile_shape, low),
            struct(small_shape, f32),
        ],
        scratch_shapes=scratch
        + [pltpu.VMEM((groups + 1, 3) + tile_shape, low), pltpu.VMEM((2 * chunks, parts) + tile_shape[1:], low)]
        + reduction_buffers(2 * chunks, parts, width)
        + reduction_buffers(groups + 1, 3, width)
        + [
            pltpu.VMEM((10,) + small_shape, f32),
            pltpu.SemaphoreType.DMA((copies,)),
            pltpu.SemaphoreType.DMA((copies,)),
            pltpu.SemaphoreType.DMA((2 * chunks,)),
            pltpu.SemaphoreType.DMA((2 * chunks,)),
            pltpu.SemaphoreType.DMA((groups + 1,)),
        ],
        compiler_params=pltpu.CompilerParams(
            collective_id=collective_id, has_side_effects=True, vmem_limit_bytes=62 * MIB
        ),
        name="reduced_backward",
    )(*operands, fc1_term.reshape(fc_shape), fc2_term.reshape(fc_shape))
    sums = [part.reshape(-1, width) for part in (qkv_sum, proj_sum, fc_sum)]
    return input_grad, sums, small


def tile_update(tall, rows, big, root, pick, product_ref, small_ref, fresh):
    columns = dot(pick, tall, COLS_BY_COLS)
    product = dot(root.astype(low), tall)
    small = dot(columns.astype(low), tall)

    @pl.when(fresh)
    def _():
        product_ref[...] = product
        small_ref[...] = small

    @pl.when(jnp.logical_not(fresh))
    def _():
        product_ref[...] += product
        small_ref[...] += small

    return 0.5 * big + 0.5 * dot(rows, tall, COLS_BY_COLS), columns


def column_pick(member, shape):
    row, column = (lax.broadcasted_iota(jnp.int32, shape, axis) for axis in range(2))
    return jnp.where(column == row + member * shape[0], 1.0, 0.0).astype(low)


def hidden_kernel(
    member_ref, tall_ref, rows_ref, big_ref, root_ref, small_ref, small_root_ref, fc2_ref,
    big_out_ref, small_out_ref, fc1_grad_ref, fc1_step_ref, fc2_grad_ref, fc2_new_ref, fc2_copy_ref,
    product_sum, small_sum,
):
    matrix, tile = pl.program_id(0), pl.program_id(1)
    pick = column_pick(member_ref[0], small_sum.shape)
    big_new, columns = tile_update(
        tall_ref[...], rows_ref[...], big_ref[0], root_ref[0], pick, product_sum, small_sum, tile == 0
    )
    big_out_ref[0] = big_new

    @pl.when(matrix == 0)
    def _():
        fc1_grad_ref[...] = columns

    @pl.when(tile == pl.num_programs(1) - 1)
    def _():
        small_out_ref[0] = 0.5 * small_ref[0] + 0.5 * small_sum[...]
        product = product_sum[...].astype(low)

        @pl.when(matrix == 0)
        def _():
            fc1_step_ref[...] = dot(small_root_ref[0], product, COLS_BY_COLS).astype(low)

        @pl.when(matrix == 1)
        def _():
            new = fc2_ref[...] - dot(product, small_root_ref[0])
            fc2_new_ref[...] = new
            fc2_copy_ref[...] = new.astype(low)
            fc2_grad_ref[...] = rows_ref[...].astype(f32)


def hidden_update(member, fc_sum, stats_hidden, roots_hidden, stats_model, small_roots, fc2_weight):
    width = fc_sum.shape[1]
    _, span, hidden_width = stats_hidden.shape
    model_rows = stats_model.shape[1]
    tiles = hidden_width // width
    last = tiles - 1
    return pl.pallas_call(
        hidden_kernel,
        grid_spec=pltpu.PrefetchScalarGridSpec(
            num_scalar_prefetch=1,
            grid=(2, tiles),
            in_specs=[
                pl.BlockSpec((width, width), lambda i, j, m: (i * tiles + j, 0)),
                pl.BlockSpec((span, width), lambda i, j, m: (i * (hidden_width // span) + m[0], 0)),
                pl.BlockSpec((1, span, width), lambda i, j, m: (i, 0, j)),
                pl.BlockSpec((1, span, width), lambda i, j, m: (i, 0, j)),
                pl.BlockSpec((1, model_rows, width), lambda i, j, m: (3 + i, 0, 0)),
                pl.BlockSpec((1, width, width), lambda i, j, m: (2 + i, 0, 0)),
                pl.BlockSpec((span, width), lambda i, j, m: (0, 0)),
            ],
            out_specs=[
                pl.BlockSpec((1, span, width), lambda i, j, m: (i, 0, j)),
                pl.BlockSpec((1, model_rows, width), lambda i, j, m: (i, 0, 0)),
                pl.BlockSpec((model_rows, width), lambda i, j, m: (0, jnp.where(i == 0, j, last))),
                pl.BlockSpec((width, span), lambda i, j, m: (0, 0)),
                pl.BlockSpec((span, width), lambda i, j, m: (0, 0)),
                pl.BlockSpec((span, width), lambda i, j, m: (0, 0)),
                pl.BlockSpec((span, width), lambda i, j, m: (0, 0)),
            ],
            scratch_shapes=[pltpu.VMEM((span, width), f32), pltpu.VMEM((model_rows, width), f32)],
        ),
        out_shape=[
            struct(stats_hidden.shape, f32),
            struct((2, model_rows, width), f32),
            struct((model_rows, hidden_width), f32),
            struct((width, span), low),
            struct((span, width), f32),
            struct((span, width), f32),
            struct((span, width), low),
        ],
        compiler_params=pltpu.CompilerParams(vmem_limit_bytes=48 * MIB),
        name="hidden_update",
    )(member, fc_sum, fc_sum, stats_hidden, roots_hidden, stats_model, small_roots, fc2_weight)


def model_kernel(
    member_ref, tall_ref, qkv_rows_ref, proj_tall_ref, proj_rows_ref, big_ref, root_ref, stats_ref, hidden_small_ref, proj_root_ref,
    small_root_ref, proj_ref,
    big_out_ref, stats_out_ref, qkv_grad_ref, qkv_step_ref, proj_grad_ref, proj_new_ref, proj_copy_ref,
    product_sum, proj_product, small_sum,
):
    tile = pl.program_id(0)
    last = pl.num_programs(0) - 1
    pick = column_pick(member_ref[0], small_sum.shape)

    @pl.when(tile < last)
    def _():
        big_new, columns = tile_update(
            tall_ref[...], qkv_rows_ref[...], big_ref[...], root_ref[...], pick, product_sum, small_sum, tile == 0
        )
        big_out_ref[...] = big_new
        qkv_grad_ref[...] = columns

    @pl.when(tile == last)
    def _():
        qkv_step_ref[...] = dot(small_root_ref[0], product_sum[...].astype(low), COLS_BY_COLS).astype(low)
        stats_out_ref[0] = 0.5 * stats_ref[0] + 0.5 * small_sum[...]
        rows = proj_rows_ref[...]
        proj_left, _ = tile_update(
            proj_tall_ref[...], rows, stats_ref[1], proj_root_ref[0], pick, proj_product, small_sum, tile == last
        )
        stats_out_ref[1] = proj_left
        stats_out_ref[2] = 0.5 * stats_ref[2] + 0.5 * small_sum[...]
        stats_out_ref[3] = hidden_small_ref[0]
        stats_out_ref[4] = hidden_small_ref[1]
        new = proj_ref[...] - dot(proj_product[...].astype(low), small_root_ref[1])
        proj_new_ref[...] = new
        proj_copy_ref[...] = new.astype(low)
        proj_grad_ref[...] = rows.astype(f32)


def model_update(
    member, qkv_sum, proj_sum, stats_qkv, roots_qkv, stats_model, hidden_small, roots_model, small_roots, proj_weight
):
    width = qkv_sum.shape[1]
    span, qkv_width = stats_qkv.shape
    model_rows = stats_model.shape[1]
    tiles = qkv_width // width

    def fixed(shape):
        return pl.BlockSpec(shape, lambda j, m: (0,) * len(shape))

    clamped = pl.BlockSpec((span, width), lambda j, m: (0, jnp.minimum(j, tiles - 1)))
    return pl.pallas_call(
        model_kernel,
        grid_spec=pltpu.PrefetchScalarGridSpec(
            num_scalar_prefetch=1,
            grid=(tiles + 1,),
            in_specs=[
                pl.BlockSpec((width, width), lambda j, m: (jnp.minimum(j, tiles - 1), 0)),
                pl.BlockSpec((span, width), lambda j, m: (m[0], 0)),
                fixed((width, width)),
                pl.BlockSpec((model_rows, width), lambda j, m: (m[0], 0)),
                clamped,
                clamped,
                fixed(stats_model.shape),
                fixed(hidden_small.shape),
                pl.BlockSpec((1, model_rows, width), lambda j, m: (1, 0, 0)),
                pl.BlockSpec((2, width, width), lambda j, m: (0, 0, 0)),
                fixed(proj_weight.shape),
            ],
            out_specs=[
                clamped,
                fixed(stats_model.shape),
                pl.BlockSpec((model_rows, width), lambda j, m: (0, jnp.minimum(j, tiles - 1))),
                fixed((width, span)),
                fixed((model_rows, width)),
                fixed((model_rows, width)),
                fixed((model_rows, width)),
            ],
            scratch_shapes=[
                pltpu.VMEM((span, width), f32),
                pltpu.VMEM((model_rows, width), f32),
                pltpu.VMEM((model_rows, width), f32),
            ],
        ),
        out_shape=[
            struct(stats_qkv.shape, f32),
            struct(stats_model.shape, f32),
            struct((model_rows, qkv_width), f32),
            struct((width, span), low),
            struct((model_rows, width), f32),
            struct((model_rows, width), f32),
            struct((model_rows, width), low),
        ],
        compiler_params=pltpu.CompilerParams(vmem_limit_bytes=48 * MIB),
        name="model_update",
    )(
        member, qkv_sum, qkv_sum, proj_sum, proj_sum, stats_qkv, roots_qkv, stats_model, hidden_small, roots_model,
        small_roots, proj_weight,
    )


def plain_update(
    sums, stats_model, stats_qkv, stats_hidden, roots_model, roots_qkv, roots_hidden, small_roots, proj_weight,
    fc2_weight,
):
    width = sums[0].shape[1]
    member = lax.axis_index("grp")
    model_rows = stats_model.shape[1]
    picked = member * model_rows + jnp.arange(model_rows, dtype=jnp.int32)
    pick = (picked[:, None] == jnp.arange(width, dtype=jnp.int32)[None, :]).astype(low)

    def statistic_update(tall, small_rows, big_rows):
        columns = dot(pick, tall, COLS_BY_COLS)
        small_new = 0.5 * small_rows + 0.5 * dot(columns.astype(low), tall)
        rows = lax.dynamic_slice_in_dim(tall, member * big_rows.shape[0], big_rows.shape[0], 0)
        big_new = 0.5 * big_rows + 0.5 * dot(rows, tall, COLS_BY_COLS)
        return small_new, big_new, columns, rows.astype(f32)

    def product_of(big_root_rows, tall):
        return dot(big_root_rows.astype(low), tall).astype(low)

    qkv, proj, fc1, fc2 = sums
    qkv_left, qkv_right, qkv_gradient, _ = statistic_update(qkv, stats_model[0], stats_qkv)
    proj_right, proj_left, _, proj_gradient = statistic_update(proj, stats_model[2], stats_model[1])
    fc1_left, fc1_right, fc1_gradient, _ = statistic_update(fc1, stats_model[3], stats_hidden[0])
    fc2_right, fc2_left, _, fc2_gradient = statistic_update(fc2, stats_model[4], stats_hidden[1])
    qkv_step = dot(small_roots[0], product_of(roots_qkv, qkv), COLS_BY_COLS).astype(low)
    fc1_step = dot(small_roots[2], product_of(roots_hidden[0], fc1), COLS_BY_COLS).astype(low)
    proj_new = proj_weight - dot(product_of(roots_model[1], proj), small_roots[1])
    fc2_new = fc2_weight - dot(product_of(roots_hidden[1], fc2), small_roots[3])
    new_stats_model = jnp.stack([qkv_left, proj_left, proj_right, fc1_left, fc2_right])
    return (
        (new_stats_model, qkv_right, jnp.stack([fc1_right, fc2_left]), qkv_step, fc1_step)
        + (qkv_gradient, proj_gradient, fc1_gradient, fc2_gradient, proj_new, fc2_new)
    )


def shards(
    plain, tokens, cotangent, window_fill, qkv_weight, proj_weight, fc1_weight, fc2_weight, vectors, vector_moments,
    bias_table, table_moments, stats_model, stats_qkv, stats_hidden, roots_model, roots_qkv, roots_hidden,
):
    width = vectors.shape[1]
    head_count = bias_table.shape[1]
    gather = functools.partial(lax.all_gather, axis_name="grp", tiled=True)
    weights = (qkv_weight, proj_weight, fc1_weight, fc2_weight)
    hot = jnp.asarray(diagonal_tables())
    diagonals = lax.dot_general(bias_table, hot, (((0,), (1,)), ((), ())), precision=lax.Precision.HIGHEST)
    if plain:
        fulls = [gather(weight.astype(low)) for weight in weights]
        base = (lax.axis_index(("rep", "grp")) * window_fill.shape[0]).astype(jnp.int32).reshape(1)
        forward = attention_forward(window_fill, base, tokens, *fulls[:2], vectors, diagonals, head_count)
    else:
        forward, fulls = gathered_forward(window_fill, tokens, weights, vectors, diagonals, head_count, 0)
    probs, mixed, normed, context, middle, normed_two = forward
    qkv_full, proj_full, fc1_full, fc2_full = fulls
    roots_low = jnp.stack([roots_model[i] for i in (0, 2, 3, 4)]).astype(low)
    roots_low, normed_two = lax.optimization_barrier((roots_low, normed_two))
    small_roots = gather(roots_low, axis=1)
    layer_output, middle_back, branch_back, fc1_term, fc2_term, fc1_bias_grad, ffn_vec = feed_forward(
        normed_two, cotangent, middle, fc1_full, fc2_full, vectors
    )
    small_roots, branch_back = lax.optimization_barrier((small_roots, branch_back))
    operands = [branch_back, middle_back, proj_full, context, normed, tokens, qkv_full, vectors, ffn_vec, fc1_bias_grad]
    if plain:
        input_gradient, att_term, small = attention_backward(probs, mixed, operands, head_count)
        small = lax.psum(small, ("rep", "grp"))
        terms = (att_term[: 3 * width], att_term[3 * width :], fc1_term, fc2_term)
        sums = [
            gather(lax.psum(lax.psum_scatter(term, "grp", scatter_dimension=0, tiled=True), "rep")) for term in terms
        ]
    else:
        input_gradient, sums, small = reduced_backward(probs, mixed, operands, head_count, fc1_term, fc2_term, 1)
    vector_total = small[: vectors.shape[0]]
    table_total = lax.dot_general(
        hot, small[SMALL_DIAG:], (((0,), (1,)), ((), ())), precision=lax.Precision.HIGHEST
    )
    if plain:
        updates = plain_update(
            sums, stats_model, stats_qkv, stats_hidden, roots_model, roots_qkv, roots_hidden, small_roots,
            proj_weight, fc2_weight,
        )
    else:
        member = lax.axis_index("grp").astype(jnp.int32).reshape(1)
        new_stats_hidden, hidden_small, fc1_gradient, fc1_step, fc2_gradient, fc2_new, fc2_copy = hidden_update(
            member, sums[2], stats_hidden, roots_hidden, stats_model, small_roots, fc2_weight
        )
        qkv_right, new_stats_model, qkv_gradient, qkv_step, proj_gradient, proj_new, proj_copy = model_update(
            member, *sums[:2], stats_qkv, roots_qkv, stats_model, hidden_small, roots_model, small_roots, proj_weight
        )
        updates = (
            (new_stats_model, qkv_right, new_stats_hidden, qkv_step, fc1_step)
            + (qkv_gradient, proj_gradient, fc1_gradient, fc2_gradient, proj_new, fc2_new)
        )
    new_stats_model, qkv_right, new_stats_hidden, qkv_step, fc1_step = updates[:5]
    qkv_gradient, proj_gradient, fc1_gradient, fc2_gradient, proj_new, fc2_new = updates[5:]
    qkv_new = qkv_weight - lax.all_to_all(qkv_step, "grp", 0, 1, tiled=True).astype(f32)
    fc1_new = fc1_weight - lax.all_to_all(fc1_step, "grp", 0, 1, tiled=True).astype(f32)
    total_tokens = tokens.shape[0] * lax.axis_size("rep") * lax.axis_size("grp")
    rate_base = total_tokens ** (-0.5)
    new_vector_moments = 0.9 * vector_moments + 0.1 * vector_total
    new_vectors = vectors - 2.0 * rate_base * new_vector_moments
    new_table_moments = 0.9 * table_moments + 0.1 * table_total
    new_table = bias_table - 8.0 * rate_base * new_table_moments
    masters = (qkv_new, proj_new, fc1_new, fc2_new)
    copies = [master.astype(low) for master in masters]
    if not plain:
        copies[1], copies[3] = proj_copy, fc2_copy
    return (
        (layer_output, input_gradient, qkv_gradient, proj_gradient, fc1_gradient, fc2_gradient)
        + masters
        + tuple(copies)
        + (new_stats_model, qkv_right, new_stats_hidden, new_vectors, new_vector_moments, new_table, new_table_moments)
    )


def solution(mesh):
    tokens, rows, blocks, copied = P(("rep", "grp"), None), P("grp", None), P(None, "grp", None), P()
    plain = (mesh.shape["rep"], mesh.shape["grp"]) != (4, 8)
    return jax.shard_map(
        functools.partial(shards, plain),
        mesh=mesh,
        in_specs=(tokens, tokens, P(("rep", "grp")))
        + (rows,) * 4
        + (copied,) * 4
        + (blocks, rows, blocks) * 2,
        out_specs=(tokens,) * 2 + (rows,) * 12 + (blocks, rows, blocks) + (copied,) * 4,
        check_vma=False,
    )
```

```python
import functools

import jax
import jax.numpy as jnp
import numpy as np
from jax import lax
from jax.experimental import pallas as pl
from jax.experimental.pallas import tpu as pltpu
from jax.sharding import PartitionSpec as P

WT = 144
SIDE = 12
SPAN = 2 * SIDE - 1
LANES = 256
DIAG = 384
ROW_TILE = 144
MIB = 1024 * 1024
low = jnp.bfloat16
f32 = jnp.float32

ROWS_BY_COLS = (((1,), (0,)), ((), ()))
COLS_BY_COLS = (((1,), (1,)), ((), ()))
ROWS_BY_ROWS = (((0,), (0,)), ((), ()))


def dot(left_matrix, right_matrix, dims=ROWS_BY_COLS):
    return lax.dot_general(left_matrix, right_matrix, dims, preferred_element_type=f32)


def standardize(values):
    centred = values - jnp.mean(values, axis=-1, keepdims=True)
    inverse = lax.rsqrt(jnp.mean(centred * centred, axis=-1, keepdims=True) + 1e-05)
    return centred * inverse, inverse


def norm_back(grad, gain, xhat, inverse):
    scaled = grad * gain
    mean_scaled = jnp.mean(scaled, axis=-1, keepdims=True)
    mean_product = jnp.mean(scaled * xhat, axis=-1, keepdims=True)
    return inverse * (scaled - mean_scaled - xhat * mean_product)


def column_sum(values):
    return jnp.sum(values, axis=0, keepdims=True)


def diagonal_tables():
    pair = np.arange(DIAG) - WT
    quotient, rest = pair // SIDE, pair % SIDE
    near = (quotient + SIDE - 1) * SPAN + rest + SIDE - 1
    far = (quotient + SIDE) * SPAN + rest - 1
    near_live = (np.abs(pair) < WT) & (quotient >= 1 - SIDE)
    far_live = (np.abs(pair) < WT) & (rest >= 1) & (quotient < SIDE - 1)
    hot = np.zeros((2, DIAG, SPAN * SPAN), np.float32)
    hot[0, np.arange(DIAG)[near_live], near[near_live]] = 1.0
    hot[1, np.arange(DIAG)[far_live], far[far_live]] = 1.0
    return hot.reshape(2 * DIAG, SPAN * SPAN)


def near_mask(shape, mirrored=False):
    column = lax.rem(lax.broadcasted_iota(jnp.int32, shape, 0), SIDE)
    if mirrored:
        column = SIDE - 1 - column
    rest = lax.rem(lax.broadcasted_iota(jnp.int32, shape, 1), SIDE)
    return column + rest < SIDE


def additive_types(heads):
    slot = np.arange(WT)
    row_high, col_high = slot // SIDE >= SIDE // 2, slot % SIDE >= SIDE // 2
    row_differs = row_high[:, None] != row_high[None, :]
    col_differs = col_high[:, None] != col_high[None, :]
    types = [
        np.where((row_differs & bool(kind // 2)) | (col_differs & bool(kind % 2)), -100.0, 0.0)
        for kind in range(4)
    ]
    return np.tile(np.stack(types), (1, 1, heads)).astype(np.float32)


def stack_mask(heads, head_size):
    lane_head = np.arange(heads * head_size) // head_size
    hot = lane_head[None, None, :] == np.arange(heads)[:, None, None]
    return np.broadcast_to(hot, (heads, WT, heads * head_size)).reshape(heads * WT, -1).astype(low)


def relative_rows(heads, diag_ref, rel_ref):
    mask = near_mask((WT, DIAG))
    for head in range(heads * rel_ref.shape[0]):
        group, place = head // heads, head % heads
        near = diag_ref[head : head + 1, :DIAG]
        far = diag_ref[head : head + 1, DIAG:]
        rolled = pltpu.roll(jnp.where(mask, near, far), DIAG - WT, 1, stride=1, stride_axis=0)
        rel_ref[group, :, place * WT : (place + 1) * WT] = rolled[:, :WT]


def stacked(block, mask_ref, heads):
    return jnp.concatenate([block] * heads, axis=0) * mask_ref[...]


def diagonal_blocks(full, heads, head_size):
    lane_head = lax.broadcasted_iota(jnp.int32, (WT, full.shape[1]), 1) // head_size
    picked = jnp.zeros((WT, full.shape[1]), f32)
    for head in range(heads):
        picked = jnp.where(lane_head == head, full[head * WT : (head + 1) * WT], picked)
    return picked


def for_row_tiles(count, body):
    def step(index, carry):
        body(pl.ds(pl.multiple_of(index * ROW_TILE, ROW_TILE), ROW_TILE))
        return carry

    lax.fori_loop(0, count // ROW_TILE, step, 0)


class Forward:
    def __init__(self, heads, head_size, refs):
        self.heads, self.head_size = heads, head_size
        self.fill, self.tokens, self.vec, self.diag, self.add, self.mask = refs[:6]
        self.probs, self.mixed_out, self.normed, self.context, self.middle, self.normed_two = refs[6:12]
        self.mixed, self.added, self.rel = refs[12:15]
        self.count, self.width = self.tokens.shape
        self.groups = self.width // LANES

    def norm_one(self):
        def body(rows):
            xhat, _ = standardize(self.tokens[rows, :].astype(f32))
            self.normed[rows, :] = (xhat * self.vec[0:1, :] + self.vec[1:2, :]).astype(low)

        for_row_tiles(self.count, body)

    def mix(self, weight_tile):
        for part in range(3):
            for tile in range(self.groups):
                start = part * self.width + tile * LANES
                sums = dot(self.normed[...], weight_tile(start))
                if part != 1:
                    row = 2 if part == 0 else 3
                    sums = sums + self.vec[row : row + 1, tile * LANES : (tile + 1) * LANES]
                self.mixed[:, start : start + LANES] = sums.astype(low)

    def attend(self, window, first_window):
        width, heads = self.width, self.heads
        rows = pl.ds(pl.multiple_of(window * WT, WT), WT)
        self.mixed_out[...] = self.mixed[rows, :]
        kind = lax.rem(first_window + window, 4)
        slot = lax.broadcasted_iota(jnp.int32, self.added.shape, 0)
        self.added[...] = jnp.where(slot < self.fill[window], self.add[kind], -1e30)
        for group in range(self.groups):
            query, key, value = (
                self.mixed[rows, part * width + group * LANES : part * width + (group + 1) * LANES]
                for part in range(3)
            )
            scores = dot(key, stacked(query, self.mask, heads), COLS_BY_COLS) * self.head_size ** (-0.5)
            scores = scores + self.rel[group] + self.added[...]
            exponent = jnp.exp(scores - jnp.max(scores, axis=0, keepdims=True))
            probs = (exponent * (1.0 / jnp.sum(exponent, axis=0, keepdims=True))).astype(low)
            self.probs[group] = probs
            full = dot(probs, value, ROWS_BY_ROWS)
            self.context[rows, group * LANES : (group + 1) * LANES] = diagonal_blocks(
                full, heads, self.head_size
            ).astype(low)

    def finish(self, weight_tile):
        for tile in range(self.groups):
            span = slice(tile * LANES, (tile + 1) * LANES)
            self.middle[:, span] = (
                self.tokens[:, span].astype(f32) + dot(self.context[...], weight_tile(tile * LANES)) + self.vec[4:5, span]
            )

        def body(rows):
            xhat, _ = standardize(self.middle[rows, :])
            self.normed_two[rows, :] = (xhat * self.vec[5:6, :] + self.vec[6:7, :]).astype(low)

        for_row_tiles(self.count, body)


def plain_forward_kernel(heads, head_size, base_ref, qkv_ref, proj_ref, *refs):
    work = Forward(heads, head_size, refs)
    window = pl.program_id(0)

    @pl.when(window == 0)
    def _():
        relative_rows(heads, work.diag, work.rel)
        work.norm_one()
        work.mix(lambda start: qkv_ref[:, start : start + LANES])

    work.attend(window, base_ref[0])

    @pl.when(window == pl.num_programs(0) - 1)
    def _():
        work.finish(lambda start: proj_ref[:, start : start + LANES])


def whole(shape):
    return pl.BlockSpec(shape, lambda *_: (0,) * len(shape), pipeline_mode=pl.Buffered(1))


def struct(shape, dtype):
    return jax.ShapeDtypeStruct(shape, dtype)


HBM = pl.BlockSpec(memory_space=pl.ANY)
SMEM = pl.BlockSpec(memory_space=pltpu.SMEM)


def forward_parts(fill, tokens, vectors, diagonals, head_count):
    count, width = tokens.shape
    windows = fill.shape[0]
    head_size = width // head_count
    heads = LANES // head_size
    groups = width // LANES
    operands = [tokens, vectors, diagonals, jnp.asarray(additive_types(heads)), jnp.asarray(stack_mask(heads, head_size))]
    in_specs = [SMEM] + [whole(operand.shape) for operand in operands]
    out_specs = [
        pl.BlockSpec((groups, WT, heads * WT), lambda w: (w, 0, 0)),
        pl.BlockSpec((WT, 3 * width), lambda w: (w, 0)),
    ] + [whole((count, width))] * 4
    out_shape = [
        struct((windows * groups, WT, heads * WT), low),
        struct((count, 3 * width), low),
        struct((count, width), low),
        struct((count, width), low),
        struct((count, width), f32),
        struct((count, width), low),
    ]
    scratch = [
        pltpu.VMEM((count, 3 * width), low),
        pltpu.VMEM((WT, heads * WT), f32),
        pltpu.VMEM((groups, WT, heads * WT), f32),
    ]
    return (heads, head_size), [fill] + operands, in_specs, out_specs, out_shape, scratch


def attention_forward(fill, base, tokens, qkv_full, proj_full, vectors, diagonals, head_count):
    sizes, operands, in_specs, out_specs, out_shape, scratch = forward_parts(
        fill, tokens, vectors, diagonals, head_count
    )
    return pl.pallas_call(
        functools.partial(plain_forward_kernel, *sizes),
        grid=(fill.shape[0],),
        in_specs=[SMEM, whole(qkv_full.shape), whole(proj_full.shape)] + in_specs,
        out_specs=out_specs,
        out_shape=out_shape,
        scratch_shapes=scratch,
        compiler_params=pltpu.CompilerParams(vmem_limit_bytes=56 * MIB),
        name="attention_forward",
    )(base, qkv_full, proj_full, *operands)


def normal_below(values, bell):
    inverse = 1.0 / (1.0 + (0.3275911 * 0.5**0.5) * jnp.abs(values))
    series = 0.5 * 1.061405429
    for term in (-1.453152027, 1.421413741, -0.284496736, 0.254829592):
        series = series * inverse + 0.5 * term
    tail = series * inverse * bell
    return jnp.where(values < 0.0, tail, 1.0 - tail)


def feed_forward_kernel(
    normed_ref, cot_ref, middle_ref, fc1_ref, fc2_ref, bias_ref, vec_ref,
    out_ref, middle_back_ref, branch_back_ref, fc1_grad_ref, fc2_grad_ref, bias_grad_ref, vec_grad_ref,
    out_sum, back_sum,
):
    step = pl.program_id(0)
    count, width = cot_ref.shape
    hidden = dot(normed_ref[...], fc1_ref[...]) + bias_ref[...]
    bell = jnp.exp(hidden * hidden * -0.5)
    below = normal_below(hidden, bell)
    active = (hidden * below).astype(low)
    slope = below + hidden * bell * ((2.0 * np.pi) ** -0.5)
    hidden_back = dot(cot_ref[...], fc2_ref[...], COLS_BY_COLS) * slope
    hidden_back = hidden_back.astype(low)
    bias_grad_ref[...] = column_sum(hidden_back.astype(f32))
    fc2_grad_ref[...] = dot(active, cot_ref[...], ROWS_BY_ROWS).astype(low)
    fc1_grad_ref[...] = dot(hidden_back, normed_ref[...], ROWS_BY_ROWS).astype(low)
    out_term = dot(active, fc2_ref[...])
    back_term = dot(hidden_back, fc1_ref[...], COLS_BY_COLS)

    @pl.when(step == 0)
    def _():
        out_sum[...] = out_term
        back_sum[...] = back_term

    @pl.when(step > 0)
    def _():
        out_sum[...] += out_term
        back_sum[...] += back_term

    @pl.when(step == pl.num_programs(0) - 1)
    def _():
        vec_grad_ref[...] = jnp.zeros_like(vec_grad_ref)

        def finish(part, carry):
            rows = pl.ds(pl.multiple_of(part * ROW_TILE, ROW_TILE), ROW_TILE)
            middle = middle_ref[rows, :]
            cot = cot_ref[rows, :].astype(f32)
            out_ref[rows, :] = (middle + out_sum[rows, :] + vec_ref[7:8, :]).astype(low)
            xhat, inverse = standardize(middle)
            grad = back_sum[rows, :]
            middle_back = cot + norm_back(grad, vec_ref[5:6, :], xhat, inverse)
            middle_back_ref[rows, :] = middle_back
            branch_back = middle_back.astype(low)
            branch_back_ref[rows, :] = branch_back
            vec_grad_ref[0:1, :] += column_sum(branch_back.astype(f32))
            vec_grad_ref[1:2, :] += column_sum(grad * xhat)
            vec_grad_ref[2:3, :] += column_sum(grad)
            vec_grad_ref[3:4, :] += column_sum(cot)
            return carry

        lax.fori_loop(0, count // ROW_TILE, finish, 0)


def feed_forward(normed, cotangent, middle, fc1_full, fc2_full, vectors):
    count, width = cotangent.shape
    hidden_width = fc1_full.shape[1]
    tile = LANES
    bias = vectors[8:].reshape(1, hidden_width)
    return pl.pallas_call(
        feed_forward_kernel,
        grid=(hidden_width // tile,),
        in_specs=[whole(x.shape) for x in (normed, cotangent, middle)]
        + [
            pl.BlockSpec((width, tile), lambda f: (0, f)),
            pl.BlockSpec((tile, width), lambda f: (f, 0)),
            pl.BlockSpec((1, tile), lambda f: (0, f)),
            whole(vectors.shape),
        ],
        out_specs=[
            whole((count, width)),
            whole((count, width)),
            whole((count, width)),
            pl.BlockSpec((tile, width), lambda f: (f, 0)),
            pl.BlockSpec((tile, width), lambda f: (f, 0)),
            pl.BlockSpec((1, tile), lambda f: (0, f)),
            whole((8, width)),
        ],
        out_shape=[
            struct((count, width), low),
            struct((count, width), f32),
            struct((count, width), low),
            struct((hidden_width, width), low),
            struct((hidden_width, width), low),
            struct((1, hidden_width), f32),
            struct((8, width), f32),
        ],
        scratch_shapes=[pltpu.VMEM((count, width), f32), pltpu.VMEM((count, width), f32)],
        compiler_params=pltpu.CompilerParams(vmem_limit_bytes=56 * MIB),
        name="feed_forward",
    )(normed, cotangent, middle, fc1_full, fc2_full, bias, vectors)


class Backward:
    def __init__(self, heads, head_size, refs, proj_grad, qkv_grad):
        self.heads, self.head_size = heads, head_size
        self.probs, self.query, self.key, self.value = refs[:4]
        self.branch_back, self.middle_back, self.proj, self.context, self.normed, self.tokens, self.qkv = refs[4:11]
        self.vec, self.mask, self.ffn_grad, self.bias_grad = refs[11:15]
        self.input_grad = refs[15]
        self.context_back, self.mixed_back, self.pairs, self.normed_back, self.small = refs[16:]
        self.proj_grad, self.qkv_grad = proj_grad, qkv_grad
        self.count, self.width = self.tokens.shape
        self.groups = self.width // LANES
        self.windows = self.count // WT

    def begin(self):
        self.pairs[...] = jnp.zeros_like(self.pairs)
        self.small[...] = jnp.zeros_like(self.small)
        for tile in range(self.groups):
            span = slice(tile * LANES, (tile + 1) * LANES)
            self.context_back[:, span] = dot(self.branch_back[...], self.proj[span, :], COLS_BY_COLS).astype(low)

    def begin_grads(self):
        for tile in range(self.groups):
            span = slice(tile * LANES, (tile + 1) * LANES)
            self.proj_grad(tile, dot(self.context[:, span], self.branch_back[...], ROWS_BY_ROWS).astype(low))

    def columns(self, part, group):
        return pl.ds(pl.multiple_of(part * self.width + group * LANES, LANES), LANES)

    def attend(self, group, window):
        heads = self.heads
        score_scale = self.head_size ** (-0.5)
        rows = pl.ds(pl.multiple_of(window * WT, WT), WT)
        query, key, value = self.query[...], self.key[...], self.value[...]
        probs_low = self.probs[0]
        probs = probs_low.astype(f32)
        back_stack = stacked(self.context_back[rows, self.columns(0, group)], self.mask, heads)
        value_back = dot(probs_low, back_stack)
        product = probs * dot(value, back_stack, COLS_BY_COLS)
        scores_back = (product - probs * jnp.sum(product, axis=0, keepdims=True)).astype(low)
        self.pairs[group] += scores_back.astype(f32)
        key_back = dot(scores_back, stacked(query, self.mask, heads)) * score_scale
        full = dot(scores_back, key, ROWS_BY_ROWS)
        query_back = diagonal_blocks(full, heads, self.head_size) * score_scale
        for part, back in enumerate((query_back, key_back, value_back)):
            self.mixed_back[rows, self.columns(part, group)] = back.astype(low)

    def group_grads(self, group):
        for part in range(3):
            block = self.mixed_back[:, self.columns(part, group)]
            self.qkv_grad(part, group, dot(block, self.normed[...], ROWS_BY_ROWS).astype(low))

    def normed_back_step(self):
        for tile in range(self.groups):
            span = slice(tile * LANES, (tile + 1) * LANES)
            self.normed_back[:, span] = dot(self.mixed_back[...], self.qkv[span, :], COLS_BY_COLS)

    def finish(self):
        width = self.width
        for row, part in ((2, 0), (3, 2)):

            def body(rows, row=row, part=part):
                block = self.mixed_back[rows, part * width : (part + 1) * width]
                self.small[row : row + 1, :] += column_sum(block.astype(f32))

            for_row_tiles(self.count, body)

        def body(rows):
            xhat, inverse = standardize(self.tokens[rows, :].astype(f32))
            grad = self.normed_back[rows, :]
            back = self.middle_back[rows, :] + norm_back(grad, self.vec[0:1, :], xhat, inverse)
            self.input_grad[rows, :] = back.astype(low)
            self.small[0:1, :] += column_sum(grad * xhat)
            self.small[1:2, :] += column_sum(grad)

        for_row_tiles(self.count, body)
        self.small[4:8, :] = self.ffn_grad[0:4, :]
        for row in range(self.bias_grad.shape[1] // width):
            self.small[8 + row : 9 + row, :] = self.bias_grad[:, row * width : (row + 1) * width]

    def diagonals(self):
        mask = near_mask((WT, DIAG), mirrored=True)
        order = [lax.broadcasted_iota(jnp.int32, (WT, WT), axis) for axis in range(2)]
        mirror = jnp.where(order[0] + order[1] == WT - 1, 1.0, 0.0).astype(f32)
        for group in range(self.groups):
            self.pairs[group] = lax.dot_general(
                mirror, self.pairs[group], ROWS_BY_COLS, precision=lax.Precision.HIGHEST, preferred_element_type=f32
            )
        for head in range(self.groups * self.heads):
            group, place = head // self.heads, head % self.heads
            block = self.pairs[group, :, place * WT : (place + 1) * WT]
            block = jnp.concatenate([block, jnp.zeros((WT, DIAG - WT), f32)], axis=1)
            rolled = pltpu.roll(block, 1, 1, stride=1, stride_axis=0)
            row = SMALL_DIAG + head
            self.small[row : row + 1, :DIAG] = column_sum(jnp.where(mask, rolled, 0.0))
            self.small[row : row + 1, DIAG : 2 * DIAG] = column_sum(jnp.where(mask, 0.0, rolled))


SMALL_DIAG = 16


def plain_backward_kernel(heads, head_size, *refs):
    weight_grad = refs[16]
    width = weight_grad.shape[1]

    def proj_grad(tile, value):
        weight_grad[3 * width + tile * LANES : 3 * width + (tile + 1) * LANES, :] = value

    def qkv_grad(part, group, value):
        weight_grad[pl.ds(pl.multiple_of(part * width + group * LANES, LANES), LANES), :] = value

    work = Backward(heads, head_size, refs[:16] + refs[18:], proj_grad, qkv_grad)
    step = pl.program_id(0)
    windows = work.windows
    busy = windows * work.groups
    group, window = step // windows, lax.rem(step, windows)

    @pl.when(step == 0)
    def _():
        work.begin()
        work.begin_grads()

    @pl.when(step < busy)
    def _():
        work.attend(group, window)

    @pl.when((step < busy) & (window == windows - 1))
    def _():
        work.group_grads(group)

    @pl.when(step == busy)
    def _():
        work.normed_back_step()
        work.finish()
        work.diagonals()
        refs[17][...] = work.small[...]


def backward_parts(probs, mixed, operands, head_count):
    count, width = operands[0].shape
    windows = count // WT
    head_size = width // head_count
    heads = LANES // head_size
    groups = width // LANES
    last = windows * groups - 1
    mask = jnp.asarray(stack_mask(heads, head_size))
    operands = operands[:8] + [mask] + operands[8:]

    def place(step):
        step = jnp.minimum(step, last)
        return step // windows, lax.rem(step, windows)

    def probs_map(step):
        group, window = place(step)
        return window * groups + group, 0, 0

    def mixed_map(part):
        def index(step):
            group, window = place(step)
            return window, part * groups + group

        return index

    in_specs = (
        [pl.BlockSpec((1, WT, heads * WT), probs_map)]
        + [pl.BlockSpec((WT, LANES), mixed_map(part)) for part in range(3)]
        + [whole(operand.shape) for operand in operands]
    )
    scratch = [
        pltpu.VMEM((count, width), low),
        pltpu.VMEM((count, 3 * width), low),
        pltpu.VMEM((groups, WT, heads * WT), f32),
        pltpu.VMEM((count, width), f32),
        pltpu.VMEM((SMALL_DIAG + head_count, width), f32),
    ]
    return (heads, head_size), [probs, mixed, mixed, mixed] + operands, in_specs, scratch, last + 1


def attention_backward(probs, mixed, operands, head_count):
    sizes, operands, in_specs, scratch, busy = backward_parts(probs, mixed, operands, head_count)
    count, width = operands[4].shape
    small_shape = (SMALL_DIAG + head_count, width)
    return pl.pallas_call(
        functools.partial(plain_backward_kernel, *sizes),
        grid=(busy + 1,),
        in_specs=in_specs,
        out_specs=[whole((count, width)), whole((4 * width, width)), whole(small_shape)],
        out_shape=[struct((count, width), low), struct((4 * width, width), low), struct(small_shape, f32)],
        scratch_shapes=scratch,
        compiler_params=pltpu.CompilerParams(vmem_limit_bytes=60 * MIB),
        name="attention_backward",
    )(*operands)


MESH = pl.DeviceIdType.MESH


class Peers:
    def __init__(self):
        self.z = lax.axis_index("rep")
        place = lax.axis_index("grp")
        self.c = lax.rem(place, 2)
        self.x = lax.rem(place // 2, 2)
        self.y = place // 4
        self.core_peer = (self.z, place + 1 - 2 * self.c)
        self.x_peer = (self.z, place + 2 - 4 * self.x)
        self.y_peer = (self.z, place + 4 - 8 * self.y)
        self.z_places = [lax.rem(self.z + step, 4) for step in range(1, 4)]
        self.z_peers = [(there, place) for there in self.z_places]

    def plane(self):
        return [self.core_peer, self.x_peer, self.y_peer]

    def everyone(self):
        return self.plane() + self.z_peers


def meet(peers):
    barrier = pltpu.get_barrier_semaphore()
    for peer in peers:
        pl.semaphore_signal(barrier, inc=1, device_id=peer, device_id_type=MESH)
    pl.semaphore_wait(barrier, len(peers))


class Copies:
    def __init__(self, send_sems, recv_sems):
        self.send_sems, self.recv_sems = send_sems, recv_sems
        self.made = []

    def make(self, ends, peer):
        copy = Copy(self, len(self.made), ends, peer)
        self.made.append(copy)
        copy.build().start()
        return copy

    def drain(self):
        for copy in self.made:
            copy.build().wait_send()


class Copy:
    def __init__(self, owner, number, ends, peer):
        self.owner, self.number, self.ends, self.peer = owner, number, ends, peer

    def build(self):
        source, target = self.ends()
        return pltpu.make_async_remote_copy(
            src_ref=source,
            dst_ref=target,
            send_sem=self.owner.send_sems.at[self.number],
            recv_sem=self.owner.recv_sems.at[self.number],
            device_id=self.peer,
            device_id_type=MESH,
        )

    def wait_recv(self):
        self.build().wait_recv()


def same(place):
    return lambda: (place(), place())


class Gather:
    def __init__(self, me, copies, source, out):
        self.me, self.copies, self.source, self.out = me, copies, source, out
        self.half = out.shape[3] // 2
        self.across = []

    def block(self, flip_y, flip_x):
        me = self.me
        return self.out.at[1 - me.y if flip_y else me.y, 1 - me.x if flip_x else me.x, me.c]

    def start(self):
        me = self.me

        def ends():
            return self.source(), self.block(False, False)

        self.by_x = self.copies.make(ends, me.x_peer)
        self.by_y = self.copies.make(ends, me.y_peer)
        self.across.append(self.copies.make(ends, me.core_peer))

    def relay(self):
        me = self.me
        self.by_x.wait_recv()
        to_y = self.copies.make(same(lambda: self.block(False, True).at[pl.ds(0, self.half)]), me.y_peer)
        self.by_y.wait_recv()
        to_x = self.copies.make(same(lambda: self.block(True, False).at[pl.ds(self.half, self.half)]), me.x_peer)
        self.relayed = (to_x, to_y)
        self.across.append(self.copies.make(same(lambda: self.block(False, True)), me.core_peer))
        self.across.append(self.copies.make(same(lambda: self.block(True, False)), me.core_peer))

    def cross(self):
        for copy in self.relayed:
            copy.wait_recv()
        self.across.append(self.copies.make(same(lambda: self.block(True, True)), self.me.core_peer))

    def wait(self):
        for copy in self.across:
            copy.wait_recv()


def gathered_forward_kernel(heads, head_size, *refs):
    qkv_shard, proj_shard, fc1_shard, fc2_shard = refs[:4]
    outs = refs[10:20]
    qkv_out, proj_out, fc1_out, fc2_out = outs[6:]
    scratch = refs[20:]
    work = Forward(heads, head_size, refs[4:10] + outs[:6] + scratch[:3])
    qkv_full, proj_full, fc1_low, fc2_low, send_sems, recv_sems, local_sems = scratch[3:]
    me = Peers()
    copies = Copies(send_sems, recv_sems)
    own = (me.y, me.x, me.c)
    qkv = Gather(me, copies, lambda: qkv_full.at[own], qkv_full)
    proj = Gather(me, copies, lambda: proj_full.at[own], proj_full)
    fc1 = Gather(me, copies, lambda: fc1_low, fc1_out)
    fc2 = Gather(me, copies, lambda: fc2_low, fc2_out)

    def local(index):
        source = (fc1_low, fc2_low, qkv_full, proj_full)[index]
        target = (fc1_out, fc2_out, qkv_out, proj_out)[index]
        return pltpu.make_async_copy(source, target.at[own] if index < 2 else target, local_sems.at[index])

    window = pl.program_id(0)
    first_window = (me.z * 8 + me.y * 4 + me.x * 2 + me.c) * pl.num_programs(0)

    def weight_tile(full):
        def tile(start):
            return full[:, :, :, :, start : start + LANES].reshape(-1, LANES)

        return tile

    @pl.when(window == 0)
    def _():
        qkv_full[own] = qkv_shard[...].astype(low)
        proj_full[own] = proj_shard[...].astype(low)
        meet(me.plane())
        qkv.start()
        proj.start()
        fc1_low[...] = fc1_shard[...].astype(low)
        fc2_low[...] = fc2_shard[...].astype(low)
        work.norm_one()
        relative_rows(heads, work.diag, work.rel)
        qkv.relay()
        proj.relay()
        fc1.start()
        fc2.start()
        local(0).start()
        local(1).start()
        qkv.cross()
        qkv.wait()
        local(2).start()
        work.mix(weight_tile(qkv_full))

    @pl.when(window == 1)
    def _():
        proj.cross()

    @pl.when(window == 3)
    def _():
        fc1.relay()

    @pl.when(window == 6)
    def _():
        fc1.cross()
        fc2.relay()

    work.attend(window, first_window)

    @pl.when(window == pl.num_programs(0) - 1)
    def _():
        proj.wait()
        local(3).start()
        work.finish(weight_tile(proj_full))
        fc2.cross()
        fc1.wait()
        fc2.wait()
        for index in range(4):
            local(index).wait()
        copies.drain()


def gathered_forward(fill, tokens, weights, vectors, diagonals, head_count, collective_id):
    sizes, operands, in_specs, out_specs, out_shape, scratch = forward_parts(
        fill, tokens, vectors, diagonals, head_count
    )
    fulls = [(2, 2, 2) + weight.shape for weight in weights]
    results = pl.pallas_call(
        functools.partial(gathered_forward_kernel, *sizes),
        grid=(fill.shape[0],),
        in_specs=[whole(weight.shape) for weight in weights] + in_specs,
        out_specs=out_specs + [HBM] * 4,
        out_shape=out_shape + [struct(full, low) for full in fulls],
        scratch_shapes=scratch
        + [pltpu.VMEM(fulls[0], low), pltpu.VMEM(fulls[1], low)]
        + [pltpu.VMEM(weight.shape, low) for weight in weights[2:]]
        + [pltpu.SemaphoreType.DMA((32,)), pltpu.SemaphoreType.DMA((32,)), pltpu.SemaphoreType.DMA((4,))],
        compiler_params=pltpu.CompilerParams(
            collective_id=collective_id, has_side_effects=True, vmem_limit_bytes=58 * MIB
        ),
        name="gathered_forward",
    )(*weights, *operands)
    return results[:6], [full.reshape(-1, weight.shape[1]) for full, weight in zip(results[6:], weights)]


PIECE = 16


class Reduction:
    def __init__(self, me, copies, term, mine, out, buffers, load_sems, store_sems):
        self.me, self.copies, self.term, self.mine, self.out = me, copies, term, mine, out
        self.core_in, self.first_in, self.second_in, self.z_in, self.final = buffers
        self.load_sems, self.store_sems = load_sems, store_sems
        self.parts = self.core_in.shape[1]
        self.half = self.core_in.shape[-1] // 2
        self.core, self.first, self.second, self.over_z, self.last_z, self.spread, self.relayed, self.across = (
            {} for _ in range(8)
        )

    def sides(self):
        return pl.ds(0, self.half), pl.ds(self.half, self.half)

    def z_columns(self, z):
        return pl.ds(pl.multiple_of(lax.rem(z, 2) * self.half, self.half), self.half)

    def loop(self, amount, body):
        def step(index, carry):
            body(index)
            return carry

        lax.fori_loop(0, amount, step, 0)

    def load(self, k):
        ref, at = self.mine
        return pltpu.make_async_copy(self.term(k, self.me.c), ref.at[k], self.load_sems.at[k])

    def store(self, k):
        me = self.me
        return pltpu.make_async_copy(
            self.final.at[k], self.out(k, me.c, me.x, me.y, (me.z // 2, slice(None), self.z_columns(me.z))),
            self.store_sems.at[k],
        )

    def start(self, k):
        me = self.me
        self.core[k] = self.copies.make(lambda: (self.term(k, 1 - me.c), self.core_in.at[k]), me.core_peer)
        if self.load_sems is not None:
            self.load(k).start()

    def finish_core(self, k):
        me = self.me
        ref, at = self.mine
        if self.load_sems is not None:
            self.load(k).wait()
        self.core[k].wait_recv()

        def add(step):
            part, x, y, row = step // 8, lax.rem(step // 4, 2), lax.rem(step // 2, 2), lax.rem(step, 2)
            place = at(k, part, x, y, row)
            ref[place] = ref[place] + self.core_in[k, part, x, y, row]

        self.loop(8 * self.parts, add)
        every = slice(None)
        self.first[k] = (
            self.copies.make(
                lambda: (
                    ref.at[at(k, every, 1 - me.x, every, every) + (every, self.sides()[0])], self.first_in.at[k, 0],
                ),
                me.x_peer,
            ),
            self.copies.make(
                lambda: (
                    ref.at[at(k, every, every, 1 - me.y, every) + (every, self.sides()[1])], self.first_in.at[k, 1],
                ),
                me.y_peer,
            ),
        )

    def finish_first(self, k):
        me = self.me
        ref, at = self.mine
        for copy in self.first[k]:
            copy.wait_recv()
        half = self.half

        def add(step):
            part, other, row = step // 4, lax.rem(step // 2, 2), lax.rem(step, 2)
            place = at(k, part, me.x, other, row) + (slice(None), slice(0, half))
            ref[place] = ref[place] + self.first_in[k, 0, part, other, row]
            place = at(k, part, other, me.y, row) + (slice(None), slice(half, 2 * half))
            ref[place] = ref[place] + self.first_in[k, 1, part, other, row]

        self.loop(4 * self.parts, add)
        every = slice(None)
        self.second[k] = (
            self.copies.make(
                lambda: (
                    ref.at[at(k, every, me.x, 1 - me.y, every) + (every, self.sides()[0])], self.second_in.at[k, 0],
                ),
                me.y_peer,
            ),
            self.copies.make(
                lambda: (
                    ref.at[at(k, every, 1 - me.x, me.y, every) + (every, self.sides()[1])], self.second_in.at[k, 1],
                ),
                me.x_peer,
            ),
        )

    def finish_second(self, k):
        me = self.me
        ref, at = self.mine
        for copy in self.second[k]:
            copy.wait_recv()
        half = self.half

        def add(step):
            part, row = step // 2, lax.rem(step, 2)
            for side, span in enumerate((slice(0, half), slice(half, 2 * half))):
                place = at(k, part, me.x, me.y, row) + (slice(None), span)
                ref[place] = ref[place] + self.second_in[k, side, part, row]

        self.loop(2 * self.parts, add)

        def piece(part, z):
            return at(k, part, me.x, me.y, z // 2) + (slice(None), self.z_columns(z))

        self.over_z[k] = [
            self.copies.make(lambda there=there: (ref.at[piece(slice(None), there)], self.z_in.at[k, me.z]), peer)
            for there, peer in zip(me.z_places, me.z_peers)
        ]

        def keep(part):
            self.z_in[k, me.z, part] = ref[piece(part, me.z)]

        self.loop(self.parts, keep)

    def finish_z(self, k):
        me = self.me
        for copy in self.over_z[k]:
            copy.wait_recv()

        def add(part):
            total = self.z_in[k, 0, part].astype(f32)
            for place in range(1, 4):
                total = total + self.z_in[k, place, part].astype(f32)
            self.final[k, part] = total.astype(low)

        self.loop(self.parts, add)
        self.last_z[k] = [
            self.copies.make(
                lambda: (
                    self.final.at[k],
                    self.out(k, me.c, me.x, me.y, (me.z // 2, slice(None), self.z_columns(me.z))),
                ),
                peer,
            )
            for peer in me.z_peers
        ]
        self.store(k).start()

    def finish_last_z(self, k):
        me = self.me
        for copy in self.last_z[k]:
            copy.wait_recv()
        self.store(k).wait()
        own = same(lambda: self.out(k, me.c, me.x, me.y, ()))
        self.spread[k] = [self.copies.make(own, peer) for peer in (me.x_peer, me.y_peer)]
        self.across[k] = [self.copies.make(own, me.core_peer)]

    def finish_spread(self, k):
        me = self.me
        by_x, by_y = self.spread[k]
        every = slice(None)
        by_y.wait_recv()
        to_x = self.copies.make(
            same(lambda: self.out(k, me.c, me.x, 1 - me.y, (every, every, self.sides()[0]))), me.x_peer
        )
        by_x.wait_recv()
        to_y = self.copies.make(
            same(lambda: self.out(k, me.c, 1 - me.x, me.y, (every, every, self.sides()[1]))), me.y_peer
        )
        self.relayed[k] = (to_x, to_y)
        self.across[k].append(self.copies.make(same(lambda: self.out(k, me.c, 1 - me.x, me.y, ())), me.core_peer))
        self.across[k].append(self.copies.make(same(lambda: self.out(k, me.c, me.x, 1 - me.y, ())), me.core_peer))

    def finish_relay(self, k):
        me = self.me
        for copy in self.relayed[k]:
            copy.wait_recv()
        self.across[k].append(self.copies.make(same(lambda: self.out(k, me.c, 1 - me.x, 1 - me.y, ())), me.core_peer))

    def wait(self, k):
        for copy in self.across[k]:
            copy.wait_recv()

    def stage(self, number, k):
        stages = (
            self.finish_core, self.finish_first, self.finish_second, self.finish_z, self.finish_last_z,
            self.finish_spread, self.finish_relay,
        )
        stages[number](k)


STAGES = 7


def reduction_buffers(amount, parts, width):
    half = width // 2
    return [
        pltpu.VMEM((amount, parts, 2, 2, 2, PIECE, width), low),
        pltpu.VMEM((amount, 2, parts, 2, 2, PIECE, half), low),
        pltpu.VMEM((amount, 2, parts, 2, PIECE, half), low),
        pltpu.VMEM((amount, 4, parts, PIECE, half), low),
        pltpu.VMEM((amount, parts, PIECE, half), low),
    ]


class SmallSum:
    def __init__(self, me, copies, small, inbox):
        self.me, self.copies, self.small, self.inbox, self.made = me, copies, small, inbox, []

    def step(self, number):
        peers = self.me.plane()
        z = self.me.z
        if number > 0:
            self.made[number - 1].wait_recv()
            self.small[...] += self.inbox[number - 1]
        if number < 3:
            self.inbox[3 + number] = self.small[...]
            self.made.append(
                self.copies.make(lambda: (self.inbox.at[3 + number], self.inbox.at[number]), peers[number])
            )
        else:
            self.inbox[6 + z] = self.small[...]
            for peer in self.me.z_peers:
                self.made.append(self.copies.make(same(lambda: self.inbox.at[6 + z]), peer))

    def finish(self):
        for copy in self.made[3:]:
            copy.wait_recv()
        self.small[...] = (self.inbox[6] + self.inbox[7]) + (self.inbox[8] + self.inbox[9])


def reduced_backward_kernel(heads, head_size, *refs):
    fc1_term, fc2_term = refs[15:17]
    input_grad, fc_out, qkv_out, proj_out, small_out = refs[17:22]
    att, fc_mine = refs[27:29]
    fc_buffers, att_buffers = refs[29:34], refs[34:39]
    inbox, send_sems, recv_sems, load_sems, fc_store_sems, att_store_sems = refs[39:]
    groups = att.shape[0] - 1
    tile_shape = (2, 2, 2, 2, PIECE, att.shape[-1])

    def proj_grad(tile, value):
        att[groups, tile] = value.reshape(tile_shape)

    def qkv_grad(part, group, value):
        att[group, part] = value.reshape(tile_shape)

    work = Backward(heads, head_size, refs[:15] + (input_grad,) + refs[22:27], proj_grad, qkv_grad)
    me = Peers()
    copies = Copies(send_sems, recv_sems)
    chunks = fc1_term.shape[0]

    def fc_term(k, c):
        return (fc1_term, fc2_term)[k % 2].at[k // 2, :, c]

    def fc_place(k, c, x, y, rest):
        return fc_out.at[(k % 2, k // 2, slice(None), c, x, y) + rest]

    def att_place(k, c, x, y, rest):
        if k == groups:
            return proj_out.at[(slice(None), c, x, y) + rest]
        return qkv_out.at[(slice(None), k, c, x, y) + rest]

    fc = Reduction(
        me, copies, fc_term, (fc_mine, lambda *place: place), fc_place, fc_buffers, load_sems, fc_store_sems
    )
    att_sum = Reduction(
        me, copies, lambda k, c: att.at[k, :, c], (att, lambda k, part, *place: (k, part, me.c) + place), att_place,
        att_buffers, None, att_store_sems,
    )
    small = SmallSum(me, copies, work.small, inbox)
    order = [(fc, k) for k in range(2 * chunks)] + [(att_sum, groups)] + [(att_sum, k) for k in range(groups)]
    waves = len(order) + STAGES - 1
    done = [0]

    def wave():
        number = done[0]
        done[0] += 1
        for index in reversed(range(len(order))):
            if 0 <= number - index < STAGES:
                which, k = order[index]
                which.stage(number - index, k)

    step = pl.program_id(0)
    windows = work.windows
    busy = windows * groups
    group, window = step // windows, lax.rem(step, windows)

    @pl.when(step == 0)
    def _():
        meet(me.everyone())
        for k in range(2 * chunks):
            fc.start(k)
        work.begin_grads()
        att_sum.start(groups)
        work.begin()

    @pl.when(step < busy)
    def _():
        work.attend(group, window)

    for number in range(groups):

        @pl.when(step == (number + 1) * windows - 1)
        def _():
            work.group_grads(number)
            att_sum.start(number)

    for number in range(waves):
        at = 2 + 3 * number
        if at >= busy:
            break

        @pl.when(step == at)
        def _():
            wave()

    @pl.when(step == busy)
    def _():
        wave()
        work.normed_back_step()
        wave()
        work.finish()
        wave()
        work.diagonals()
        small.step(0)
        for number in range(1, 5):
            wave()
            if number < 4:
                small.step(number)
            else:
                small.finish()
        small_out[...] = work.small[...]
        while done[0] < waves:
            wave()
        for which, k in order:
            which.wait(k)
        copies.drain()


def reduced_backward(probs, mixed, operands, head_count, fc1_term, fc2_term, collective_id):
    sizes, operands, in_specs, scratch, busy = backward_parts(probs, mixed, operands, head_count)
    count, width = operands[4].shape
    hidden_width = fc1_term.shape[0]
    groups = width // LANES
    tile_shape = (2, 2, 2, 2, PIECE, width)
    chunks = 2
    parts = hidden_width // LANES // chunks
    small_shape = (SMALL_DIAG + head_count, width)
    fc_shape = (chunks, parts) + tile_shape
    copies = 19 * (2 * chunks + groups + 1) + 6
    input_grad, fc_sum, qkv_sum, proj_sum, small = pl.pallas_call(
        functools.partial(reduced_backward_kernel, *sizes),
        grid=(busy + 1,),
        in_specs=in_specs + [HBM] * 2,
        out_specs=[whole((count, width))] + [HBM] * 3 + [whole(small_shape)],
        out_shape=[
            struct((count, width), low),
            struct((2,) + fc_shape, low),
            struct((3, groups) + tile_shape, low),
            struct((groups,) + tile_shape, low),
            struct(small_shape, f32),
        ],
        scratch_shapes=scratch
        + [pltpu.VMEM((groups + 1, 3) + tile_shape, low), pltpu.VMEM((2 * chunks, parts) + tile_shape[1:], low)]
        + reduction_buffers(2 * chunks, parts, width)
        + reduction_buffers(groups + 1, 3, width)
        + [
            pltpu.VMEM((10,) + small_shape, f32),
            pltpu.SemaphoreType.DMA((copies,)),
            pltpu.SemaphoreType.DMA((copies,)),
            pltpu.SemaphoreType.DMA((2 * chunks,)),
            pltpu.SemaphoreType.DMA((2 * chunks,)),
            pltpu.SemaphoreType.DMA((groups + 1,)),
        ],
        compiler_params=pltpu.CompilerParams(
            collective_id=collective_id, has_side_effects=True, vmem_limit_bytes=62 * MIB
        ),
        name="reduced_backward",
    )(*operands, fc1_term.reshape(fc_shape), fc2_term.reshape(fc_shape))
    sums = [part.reshape(-1, width) for part in (qkv_sum, proj_sum, fc_sum)]
    return input_grad, sums, small


def tile_update(tall, rows, big, root, pick, sum_ref, fresh):
    span = rows.shape[0]
    across = dot(jnp.concatenate([rows, pick], axis=0), tall, COLS_BY_COLS)
    columns = across[span:]
    term = dot(jnp.concatenate([root.astype(low), columns.astype(low)], axis=0), tall)

    @pl.when(fresh)
    def _():
        sum_ref[...] = term

    @pl.when(jnp.logical_not(fresh))
    def _():
        sum_ref[...] += term

    return 0.5 * big + 0.5 * across[:span], columns


def column_pick(member, shape):
    row, column = (lax.broadcasted_iota(jnp.int32, shape, axis) for axis in range(2))
    return jnp.where(column == row + member * shape[0], 1.0, 0.0).astype(low)


def hidden_kernel(
    member_ref, tall_ref, rows_ref, big_ref, root_ref, small_ref, small_root_ref, fc2_ref,
    big_out_ref, small_out_ref, fc1_grad_ref, fc1_step_ref, fc2_grad_ref, fc2_new_ref, fc2_copy_ref,
    sum_ref,
):
    matrix, tile = pl.program_id(0), pl.program_id(1)
    span = rows_ref.shape[0]
    pick = column_pick(member_ref[0], small_ref.shape[1:])
    big_new, columns = tile_update(
        tall_ref[...], rows_ref[...], big_ref[0], root_ref[0], pick, sum_ref, tile == 0
    )
    big_out_ref[0] = big_new

    @pl.when(matrix == 0)
    def _():
        fc1_grad_ref[...] = columns

    @pl.when(tile == pl.num_programs(1) - 1)
    def _():
        small_out_ref[0] = 0.5 * small_ref[0] + 0.5 * sum_ref[span:, :]
        product = sum_ref[:span, :].astype(low)

        @pl.when(matrix == 0)
        def _():
            fc1_step_ref[...] = dot(small_root_ref[0], product, COLS_BY_COLS).astype(low)

        @pl.when(matrix == 1)
        def _():
            new = fc2_ref[...] - dot(product, small_root_ref[0])
            fc2_new_ref[...] = new
            fc2_copy_ref[...] = new.astype(low)
            fc2_grad_ref[...] = rows_ref[...].astype(f32)


def hidden_update(member, fc_sum, stats_hidden, roots_hidden, stats_model, small_roots, fc2_weight):
    width = fc_sum.shape[1]
    _, span, hidden_width = stats_hidden.shape
    model_rows = stats_model.shape[1]
    tiles = hidden_width // width
    last = tiles - 1
    return pl.pallas_call(
        hidden_kernel,
        grid_spec=pltpu.PrefetchScalarGridSpec(
            num_scalar_prefetch=1,
            grid=(2, tiles),
            in_specs=[
                pl.BlockSpec((width, width), lambda i, j, m: (i * tiles + j, 0)),
                pl.BlockSpec((span, width), lambda i, j, m: (i * (hidden_width // span) + m[0], 0)),
                pl.BlockSpec((1, span, width), lambda i, j, m: (i, 0, j)),
                pl.BlockSpec((1, span, width), lambda i, j, m: (i, 0, j)),
                pl.BlockSpec((1, model_rows, width), lambda i, j, m: (3 + i, 0, 0)),
                pl.BlockSpec((1, width, width), lambda i, j, m: (2 + i, 0, 0)),
                pl.BlockSpec((span, width), lambda i, j, m: (0, 0)),
            ],
            out_specs=[
                pl.BlockSpec((1, span, width), lambda i, j, m: (i, 0, j)),
                pl.BlockSpec((1, model_rows, width), lambda i, j, m: (i, 0, 0)),
                pl.BlockSpec((model_rows, width), lambda i, j, m: (0, jnp.where(i == 0, j, last))),
                pl.BlockSpec((width, span), lambda i, j, m: (0, 0)),
                pl.BlockSpec((span, width), lambda i, j, m: (0, 0)),
                pl.BlockSpec((span, width), lambda i, j, m: (0, 0)),
                pl.BlockSpec((span, width), lambda i, j, m: (0, 0)),
            ],
            scratch_shapes=[pltpu.VMEM((span + model_rows, width), f32)],
        ),
        out_shape=[
            struct(stats_hidden.shape, f32),
            struct((2, model_rows, width), f32),
            struct((model_rows, hidden_width), f32),
            struct((width, span), low),
            struct((span, width), f32),
            struct((span, width), f32),
            struct((span, width), low),
        ],
        compiler_params=pltpu.CompilerParams(vmem_limit_bytes=48 * MIB),
        name="hidden_update",
    )(member, fc_sum, fc_sum, stats_hidden, roots_hidden, stats_model, small_roots, fc2_weight)


def exchange_places(me):
    member = me.y * 4 + me.x * 2 + me.c
    return member, [lax.rem(member + step, 8) for step in range(1, 8)]


class Exchange:
    def __init__(self, me, copies, blocks, inbox):
        self.me, self.copies, self.blocks, self.inbox = me, copies, blocks, inbox

    def start(self):
        member, others = exchange_places(self.me)
        self.made = [
            self.copies.make(lambda there=there: (self.blocks.at[there], self.inbox.at[member]), (self.me.z, there))
            for there in others
        ]

    def wait(self):
        for copy in self.made:
            copy.wait_recv()


def exchange_kernel(amount, *refs):
    blocks, inboxes = refs[:amount], refs[amount : 2 * amount]
    send_sems, recv_sems, local_sems = refs[2 * amount :]
    me = Peers()
    copies = Copies(send_sems, recv_sems)
    member, others = exchange_places(me)
    meet([(me.z, there) for there in others])
    exchanges = [Exchange(me, copies, source, inbox) for source, inbox in zip(blocks, inboxes)]
    own = [
        pltpu.make_async_copy(source.at[member], inbox.at[member], local_sems.at[index])
        for index, (source, inbox) in enumerate(zip(blocks, inboxes))
    ]
    for copy in own:
        copy.start()
    for exchange in exchanges:
        exchange.start()
    for exchange in exchanges:
        exchange.wait()
    for copy in own:
        copy.wait()
    copies.drain()


def exchange_rows(steps, collective_id):
    amount = len(steps)
    blocks = [step.reshape(8, step.shape[0] // 8, step.shape[1]) for step in steps]
    vmem = pl.BlockSpec(memory_space=pltpu.VMEM)
    return pl.pallas_call(
        functools.partial(exchange_kernel, amount),
        in_specs=[vmem] * amount,
        out_specs=[vmem] * amount,
        out_shape=[struct(block.shape, low) for block in blocks],
        scratch_shapes=[
            pltpu.SemaphoreType.DMA((7 * amount,)),
            pltpu.SemaphoreType.DMA((7 * amount,)),
            pltpu.SemaphoreType.DMA((amount,)),
        ],
        compiler_params=pltpu.CompilerParams(collective_id=collective_id, has_side_effects=True),
        name="exchange_rows",
    )(*blocks)


def apply_kernel(amount, *refs):
    for index in range(amount):
        old, blocks, new_ref, copy_ref = (refs[index + part * amount] for part in range(4))
        step = jnp.concatenate([blocks[place] for place in range(blocks.shape[0])], axis=1)
        new = old[...] - step.astype(f32)
        new_ref[...] = new
        copy_ref[...] = new.astype(low)


def apply_steps(weights, inboxes):
    return pl.pallas_call(
        functools.partial(apply_kernel, len(weights)),
        out_shape=[struct(weight.shape, dtype) for dtype in (f32, low) for weight in weights],
        compiler_params=pltpu.CompilerParams(vmem_limit_bytes=32 * MIB),
        name="apply_steps",
    )(*weights, *inboxes)


def model_kernel(
    member_ref, tall_ref, qkv_rows_ref, proj_tall_ref, proj_rows_ref, big_ref, root_ref, stats_ref, hidden_small_ref, proj_root_ref,
    small_root_ref, proj_ref,
    big_out_ref, stats_out_ref, qkv_grad_ref, qkv_step_ref, proj_grad_ref, proj_new_ref, proj_copy_ref,
    sum_ref, proj_sum_ref,
):
    tile = pl.program_id(0)
    span = qkv_rows_ref.shape[0]
    model_rows = proj_rows_ref.shape[0]
    last = pl.num_programs(0) - 1
    pick = column_pick(member_ref[0], proj_rows_ref.shape)

    @pl.when(tile < last)
    def _():
        big_new, columns = tile_update(
            tall_ref[...], qkv_rows_ref[...], big_ref[...], root_ref[...], pick, sum_ref, tile == 0
        )
        big_out_ref[...] = big_new
        qkv_grad_ref[...] = columns

    @pl.when(tile == last)
    def _():
        qkv_step_ref[...] = dot(small_root_ref[0], sum_ref[:span, :].astype(low), COLS_BY_COLS).astype(low)
        stats_out_ref[0] = 0.5 * stats_ref[0] + 0.5 * sum_ref[span:, :]
        rows = proj_rows_ref[...]
        proj_left, _ = tile_update(
            proj_tall_ref[...], rows, stats_ref[1], proj_root_ref[0], pick, proj_sum_ref, tile == last
        )
        stats_out_ref[1] = proj_left
        stats_out_ref[2] = 0.5 * stats_ref[2] + 0.5 * proj_sum_ref[model_rows:, :]
        stats_out_ref[3] = hidden_small_ref[0]
        stats_out_ref[4] = hidden_small_ref[1]
        new = proj_ref[...] - dot(proj_sum_ref[:model_rows, :].astype(low), small_root_ref[1])
        proj_new_ref[...] = new
        proj_copy_ref[...] = new.astype(low)
        proj_grad_ref[...] = rows.astype(f32)


def model_update(
    member, qkv_sum, proj_sum, stats_qkv, roots_qkv, stats_model, hidden_small, roots_model, small_roots, proj_weight
):
    width = qkv_sum.shape[1]
    span, qkv_width = stats_qkv.shape
    model_rows = stats_model.shape[1]
    tiles = qkv_width // width

    def fixed(shape):
        return pl.BlockSpec(shape, lambda j, m: (0,) * len(shape))

    clamped = pl.BlockSpec((span, width), lambda j, m: (0, jnp.minimum(j, tiles - 1)))
    return pl.pallas_call(
        model_kernel,
        grid_spec=pltpu.PrefetchScalarGridSpec(
            num_scalar_prefetch=1,
            grid=(tiles + 1,),
            in_specs=[
                pl.BlockSpec((width, width), lambda j, m: (jnp.minimum(j, tiles - 1), 0)),
                pl.BlockSpec((span, width), lambda j, m: (m[0], 0)),
                fixed((width, width)),
                pl.BlockSpec((model_rows, width), lambda j, m: (m[0], 0)),
                clamped,
                clamped,
                fixed(stats_model.shape),
                fixed(hidden_small.shape),
                pl.BlockSpec((1, model_rows, width), lambda j, m: (1, 0, 0)),
                pl.BlockSpec((2, width, width), lambda j, m: (0, 0, 0)),
                fixed(proj_weight.shape),
            ],
            out_specs=[
                clamped,
                fixed(stats_model.shape),
                pl.BlockSpec((model_rows, width), lambda j, m: (0, jnp.minimum(j, tiles - 1))),
                fixed((width, span)),
                fixed((model_rows, width)),
                fixed((model_rows, width)),
                fixed((model_rows, width)),
            ],
            scratch_shapes=[
                pltpu.VMEM((span + model_rows, width), f32),
                pltpu.VMEM((2 * model_rows, width), f32),
            ],
        ),
        out_shape=[
            struct(stats_qkv.shape, f32),
            struct(stats_model.shape, f32),
            struct((model_rows, qkv_width), f32),
            struct((width, span), low),
            struct((model_rows, width), f32),
            struct((model_rows, width), f32),
            struct((model_rows, width), low),
        ],
        compiler_params=pltpu.CompilerParams(vmem_limit_bytes=48 * MIB),
        name="model_update",
    )(
        member, qkv_sum, qkv_sum, proj_sum, proj_sum, stats_qkv, roots_qkv, stats_model, hidden_small, roots_model,
        small_roots, proj_weight,
    )


def plain_update(
    sums, stats_model, stats_qkv, stats_hidden, roots_model, roots_qkv, roots_hidden, small_roots, weights
):
    width = sums[0].shape[1]
    member = lax.axis_index("grp")
    model_rows = stats_model.shape[1]
    picked = member * model_rows + jnp.arange(model_rows, dtype=jnp.int32)
    pick = (picked[:, None] == jnp.arange(width, dtype=jnp.int32)[None, :]).astype(low)

    def statistic_update(tall, small_rows, big_rows):
        columns = dot(pick, tall, COLS_BY_COLS)
        small_new = 0.5 * small_rows + 0.5 * dot(columns.astype(low), tall)
        rows = lax.dynamic_slice_in_dim(tall, member * big_rows.shape[0], big_rows.shape[0], 0)
        big_new = 0.5 * big_rows + 0.5 * dot(rows, tall, COLS_BY_COLS)
        return small_new, big_new, columns, rows.astype(f32)

    def product_of(big_root_rows, tall):
        return dot(big_root_rows.astype(low), tall).astype(low)

    qkv, proj, fc1, fc2 = sums
    qkv_left, qkv_right, qkv_gradient, _ = statistic_update(qkv, stats_model[0], stats_qkv)
    proj_right, proj_left, _, proj_gradient = statistic_update(proj, stats_model[2], stats_model[1])
    fc1_left, fc1_right, fc1_gradient, _ = statistic_update(fc1, stats_model[3], stats_hidden[0])
    fc2_right, fc2_left, _, fc2_gradient = statistic_update(fc2, stats_model[4], stats_hidden[1])
    qkv_step = dot(small_roots[0], product_of(roots_qkv, qkv), COLS_BY_COLS).astype(low)
    fc1_step = dot(small_roots[2], product_of(roots_hidden[0], fc1), COLS_BY_COLS).astype(low)
    qkv_weight, proj_weight, fc1_weight, fc2_weight = weights
    qkv_new = qkv_weight - lax.all_to_all(qkv_step, "grp", 0, 1, tiled=True).astype(f32)
    fc1_new = fc1_weight - lax.all_to_all(fc1_step, "grp", 0, 1, tiled=True).astype(f32)
    proj_new = proj_weight - dot(product_of(roots_model[1], proj), small_roots[1])
    fc2_new = fc2_weight - dot(product_of(roots_hidden[1], fc2), small_roots[3])
    new_stats_model = jnp.stack([qkv_left, proj_left, proj_right, fc1_left, fc2_right])
    return (
        (new_stats_model, qkv_right, jnp.stack([fc1_right, fc2_left])),
        (qkv_gradient, proj_gradient, fc1_gradient, fc2_gradient),
        (qkv_new, proj_new, fc1_new, fc2_new),
    )


def shards(
    plain, tokens, cotangent, window_fill, qkv_weight, proj_weight, fc1_weight, fc2_weight, vectors, vector_moments,
    bias_table, table_moments, stats_model, stats_qkv, stats_hidden, roots_model, roots_qkv, roots_hidden,
):
    width = vectors.shape[1]
    head_count = bias_table.shape[1]
    gather = functools.partial(lax.all_gather, axis_name="grp", tiled=True)
    weights = (qkv_weight, proj_weight, fc1_weight, fc2_weight)
    hot = jnp.asarray(diagonal_tables())
    diagonals = lax.dot_general(bias_table, hot, (((0,), (1,)), ((), ())), precision=lax.Precision.HIGHEST)
    if plain:
        fulls = [gather(weight.astype(low)) for weight in weights]
        base = (lax.axis_index(("rep", "grp")) * window_fill.shape[0]).astype(jnp.int32).reshape(1)
        forward = attention_forward(window_fill, base, tokens, *fulls[:2], vectors, diagonals, head_count)
    else:
        forward, fulls = gathered_forward(window_fill, tokens, weights, vectors, diagonals, head_count, 0)
    probs, mixed, normed, context, middle, normed_two = forward
    qkv_full, proj_full, fc1_full, fc2_full = fulls
    roots_low = jnp.stack([roots_model[i] for i in (0, 2, 3, 4)]).astype(low)
    roots_low, normed_two = lax.optimization_barrier((roots_low, normed_two))
    small_roots = gather(roots_low, axis=1)
    layer_output, middle_back, branch_back, fc1_term, fc2_term, fc1_bias_grad, ffn_vec = feed_forward(
        normed_two, cotangent, middle, fc1_full, fc2_full, vectors
    )
    small_roots, branch_back = lax.optimization_barrier((small_roots, branch_back))
    operands = [branch_back, middle_back, proj_full, context, normed, tokens, qkv_full, vectors, ffn_vec, fc1_bias_grad]
    if plain:
        input_gradient, att_term, small = attention_backward(probs, mixed, operands, head_count)
        small = lax.psum(small, ("rep", "grp"))
        terms = (att_term[: 3 * width], att_term[3 * width :], fc1_term, fc2_term)
        sums = [
            gather(lax.psum(lax.psum_scatter(term, "grp", scatter_dimension=0, tiled=True), "rep")) for term in terms
        ]
    else:
        input_gradient, sums, small = reduced_backward(probs, mixed, operands, head_count, fc1_term, fc2_term, 1)
    vector_total = small[: vectors.shape[0]]
    table_total = lax.dot_general(
        hot, small[SMALL_DIAG:], (((0,), (1,)), ((), ())), precision=lax.Precision.HIGHEST
    )
    if plain:
        statistics, gradients, masters = plain_update(
            sums, stats_model, stats_qkv, stats_hidden, roots_model, roots_qkv, roots_hidden, small_roots, weights
        )
        copies = tuple(master.astype(low) for master in masters)
    else:
        member = lax.axis_index("grp").astype(jnp.int32).reshape(1)
        new_stats_hidden, hidden_small, fc1_gradient, fc1_step, fc2_gradient, fc2_new, fc2_copy = hidden_update(
            member, sums[2], stats_hidden, roots_hidden, stats_model, small_roots, fc2_weight
        )
        qkv_right, new_stats_model, qkv_gradient, qkv_step, proj_gradient, proj_new, proj_copy = model_update(
            member, *sums[:2], stats_qkv, roots_qkv, stats_model, hidden_small, roots_model, small_roots, proj_weight
        )
        inboxes = exchange_rows((qkv_step, fc1_step), 2)
        qkv_new, fc1_new, qkv_copy, fc1_copy = apply_steps((qkv_weight, fc1_weight), inboxes)
        statistics = (new_stats_model, qkv_right, new_stats_hidden)
        gradients = (qkv_gradient, proj_gradient, fc1_gradient, fc2_gradient)
        masters = (qkv_new, proj_new, fc1_new, fc2_new)
        copies = (qkv_copy, proj_copy, fc1_copy, fc2_copy)
    total_tokens = tokens.shape[0] * lax.axis_size("rep") * lax.axis_size("grp")
    rate_base = total_tokens ** (-0.5)
    new_vector_moments = 0.9 * vector_moments + 0.1 * vector_total
    new_vectors = vectors - 2.0 * rate_base * new_vector_moments
    new_table_moments = 0.9 * table_moments + 0.1 * table_total
    new_table = bias_table - 8.0 * rate_base * new_table_moments
    return (
        (layer_output, input_gradient)
        + gradients
        + masters
        + copies
        + statistics
        + (new_vectors, new_vector_moments, new_table, new_table_moments)
    )


def solution(mesh):
    tokens, rows, blocks, copied = P(("rep", "grp"), None), P("grp", None), P(None, "grp", None), P()
    plain = (mesh.shape["rep"], mesh.shape["grp"]) != (4, 8)
    return jax.shard_map(
        functools.partial(shards, plain),
        mesh=mesh,
        in_specs=(tokens, tokens, P(("rep", "grp")))
        + (rows,) * 4
        + (copied,) * 4
        + (blocks, rows, blocks) * 2,
        out_specs=(tokens,) * 2 + (rows,) * 12 + (blocks, rows, blocks) + (copied,) * 4,
        check_vma=False,
    )
```

```python
import functools

import jax
import jax.numpy as jnp
import numpy as np
from jax import lax
from jax.experimental import pallas as pl
from jax.experimental.pallas import tpu as pltpu
from jax.sharding import PartitionSpec as P

WT = 144
SIDE = 12
SPAN = 2 * SIDE - 1
LANES = 256
DIAG = 384
ROW_TILE = 144
MIB = 1024 * 1024
low = jnp.bfloat16
f32 = jnp.float32

ROWS_BY_COLS = (((1,), (0,)), ((), ()))
COLS_BY_COLS = (((1,), (1,)), ((), ()))
ROWS_BY_ROWS = (((0,), (0,)), ((), ()))


def dot(left_matrix, right_matrix, dims=ROWS_BY_COLS):
    return lax.dot_general(left_matrix, right_matrix, dims, preferred_element_type=f32)


def standardize(values):
    centred = values - jnp.mean(values, axis=-1, keepdims=True)
    inverse = lax.rsqrt(jnp.mean(centred * centred, axis=-1, keepdims=True) + 1e-05)
    return centred * inverse, inverse


def norm_back(grad, gain, xhat, inverse):
    scaled = grad * gain
    mean_scaled = jnp.mean(scaled, axis=-1, keepdims=True)
    mean_product = jnp.mean(scaled * xhat, axis=-1, keepdims=True)
    return inverse * (scaled - mean_scaled - xhat * mean_product)


def column_sum(values):
    return jnp.sum(values, axis=0, keepdims=True)


def diagonal_tables():
    pair = np.arange(DIAG) - WT
    quotient, rest = pair // SIDE, pair % SIDE
    near = (quotient + SIDE - 1) * SPAN + rest + SIDE - 1
    far = (quotient + SIDE) * SPAN + rest - 1
    near_live = (np.abs(pair) < WT) & (quotient >= 1 - SIDE)
    far_live = (np.abs(pair) < WT) & (rest >= 1) & (quotient < SIDE - 1)
    hot = np.zeros((2, DIAG, SPAN * SPAN), np.float32)
    hot[0, np.arange(DIAG)[near_live], near[near_live]] = 1.0
    hot[1, np.arange(DIAG)[far_live], far[far_live]] = 1.0
    return hot.reshape(2 * DIAG, SPAN * SPAN)


def near_mask(shape, mirrored=False):
    column = lax.rem(lax.broadcasted_iota(jnp.int32, shape, 0), SIDE)
    if mirrored:
        column = SIDE - 1 - column
    rest = lax.rem(lax.broadcasted_iota(jnp.int32, shape, 1), SIDE)
    return column + rest < SIDE


def additive_types(heads):
    slot = np.arange(WT)
    row_high, col_high = slot // SIDE >= SIDE // 2, slot % SIDE >= SIDE // 2
    row_differs = row_high[:, None] != row_high[None, :]
    col_differs = col_high[:, None] != col_high[None, :]
    types = [
        np.where((row_differs & bool(kind // 2)) | (col_differs & bool(kind % 2)), -100.0, 0.0)
        for kind in range(4)
    ]
    return np.tile(np.stack(types), (1, 1, heads)).astype(np.float32)


def stack_mask(heads, head_size):
    lane_head = np.arange(heads * head_size) // head_size
    hot = lane_head[None, None, :] == np.arange(heads)[:, None, None]
    return np.broadcast_to(hot, (heads, WT, heads * head_size)).reshape(heads * WT, -1).astype(low)


def relative_rows(heads, diag_ref, rel_ref):
    mask = near_mask((WT, DIAG))
    for head in range(heads * rel_ref.shape[0]):
        group, place = head // heads, head % heads
        near = diag_ref[head : head + 1, :DIAG]
        far = diag_ref[head : head + 1, DIAG:]
        rolled = pltpu.roll(jnp.where(mask, near, far), DIAG - WT, 1, stride=1, stride_axis=0)
        rel_ref[group, :, place * WT : (place + 1) * WT] = rolled[:, :WT]


def stacked(block, mask_ref, heads):
    return jnp.concatenate([block] * heads, axis=0) * mask_ref[...]


def diagonal_blocks(full, heads, head_size):
    lane_head = lax.broadcasted_iota(jnp.int32, (WT, full.shape[1]), 1) // head_size
    picked = jnp.zeros((WT, full.shape[1]), f32)
    for head in range(heads):
        picked = jnp.where(lane_head == head, full[head * WT : (head + 1) * WT], picked)
    return picked


def for_row_tiles(count, body):
    def step(index, carry):
        body(pl.ds(pl.multiple_of(index * ROW_TILE, ROW_TILE), ROW_TILE))
        return carry

    lax.fori_loop(0, count // ROW_TILE, step, 0)


class Forward:
    def __init__(self, heads, head_size, refs):
        self.heads, self.head_size = heads, head_size
        self.fill, self.tokens, self.vec, self.diag, self.add, self.mask = refs[:6]
        self.probs, self.mixed_out, self.normed, self.context, self.middle, self.normed_two = refs[6:12]
        self.mixed, self.added, self.rel = refs[12:15]
        self.count, self.width = self.tokens.shape
        self.groups = self.width // LANES

    def norm_one(self):
        def body(rows):
            xhat, _ = standardize(self.tokens[rows, :].astype(f32))
            self.normed[rows, :] = (xhat * self.vec[0:1, :] + self.vec[1:2, :]).astype(low)

        for_row_tiles(self.count, body)

    def mix(self, weight_tile):
        for part in range(3):
            for tile in range(self.groups):
                start = part * self.width + tile * LANES
                sums = dot(self.normed[...], weight_tile(start))
                if part != 1:
                    row = 2 if part == 0 else 3
                    sums = sums + self.vec[row : row + 1, tile * LANES : (tile + 1) * LANES]
                self.mixed[:, start : start + LANES] = sums.astype(low)

    def attend(self, window, first_window):
        width, heads = self.width, self.heads
        rows = pl.ds(pl.multiple_of(window * WT, WT), WT)
        self.mixed_out[...] = self.mixed[rows, :]
        kind = lax.rem(first_window + window, 4)
        slot = lax.broadcasted_iota(jnp.int32, self.added.shape, 0)
        self.added[...] = jnp.where(slot < self.fill[window], self.add[kind], -1e30)
        for group in range(self.groups):
            query, key, value = (
                self.mixed[rows, part * width + group * LANES : part * width + (group + 1) * LANES]
                for part in range(3)
            )
            scores = dot(key, stacked(query, self.mask, heads), COLS_BY_COLS) * self.head_size ** (-0.5)
            scores = scores + self.rel[group] + self.added[...]
            exponent = jnp.exp(scores - jnp.max(scores, axis=0, keepdims=True))
            probs = (exponent * (1.0 / jnp.sum(exponent, axis=0, keepdims=True))).astype(low)
            self.probs[group] = probs
            full = dot(probs, value, ROWS_BY_ROWS)
            self.context[rows, group * LANES : (group + 1) * LANES] = diagonal_blocks(
                full, heads, self.head_size
            ).astype(low)

    def finish(self, weight_tile):
        for tile in range(self.groups):
            span = slice(tile * LANES, (tile + 1) * LANES)
            self.middle[:, span] = (
                self.tokens[:, span].astype(f32) + dot(self.context[...], weight_tile(tile * LANES)) + self.vec[4:5, span]
            )

        def body(rows):
            xhat, _ = standardize(self.middle[rows, :])
            self.normed_two[rows, :] = (xhat * self.vec[5:6, :] + self.vec[6:7, :]).astype(low)

        for_row_tiles(self.count, body)


def plain_forward_kernel(heads, head_size, base_ref, qkv_ref, proj_ref, *refs):
    work = Forward(heads, head_size, refs)
    window = pl.program_id(0)

    @pl.when(window == 0)
    def _():
        relative_rows(heads, work.diag, work.rel)
        work.norm_one()
        work.mix(lambda start: qkv_ref[:, start : start + LANES])

    work.attend(window, base_ref[0])

    @pl.when(window == pl.num_programs(0) - 1)
    def _():
        work.finish(lambda start: proj_ref[:, start : start + LANES])


def whole(shape):
    return pl.BlockSpec(shape, lambda *_: (0,) * len(shape), pipeline_mode=pl.Buffered(1))


def struct(shape, dtype):
    return jax.ShapeDtypeStruct(shape, dtype)


HBM = pl.BlockSpec(memory_space=pl.ANY)
SMEM = pl.BlockSpec(memory_space=pltpu.SMEM)


def forward_parts(fill, tokens, vectors, diagonals, head_count):
    count, width = tokens.shape
    windows = fill.shape[0]
    head_size = width // head_count
    heads = LANES // head_size
    groups = width // LANES
    operands = [tokens, vectors, diagonals, jnp.asarray(additive_types(heads)), jnp.asarray(stack_mask(heads, head_size))]
    in_specs = [SMEM] + [whole(operand.shape) for operand in operands]
    out_specs = [
        pl.BlockSpec((groups, WT, heads * WT), lambda w: (w, 0, 0)),
        pl.BlockSpec((WT, 3 * width), lambda w: (w, 0)),
    ] + [whole((count, width))] * 4
    out_shape = [
        struct((windows * groups, WT, heads * WT), low),
        struct((count, 3 * width), low),
        struct((count, width), low),
        struct((count, width), low),
        struct((count, width), f32),
        struct((count, width), low),
    ]
    scratch = [
        pltpu.VMEM((count, 3 * width), low),
        pltpu.VMEM((WT, heads * WT), f32),
        pltpu.VMEM((groups, WT, heads * WT), f32),
    ]
    return (heads, head_size), [fill] + operands, in_specs, out_specs, out_shape, scratch


def attention_forward(fill, base, tokens, qkv_full, proj_full, vectors, diagonals, head_count):
    sizes, operands, in_specs, out_specs, out_shape, scratch = forward_parts(
        fill, tokens, vectors, diagonals, head_count
    )
    return pl.pallas_call(
        functools.partial(plain_forward_kernel, *sizes),
        grid=(fill.shape[0],),
        in_specs=[SMEM, whole(qkv_full.shape), whole(proj_full.shape)] + in_specs,
        out_specs=out_specs,
        out_shape=out_shape,
        scratch_shapes=scratch,
        compiler_params=pltpu.CompilerParams(vmem_limit_bytes=56 * MIB),
        name="attention_forward",
    )(base, qkv_full, proj_full, *operands)


def normal_below(values, bell):
    scale = 1.0 + (0.3275911 * 0.5**0.5) * jnp.abs(values)
    inverse = pl.reciprocal(scale, approx=True)
    inverse = inverse * (2.0 - scale * inverse)
    series = 0.5 * 1.061405429
    for term in (-1.453152027, 1.421413741, -0.284496736, 0.254829592):
        series = series * inverse + 0.5 * term
    tail = series * inverse * bell
    return jnp.where(values < 0.0, tail, 1.0 - tail)


FFN_ROWS = 336
FFN_CHUNK = 48


class FeedForward:
    def __init__(self, refs):
        self.normed, self.cot, self.middle, self.fc1, self.fc2, self.bias, self.vec = refs[:7]
        self.out, self.middle_back, self.branch_back, self.bias_grad, self.vec_grad = refs[7:12]
        self.out_sum, self.back_sum, self.hidden, self.active_back, self.active, self.hidden_back = refs[12:18]
        self.count, self.width = self.cot.shape

    def begin(self):
        self.out_sum[...] = jnp.zeros_like(self.out_sum)
        self.back_sum[...] = jnp.zeros_like(self.back_sum)

    def tile(self):
        fc1 = self.fc1[...].reshape(self.width, LANES)
        fc2 = self.fc2[...]
        spans = [slice(start, start + FFN_ROWS) for start in range(0, self.count, FFN_ROWS)]

        def enter(rows):
            self.hidden[rows, :] = dot(self.normed[rows, :], fc1)
            self.active_back[rows, :] = dot(self.cot[rows, :], fc2, COLS_BY_COLS)

        def bend(rows):
            total = jnp.zeros((8, LANES), f32)
            for start in range(rows.start, rows.stop, FFN_CHUNK):
                chunk = slice(start, start + FFN_CHUNK)
                hidden = self.hidden[chunk, :] + self.bias[...]
                bell = jnp.exp(hidden * hidden * -0.5)
                below = normal_below(hidden, bell)
                self.active[chunk, :] = (hidden * below).astype(low)
                slope = below + hidden * bell * ((2.0 * np.pi) ** -0.5)
                back = (self.active_back[chunk, :] * slope).astype(low)
                self.hidden_back[chunk, :] = back
                total = total + jnp.sum(back.astype(f32).reshape(-1, 8, LANES), axis=0)
            return total

        def leave(rows):
            self.out_sum[rows, :] += dot(self.active[rows, :], fc2)
            self.back_sum[rows, :] += dot(self.hidden_back[rows, :], fc1, COLS_BY_COLS)

        total = jnp.zeros((8, LANES), f32)
        amount = len(spans)
        for index in range(amount + 2):
            if index < amount:
                enter(spans[index])
            if 0 <= index - 1 < amount:
                total = total + bend(spans[index - 1])
            if 0 <= index - 2 < amount:
                leave(spans[index - 2])
        self.bias_grad[...] = column_sum(total)
        fc1_grad = dot(self.hidden_back[...], self.normed[...], ROWS_BY_ROWS).astype(low)
        fc2_grad = dot(self.active[...], self.cot[...], ROWS_BY_ROWS).astype(low)
        return fc1_grad, fc2_grad

    def finish(self):
        self.vec_grad[...] = jnp.zeros_like(self.vec_grad)

        def body(rows):
            middle = self.middle[rows, :]
            cot = self.cot[rows, :].astype(f32)
            self.out[rows, :] = (middle + self.out_sum[rows, :] + self.vec[7:8, :]).astype(low)
            xhat, inverse = standardize(middle)
            grad = self.back_sum[rows, :]
            middle_back = cot + norm_back(grad, self.vec[5:6, :], xhat, inverse)
            self.middle_back[rows, :] = middle_back
            branch_back = middle_back.astype(low)
            self.branch_back[rows, :] = branch_back
            self.vec_grad[0:1, :] += column_sum(branch_back.astype(f32))
            self.vec_grad[1:2, :] += column_sum(grad * xhat)
            self.vec_grad[2:3, :] += column_sum(grad)
            self.vec_grad[3:4, :] += column_sum(cot)

        for_row_tiles(self.count, body)


def plain_feed_forward_kernel(*refs):
    work = FeedForward(refs[:12] + refs[14:])
    fc1_grad_ref, fc2_grad_ref = refs[12:14]
    step = pl.program_id(0)

    @pl.when(step == 0)
    def _():
        work.begin()

    fc1_grad_ref[...], fc2_grad_ref[...] = work.tile()

    @pl.when(step == pl.num_programs(0) - 1)
    def _():
        work.finish()


def feed_forward_parts(normed, cotangent, middle, fc1_tiles, fc2_full, vectors):
    count, width = cotangent.shape
    hidden_width = fc2_full.shape[0]
    tiles = hidden_width // LANES
    bias = vectors[8:].reshape(1, hidden_width)
    in_specs = (
        [whole(x.shape) for x in (normed, cotangent, middle)]
        + [
            pl.BlockSpec(fc1_tiles.shape[:3] + (1,) + fc1_tiles.shape[4:], lambda f: (0, 0, 0, f, 0, 0)),
            pl.BlockSpec((LANES, width), lambda f: (f, 0)),
            pl.BlockSpec((1, LANES), lambda f: (0, f)),
            whole(vectors.shape),
        ]
    )
    out_specs = [whole((count, width))] * 3 + [pl.BlockSpec((1, LANES), lambda f: (0, f)), whole((8, width))]
    out_shape = [
        struct((count, width), low),
        struct((count, width), f32),
        struct((count, width), low),
        struct((1, hidden_width), f32),
        struct((8, width), f32),
    ]
    scratch = [
        pltpu.VMEM((count, width), f32),
        pltpu.VMEM((count, width), f32),
        pltpu.VMEM((count, LANES), f32),
        pltpu.VMEM((count, LANES), f32),
        pltpu.VMEM((count, LANES), low),
        pltpu.VMEM((count, LANES), low),
    ]
    operands = [normed, cotangent, middle, fc1_tiles, fc2_full, bias, vectors]
    return operands, in_specs, out_specs, out_shape, scratch, tiles


def feed_forward(normed, cotangent, middle, fc1_tiles, fc2_full, vectors):
    operands, in_specs, out_specs, out_shape, scratch, tiles = feed_forward_parts(
        normed, cotangent, middle, fc1_tiles, fc2_full, vectors
    )
    width = cotangent.shape[1]
    return pl.pallas_call(
        plain_feed_forward_kernel,
        grid=(tiles,),
        in_specs=in_specs,
        out_specs=out_specs + [pl.BlockSpec((LANES, width), lambda f: (f, 0))] * 2,
        out_shape=out_shape + [struct((tiles * LANES, width), low)] * 2,
        scratch_shapes=scratch,
        compiler_params=pltpu.CompilerParams(vmem_limit_bytes=56 * MIB),
        name="feed_forward",
    )(*operands)


class Backward:
    def __init__(self, heads, head_size, refs, proj_grad, qkv_grad):
        self.heads, self.head_size = heads, head_size
        self.probs, self.query, self.key, self.value = refs[:4]
        self.branch_back, self.middle_back, self.proj, self.context, self.normed, self.tokens, self.qkv = refs[4:11]
        self.vec, self.mask, self.ffn_grad, self.bias_grad = refs[11:15]
        self.input_grad = refs[15]
        self.context_back, self.mixed_back, self.pairs, self.normed_back, self.small = refs[16:]
        self.proj_grad, self.qkv_grad = proj_grad, qkv_grad
        self.count, self.width = self.tokens.shape
        self.groups = self.width // LANES
        self.windows = self.count // WT

    def begin(self):
        self.pairs[...] = jnp.zeros_like(self.pairs)
        self.small[...] = jnp.zeros_like(self.small)
        for tile in range(self.groups):
            span = slice(tile * LANES, (tile + 1) * LANES)
            self.context_back[:, span] = dot(self.branch_back[...], self.proj[span, :], COLS_BY_COLS).astype(low)

    def begin_grads(self):
        for tile in range(self.groups):
            span = slice(tile * LANES, (tile + 1) * LANES)
            self.proj_grad(tile, dot(self.context[:, span], self.branch_back[...], ROWS_BY_ROWS).astype(low))

    def columns(self, part, group):
        return pl.ds(pl.multiple_of(part * self.width + group * LANES, LANES), LANES)

    def attend(self, group, window):
        heads = self.heads
        score_scale = self.head_size ** (-0.5)
        rows = pl.ds(pl.multiple_of(window * WT, WT), WT)
        query, key, value = self.query[...], self.key[...], self.value[...]
        probs_low = self.probs[0]
        probs = probs_low.astype(f32)
        back_stack = stacked(self.context_back[rows, self.columns(0, group)], self.mask, heads)
        value_back = dot(probs_low, back_stack)
        product = probs * dot(value, back_stack, COLS_BY_COLS)
        scores_back = (product - probs * jnp.sum(product, axis=0, keepdims=True)).astype(low)
        self.pairs[group] += scores_back.astype(f32)
        key_back = dot(scores_back, stacked(query, self.mask, heads)) * score_scale
        full = dot(scores_back, key, ROWS_BY_ROWS)
        query_back = diagonal_blocks(full, heads, self.head_size) * score_scale
        for part, back in enumerate((query_back, key_back, value_back)):
            self.mixed_back[rows, self.columns(part, group)] = back.astype(low)

    def group_grads(self, group):
        for part in range(3):
            block = self.mixed_back[:, self.columns(part, group)]
            self.qkv_grad(part, group, dot(block, self.normed[...], ROWS_BY_ROWS).astype(low))

    def normed_back_step(self):
        for tile in range(self.groups):
            span = slice(tile * LANES, (tile + 1) * LANES)
            self.normed_back[:, span] = dot(self.mixed_back[...], self.qkv[span, :], COLS_BY_COLS)

    def finish(self):
        width = self.width
        for row, part in ((2, 0), (3, 2)):

            def body(rows, row=row, part=part):
                block = self.mixed_back[rows, part * width : (part + 1) * width]
                self.small[row : row + 1, :] += column_sum(block.astype(f32))

            for_row_tiles(self.count, body)

        def body(rows):
            xhat, inverse = standardize(self.tokens[rows, :].astype(f32))
            grad = self.normed_back[rows, :]
            back = self.middle_back[rows, :] + norm_back(grad, self.vec[0:1, :], xhat, inverse)
            self.input_grad[rows, :] = back.astype(low)
            self.small[0:1, :] += column_sum(grad * xhat)
            self.small[1:2, :] += column_sum(grad)

        for_row_tiles(self.count, body)
        self.small[4:8, :] = self.ffn_grad[0:4, :]
        for row in range(self.bias_grad.shape[1] // width):
            self.small[8 + row : 9 + row, :] = self.bias_grad[:, row * width : (row + 1) * width]

    def diagonals(self):
        mask = near_mask((WT, DIAG), mirrored=True)
        order = [lax.broadcasted_iota(jnp.int32, (WT, WT), axis) for axis in range(2)]
        mirror = jnp.where(order[0] + order[1] == WT - 1, 1.0, 0.0).astype(f32)
        for group in range(self.groups):
            self.pairs[group] = lax.dot_general(
                mirror, self.pairs[group], ROWS_BY_COLS, precision=lax.Precision.HIGHEST, preferred_element_type=f32
            )
        for head in range(self.groups * self.heads):
            group, place = head // self.heads, head % self.heads
            block = self.pairs[group, :, place * WT : (place + 1) * WT]
            block = jnp.concatenate([block, jnp.zeros((WT, DIAG - WT), f32)], axis=1)
            rolled = pltpu.roll(block, 1, 1, stride=1, stride_axis=0)
            row = SMALL_DIAG + head
            self.small[row : row + 1, :DIAG] = column_sum(jnp.where(mask, rolled, 0.0))
            self.small[row : row + 1, DIAG : 2 * DIAG] = column_sum(jnp.where(mask, 0.0, rolled))


SMALL_DIAG = 16


def plain_backward_kernel(heads, head_size, *refs):
    weight_grad = refs[16]
    width = weight_grad.shape[1]

    def proj_grad(tile, value):
        weight_grad[3 * width + tile * LANES : 3 * width + (tile + 1) * LANES, :] = value

    def qkv_grad(part, group, value):
        weight_grad[pl.ds(pl.multiple_of(part * width + group * LANES, LANES), LANES), :] = value

    work = Backward(heads, head_size, refs[:16] + refs[18:], proj_grad, qkv_grad)
    step = pl.program_id(0)
    windows = work.windows
    busy = windows * work.groups
    group, window = step // windows, lax.rem(step, windows)

    @pl.when(step == 0)
    def _():
        work.begin()
        work.begin_grads()

    @pl.when(step < busy)
    def _():
        work.attend(group, window)

    @pl.when((step < busy) & (window == windows - 1))
    def _():
        work.group_grads(group)

    @pl.when(step == busy)
    def _():
        work.normed_back_step()
        work.finish()
        work.diagonals()
        refs[17][...] = work.small[...]


def backward_parts(probs, mixed, operands, head_count):
    count, width = operands[0].shape
    windows = count // WT
    head_size = width // head_count
    heads = LANES // head_size
    groups = width // LANES
    last = windows * groups - 1
    mask = jnp.asarray(stack_mask(heads, head_size))
    operands = operands[:8] + [mask] + operands[8:]

    def place(step):
        step = jnp.minimum(step, last)
        return step // windows, lax.rem(step, windows)

    def probs_map(step):
        group, window = place(step)
        return window * groups + group, 0, 0

    def mixed_map(part):
        def index(step):
            group, window = place(step)
            return window, part * groups + group

        return index

    in_specs = (
        [pl.BlockSpec((1, WT, heads * WT), probs_map)]
        + [pl.BlockSpec((WT, LANES), mixed_map(part)) for part in range(3)]
        + [whole(operand.shape) for operand in operands]
    )
    scratch = [
        pltpu.VMEM((count, width), low),
        pltpu.VMEM((count, 3 * width), low),
        pltpu.VMEM((groups, WT, heads * WT), f32),
        pltpu.VMEM((count, width), f32),
        pltpu.VMEM((SMALL_DIAG + head_count, width), f32),
    ]
    return (heads, head_size), [probs, mixed, mixed, mixed] + operands, in_specs, scratch, last + 1


def attention_backward(probs, mixed, operands, head_count):
    sizes, operands, in_specs, scratch, busy = backward_parts(probs, mixed, operands, head_count)
    count, width = operands[4].shape
    small_shape = (SMALL_DIAG + head_count, width)
    return pl.pallas_call(
        functools.partial(plain_backward_kernel, *sizes),
        grid=(busy + 1,),
        in_specs=in_specs,
        out_specs=[whole((count, width)), whole((4 * width, width)), whole(small_shape)],
        out_shape=[struct((count, width), low), struct((4 * width, width), low), struct(small_shape, f32)],
        scratch_shapes=scratch,
        compiler_params=pltpu.CompilerParams(vmem_limit_bytes=60 * MIB),
        name="attention_backward",
    )(*operands)


MESH = pl.DeviceIdType.MESH


class Peers:
    def __init__(self):
        self.z = lax.axis_index("rep")
        place = lax.axis_index("grp")
        self.c = lax.rem(place, 2)
        self.x = lax.rem(place // 2, 2)
        self.y = place // 4
        self.core_peer = (self.z, place + 1 - 2 * self.c)
        self.x_peer = (self.z, place + 2 - 4 * self.x)
        self.y_peer = (self.z, place + 4 - 8 * self.y)
        self.z_places = [lax.rem(self.z + step, 4) for step in range(1, 4)]
        self.z_peers = [(there, place) for there in self.z_places]

    def plane(self):
        return [self.core_peer, self.x_peer, self.y_peer]

    def everyone(self):
        return self.plane() + self.z_peers


def meet(peers):
    barrier = pltpu.get_barrier_semaphore()
    for peer in peers:
        pl.semaphore_signal(barrier, inc=1, device_id=peer, device_id_type=MESH)
    pl.semaphore_wait(barrier, len(peers))


class Copies:
    def __init__(self, send_sems, recv_sems):
        self.send_sems, self.recv_sems = send_sems, recv_sems
        self.made = []

    def make(self, ends, peer):
        copy = Copy(self, len(self.made), ends, peer)
        self.made.append(copy)
        copy.build().start()
        return copy

    def drain(self):
        for copy in self.made:
            copy.build().wait_send()


class Copy:
    def __init__(self, owner, number, ends, peer):
        self.owner, self.number, self.ends, self.peer = owner, number, ends, peer

    def build(self):
        source, target = self.ends()
        return pltpu.make_async_remote_copy(
            src_ref=source,
            dst_ref=target,
            send_sem=self.owner.send_sems.at[self.number],
            recv_sem=self.owner.recv_sems.at[self.number],
            device_id=self.peer,
            device_id_type=MESH,
        )

    def wait_recv(self):
        self.build().wait_recv()


def same(place):
    return lambda: (place(), place())


class Gather:
    def __init__(self, me, copies, source, out):
        self.me, self.copies, self.source, self.out = me, copies, source, out
        self.half = out.shape[3] // 2
        self.across = []

    def block(self, flip_y, flip_x):
        me = self.me
        return self.out.at[1 - me.y if flip_y else me.y, 1 - me.x if flip_x else me.x, me.c]

    def start(self):
        me = self.me

        def ends():
            return self.source(), self.block(False, False)

        self.by_x = self.copies.make(ends, me.x_peer)
        self.by_y = self.copies.make(ends, me.y_peer)
        self.across.append(self.copies.make(ends, me.core_peer))

    def relay(self):
        me = self.me
        self.by_x.wait_recv()
        to_y = self.copies.make(same(lambda: self.block(False, True).at[pl.ds(0, self.half)]), me.y_peer)
        self.by_y.wait_recv()
        to_x = self.copies.make(same(lambda: self.block(True, False).at[pl.ds(self.half, self.half)]), me.x_peer)
        self.relayed = (to_x, to_y)
        self.across.append(self.copies.make(same(lambda: self.block(False, True)), me.core_peer))
        self.across.append(self.copies.make(same(lambda: self.block(True, False)), me.core_peer))

    def cross(self):
        for copy in self.relayed:
            copy.wait_recv()
        self.across.append(self.copies.make(same(lambda: self.block(True, True)), self.me.core_peer))

    def wait(self):
        for copy in self.across:
            copy.wait_recv()


def gathered_forward_kernel(heads, head_size, *refs):
    qkv_shard, proj_shard, fc1_shard, fc2_shard = refs[:4]
    outs = refs[10:20]
    qkv_out, proj_out, fc1_out, fc2_out = outs[6:]
    scratch = refs[20:]
    work = Forward(heads, head_size, refs[4:10] + outs[:6] + scratch[:3])
    qkv_full, proj_full, fc1_low, fc2_low, send_sems, recv_sems, local_sems = scratch[3:]
    me = Peers()
    copies = Copies(send_sems, recv_sems)
    own = (me.y, me.x, me.c)
    qkv = Gather(me, copies, lambda: qkv_full.at[own], qkv_full)
    proj = Gather(me, copies, lambda: proj_full.at[own], proj_full)
    fc1 = Gather(me, copies, lambda: fc1_low, fc1_out)
    fc2 = Gather(me, copies, lambda: fc2_low, fc2_out)

    def local(index):
        source = (fc1_low, fc2_low, qkv_full, proj_full)[index]
        target = (fc1_out, fc2_out, qkv_out, proj_out)[index]
        return pltpu.make_async_copy(source, target.at[own] if index < 2 else target, local_sems.at[index])

    window = pl.program_id(0)
    first_window = (me.z * 8 + me.y * 4 + me.x * 2 + me.c) * pl.num_programs(0)

    def weight_tile(full):
        def tile(start):
            return full[:, :, :, :, start : start + LANES].reshape(-1, LANES)

        return tile

    @pl.when(window == 0)
    def _():
        qkv_full[own] = qkv_shard[...].astype(low)
        proj_full[own] = proj_shard[...].astype(low)
        meet(me.plane())
        qkv.start()
        proj.start()
        for tile in range(fc1_low.shape[0]):
            fc1_low[tile] = fc1_shard[:, tile * LANES : (tile + 1) * LANES].astype(low)
        fc2_low[...] = fc2_shard[...].astype(low)
        work.norm_one()
        relative_rows(heads, work.diag, work.rel)
        qkv.relay()
        proj.relay()
        fc1.start()
        fc2.start()
        local(0).start()
        local(1).start()
        qkv.cross()
        qkv.wait()
        local(2).start()
        work.mix(weight_tile(qkv_full))

    @pl.when(window == 1)
    def _():
        proj.cross()

    @pl.when(window == 3)
    def _():
        fc1.relay()

    @pl.when(window == 6)
    def _():
        fc1.cross()
        fc2.relay()

    work.attend(window, first_window)

    @pl.when(window == pl.num_programs(0) - 1)
    def _():
        proj.wait()
        local(3).start()
        work.finish(weight_tile(proj_full))
        fc2.cross()
        fc1.wait()
        fc2.wait()
        for index in range(4):
            local(index).wait()
        copies.drain()


def gathered_forward(fill, tokens, weights, vectors, diagonals, head_count, collective_id):
    sizes, operands, in_specs, out_specs, out_shape, scratch = forward_parts(
        fill, tokens, vectors, diagonals, head_count
    )
    shapes = [weight.shape for weight in weights]
    shapes[2] = (shapes[2][1] // LANES, shapes[2][0], LANES)
    fulls = [(2, 2, 2) + shape for shape in shapes]
    results = pl.pallas_call(
        functools.partial(gathered_forward_kernel, *sizes),
        grid=(fill.shape[0],),
        in_specs=[whole(weight.shape) for weight in weights] + in_specs,
        out_specs=out_specs + [HBM] * 4,
        out_shape=out_shape + [struct(full, low) for full in fulls],
        scratch_shapes=scratch
        + [pltpu.VMEM(fulls[0], low), pltpu.VMEM(fulls[1], low)]
        + [pltpu.VMEM(shape, low) for shape in shapes[2:]]
        + [pltpu.SemaphoreType.DMA((32,)), pltpu.SemaphoreType.DMA((32,)), pltpu.SemaphoreType.DMA((4,))],
        compiler_params=pltpu.CompilerParams(
            collective_id=collective_id, has_side_effects=True, vmem_limit_bytes=58 * MIB
        ),
        name="gathered_forward",
    )(*weights, *operands)
    qkv_full, proj_full, fc1_tiles, fc2_full = results[6:]
    return results[:6], [
        qkv_full.reshape(-1, shapes[0][1]), proj_full.reshape(-1, shapes[1][1]), fc1_tiles,
        fc2_full.reshape(-1, shapes[3][1]),
    ]


PIECE = 16


class Reduction:
    def __init__(self, me, copies, term, mine, out, buffers, load_sems, store_sems):
        self.me, self.copies, self.term, self.mine, self.out = me, copies, term, mine, out
        self.core_in, self.first_in, self.second_in, self.z_in, self.final = buffers
        self.load_sems, self.store_sems = load_sems, store_sems
        self.parts, self.half = buffers[0].shape[1], buffers[0].shape[-1] // 2
        self.kept = None
        self.core, self.first, self.second, self.over_z, self.last_z, self.spread, self.relayed, self.across = (
            {} for _ in range(8)
        )

    def sides(self):
        return pl.ds(0, self.half), pl.ds(self.half, self.half)

    def z_columns(self, z):
        return pl.ds(pl.multiple_of(lax.rem(z, 2) * self.half, self.half), self.half)

    def loop(self, amount, body):
        def step(index, carry):
            body(index)
            return carry

        lax.fori_loop(0, amount, step, 0)

    def load(self, k):
        ref, at = self.mine
        return pltpu.make_async_copy(self.term(k, self.me.c), ref.at[k], self.load_sems.at[k])

    def store(self, k):
        me = self.me
        return pltpu.make_async_copy(
            self.final.at[k], self.out(k, me.c, me.x, me.y, (me.z // 2, slice(None), self.z_columns(me.z))),
            self.store_sems.at[k],
        )

    def start(self, k):
        me = self.me
        self.core[k] = self.copies.make(lambda: (self.term(k, 1 - me.c), self.core_in.at[k]), me.core_peer)
        if self.load_sems is not None:
            self.load(k).start()

    def finish_core(self, k):
        me = self.me
        ref, at = self.mine
        if self.load_sems is not None:
            self.load(k).wait()
        self.core[k].wait_recv()

        def add(step):
            part, x, y, row = step // 8, lax.rem(step // 4, 2), lax.rem(step // 2, 2), lax.rem(step, 2)
            place = at(k, part, x, y, row)
            ref[place] = ref[place] + self.core_in[k, part, x, y, row]

        self.loop(8 * self.parts, add)
        every = slice(None)
        self.first[k] = (
            self.copies.make(
                lambda: (
                    ref.at[at(k, every, 1 - me.x, every, every) + (every, self.sides()[0])], self.first_in.at[k, 0],
                ),
                me.x_peer,
            ),
            self.copies.make(
                lambda: (
                    ref.at[at(k, every, every, 1 - me.y, every) + (every, self.sides()[1])], self.first_in.at[k, 1],
                ),
                me.y_peer,
            ),
        )

    def finish_first(self, k):
        me = self.me
        ref, at = self.mine
        for copy in self.first[k]:
            copy.wait_recv()
        half = self.half

        def add(step):
            part, other, row = step // 4, lax.rem(step // 2, 2), lax.rem(step, 2)
            place = at(k, part, me.x, other, row) + (slice(None), slice(0, half))
            ref[place] = ref[place] + self.first_in[k, 0, part, other, row]
            place = at(k, part, other, me.y, row) + (slice(None), slice(half, 2 * half))
            ref[place] = ref[place] + self.first_in[k, 1, part, other, row]

        self.loop(4 * self.parts, add)
        every = slice(None)
        self.second[k] = (
            self.copies.make(
                lambda: (
                    ref.at[at(k, every, me.x, 1 - me.y, every) + (every, self.sides()[0])], self.second_in.at[k, 0],
                ),
                me.y_peer,
            ),
            self.copies.make(
                lambda: (
                    ref.at[at(k, every, 1 - me.x, me.y, every) + (every, self.sides()[1])], self.second_in.at[k, 1],
                ),
                me.x_peer,
            ),
        )

    def add_second(self, k):
        me = self.me
        ref, at = self.mine
        for copy in self.second[k]:
            copy.wait_recv()
        half = self.half

        def add(step):
            part, row = step // 2, lax.rem(step, 2)
            for side, span in enumerate((slice(0, half), slice(half, 2 * half))):
                place = at(k, part, me.x, me.y, row) + (slice(None), span)
                ref[place] = ref[place] + self.second_in[k, side, part, row]

        self.loop(2 * self.parts, add)

    def store_piece(self, k, target):
        ref, at = self.mine
        every = slice(None)
        source = ref.at[at(k, every, self.me.x, self.me.y, every)]
        return pltpu.make_async_copy(source, target.at[k], self.store_sems.at[k])

    def keep_piece(self, k, source):
        return pltpu.make_async_copy(
            source.at[k, :, self.me.z // 2, :, self.z_columns(self.me.z)], self.z_in.at[k, self.me.z], self.load_sems.at[k]
        )

    def start_z(self, k, source):
        self.kept = source
        self.over_z[k] = [
            self.copies.make(
                lambda there=there: (
                    source.at[k, :, there // 2, :, self.z_columns(there)], self.z_in.at[k, self.me.z],
                ),
                peer,
            )
            for there, peer in zip(self.me.z_places, self.me.z_peers)
        ]
        self.keep_piece(k, source).start()

    def finish_second(self, k):
        me = self.me
        ref, at = self.mine
        self.add_second(k)

        def piece(part, z):
            return at(k, part, me.x, me.y, z // 2) + (slice(None), self.z_columns(z))

        self.over_z[k] = [
            self.copies.make(lambda there=there: (ref.at[piece(slice(None), there)], self.z_in.at[k, me.z]), peer)
            for there, peer in zip(me.z_places, me.z_peers)
        ]

        def keep(part):
            self.z_in[k, me.z, part] = ref[piece(part, me.z)]

        self.loop(self.parts, keep)

    def finish_z(self, k):
        me = self.me
        for copy in self.over_z[k]:
            copy.wait_recv()
        if self.kept is not None:
            self.keep_piece(k, self.kept).wait()

        def add(part):
            total = self.z_in[k, 0, part].astype(f32)
            for place in range(1, 4):
                total = total + self.z_in[k, place, part].astype(f32)
            self.final[k, part] = total.astype(low)

        self.loop(self.parts, add)
        self.last_z[k] = [
            self.copies.make(
                lambda: (
                    self.final.at[k],
                    self.out(k, me.c, me.x, me.y, (me.z // 2, slice(None), self.z_columns(me.z))),
                ),
                peer,
            )
            for peer in me.z_peers
        ]
        self.store(k).start()

    def finish_last_z(self, k):
        me = self.me
        for copy in self.last_z[k]:
            copy.wait_recv()
        self.store(k).wait()
        own = same(lambda: self.out(k, me.c, me.x, me.y, ()))
        self.spread[k] = [self.copies.make(own, peer) for peer in (me.x_peer, me.y_peer)]
        self.across[k] = [self.copies.make(own, me.core_peer)]

    def finish_spread(self, k):
        me = self.me
        by_x, by_y = self.spread[k]
        every = slice(None)
        by_y.wait_recv()
        to_x = self.copies.make(
            same(lambda: self.out(k, me.c, me.x, 1 - me.y, (every, every, self.sides()[0]))), me.x_peer
        )
        by_x.wait_recv()
        to_y = self.copies.make(
            same(lambda: self.out(k, me.c, 1 - me.x, me.y, (every, every, self.sides()[1]))), me.y_peer
        )
        self.relayed[k] = (to_x, to_y)
        self.across[k].append(self.copies.make(same(lambda: self.out(k, me.c, 1 - me.x, me.y, ())), me.core_peer))
        self.across[k].append(self.copies.make(same(lambda: self.out(k, me.c, me.x, 1 - me.y, ())), me.core_peer))

    def finish_relay(self, k):
        me = self.me
        for copy in self.relayed[k]:
            copy.wait_recv()
        self.across[k].append(self.copies.make(same(lambda: self.out(k, me.c, 1 - me.x, 1 - me.y, ())), me.core_peer))

    def wait(self, k):
        for copy in self.across[k]:
            copy.wait_recv()

    def stage(self, number, k):
        stages = (
            self.finish_core, self.finish_first, self.finish_second, self.finish_z, self.finish_last_z,
            self.finish_spread, self.finish_relay,
        )
        stages[number](k)


STAGES = 7


def reduction_buffers(amount, parts, width):
    half = width // 2
    return [
        pltpu.VMEM((amount, parts, 2, 2, 2, PIECE, width), low),
        pltpu.VMEM((amount, 2, parts, 2, 2, PIECE, half), low),
        pltpu.VMEM((amount, 2, parts, 2, PIECE, half), low),
        pltpu.VMEM((amount, 4, parts, PIECE, half), low),
        pltpu.VMEM((amount, parts, PIECE, half), low),
    ]


def reduced_feed_forward_kernel(*refs):
    later_fc1, later_fc2, piece_out = refs[12:15]
    term, core_in, first_in, second_in, send_sems, recv_sems, store_sems = refs[21:]
    work = FeedForward(refs[:12] + refs[15:21])
    me = Peers()
    copies = Copies(send_sems, recv_sems)
    early = term.shape[1]
    tile_shape = term.shape[2:]
    buffers = (core_in, first_in, second_in, None, None)
    first_half = Reduction(
        me, copies, lambda k, c: term.at[k, :, c], (term, lambda k, part, *place: (k, part, me.c) + place), None, buffers,
        None, store_sems,
    )
    step = pl.program_id(0)
    last = pl.num_programs(0) - 1

    @pl.when(step == 0)
    def _():
        work.begin()
        meet(me.plane())

    fc1_grad, fc2_grad = work.tile()

    @pl.when(step < early)
    def _():
        term[0, step] = fc1_grad.reshape(tile_shape)
        term[1, step] = fc2_grad.reshape(tile_shape)

    @pl.when(step >= early)
    def _():
        later_fc1[...] = fc1_grad
        later_fc2[...] = fc2_grad

    @pl.when(step == early - 1)
    def _():
        for k in range(2):
            first_half.start(k)

    @pl.when(step == early + 1)
    def _():
        for k in range(2):
            first_half.finish_core(k)

    @pl.when(step == last - 1)
    def _():
        for k in range(2):
            first_half.finish_first(k)

    @pl.when(step == last)
    def _():
        work.finish()
        for k in range(2):
            first_half.add_second(k)
            first_half.store_piece(k, piece_out).start()
        for k in range(2):
            first_half.store_piece(k, piece_out).wait()
        copies.drain()


def reduced_feed_forward(normed, cotangent, middle, fc1_tiles, fc2_full, vectors, collective_id):
    operands, in_specs, out_specs, out_shape, scratch, tiles = feed_forward_parts(
        normed, cotangent, middle, fc1_tiles, fc2_full, vectors
    )
    width = cotangent.shape[1]
    early = tiles // 2
    tile_shape = (2, 2, 2, 2, PIECE, width)
    later = pl.BlockSpec((LANES, width), lambda f: (jnp.maximum(f - early, 0), 0))
    return pl.pallas_call(
        reduced_feed_forward_kernel,
        grid=(tiles,),
        in_specs=in_specs,
        out_specs=out_specs + [later] * 2 + [HBM],
        out_shape=out_shape
        + [struct(((tiles - early) * LANES, width), low)] * 2
        + [struct((2, early, 2, PIECE, width), low)],
        scratch_shapes=scratch
        + [pltpu.VMEM((2, early) + tile_shape, low)]
        + reduction_buffers(2, early, width)[:3]
        + [pltpu.SemaphoreType.DMA((10,)), pltpu.SemaphoreType.DMA((10,)), pltpu.SemaphoreType.DMA((2,))],
        compiler_params=pltpu.CompilerParams(
            collective_id=collective_id, has_side_effects=True, vmem_limit_bytes=58 * MIB
        ),
        name="reduced_feed_forward",
    )(*operands)


class SmallSum:
    def __init__(self, me, copies, small, inbox):
        self.me, self.copies, self.small, self.inbox, self.made = me, copies, small, inbox, []

    def step(self, number):
        peers = self.me.plane()
        z = self.me.z
        if number > 0:
            self.made[number - 1].wait_recv()
            self.small[...] += self.inbox[number - 1]
        if number < 3:
            self.inbox[3 + number] = self.small[...]
            self.made.append(
                self.copies.make(lambda: (self.inbox.at[3 + number], self.inbox.at[number]), peers[number])
            )
        else:
            self.inbox[6 + z] = self.small[...]
            for peer in self.me.z_peers:
                self.made.append(self.copies.make(same(lambda: self.inbox.at[6 + z]), peer))

    def finish(self):
        for copy in self.made[3:]:
            copy.wait_recv()
        self.small[...] = (self.inbox[6] + self.inbox[7]) + (self.inbox[8] + self.inbox[9])


def reduced_backward_kernel(heads, head_size, *refs):
    fc1_term, fc2_term, piece = refs[15:18]
    input_grad, fc_out, qkv_out, proj_out, small_out = refs[18:23]
    att, fc_mine = refs[28:30]
    fc_buffers, att_buffers, early_buffers = refs[30:35], refs[35:40], refs[40:42]
    inbox, send_sems, recv_sems, load_sems, early_load_sems, fc_store_sems, early_store_sems, att_store_sems = refs[42:]
    groups = att.shape[0] - 1
    tile_shape = (2, 2, 2, 2, PIECE, att.shape[-1])

    def proj_grad(tile, value):
        att[groups, tile] = value.reshape(tile_shape)

    def qkv_grad(part, group, value):
        att[group, part] = value.reshape(tile_shape)

    work = Backward(heads, head_size, refs[:15] + (input_grad,) + refs[23:28], proj_grad, qkv_grad)
    me = Peers()
    copies = Copies(send_sems, recv_sems)

    def fc_place(half):
        return lambda k, c, x, y, rest: fc_out.at[(k, half, slice(None), c, x, y) + rest]

    def att_place(k, c, x, y, rest):
        if k == groups:
            return proj_out.at[(slice(None), c, x, y) + rest]
        return qkv_out.at[(slice(None), k, c, x, y) + rest]

    early = Reduction(
        me, copies, None, None, fc_place(0), (fc_buffers[0], None, None) + early_buffers, early_load_sems,
        early_store_sems,
    )
    fc = Reduction(
        me, copies, lambda k, c: (fc1_term, fc2_term)[k].at[:, c], (fc_mine, lambda *place: place), fc_place(1),
        fc_buffers, load_sems, fc_store_sems,
    )
    att_sum = Reduction(
        me, copies, lambda k, c: att.at[k, :, c], (att, lambda k, part, *place: (k, part, me.c) + place), att_place,
        att_buffers, None, att_store_sems,
    )
    small = SmallSum(me, copies, work.small, inbox)
    order = [(early, 0, -3), (early, 1, -3), (fc, 0, 0), (fc, 1, 1), (att_sum, groups, 2)]
    order += [(att_sum, k, 3 + k) for k in range(groups)]
    waves = 2 + groups + STAGES
    done = [0]

    def wave():
        number = done[0]
        done[0] += 1
        for which, k, first in reversed(order):
            if 0 <= number - first < STAGES:
                which.stage(number - first, k)

    step = pl.program_id(0)
    windows = work.windows
    busy = windows * groups
    group, window = step // windows, lax.rem(step, windows)

    @pl.when(step == 0)
    def _():
        meet(me.everyone())
        for k in range(2):
            early.start_z(k, piece)
            fc.start(k)
        work.begin_grads()
        att_sum.start(groups)
        work.begin()

    @pl.when(step < busy)
    def _():
        work.attend(group, window)

    for number in range(groups):

        @pl.when(step == (number + 1) * windows - 1)
        def _():
            work.group_grads(number)
            att_sum.start(number)

    for at in (2, 5, 8, 11, 15, 20):

        @pl.when(step == at)
        def _():
            wave()

    @pl.when(step == busy)
    def _():
        work.normed_back_step()
        wave()
        work.finish()
        wave()
        work.diagonals()
        small.step(0)
        for number in range(1, 5):
            wave()
            if number < 4:
                small.step(number)
            else:
                small.finish()
        small_out[...] = work.small[...]
        while done[0] < waves:
            wave()
        for which, k, _ in order:
            which.wait(k)
        copies.drain()


def reduced_backward(probs, mixed, operands, head_count, fc1_term, fc2_term, piece, collective_id):
    sizes, operands, in_specs, scratch, busy = backward_parts(probs, mixed, operands, head_count)
    count, width = operands[4].shape
    groups = width // LANES
    tile_shape = (2, 2, 2, 2, PIECE, width)
    parts = fc1_term.shape[0] // LANES
    small_shape = (SMALL_DIAG + head_count, width)
    copies = 14 * 2 + 19 * (2 + groups + 1) + 6
    buffers = reduction_buffers(2, parts, width)
    input_grad, fc_sum, qkv_sum, proj_sum, small = pl.pallas_call(
        functools.partial(reduced_backward_kernel, *sizes),
        grid=(busy + 1,),
        in_specs=in_specs + [HBM] * 3,
        out_specs=[whole((count, width))] + [HBM] * 3 + [whole(small_shape)],
        out_shape=[
            struct((count, width), low),
            struct((2, 2, parts) + tile_shape, low),
            struct((3, groups) + tile_shape, low),
            struct((groups,) + tile_shape, low),
            struct(small_shape, f32),
        ],
        scratch_shapes=scratch
        + [pltpu.VMEM((groups + 1, 3) + tile_shape, low), pltpu.VMEM((2, parts) + tile_shape[1:], low)]
        + buffers
        + reduction_buffers(groups + 1, 3, width)
        + buffers[3:]
        + [
            pltpu.VMEM((10,) + small_shape, f32),
            pltpu.SemaphoreType.DMA((copies,)),
            pltpu.SemaphoreType.DMA((copies,)),
        ]
        + [pltpu.SemaphoreType.DMA((2,))] * 4
        + [pltpu.SemaphoreType.DMA((groups + 1,))],
        compiler_params=pltpu.CompilerParams(
            collective_id=collective_id, has_side_effects=True, vmem_limit_bytes=62 * MIB
        ),
        name="reduced_backward",
    )(*operands, fc1_term.reshape((parts,) + tile_shape), fc2_term.reshape((parts,) + tile_shape), piece)
    sums = [part.reshape(-1, width) for part in (qkv_sum, proj_sum, fc_sum)]
    return input_grad, sums, small


def tile_update(tall, rows, big, root, pick, sum_ref, fresh):
    span = rows.shape[0]
    across = dot(jnp.concatenate([rows, pick], axis=0), tall, COLS_BY_COLS)
    columns = across[span:]
    term = dot(jnp.concatenate([root.astype(low), columns.astype(low)], axis=0), tall)

    @pl.when(fresh)
    def _():
        sum_ref[...] = term

    @pl.when(jnp.logical_not(fresh))
    def _():
        sum_ref[...] += term

    return 0.5 * big + 0.5 * across[:span], columns


def column_pick(member, shape):
    row, column = (lax.broadcasted_iota(jnp.int32, shape, axis) for axis in range(2))
    return jnp.where(column == row + member * shape[0], 1.0, 0.0).astype(low)


def hidden_kernel(
    member_ref, tall_ref, rows_ref, big_ref, root_ref, small_ref, small_root_ref, fc2_ref,
    big_out_ref, small_out_ref, fc1_grad_ref, fc1_step_ref, fc2_grad_ref, fc2_new_ref, fc2_copy_ref,
    sum_ref,
):
    matrix, tile = pl.program_id(0), pl.program_id(1)
    span = rows_ref.shape[0]
    pick = column_pick(member_ref[0], small_ref.shape[1:])
    big_new, columns = tile_update(
        tall_ref[...], rows_ref[...], big_ref[0], root_ref[0], pick, sum_ref, tile == 0
    )
    big_out_ref[0] = big_new

    @pl.when(matrix == 0)
    def _():
        fc1_grad_ref[...] = columns

    @pl.when(tile == pl.num_programs(1) - 1)
    def _():
        small_out_ref[0] = 0.5 * small_ref[0] + 0.5 * sum_ref[span:, :]
        product = sum_ref[:span, :].astype(low)

        @pl.when(matrix == 0)
        def _():
            fc1_step_ref[...] = dot(small_root_ref[0], product, COLS_BY_COLS).astype(low)

        @pl.when(matrix == 1)
        def _():
            new = fc2_ref[...] - dot(product, small_root_ref[0])
            fc2_new_ref[...] = new
            fc2_copy_ref[...] = new.astype(low)
            fc2_grad_ref[...] = rows_ref[...].astype(f32)


def hidden_update(member, fc_sum, stats_hidden, roots_hidden, stats_model, small_roots, fc2_weight):
    width = fc_sum.shape[1]
    _, span, hidden_width = stats_hidden.shape
    model_rows = stats_model.shape[1]
    tiles = hidden_width // width
    last = tiles - 1
    return pl.pallas_call(
        hidden_kernel,
        grid_spec=pltpu.PrefetchScalarGridSpec(
            num_scalar_prefetch=1,
            grid=(2, tiles),
            in_specs=[
                pl.BlockSpec((width, width), lambda i, j, m: (i * tiles + j, 0)),
                pl.BlockSpec((span, width), lambda i, j, m: (i * (hidden_width // span) + m[0], 0)),
                pl.BlockSpec((1, span, width), lambda i, j, m: (i, 0, j)),
                pl.BlockSpec((1, span, width), lambda i, j, m: (i, 0, j)),
                pl.BlockSpec((1, model_rows, width), lambda i, j, m: (3 + i, 0, 0)),
                pl.BlockSpec((1, width, width), lambda i, j, m: (2 + i, 0, 0)),
                pl.BlockSpec((span, width), lambda i, j, m: (0, 0)),
            ],
            out_specs=[
                pl.BlockSpec((1, span, width), lambda i, j, m: (i, 0, j)),
                pl.BlockSpec((1, model_rows, width), lambda i, j, m: (i, 0, 0)),
                pl.BlockSpec((model_rows, width), lambda i, j, m: (0, jnp.where(i == 0, j, last))),
                pl.BlockSpec((width, span), lambda i, j, m: (0, 0)),
                pl.BlockSpec((span, width), lambda i, j, m: (0, 0)),
                pl.BlockSpec((span, width), lambda i, j, m: (0, 0)),
                pl.BlockSpec((span, width), lambda i, j, m: (0, 0)),
            ],
            scratch_shapes=[pltpu.VMEM((span + model_rows, width), f32)],
        ),
        out_shape=[
            struct(stats_hidden.shape, f32),
            struct((2, model_rows, width), f32),
            struct((model_rows, hidden_width), f32),
            struct((width, span), low),
            struct((span, width), f32),
            struct((span, width), f32),
            struct((span, width), low),
        ],
        compiler_params=pltpu.CompilerParams(vmem_limit_bytes=48 * MIB),
        name="hidden_update",
    )(member, fc_sum, fc_sum, stats_hidden, roots_hidden, stats_model, small_roots, fc2_weight)


def exchange_places(me):
    member = me.y * 4 + me.x * 2 + me.c
    return member, [lax.rem(member + step, 8) for step in range(1, 8)]


class Exchange:
    def __init__(self, me, copies, blocks, inbox):
        self.me, self.copies, self.blocks, self.inbox = me, copies, blocks, inbox

    def start(self):
        member, others = exchange_places(self.me)
        self.made = [
            self.copies.make(lambda there=there: (self.blocks.at[there], self.inbox.at[member]), (self.me.z, there))
            for there in others
        ]

    def wait(self):
        for copy in self.made:
            copy.wait_recv()


def exchange_kernel(amount, *refs):
    blocks, inboxes = refs[:amount], refs[amount : 2 * amount]
    send_sems, recv_sems, local_sems = refs[2 * amount :]
    me = Peers()
    copies = Copies(send_sems, recv_sems)
    member, others = exchange_places(me)
    meet([(me.z, there) for there in others])
    exchanges = [Exchange(me, copies, source, inbox) for source, inbox in zip(blocks, inboxes)]
    own = [
        pltpu.make_async_copy(source.at[member], inbox.at[member], local_sems.at[index])
        for index, (source, inbox) in enumerate(zip(blocks, inboxes))
    ]
    for copy in own:
        copy.start()
    for exchange in exchanges:
        exchange.start()
    for exchange in exchanges:
        exchange.wait()
    for copy in own:
        copy.wait()
    copies.drain()


def exchange_rows(steps, collective_id):
    amount = len(steps)
    blocks = [step.reshape(8, step.shape[0] // 8, step.shape[1]) for step in steps]
    vmem = pl.BlockSpec(memory_space=pltpu.VMEM)
    return pl.pallas_call(
        functools.partial(exchange_kernel, amount),
        in_specs=[vmem] * amount,
        out_specs=[vmem] * amount,
        out_shape=[struct(block.shape, low) for block in blocks],
        scratch_shapes=[
            pltpu.SemaphoreType.DMA((7 * amount,)),
            pltpu.SemaphoreType.DMA((7 * amount,)),
            pltpu.SemaphoreType.DMA((amount,)),
        ],
        compiler_params=pltpu.CompilerParams(collective_id=collective_id, has_side_effects=True),
        name="exchange_rows",
    )(*blocks)


def apply_kernel(amount, *refs):
    for index in range(amount):
        old, blocks, new_ref, copy_ref = (refs[index + part * amount] for part in range(4))
        step = jnp.concatenate([blocks[place] for place in range(blocks.shape[0])], axis=1)
        new = old[...] - step.astype(f32)
        new_ref[...] = new
        copy_ref[...] = new.astype(low)


def apply_steps(weights, inboxes):
    return pl.pallas_call(
        functools.partial(apply_kernel, len(weights)),
        out_shape=[struct(weight.shape, dtype) for dtype in (f32, low) for weight in weights],
        compiler_params=pltpu.CompilerParams(vmem_limit_bytes=32 * MIB),
        name="apply_steps",
    )(*weights, *inboxes)


def model_kernel(
    member_ref, tall_ref, qkv_rows_ref, proj_tall_ref, proj_rows_ref, big_ref, root_ref, stats_ref, hidden_small_ref, proj_root_ref,
    small_root_ref, proj_ref,
    big_out_ref, stats_out_ref, qkv_grad_ref, qkv_step_ref, proj_grad_ref, proj_new_ref, proj_copy_ref,
    sum_ref, proj_sum_ref,
):
    tile = pl.program_id(0)
    span = qkv_rows_ref.shape[0]
    model_rows = proj_rows_ref.shape[0]
    last = pl.num_programs(0) - 1
    pick = column_pick(member_ref[0], proj_rows_ref.shape)

    @pl.when(tile < last)
    def _():
        big_new, columns = tile_update(
            tall_ref[...], qkv_rows_ref[...], big_ref[...], root_ref[...], pick, sum_ref, tile == 0
        )
        big_out_ref[...] = big_new
        qkv_grad_ref[...] = columns

    @pl.when(tile == last)
    def _():
        qkv_step_ref[...] = dot(small_root_ref[0], sum_ref[:span, :].astype(low), COLS_BY_COLS).astype(low)
        stats_out_ref[0] = 0.5 * stats_ref[0] + 0.5 * sum_ref[span:, :]
        rows = proj_rows_ref[...]
        proj_left, _ = tile_update(
            proj_tall_ref[...], rows, stats_ref[1], proj_root_ref[0], pick, proj_sum_ref, tile == last
        )
        stats_out_ref[1] = proj_left
        stats_out_ref[2] = 0.5 * stats_ref[2] + 0.5 * proj_sum_ref[model_rows:, :]
        stats_out_ref[3] = hidden_small_ref[0]
        stats_out_ref[4] = hidden_small_ref[1]
        new = proj_ref[...] - dot(proj_sum_ref[:model_rows, :].astype(low), small_root_ref[1])
        proj_new_ref[...] = new
        proj_copy_ref[...] = new.astype(low)
        proj_grad_ref[...] = rows.astype(f32)


def model_update(
    member, qkv_sum, proj_sum, stats_qkv, roots_qkv, stats_model, hidden_small, roots_model, small_roots, proj_weight
):
    width = qkv_sum.shape[1]
    span, qkv_width = stats_qkv.shape
    model_rows = stats_model.shape[1]
    tiles = qkv_width // width

    def fixed(shape):
        return pl.BlockSpec(shape, lambda j, m: (0,) * len(shape))

    clamped = pl.BlockSpec((span, width), lambda j, m: (0, jnp.minimum(j, tiles - 1)))
    return pl.pallas_call(
        model_kernel,
        grid_spec=pltpu.PrefetchScalarGridSpec(
            num_scalar_prefetch=1,
            grid=(tiles + 1,),
            in_specs=[
                pl.BlockSpec((width, width), lambda j, m: (jnp.minimum(j, tiles - 1), 0)),
                pl.BlockSpec((span, width), lambda j, m: (m[0], 0)),
                fixed((width, width)),
                pl.BlockSpec((model_rows, width), lambda j, m: (m[0], 0)),
                clamped,
                clamped,
                fixed(stats_model.shape),
                fixed(hidden_small.shape),
                pl.BlockSpec((1, model_rows, width), lambda j, m: (1, 0, 0)),
                pl.BlockSpec((2, width, width), lambda j, m: (0, 0, 0)),
                fixed(proj_weight.shape),
            ],
            out_specs=[
                clamped,
                fixed(stats_model.shape),
                pl.BlockSpec((model_rows, width), lambda j, m: (0, jnp.minimum(j, tiles - 1))),
                fixed((width, span)),
                fixed((model_rows, width)),
                fixed((model_rows, width)),
                fixed((model_rows, width)),
            ],
            scratch_shapes=[
                pltpu.VMEM((span + model_rows, width), f32),
                pltpu.VMEM((2 * model_rows, width), f32),
            ],
        ),
        out_shape=[
            struct(stats_qkv.shape, f32),
            struct(stats_model.shape, f32),
            struct((model_rows, qkv_width), f32),
            struct((width, span), low),
            struct((model_rows, width), f32),
            struct((model_rows, width), f32),
            struct((model_rows, width), low),
        ],
        compiler_params=pltpu.CompilerParams(vmem_limit_bytes=48 * MIB),
        name="model_update",
    )(
        member, qkv_sum, qkv_sum, proj_sum, proj_sum, stats_qkv, roots_qkv, stats_model, hidden_small, roots_model,
        small_roots, proj_weight,
    )


def plain_update(
    sums, stats_model, stats_qkv, stats_hidden, roots_model, roots_qkv, roots_hidden, small_roots, weights
):
    width = sums[0].shape[1]
    member = lax.axis_index("grp")
    model_rows = stats_model.shape[1]
    picked = member * model_rows + jnp.arange(model_rows, dtype=jnp.int32)
    pick = (picked[:, None] == jnp.arange(width, dtype=jnp.int32)[None, :]).astype(low)

    def statistic_update(tall, small_rows, big_rows):
        columns = dot(pick, tall, COLS_BY_COLS)
        small_new = 0.5 * small_rows + 0.5 * dot(columns.astype(low), tall)
        rows = lax.dynamic_slice_in_dim(tall, member * big_rows.shape[0], big_rows.shape[0], 0)
        big_new = 0.5 * big_rows + 0.5 * dot(rows, tall, COLS_BY_COLS)
        return small_new, big_new, columns, rows.astype(f32)

    def product_of(big_root_rows, tall):
        return dot(big_root_rows.astype(low), tall).astype(low)

    qkv, proj, fc1, fc2 = sums
    qkv_left, qkv_right, qkv_gradient, _ = statistic_update(qkv, stats_model[0], stats_qkv)
    proj_right, proj_left, _, proj_gradient = statistic_update(proj, stats_model[2], stats_model[1])
    fc1_left, fc1_right, fc1_gradient, _ = statistic_update(fc1, stats_model[3], stats_hidden[0])
    fc2_right, fc2_left, _, fc2_gradient = statistic_update(fc2, stats_model[4], stats_hidden[1])
    qkv_step = dot(small_roots[0], product_of(roots_qkv, qkv), COLS_BY_COLS).astype(low)
    fc1_step = dot(small_roots[2], product_of(roots_hidden[0], fc1), COLS_BY_COLS).astype(low)
    qkv_weight, proj_weight, fc1_weight, fc2_weight = weights
    qkv_new = qkv_weight - lax.all_to_all(qkv_step, "grp", 0, 1, tiled=True).astype(f32)
    fc1_new = fc1_weight - lax.all_to_all(fc1_step, "grp", 0, 1, tiled=True).astype(f32)
    proj_new = proj_weight - dot(product_of(roots_model[1], proj), small_roots[1])
    fc2_new = fc2_weight - dot(product_of(roots_hidden[1], fc2), small_roots[3])
    new_stats_model = jnp.stack([qkv_left, proj_left, proj_right, fc1_left, fc2_right])
    return (
        (new_stats_model, qkv_right, jnp.stack([fc1_right, fc2_left])),
        (qkv_gradient, proj_gradient, fc1_gradient, fc2_gradient),
        (qkv_new, proj_new, fc1_new, fc2_new),
    )


def shards(
    plain, tokens, cotangent, window_fill, qkv_weight, proj_weight, fc1_weight, fc2_weight, vectors, vector_moments,
    bias_table, table_moments, stats_model, stats_qkv, stats_hidden, roots_model, roots_qkv, roots_hidden,
):
    width = vectors.shape[1]
    head_count = bias_table.shape[1]
    gather = functools.partial(lax.all_gather, axis_name="grp", tiled=True)
    weights = (qkv_weight, proj_weight, fc1_weight, fc2_weight)
    hot = jnp.asarray(diagonal_tables())
    diagonals = lax.dot_general(bias_table, hot, (((0,), (1,)), ((), ())), precision=lax.Precision.HIGHEST)
    if plain:
        fulls = [gather(weight.astype(low)) for weight in weights]
        base = (lax.axis_index(("rep", "grp")) * window_fill.shape[0]).astype(jnp.int32).reshape(1)
        forward = attention_forward(window_fill, base, tokens, *fulls[:2], vectors, diagonals, head_count)
    else:
        forward, fulls = gathered_forward(window_fill, tokens, weights, vectors, diagonals, head_count, 0)
    probs, mixed, normed, context, middle, normed_two = forward
    qkv_full, proj_full, fc1_full, fc2_full = fulls
    if plain:
        fc1_full = jnp.swapaxes(fc1_full.reshape(width, -1, LANES), 0, 1)[None, None, None]
    roots_low = jnp.stack([roots_model[i] for i in (0, 2, 3, 4)]).astype(low)
    roots_low, normed_two = lax.optimization_barrier((roots_low, normed_two))
    small_roots = gather(roots_low, axis=1)
    ffn_operands = (normed_two, cotangent, middle, fc1_full, fc2_full, vectors)
    ffn = feed_forward(*ffn_operands) if plain else reduced_feed_forward(*ffn_operands, 3)
    layer_output, middle_back, branch_back, fc1_bias_grad, ffn_vec, fc1_term, fc2_term = ffn[:7]
    small_roots, branch_back = lax.optimization_barrier((small_roots, branch_back))
    operands = [branch_back, middle_back, proj_full, context, normed, tokens, qkv_full, vectors, ffn_vec, fc1_bias_grad]
    if plain:
        input_gradient, att_term, small = attention_backward(probs, mixed, operands, head_count)
        small = lax.psum(small, ("rep", "grp"))
        terms = (att_term[: 3 * width], att_term[3 * width :], fc1_term, fc2_term)
        sums = [
            gather(lax.psum(lax.psum_scatter(term, "grp", scatter_dimension=0, tiled=True), "rep")) for term in terms
        ]
    else:
        input_gradient, sums, small = reduced_backward(probs, mixed, operands, head_count, *ffn[5:], 1)
    vector_total = small[: vectors.shape[0]]
    table_total = lax.dot_general(
        hot, small[SMALL_DIAG:], (((0,), (1,)), ((), ())), precision=lax.Precision.HIGHEST
    )
    if plain:
        statistics, gradients, masters = plain_update(
            sums, stats_model, stats_qkv, stats_hidden, roots_model, roots_qkv, roots_hidden, small_roots, weights
        )
        copies = tuple(master.astype(low) for master in masters)
    else:
        member = lax.axis_index("grp").astype(jnp.int32).reshape(1)
        new_stats_hidden, hidden_small, fc1_gradient, fc1_step, fc2_gradient, fc2_new, fc2_copy = hidden_update(
            member, sums[2], stats_hidden, roots_hidden, stats_model, small_roots, fc2_weight
        )
        qkv_right, new_stats_model, qkv_gradient, qkv_step, proj_gradient, proj_new, proj_copy = model_update(
            member, *sums[:2], stats_qkv, roots_qkv, stats_model, hidden_small, roots_model, small_roots, proj_weight
        )
        inboxes = exchange_rows((qkv_step, fc1_step), 2)
        qkv_new, fc1_new, qkv_copy, fc1_copy = apply_steps((qkv_weight, fc1_weight), inboxes)
        statistics = (new_stats_model, qkv_right, new_stats_hidden)
        gradients = (qkv_gradient, proj_gradient, fc1_gradient, fc2_gradient)
        masters = (qkv_new, proj_new, fc1_new, fc2_new)
        copies = (qkv_copy, proj_copy, fc1_copy, fc2_copy)
    total_tokens = tokens.shape[0] * lax.axis_size("rep") * lax.axis_size("grp")
    rate_base = total_tokens ** (-0.5)
    new_vector_moments = 0.9 * vector_moments + 0.1 * vector_total
    new_vectors = vectors - 2.0 * rate_base * new_vector_moments
    new_table_moments = 0.9 * table_moments + 0.1 * table_total
    new_table = bias_table - 8.0 * rate_base * new_table_moments
    return (
        (layer_output, input_gradient)
        + gradients
        + masters
        + copies
        + statistics
        + (new_vectors, new_vector_moments, new_table, new_table_moments)
    )


def solution(mesh):
    tokens, rows, blocks, copied = P(("rep", "grp"), None), P("grp", None), P(None, "grp", None), P()
    plain = (mesh.shape["rep"], mesh.shape["grp"]) != (4, 8)
    return jax.shard_map(
        functools.partial(shards, plain),
        mesh=mesh,
        in_specs=(tokens, tokens, P(("rep", "grp")))
        + (rows,) * 4
        + (copied,) * 4
        + (blocks, rows, blocks) * 2,
        out_specs=(tokens,) * 2 + (rows,) * 12 + (blocks, rows, blocks) + (copied,) * 4,
        check_vma=False,
    )
```

```python
import functools

import jax
import jax.numpy as jnp
import numpy as np
from jax import lax
from jax.experimental import pallas as pl
from jax.experimental.pallas import tpu as pltpu
from jax.sharding import PartitionSpec as P

WT = 144
SIDE = 12
SPAN = 2 * SIDE - 1
LANES = 256
DIAG = 384
ROW_TILE = 144
MIB = 1024 * 1024
low = jnp.bfloat16
f32 = jnp.float32

ROWS_BY_COLS = (((1,), (0,)), ((), ()))
COLS_BY_COLS = (((1,), (1,)), ((), ()))
ROWS_BY_ROWS = (((0,), (0,)), ((), ()))


def dot(left_matrix, right_matrix, dims=ROWS_BY_COLS):
    return lax.dot_general(left_matrix, right_matrix, dims, preferred_element_type=f32)


def standardize(values):
    centred = values - jnp.mean(values, axis=-1, keepdims=True)
    inverse = lax.rsqrt(jnp.mean(centred * centred, axis=-1, keepdims=True) + 1e-05)
    return centred * inverse, inverse


def norm_back(grad, gain, xhat, inverse):
    scaled = grad * gain
    mean_scaled = jnp.mean(scaled, axis=-1, keepdims=True)
    mean_product = jnp.mean(scaled * xhat, axis=-1, keepdims=True)
    return inverse * (scaled - mean_scaled - xhat * mean_product)


def column_sum(values):
    return jnp.sum(values, axis=0, keepdims=True)


def diagonal_tables():
    pair = np.arange(DIAG) - WT
    quotient, rest = pair // SIDE, pair % SIDE
    near = (quotient + SIDE - 1) * SPAN + rest + SIDE - 1
    far = (quotient + SIDE) * SPAN + rest - 1
    near_live = (np.abs(pair) < WT) & (quotient >= 1 - SIDE)
    far_live = (np.abs(pair) < WT) & (rest >= 1) & (quotient < SIDE - 1)
    hot = np.zeros((2, DIAG, SPAN * SPAN), np.float32)
    hot[0, np.arange(DIAG)[near_live], near[near_live]] = 1.0
    hot[1, np.arange(DIAG)[far_live], far[far_live]] = 1.0
    return hot.reshape(2 * DIAG, SPAN * SPAN)


def near_mask(shape, mirrored=False):
    column = lax.rem(lax.broadcasted_iota(jnp.int32, shape, 0), SIDE)
    if mirrored:
        column = SIDE - 1 - column
    rest = lax.rem(lax.broadcasted_iota(jnp.int32, shape, 1), SIDE)
    return column + rest < SIDE


def additive_types(heads):
    slot = np.arange(WT)
    row_high, col_high = slot // SIDE >= SIDE // 2, slot % SIDE >= SIDE // 2
    row_differs = row_high[:, None] != row_high[None, :]
    col_differs = col_high[:, None] != col_high[None, :]
    types = [
        np.where((row_differs & bool(kind // 2)) | (col_differs & bool(kind % 2)), -100.0, 0.0)
        for kind in range(4)
    ]
    return np.tile(np.stack(types), (1, 1, heads)).astype(np.float32)


def stack_mask(heads, head_size):
    lane_head = np.arange(heads * head_size) // head_size
    hot = lane_head[None, None, :] == np.arange(heads)[:, None, None]
    return np.broadcast_to(hot, (heads, WT, heads * head_size)).reshape(heads * WT, -1).astype(low)


def relative_rows(heads, diag_ref, rel_ref):
    mask = near_mask((WT, DIAG))
    for head in range(heads * rel_ref.shape[0]):
        group, place = head // heads, head % heads
        near = diag_ref[head : head + 1, :DIAG]
        far = diag_ref[head : head + 1, DIAG:]
        rolled = pltpu.roll(jnp.where(mask, near, far), DIAG - WT, 1, stride=1, stride_axis=0)
        rel_ref[group, :, place * WT : (place + 1) * WT] = rolled[:, :WT]


def stacked(block, mask_ref, heads):
    return jnp.concatenate([block] * heads, axis=0) * mask_ref[...]


def diagonal_blocks(full, heads, head_size):
    lane_head = lax.broadcasted_iota(jnp.int32, (WT, full.shape[1]), 1) // head_size
    picked = jnp.zeros((WT, full.shape[1]), f32)
    for head in range(heads):
        picked = jnp.where(lane_head == head, full[head * WT : (head + 1) * WT], picked)
    return picked


def for_row_tiles(count, body):
    def step(index, carry):
        body(pl.ds(pl.multiple_of(index * ROW_TILE, ROW_TILE), ROW_TILE))
        return carry

    lax.fori_loop(0, count // ROW_TILE, step, 0)


class Forward:
    def __init__(self, heads, head_size, refs):
        self.heads, self.head_size = heads, head_size
        self.fill, self.tokens, self.vec, self.diag, self.add, self.mask = refs[:6]
        self.probs, self.mixed_out, self.normed, self.context, self.middle, self.normed_two = refs[6:12]
        self.mixed, self.added, self.rel = refs[12:15]
        self.count, self.width = self.tokens.shape
        self.groups = self.width // LANES

    def norm_one(self):
        def body(rows):
            xhat, _ = standardize(self.tokens[rows, :].astype(f32))
            self.normed[rows, :] = (xhat * self.vec[0:1, :] + self.vec[1:2, :]).astype(low)

        for_row_tiles(self.count, body)

    def mix(self, weight_tile):
        for part in range(3):
            for tile in range(self.groups):
                start = part * self.width + tile * LANES
                sums = dot(self.normed[...], weight_tile(start))
                if part != 1:
                    row = 2 if part == 0 else 3
                    sums = sums + self.vec[row : row + 1, tile * LANES : (tile + 1) * LANES]
                self.mixed[:, start : start + LANES] = sums.astype(low)

    def attend(self, window, first_window):
        width, heads = self.width, self.heads
        rows = pl.ds(pl.multiple_of(window * WT, WT), WT)
        self.mixed_out[...] = self.mixed[rows, :]
        kind = lax.rem(first_window + window, 4)
        slot = lax.broadcasted_iota(jnp.int32, self.added.shape, 0)
        self.added[...] = jnp.where(slot < self.fill[window], self.add[kind], -1e30)
        for group in range(self.groups):
            query, key, value = (
                self.mixed[rows, part * width + group * LANES : part * width + (group + 1) * LANES]
                for part in range(3)
            )
            scores = dot(key, stacked(query, self.mask, heads), COLS_BY_COLS) * self.head_size ** (-0.5)
            scores = scores + self.rel[group] + self.added[...]
            exponent = jnp.exp(scores - jnp.max(scores, axis=0, keepdims=True))
            probs = (exponent * (1.0 / jnp.sum(exponent, axis=0, keepdims=True))).astype(low)
            self.probs[group] = probs
            full = dot(probs, value, ROWS_BY_ROWS)
            self.context[rows, group * LANES : (group + 1) * LANES] = diagonal_blocks(
                full, heads, self.head_size
            ).astype(low)

    def finish(self, weight_tile):
        for tile in range(self.groups):
            span = slice(tile * LANES, (tile + 1) * LANES)
            self.middle[:, span] = (
                self.tokens[:, span].astype(f32) + dot(self.context[...], weight_tile(tile * LANES)) + self.vec[4:5, span]
            )

        def body(rows):
            xhat, _ = standardize(self.middle[rows, :])
            self.normed_two[rows, :] = (xhat * self.vec[5:6, :] + self.vec[6:7, :]).astype(low)

        for_row_tiles(self.count, body)


def plain_forward_kernel(heads, head_size, base_ref, qkv_ref, proj_ref, *refs):
    work = Forward(heads, head_size, refs)
    window = pl.program_id(0)

    @pl.when(window == 0)
    def _():
        relative_rows(heads, work.diag, work.rel)
        work.norm_one()
        work.mix(lambda start: qkv_ref[:, start : start + LANES])

    work.attend(window, base_ref[0])

    @pl.when(window == pl.num_programs(0) - 1)
    def _():
        work.finish(lambda start: proj_ref[:, start : start + LANES])


def whole(shape):
    return pl.BlockSpec(shape, lambda *_: (0,) * len(shape), pipeline_mode=pl.Buffered(1))


def struct(shape, dtype):
    return jax.ShapeDtypeStruct(shape, dtype)


HBM = pl.BlockSpec(memory_space=pl.ANY)
SMEM = pl.BlockSpec(memory_space=pltpu.SMEM)


def forward_parts(fill, tokens, vectors, diagonals, head_count):
    count, width = tokens.shape
    windows = fill.shape[0]
    head_size = width // head_count
    heads = LANES // head_size
    groups = width // LANES
    operands = [tokens, vectors, diagonals, jnp.asarray(additive_types(heads)), jnp.asarray(stack_mask(heads, head_size))]
    in_specs = [SMEM] + [whole(operand.shape) for operand in operands]
    out_specs = [
        pl.BlockSpec((groups, WT, heads * WT), lambda w: (w, 0, 0)),
        pl.BlockSpec((WT, 3 * width), lambda w: (w, 0)),
    ] + [whole((count, width))] * 4
    out_shape = [
        struct((windows * groups, WT, heads * WT), low),
        struct((count, 3 * width), low),
        struct((count, width), low),
        struct((count, width), low),
        struct((count, width), f32),
        struct((count, width), low),
    ]
    scratch = [
        pltpu.VMEM((count, 3 * width), low),
        pltpu.VMEM((WT, heads * WT), f32),
        pltpu.VMEM((groups, WT, heads * WT), f32),
    ]
    return (heads, head_size), [fill] + operands, in_specs, out_specs, out_shape, scratch


def attention_forward(fill, base, tokens, qkv_full, proj_full, vectors, diagonals, head_count):
    sizes, operands, in_specs, out_specs, out_shape, scratch = forward_parts(
        fill, tokens, vectors, diagonals, head_count
    )
    return pl.pallas_call(
        functools.partial(plain_forward_kernel, *sizes),
        grid=(fill.shape[0],),
        in_specs=[SMEM, whole(qkv_full.shape), whole(proj_full.shape)] + in_specs,
        out_specs=out_specs,
        out_shape=out_shape,
        scratch_shapes=scratch,
        compiler_params=pltpu.CompilerParams(vmem_limit_bytes=56 * MIB),
        name="attention_forward",
    )(base, qkv_full, proj_full, *operands)


FFN_TILE = 512
FFN_ROWS = 336
FFN_CHUNK = 16


class FeedForward:
    def __init__(self, refs):
        self.normed, self.cot, self.middle, self.fc1, self.fc2, self.bias, self.vec = refs[:7]
        self.out, self.middle_back, self.branch_back, self.bias_grad, self.vec_grad = refs[7:12]
        self.out_sum, self.back_sum, self.hidden, self.active_back, self.active, self.hidden_back = refs[12:18]
        self.count, self.width = self.cot.shape

    def begin(self):
        self.out_sum[...] = jnp.zeros_like(self.out_sum)
        self.back_sum[...] = jnp.zeros_like(self.back_sum)

    def tile(self):
        fc1 = self.fc1[...].reshape(self.width, FFN_TILE)
        fc2 = self.fc2[...]
        spans = [slice(start, start + FFN_ROWS) for start in range(0, self.count, FFN_ROWS)]

        def enter(rows):
            self.hidden[rows, :] = dot(self.normed[rows, :], fc1)
            self.active_back[rows, :] = dot(self.cot[rows, :], fc2, COLS_BY_COLS)

        def bend(rows):
            total = jnp.zeros((8, FFN_TILE), f32)
            for start in range(rows.start, rows.stop, FFN_CHUNK):
                chunk = slice(start, start + FFN_CHUNK)
                hidden = self.hidden[chunk, :] + self.bias[...]
                bell = jnp.exp(hidden * hidden * -0.5)
                below = 0.5 + 0.5 * lax.erf(hidden * (0.5**0.5))
                self.active[chunk, :] = (hidden * below).astype(low)
                slope = below + hidden * bell * ((2.0 * np.pi) ** -0.5)
                back = (self.active_back[chunk, :] * slope).astype(low)
                self.hidden_back[chunk, :] = back
                total = total + jnp.sum(back.astype(f32).reshape(-1, 8, FFN_TILE), axis=0)
            return total

        def leave(rows):
            self.out_sum[rows, :] += dot(self.active[rows, :], fc2)
            self.back_sum[rows, :] += dot(self.hidden_back[rows, :], fc1, COLS_BY_COLS)

        total = jnp.zeros((8, FFN_TILE), f32)
        amount = len(spans)
        for index in range(amount + 2):
            if index < amount:
                enter(spans[index])
            if 0 <= index - 1 < amount:
                total = total + bend(spans[index - 1])
            if 0 <= index - 2 < amount:
                leave(spans[index - 2])
        self.bias_grad[...] = column_sum(total)
        fc1_grad = dot(self.hidden_back[...], self.normed[...], ROWS_BY_ROWS).astype(low)
        fc2_grad = dot(self.active[...], self.cot[...], ROWS_BY_ROWS).astype(low)
        return fc1_grad, fc2_grad

    def finish(self):
        self.vec_grad[...] = jnp.zeros_like(self.vec_grad)

        def body(rows):
            middle = self.middle[rows, :]
            cot = self.cot[rows, :].astype(f32)
            self.out[rows, :] = (middle + self.out_sum[rows, :] + self.vec[7:8, :]).astype(low)
            xhat, inverse = standardize(middle)
            grad = self.back_sum[rows, :]
            middle_back = cot + norm_back(grad, self.vec[5:6, :], xhat, inverse)
            self.middle_back[rows, :] = middle_back
            branch_back = middle_back.astype(low)
            self.branch_back[rows, :] = branch_back
            self.vec_grad[0:1, :] += column_sum(branch_back.astype(f32))
            self.vec_grad[1:2, :] += column_sum(grad * xhat)
            self.vec_grad[2:3, :] += column_sum(grad)
            self.vec_grad[3:4, :] += column_sum(cot)

        for_row_tiles(self.count, body)


def plain_feed_forward_kernel(*refs):
    work = FeedForward(refs[:12] + refs[14:])
    fc1_grad_ref, fc2_grad_ref = refs[12:14]
    step = pl.program_id(0)

    @pl.when(step == 0)
    def _():
        work.begin()

    fc1_grad_ref[...], fc2_grad_ref[...] = work.tile()

    @pl.when(step == pl.num_programs(0) - 1)
    def _():
        work.finish()


def feed_forward_parts(normed, cotangent, middle, fc1_tiles, fc2_full, vectors):
    count, width = cotangent.shape
    hidden_width = fc2_full.shape[0]
    tiles = hidden_width // FFN_TILE
    bias = vectors[8:].reshape(1, hidden_width)
    in_specs = (
        [whole(x.shape) for x in (normed, cotangent, middle)]
        + [
            pl.BlockSpec(fc1_tiles.shape[:3] + (1,) + fc1_tiles.shape[4:], lambda f: (0, 0, 0, f, 0, 0)),
            pl.BlockSpec((FFN_TILE, width), lambda f: (f, 0)),
            pl.BlockSpec((1, FFN_TILE), lambda f: (0, f)),
            whole(vectors.shape),
        ]
    )
    out_specs = [whole((count, width))] * 3 + [pl.BlockSpec((1, FFN_TILE), lambda f: (0, f)), whole((8, width))]
    out_shape = [
        struct((count, width), low),
        struct((count, width), f32),
        struct((count, width), low),
        struct((1, hidden_width), f32),
        struct((8, width), f32),
    ]
    scratch = [
        pltpu.VMEM((count, width), f32),
        pltpu.VMEM((count, width), f32),
        pltpu.VMEM((count, FFN_TILE), f32),
        pltpu.VMEM((count, FFN_TILE), f32),
        pltpu.VMEM((count, FFN_TILE), low),
        pltpu.VMEM((count, FFN_TILE), low),
    ]
    operands = [normed, cotangent, middle, fc1_tiles, fc2_full, bias, vectors]
    return operands, in_specs, out_specs, out_shape, scratch, tiles


def feed_forward(normed, cotangent, middle, fc1_tiles, fc2_full, vectors):
    operands, in_specs, out_specs, out_shape, scratch, tiles = feed_forward_parts(
        normed, cotangent, middle, fc1_tiles, fc2_full, vectors
    )
    width = cotangent.shape[1]
    return pl.pallas_call(
        plain_feed_forward_kernel,
        grid=(tiles,),
        in_specs=in_specs,
        out_specs=out_specs + [pl.BlockSpec((FFN_TILE, width), lambda f: (f, 0))] * 2,
        out_shape=out_shape + [struct((tiles * FFN_TILE, width), low)] * 2,
        scratch_shapes=scratch,
        compiler_params=pltpu.CompilerParams(vmem_limit_bytes=56 * MIB),
        name="feed_forward",
    )(*operands)


class Backward:
    def __init__(self, heads, head_size, refs, proj_grad, qkv_grad):
        self.heads, self.head_size = heads, head_size
        self.probs, self.query, self.key, self.value = refs[:4]
        self.branch_back, self.middle_back, self.proj, self.context, self.normed, self.tokens, self.qkv = refs[4:11]
        self.vec, self.mask, self.ffn_grad, self.bias_grad = refs[11:15]
        self.input_grad = refs[15]
        self.context_back, self.mixed_back, self.pairs, self.normed_back, self.small = refs[16:]
        self.proj_grad, self.qkv_grad = proj_grad, qkv_grad
        self.count, self.width = self.tokens.shape
        self.groups = self.width // LANES
        self.windows = self.count // WT

    def begin(self):
        self.pairs[...] = jnp.zeros_like(self.pairs)
        self.small[...] = jnp.zeros_like(self.small)
        for tile in range(self.groups):
            span = slice(tile * LANES, (tile + 1) * LANES)
            self.context_back[:, span] = dot(self.branch_back[...], self.proj[span, :], COLS_BY_COLS).astype(low)

    def begin_grads(self):
        for tile in range(self.groups):
            span = slice(tile * LANES, (tile + 1) * LANES)
            self.proj_grad(tile, dot(self.context[:, span], self.branch_back[...], ROWS_BY_ROWS).astype(low))

    def columns(self, part, group):
        return pl.ds(pl.multiple_of(part * self.width + group * LANES, LANES), LANES)

    def attend(self, group, window):
        heads = self.heads
        score_scale = self.head_size ** (-0.5)
        rows = pl.ds(pl.multiple_of(window * WT, WT), WT)
        query, key, value = self.query[...], self.key[...], self.value[...]
        probs_low = self.probs[0]
        probs = probs_low.astype(f32)
        back_stack = stacked(self.context_back[rows, self.columns(0, group)], self.mask, heads)
        value_back = dot(probs_low, back_stack)
        product = probs * dot(value, back_stack, COLS_BY_COLS)
        scores_back = (product - probs * jnp.sum(product, axis=0, keepdims=True)).astype(low)
        self.pairs[group] += scores_back.astype(f32)
        key_back = dot(scores_back, stacked(query, self.mask, heads)) * score_scale
        full = dot(scores_back, key, ROWS_BY_ROWS)
        query_back = diagonal_blocks(full, heads, self.head_size) * score_scale
        for part, back in enumerate((query_back, key_back, value_back)):
            self.mixed_back[rows, self.columns(part, group)] = back.astype(low)

    def group_grads(self, group):
        for part in range(3):
            block = self.mixed_back[:, self.columns(part, group)]
            self.qkv_grad(part, group, dot(block, self.normed[...], ROWS_BY_ROWS).astype(low))

    def normed_back_step(self):
        for tile in range(self.groups):
            span = slice(tile * LANES, (tile + 1) * LANES)
            self.normed_back[:, span] = dot(self.mixed_back[...], self.qkv[span, :], COLS_BY_COLS)

    def finish(self):
        width = self.width
        for row, part in ((2, 0), (3, 2)):

            def body(rows, row=row, part=part):
                block = self.mixed_back[rows, part * width : (part + 1) * width]
                self.small[row : row + 1, :] += column_sum(block.astype(f32))

            for_row_tiles(self.count, body)

        def body(rows):
            xhat, inverse = standardize(self.tokens[rows, :].astype(f32))
            grad = self.normed_back[rows, :]
            back = self.middle_back[rows, :] + norm_back(grad, self.vec[0:1, :], xhat, inverse)
            self.input_grad[rows, :] = back.astype(low)
            self.small[0:1, :] += column_sum(grad * xhat)
            self.small[1:2, :] += column_sum(grad)

        for_row_tiles(self.count, body)
        self.small[4:8, :] = self.ffn_grad[0:4, :]
        for row in range(self.bias_grad.shape[1] // width):
            self.small[8 + row : 9 + row, :] = self.bias_grad[:, row * width : (row + 1) * width]

    def diagonals(self):
        mask = near_mask((WT, DIAG), mirrored=True)
        order = [lax.broadcasted_iota(jnp.int32, (WT, WT), axis) for axis in range(2)]
        mirror = jnp.where(order[0] + order[1] == WT - 1, 1.0, 0.0).astype(f32)
        for group in range(self.groups):
            self.pairs[group] = lax.dot_general(
                mirror, self.pairs[group], ROWS_BY_COLS, precision=lax.Precision.HIGHEST, preferred_element_type=f32
            )
        for head in range(self.groups * self.heads):
            group, place = head // self.heads, head % self.heads
            block = self.pairs[group, :, place * WT : (place + 1) * WT]
            block = jnp.concatenate([block, jnp.zeros((WT, DIAG - WT), f32)], axis=1)
            rolled = pltpu.roll(block, 1, 1, stride=1, stride_axis=0)
            row = SMALL_DIAG + head
            self.small[row : row + 1, :DIAG] = column_sum(jnp.where(mask, rolled, 0.0))
            self.small[row : row + 1, DIAG : 2 * DIAG] = column_sum(jnp.where(mask, 0.0, rolled))


SMALL_DIAG = 16


def plain_backward_kernel(heads, head_size, *refs):
    weight_grad = refs[16]
    width = weight_grad.shape[1]

    def proj_grad(tile, value):
        weight_grad[3 * width + tile * LANES : 3 * width + (tile + 1) * LANES, :] = value

    def qkv_grad(part, group, value):
        weight_grad[pl.ds(pl.multiple_of(part * width + group * LANES, LANES), LANES), :] = value

    work = Backward(heads, head_size, refs[:16] + refs[18:], proj_grad, qkv_grad)
    step = pl.program_id(0)
    windows = work.windows
    busy = windows * work.groups
    group, window = step // windows, lax.rem(step, windows)

    @pl.when(step == 0)
    def _():
        work.begin()
        work.begin_grads()

    @pl.when(step < busy)
    def _():
        work.attend(group, window)

    @pl.when((step < busy) & (window == windows - 1))
    def _():
        work.group_grads(group)

    @pl.when(step == busy)
    def _():
        work.normed_back_step()
        work.finish()
        work.diagonals()
        refs[17][...] = work.small[...]


def backward_parts(probs, mixed, operands, head_count):
    count, width = operands[0].shape
    windows = count // WT
    head_size = width // head_count
    heads = LANES // head_size
    groups = width // LANES
    last = windows * groups - 1
    mask = jnp.asarray(stack_mask(heads, head_size))
    operands = operands[:8] + [mask] + operands[8:]

    def place(step):
        step = jnp.minimum(step, last)
        return step // windows, lax.rem(step, windows)

    def probs_map(step):
        group, window = place(step)
        return window * groups + group, 0, 0

    def mixed_map(part):
        def index(step):
            group, window = place(step)
            return window, part * groups + group

        return index

    in_specs = (
        [pl.BlockSpec((1, WT, heads * WT), probs_map)]
        + [pl.BlockSpec((WT, LANES), mixed_map(part)) for part in range(3)]
        + [whole(operand.shape) for operand in operands]
    )
    scratch = [
        pltpu.VMEM((count, width), low),
        pltpu.VMEM((count, 3 * width), low),
        pltpu.VMEM((groups, WT, heads * WT), f32),
        pltpu.VMEM((count, width), f32),
        pltpu.VMEM((SMALL_DIAG + head_count, width), f32),
    ]
    return (heads, head_size), [probs, mixed, mixed, mixed] + operands, in_specs, scratch, last + 1


def attention_backward(probs, mixed, operands, head_count):
    sizes, operands, in_specs, scratch, busy = backward_parts(probs, mixed, operands, head_count)
    count, width = operands[4].shape
    small_shape = (SMALL_DIAG + head_count, width)
    return pl.pallas_call(
        functools.partial(plain_backward_kernel, *sizes),
        grid=(busy + 1,),
        in_specs=in_specs,
        out_specs=[whole((count, width)), whole((4 * width, width)), whole(small_shape)],
        out_shape=[struct((count, width), low), struct((4 * width, width), low), struct(small_shape, f32)],
        scratch_shapes=scratch,
        compiler_params=pltpu.CompilerParams(vmem_limit_bytes=60 * MIB),
        name="attention_backward",
    )(*operands)


MESH = pl.DeviceIdType.MESH


class Peers:
    def __init__(self):
        self.z = lax.axis_index("rep")
        place = lax.axis_index("grp")
        self.c = lax.rem(place, 2)
        self.x = lax.rem(place // 2, 2)
        self.y = place // 4
        self.core_peer = (self.z, place + 1 - 2 * self.c)
        self.x_peer = (self.z, place + 2 - 4 * self.x)
        self.y_peer = (self.z, place + 4 - 8 * self.y)
        self.odd = lax.rem(self.z, 2)
        self.even = 1 - self.odd
        to_x, to_y = 2 - 4 * self.x, 4 - 8 * self.y
        self.first_peer = (self.z, place + self.even * to_x + self.odd * to_y)
        self.second_peer = (self.z, place + self.odd * to_x + self.even * to_y)
        self.pair_peer = (self.z + 1 - 2 * self.odd, place)
        self.z_places = [lax.rem(self.z + step, 4) for step in range(1, 4)]
        self.z_peers = [(there, place) for there in self.z_places]

    def plane(self):
        return [self.core_peer, self.x_peer, self.y_peer]

    def everyone(self):
        return self.plane() + self.z_peers


def meet(peers):
    barrier = pltpu.get_barrier_semaphore()
    for peer in peers:
        pl.semaphore_signal(barrier, inc=1, device_id=peer, device_id_type=MESH)
    pl.semaphore_wait(barrier, len(peers))


class Copies:
    def __init__(self, send_sems, recv_sems):
        self.send_sems, self.recv_sems = send_sems, recv_sems
        self.made = []

    def make(self, ends, peer):
        copy = Copy(self, len(self.made), ends, peer)
        self.made.append(copy)
        copy.build().start()
        return copy

    def drain(self):
        for copy in self.made:
            copy.build().wait_send()


class Copy:
    def __init__(self, owner, number, ends, peer):
        self.owner, self.number, self.ends, self.peer = owner, number, ends, peer

    def build(self):
        source, target = self.ends()
        return pltpu.make_async_remote_copy(
            src_ref=source,
            dst_ref=target,
            send_sem=self.owner.send_sems.at[self.number],
            recv_sem=self.owner.recv_sems.at[self.number],
            device_id=self.peer,
            device_id_type=MESH,
        )

    def wait_recv(self):
        self.build().wait_recv()


def same(place):
    return lambda: (place(), place())


class Gather:
    def __init__(self, me, copies, source, out):
        self.me, self.copies, self.source, self.out = me, copies, source, out
        self.half = out.shape[3] // 2
        self.across = []

    def block(self, flip_y, flip_x):
        me = self.me
        return self.out.at[1 - me.y if flip_y else me.y, 1 - me.x if flip_x else me.x, me.c]

    def start(self):
        me = self.me

        def ends():
            return self.source(), self.block(False, False)

        self.by_x = self.copies.make(ends, me.x_peer)
        self.by_y = self.copies.make(ends, me.y_peer)
        self.across.append(self.copies.make(ends, me.core_peer))

    def relay(self):
        me = self.me
        self.by_x.wait_recv()
        to_y = self.copies.make(same(lambda: self.block(False, True).at[pl.ds(0, self.half)]), me.y_peer)
        self.by_y.wait_recv()
        to_x = self.copies.make(same(lambda: self.block(True, False).at[pl.ds(self.half, self.half)]), me.x_peer)
        self.relayed = (to_x, to_y)
        self.across.append(self.copies.make(same(lambda: self.block(False, True)), me.core_peer))
        self.across.append(self.copies.make(same(lambda: self.block(True, False)), me.core_peer))

    def cross(self):
        for copy in self.relayed:
            copy.wait_recv()
        self.across.append(self.copies.make(same(lambda: self.block(True, True)), self.me.core_peer))

    def wait(self):
        for copy in self.across:
            copy.wait_recv()


class PairGather:
    def __init__(self, me, copies, source, out, span):
        self.me, self.copies, self.source, self.out, self.span = me, copies, source, out, span
        self.across = []

    def block(self, flip_y, flip_x):
        me = self.me
        return self.out.at[me.y + flip_y * (1 - 2 * me.y), me.x + flip_x * (1 - 2 * me.x), me.c].at[self.span]

    def give(self, flip_y, flip_x, peer):
        return self.copies.make(same(lambda: self.block(flip_y, flip_x)), peer)

    def start(self):
        me = self.me

        def ends():
            return self.source.at[self.span], self.block(0, 0)

        self.first = self.copies.make(ends, me.first_peer)
        self.across.append(self.copies.make(ends, me.core_peer))

    def relay(self):
        me = self.me
        self.first.wait_recv()
        self.second = self.give(me.odd, me.even, me.second_peer)
        self.third = self.give(me.odd, me.even, me.pair_peer)
        self.across.append(self.give(me.odd, me.even, me.core_peer))

    def cross(self):
        me = self.me
        self.second.wait_recv()
        self.across.append(self.give(1, 1, me.core_peer))
        self.third.wait_recv()
        self.across.append(self.give(me.even, me.odd, me.core_peer))

    def wait(self):
        for copy in self.across:
            copy.wait_recv()


def gathered_forward_kernel(heads, head_size, *refs):
    qkv_shard, proj_shard, fc1_shard, fc2_shard = refs[:4]
    outs = refs[10:20]
    qkv_out, proj_out, fc1_out, fc2_out = outs[6:]
    scratch = refs[20:]
    work = Forward(heads, head_size, refs[4:10] + outs[:6] + scratch[:3])
    qkv_full, proj_full, fc1_low, fc2_low, send_sems, recv_sems, local_sems = scratch[3:]
    me = Peers()
    copies = Copies(send_sems, recv_sems)
    own = (me.y, me.x, me.c)
    qkv = Gather(me, copies, lambda: qkv_full.at[own], qkv_full)
    proj = Gather(me, copies, lambda: proj_full.at[own], proj_full)
    hidden_parts = []
    for source, out in ((fc1_low, fc1_out), (fc2_low, fc2_out)):
        half = out.shape[3] // 2
        hidden_parts += [PairGather(me, copies, source, out, pl.ds(start, half)) for start in (0, half)]

    def local(index):
        source = (fc1_low, fc2_low, qkv_full, proj_full)[index]
        target = (fc1_out, fc2_out, qkv_out, proj_out)[index]
        return pltpu.make_async_copy(source, target.at[own] if index < 2 else target, local_sems.at[index])

    window = pl.program_id(0)
    first_window = (me.z * 8 + me.y * 4 + me.x * 2 + me.c) * pl.num_programs(0)

    def weight_tile(full):
        def tile(start):
            return full[:, :, :, :, start : start + LANES].reshape(-1, LANES)

        return tile

    @pl.when(window == 0)
    def _():
        qkv_full[own] = qkv_shard[...].astype(low)
        proj_full[own] = proj_shard[...].astype(low)
        meet(me.plane() + [me.pair_peer])
        qkv.start()
        proj.start()
        for tile in range(fc1_low.shape[0]):
            fc1_low[tile] = fc1_shard[:, tile * FFN_TILE : (tile + 1) * FFN_TILE].astype(low)
        fc2_low[...] = fc2_shard[...].astype(low)
        work.norm_one()
        relative_rows(heads, work.diag, work.rel)
        qkv.relay()
        proj.relay()
        for part in hidden_parts:
            part.start()
        local(0).start()
        local(1).start()
        qkv.cross()
        qkv.wait()
        local(2).start()
        work.mix(weight_tile(qkv_full))

    for at, steps in (
        (1, (proj.cross, hidden_parts[0].relay)),
        (2, (hidden_parts[1].relay,)),
        (3, (hidden_parts[0].cross,)),
        (4, (hidden_parts[2].relay,)),
        (5, (hidden_parts[1].cross,)),
        (6, (hidden_parts[3].relay,)),
    ):

        @pl.when(window == at)
        def _():
            for advance in steps:
                advance()

    work.attend(window, first_window)

    @pl.when(window == pl.num_programs(0) - 1)
    def _():
        proj.wait()
        local(3).start()
        work.finish(weight_tile(proj_full))
        hidden_parts[2].cross()
        hidden_parts[3].cross()
        for part in hidden_parts:
            part.wait()
        for index in range(4):
            local(index).wait()
        copies.drain()


def gathered_forward(fill, tokens, weights, vectors, diagonals, head_count, collective_id):
    sizes, operands, in_specs, out_specs, out_shape, scratch = forward_parts(
        fill, tokens, vectors, diagonals, head_count
    )
    shapes = [weight.shape for weight in weights]
    shapes[2] = (shapes[2][1] // FFN_TILE, shapes[2][0], FFN_TILE)
    fulls = [(2, 2, 2) + shape for shape in shapes]
    results = pl.pallas_call(
        functools.partial(gathered_forward_kernel, *sizes),
        grid=(fill.shape[0],),
        in_specs=[whole(weight.shape) for weight in weights] + in_specs,
        out_specs=out_specs + [HBM] * 4,
        out_shape=out_shape + [struct(full, low) for full in fulls],
        scratch_shapes=scratch
        + [pltpu.VMEM(fulls[0], low), pltpu.VMEM(fulls[1], low)]
        + [pltpu.VMEM(shape, low) for shape in shapes[2:]]
        + [pltpu.SemaphoreType.DMA((44,)), pltpu.SemaphoreType.DMA((44,)), pltpu.SemaphoreType.DMA((4,))],
        compiler_params=pltpu.CompilerParams(
            collective_id=collective_id, has_side_effects=True, vmem_limit_bytes=58 * MIB
        ),
        name="gathered_forward",
    )(*weights, *operands)
    qkv_full, proj_full, fc1_tiles, fc2_full = results[6:]
    return results[:6], [
        qkv_full.reshape(-1, shapes[0][1]), proj_full.reshape(-1, shapes[1][1]), fc1_tiles,
        fc2_full.reshape(-1, shapes[3][1]),
    ]


PIECE = 16


class Reduction:
    def __init__(self, me, copies, term, mine, out, buffers, load_sems, store_sems):
        self.me, self.copies, self.term, self.mine, self.out = me, copies, term, mine, out
        self.core_in, self.first_in, self.second_in, self.z_in, self.final = buffers
        self.load_sems, self.store_sems = load_sems, store_sems
        self.parts, self.half = buffers[0].shape[1], buffers[0].shape[-1] // 2
        self.kept = None
        self.core, self.first, self.second, self.over_z, self.last_z, self.spread, self.relayed, self.across = (
            {} for _ in range(8)
        )

    def sides(self):
        return pl.ds(0, self.half), pl.ds(self.half, self.half)

    def z_columns(self, z):
        return pl.ds(pl.multiple_of(lax.rem(z, 2) * self.half, self.half), self.half)

    def loop(self, amount, body):
        def step(index, carry):
            body(index)
            return carry

        lax.fori_loop(0, amount, step, 0)

    def load(self, k):
        ref, at = self.mine
        return pltpu.make_async_copy(self.term(k, self.me.c), ref.at[k], self.load_sems.at[k])

    def store(self, k):
        me = self.me
        return pltpu.make_async_copy(
            self.final.at[k], self.out(k, me.c, me.x, me.y, (me.z // 2, slice(None), self.z_columns(me.z))),
            self.store_sems.at[k],
        )

    def start(self, k):
        me = self.me
        self.core[k] = self.copies.make(lambda: (self.term(k, 1 - me.c), self.core_in.at[k]), me.core_peer)
        if self.load_sems is not None:
            self.load(k).start()

    def finish_core(self, k):
        me = self.me
        ref, at = self.mine
        if self.load_sems is not None:
            self.load(k).wait()
        self.core[k].wait_recv()

        def add(step):
            part, x, y, row = step // 8, lax.rem(step // 4, 2), lax.rem(step // 2, 2), lax.rem(step, 2)
            place = at(k, part, x, y, row)
            ref[place] = ref[place] + self.core_in[k, part, x, y, row]

        self.loop(8 * self.parts, add)
        every = slice(None)
        self.first[k] = (
            self.copies.make(
                lambda: (
                    ref.at[at(k, every, 1 - me.x, every, every) + (every, self.sides()[0])], self.first_in.at[k, 0],
                ),
                me.x_peer,
            ),
            self.copies.make(
                lambda: (
                    ref.at[at(k, every, every, 1 - me.y, every) + (every, self.sides()[1])], self.first_in.at[k, 1],
                ),
                me.y_peer,
            ),
        )

    def finish_first(self, k):
        me = self.me
        ref, at = self.mine
        for copy in self.first[k]:
            copy.wait_recv()
        half = self.half

        def add(step):
            part, other, row = step // 4, lax.rem(step // 2, 2), lax.rem(step, 2)
            place = at(k, part, me.x, other, row) + (slice(None), slice(0, half))
            ref[place] = ref[place] + self.first_in[k, 0, part, other, row]
            place = at(k, part, other, me.y, row) + (slice(None), slice(half, 2 * half))
            ref[place] = ref[place] + self.first_in[k, 1, part, other, row]

        self.loop(4 * self.parts, add)
        every = slice(None)
        self.second[k] = (
            self.copies.make(
                lambda: (
                    ref.at[at(k, every, me.x, 1 - me.y, every) + (every, self.sides()[0])], self.second_in.at[k, 0],
                ),
                me.y_peer,
            ),
            self.copies.make(
                lambda: (
                    ref.at[at(k, every, 1 - me.x, me.y, every) + (every, self.sides()[1])], self.second_in.at[k, 1],
                ),
                me.x_peer,
            ),
        )

    def add_second(self, k):
        me = self.me
        ref, at = self.mine
        for copy in self.second[k]:
            copy.wait_recv()
        half = self.half

        def add(step):
            part, row = step // 2, lax.rem(step, 2)
            for side, span in enumerate((slice(0, half), slice(half, 2 * half))):
                place = at(k, part, me.x, me.y, row) + (slice(None), span)
                ref[place] = ref[place] + self.second_in[k, side, part, row]

        self.loop(2 * self.parts, add)

    def store_piece(self, k, target):
        ref, at = self.mine
        every = slice(None)
        source = ref.at[at(k, every, self.me.x, self.me.y, every)]
        return pltpu.make_async_copy(source, target.at[k], self.store_sems.at[k])

    def keep_piece(self, k, source):
        return pltpu.make_async_copy(
            source.at[k, :, self.me.z // 2, :, self.z_columns(self.me.z)], self.z_in.at[k, self.me.z], self.load_sems.at[k]
        )

    def start_z(self, k, source):
        self.kept = source
        self.over_z[k] = [
            self.copies.make(
                lambda there=there: (
                    source.at[k, :, there // 2, :, self.z_columns(there)], self.z_in.at[k, self.me.z],
                ),
                peer,
            )
            for there, peer in zip(self.me.z_places, self.me.z_peers)
        ]
        self.keep_piece(k, source).start()

    def finish_second(self, k):
        me = self.me
        ref, at = self.mine
        self.add_second(k)

        def piece(part, z):
            return at(k, part, me.x, me.y, z // 2) + (slice(None), self.z_columns(z))

        self.over_z[k] = [
            self.copies.make(lambda there=there: (ref.at[piece(slice(None), there)], self.z_in.at[k, me.z]), peer)
            for there, peer in zip(me.z_places, me.z_peers)
        ]

        def keep(part):
            self.z_in[k, me.z, part] = ref[piece(part, me.z)]

        self.loop(self.parts, keep)

    def finish_z(self, k):
        me = self.me
        for copy in self.over_z[k]:
            copy.wait_recv()
        if self.kept is not None:
            self.keep_piece(k, self.kept).wait()

        def add(part):
            total = self.z_in[k, 0, part].astype(f32)
            for place in range(1, 4):
                total = total + self.z_in[k, place, part].astype(f32)
            self.final[k, part] = total.astype(low)

        self.loop(self.parts, add)
        self.last_z[k] = [
            self.copies.make(
                lambda: (
                    self.final.at[k],
                    self.out(k, me.c, me.x, me.y, (me.z // 2, slice(None), self.z_columns(me.z))),
                ),
                peer,
            )
            for peer in me.z_peers
        ]
        self.store(k).start()

    def finish_last_z(self, k):
        me = self.me
        for copy in self.last_z[k]:
            copy.wait_recv()
        self.store(k).wait()
        own = same(lambda: self.out(k, me.c, me.x, me.y, ()))
        self.spread[k] = [self.copies.make(own, peer) for peer in (me.x_peer, me.y_peer)]
        self.across[k] = [self.copies.make(own, me.core_peer)]

    def finish_spread(self, k):
        me = self.me
        by_x, by_y = self.spread[k]
        every = slice(None)
        by_y.wait_recv()
        to_x = self.copies.make(
            same(lambda: self.out(k, me.c, me.x, 1 - me.y, (every, every, self.sides()[0]))), me.x_peer
        )
        by_x.wait_recv()
        to_y = self.copies.make(
            same(lambda: self.out(k, me.c, 1 - me.x, me.y, (every, every, self.sides()[1]))), me.y_peer
        )
        self.relayed[k] = (to_x, to_y)
        self.across[k].append(self.copies.make(same(lambda: self.out(k, me.c, 1 - me.x, me.y, ())), me.core_peer))
        self.across[k].append(self.copies.make(same(lambda: self.out(k, me.c, me.x, 1 - me.y, ())), me.core_peer))

    def finish_relay(self, k):
        me = self.me
        for copy in self.relayed[k]:
            copy.wait_recv()
        self.across[k].append(self.copies.make(same(lambda: self.out(k, me.c, 1 - me.x, 1 - me.y, ())), me.core_peer))

    def wait(self, k):
        for copy in self.across[k]:
            copy.wait_recv()

    def stage(self, number, k):
        stages = (
            self.finish_core, self.finish_first, self.finish_second, self.finish_z, self.finish_last_z,
            self.finish_spread, self.finish_relay,
        )
        stages[number](k)


STAGES = 7


def reduction_buffers(amount, parts, width):
    half = width // 2
    return [
        pltpu.VMEM((amount, parts, 2, 2, 2, PIECE, width), low),
        pltpu.VMEM((amount, 2, parts, 2, 2, PIECE, half), low),
        pltpu.VMEM((amount, 2, parts, 2, PIECE, half), low),
        pltpu.VMEM((amount, 4, parts, PIECE, half), low),
        pltpu.VMEM((amount, parts, PIECE, half), low),
    ]


def reduced_feed_forward_kernel(*refs):
    later_fc1, later_fc2, piece_out = refs[12:15]
    term, core_in, first_in, second_in, send_sems, recv_sems, store_sems = refs[21:]
    work = FeedForward(refs[:12] + refs[15:21])
    me = Peers()
    copies = Copies(send_sems, recv_sems)
    per_tile = FFN_TILE // LANES
    early = term.shape[1] // per_tile
    tile_shape = (per_tile,) + term.shape[2:]
    buffers = (core_in, first_in, second_in, None, None)
    first_half = Reduction(
        me, copies, lambda k, c: term.at[k, :, c], (term, lambda k, part, *place: (k, part, me.c) + place), None, buffers,
        None, store_sems,
    )
    step = pl.program_id(0)
    last = pl.num_programs(0) - 1

    @pl.when(step == 0)
    def _():
        work.begin()
        meet(me.plane())

    fc1_grad, fc2_grad = work.tile()

    @pl.when(step < early)
    def _():
        term[0, pl.ds(step * per_tile, per_tile)] = fc1_grad.reshape(tile_shape)
        term[1, pl.ds(step * per_tile, per_tile)] = fc2_grad.reshape(tile_shape)

    @pl.when(step >= early)
    def _():
        later_fc1[...] = fc1_grad
        later_fc2[...] = fc2_grad

    @pl.when(step == early - 1)
    def _():
        for k in range(2):
            first_half.start(k)

    @pl.when(step == early)
    def _():
        for k in range(2):
            first_half.finish_core(k)

    @pl.when(step == last)
    def _():
        for k in range(2):
            first_half.finish_first(k)
        work.finish()
        for k in range(2):
            first_half.add_second(k)
            first_half.store_piece(k, piece_out).start()
        for k in range(2):
            first_half.store_piece(k, piece_out).wait()
        copies.drain()


def reduced_feed_forward(normed, cotangent, middle, fc1_tiles, fc2_full, vectors, collective_id):
    operands, in_specs, out_specs, out_shape, scratch, tiles = feed_forward_parts(
        normed, cotangent, middle, fc1_tiles, fc2_full, vectors
    )
    width = cotangent.shape[1]
    early = tiles // 2
    tile_shape = (2, 2, 2, 2, PIECE, width)
    parts = early * FFN_TILE // LANES
    later = pl.BlockSpec((FFN_TILE, width), lambda f: (jnp.maximum(f - early, 0), 0))
    return pl.pallas_call(
        reduced_feed_forward_kernel,
        grid=(tiles,),
        in_specs=in_specs,
        out_specs=out_specs + [later] * 2 + [HBM],
        out_shape=out_shape
        + [struct(((tiles - early) * FFN_TILE, width), low)] * 2
        + [struct((2, parts, 2, PIECE, width), low)],
        scratch_shapes=scratch
        + [pltpu.VMEM((2, parts) + tile_shape, low)]
        + reduction_buffers(2, parts, width)[:3]
        + [pltpu.SemaphoreType.DMA((10,)), pltpu.SemaphoreType.DMA((10,)), pltpu.SemaphoreType.DMA((2,))],
        compiler_params=pltpu.CompilerParams(
            collective_id=collective_id, has_side_effects=True, vmem_limit_bytes=58 * MIB
        ),
        name="reduced_feed_forward",
    )(*operands)


class SmallSum:
    def __init__(self, me, copies, small, inbox):
        self.me, self.copies, self.small, self.inbox, self.made = me, copies, small, inbox, []

    def step(self, number):
        peers = self.me.plane()
        z = self.me.z
        if number > 0:
            self.made[number - 1].wait_recv()
            self.small[...] += self.inbox[number - 1]
        if number < 3:
            self.inbox[3 + number] = self.small[...]
            self.made.append(
                self.copies.make(lambda: (self.inbox.at[3 + number], self.inbox.at[number]), peers[number])
            )
        else:
            self.inbox[6 + z] = self.small[...]
            for peer in self.me.z_peers:
                self.made.append(self.copies.make(same(lambda: self.inbox.at[6 + z]), peer))

    def finish(self):
        for copy in self.made[3:]:
            copy.wait_recv()
        self.small[...] = (self.inbox[6] + self.inbox[7]) + (self.inbox[8] + self.inbox[9])


def reduced_backward_kernel(heads, head_size, *refs):
    fc1_term, fc2_term, piece = refs[15:18]
    input_grad, fc_out, qkv_out, proj_out, small_out = refs[18:23]
    att, fc_mine = refs[28:30]
    fc_buffers, att_buffers, early_buffers = refs[30:35], refs[35:40], refs[40:42]
    inbox, send_sems, recv_sems, load_sems, early_load_sems, fc_store_sems, early_store_sems, att_store_sems = refs[42:]
    groups = att.shape[0] - 1
    tile_shape = (2, 2, 2, 2, PIECE, att.shape[-1])

    def proj_grad(tile, value):
        att[groups, tile] = value.reshape(tile_shape)

    def qkv_grad(part, group, value):
        att[group, part] = value.reshape(tile_shape)

    work = Backward(heads, head_size, refs[:15] + (input_grad,) + refs[23:28], proj_grad, qkv_grad)
    me = Peers()
    copies = Copies(send_sems, recv_sems)

    def fc_place(half):
        return lambda k, c, x, y, rest: fc_out.at[(k, half, slice(None), c, x, y) + rest]

    def att_place(k, c, x, y, rest):
        if k == groups:
            return proj_out.at[(slice(None), c, x, y) + rest]
        return qkv_out.at[(slice(None), k, c, x, y) + rest]

    early = Reduction(
        me, copies, None, None, fc_place(0), (fc_buffers[0], None, None) + early_buffers, early_load_sems,
        early_store_sems,
    )
    fc = Reduction(
        me, copies, lambda k, c: (fc1_term, fc2_term)[k].at[:, c], (fc_mine, lambda *place: place), fc_place(1),
        fc_buffers, load_sems, fc_store_sems,
    )
    att_sum = Reduction(
        me, copies, lambda k, c: att.at[k, :, c], (att, lambda k, part, *place: (k, part, me.c) + place), att_place,
        att_buffers, None, att_store_sems,
    )
    small = SmallSum(me, copies, work.small, inbox)
    order = [(early, 0, -3), (early, 1, -3), (fc, 0, 0), (fc, 1, 1), (att_sum, groups, 2)]
    order += [(att_sum, k, 3 + k) for k in range(groups)]
    waves = 2 + groups + STAGES
    done = [0]

    def wave():
        number = done[0]
        done[0] += 1
        for which, k, first in reversed(order):
            if 0 <= number - first < STAGES:
                which.stage(number - first, k)

    step = pl.program_id(0)
    windows = work.windows
    busy = windows * groups
    group, window = step // windows, lax.rem(step, windows)

    @pl.when(step == 0)
    def _():
        meet(me.everyone())
        for k in range(2):
            early.start_z(k, piece)
            fc.start(k)
        work.begin_grads()
        att_sum.start(groups)
        work.begin()

    @pl.when(step < busy)
    def _():
        work.attend(group, window)

    for number in range(groups):

        @pl.when(step == (number + 1) * windows - 1)
        def _():
            work.group_grads(number)
            att_sum.start(number)

    for at in (2, 5, 8, 11, 15, 20):

        @pl.when(step == at)
        def _():
            wave()

    @pl.when(step == busy)
    def _():
        work.normed_back_step()
        wave()
        work.finish()
        wave()
        work.diagonals()
        small.step(0)
        for number in range(1, 5):
            wave()
            if number < 4:
                small.step(number)
            else:
                small.finish()
        small_out[...] = work.small[...]
        while done[0] < waves:
            wave()
        for which, k, _ in order:
            which.wait(k)
        copies.drain()


def reduced_backward(probs, mixed, operands, head_count, fc1_term, fc2_term, piece, collective_id):
    sizes, operands, in_specs, scratch, busy = backward_parts(probs, mixed, operands, head_count)
    count, width = operands[4].shape
    groups = width // LANES
    tile_shape = (2, 2, 2, 2, PIECE, width)
    parts = fc1_term.shape[0] // LANES
    small_shape = (SMALL_DIAG + head_count, width)
    copies = 14 * 2 + 19 * (2 + groups + 1) + 6
    buffers = reduction_buffers(2, parts, width)
    input_grad, fc_sum, qkv_sum, proj_sum, small = pl.pallas_call(
        functools.partial(reduced_backward_kernel, *sizes),
        grid=(busy + 1,),
        in_specs=in_specs + [HBM] * 3,
        out_specs=[whole((count, width))] + [HBM] * 3 + [whole(small_shape)],
        out_shape=[
            struct((count, width), low),
            struct((2, 2, parts) + tile_shape, low),
            struct((3, groups) + tile_shape, low),
            struct((groups,) + tile_shape, low),
            struct(small_shape, f32),
        ],
        scratch_shapes=scratch
        + [pltpu.VMEM((groups + 1, 3) + tile_shape, low), pltpu.VMEM((2, parts) + tile_shape[1:], low)]
        + buffers
        + reduction_buffers(groups + 1, 3, width)
        + buffers[3:]
        + [
            pltpu.VMEM((10,) + small_shape, f32),
            pltpu.SemaphoreType.DMA((copies,)),
            pltpu.SemaphoreType.DMA((copies,)),
        ]
        + [pltpu.SemaphoreType.DMA((2,))] * 4
        + [pltpu.SemaphoreType.DMA((groups + 1,))],
        compiler_params=pltpu.CompilerParams(
            collective_id=collective_id, has_side_effects=True, vmem_limit_bytes=62 * MIB
        ),
        name="reduced_backward",
    )(*operands, fc1_term.reshape((parts,) + tile_shape), fc2_term.reshape((parts,) + tile_shape), piece)
    sums = [part.reshape(-1, width) for part in (qkv_sum, proj_sum, fc_sum)]
    return input_grad, sums, small


def tile_update(tall, rows, big, root, pick, sum_ref, fresh):
    span = rows.shape[0]
    across = dot(jnp.concatenate([rows, pick], axis=0), tall, COLS_BY_COLS)
    columns = across[span:]
    term = dot(jnp.concatenate([root.astype(low), columns.astype(low)], axis=0), tall)

    @pl.when(fresh)
    def _():
        sum_ref[...] = term

    @pl.when(jnp.logical_not(fresh))
    def _():
        sum_ref[...] += term

    return 0.5 * big + 0.5 * across[:span], columns


def column_pick(member, shape):
    row, column = (lax.broadcasted_iota(jnp.int32, shape, axis) for axis in range(2))
    return jnp.where(column == row + member * shape[0], 1.0, 0.0).astype(low)


def hidden_kernel(
    member_ref, tall_ref, rows_ref, big_ref, root_ref, small_ref, small_root_ref, fc2_ref,
    big_out_ref, small_out_ref, fc1_grad_ref, fc1_step_ref, fc2_grad_ref, fc2_new_ref, fc2_copy_ref,
    sum_ref,
):
    matrix, tile = pl.program_id(0), pl.program_id(1)
    span = rows_ref.shape[0]
    pick = column_pick(member_ref[0], small_ref.shape[1:])
    big_new, columns = tile_update(
        tall_ref[...], rows_ref[...], big_ref[0], root_ref[0], pick, sum_ref, tile == 0
    )
    big_out_ref[0] = big_new

    @pl.when(matrix == 0)
    def _():
        fc1_grad_ref[...] = columns

    @pl.when(tile == pl.num_programs(1) - 1)
    def _():
        small_out_ref[0] = 0.5 * small_ref[0] + 0.5 * sum_ref[span:, :]
        product = sum_ref[:span, :].astype(low)

        @pl.when(matrix == 0)
        def _():
            fc1_step_ref[...] = dot(small_root_ref[0], product, COLS_BY_COLS).astype(low)

        @pl.when(matrix == 1)
        def _():
            new = fc2_ref[...] - dot(product, small_root_ref[0])
            fc2_new_ref[...] = new
            fc2_copy_ref[...] = new.astype(low)
            fc2_grad_ref[...] = rows_ref[...].astype(f32)


def hidden_update(member, fc_sum, stats_hidden, roots_hidden, stats_model, small_roots, fc2_weight):
    width = fc_sum.shape[1]
    _, span, hidden_width = stats_hidden.shape
    model_rows = stats_model.shape[1]
    tiles = hidden_width // width
    last = tiles - 1
    return pl.pallas_call(
        hidden_kernel,
        grid_spec=pltpu.PrefetchScalarGridSpec(
            num_scalar_prefetch=1,
            grid=(2, tiles),
            in_specs=[
                pl.BlockSpec((width, width), lambda i, j, m: (i * tiles + j, 0)),
                pl.BlockSpec((span, width), lambda i, j, m: (i * (hidden_width // span) + m[0], 0)),
                pl.BlockSpec((1, span, width), lambda i, j, m: (i, 0, j)),
                pl.BlockSpec((1, span, width), lambda i, j, m: (i, 0, j)),
                pl.BlockSpec((1, model_rows, width), lambda i, j, m: (3 + i, 0, 0)),
                pl.BlockSpec((1, width, width), lambda i, j, m: (2 + i, 0, 0)),
                pl.BlockSpec((span, width), lambda i, j, m: (0, 0)),
            ],
            out_specs=[
                pl.BlockSpec((1, span, width), lambda i, j, m: (i, 0, j)),
                pl.BlockSpec((1, model_rows, width), lambda i, j, m: (i, 0, 0)),
                pl.BlockSpec((model_rows, width), lambda i, j, m: (0, jnp.where(i == 0, j, last))),
                pl.BlockSpec((width, span), lambda i, j, m: (0, 0)),
                pl.BlockSpec((span, width), lambda i, j, m: (0, 0)),
                pl.BlockSpec((span, width), lambda i, j, m: (0, 0)),
                pl.BlockSpec((span, width), lambda i, j, m: (0, 0)),
            ],
            scratch_shapes=[pltpu.VMEM((span + model_rows, width), f32)],
        ),
        out_shape=[
            struct(stats_hidden.shape, f32),
            struct((2, model_rows, width), f32),
            struct((model_rows, hidden_width), f32),
            struct((width, span), low),
            struct((span, width), f32),
            struct((span, width), f32),
            struct((span, width), low),
        ],
        compiler_params=pltpu.CompilerParams(vmem_limit_bytes=48 * MIB),
        name="hidden_update",
    )(member, fc_sum, fc_sum, stats_hidden, roots_hidden, stats_model, small_roots, fc2_weight)


def exchange_places(me):
    member = me.y * 4 + me.x * 2 + me.c
    return member, [lax.rem(member + step, 8) for step in range(1, 8)]


class Exchange:
    def __init__(self, me, copies, blocks, inbox):
        self.me, self.copies, self.blocks, self.inbox = me, copies, blocks, inbox

    def start(self):
        member, others = exchange_places(self.me)
        self.made = [
            self.copies.make(lambda there=there: (self.blocks.at[there], self.inbox.at[member]), (self.me.z, there))
            for there in others
        ]

    def wait(self):
        for copy in self.made:
            copy.wait_recv()


def exchange_kernel(amount, *refs):
    blocks, inboxes = refs[:amount], refs[amount : 2 * amount]
    send_sems, recv_sems, local_sems = refs[2 * amount :]
    me = Peers()
    copies = Copies(send_sems, recv_sems)
    member, others = exchange_places(me)
    meet([(me.z, there) for there in others])
    exchanges = [Exchange(me, copies, source, inbox) for source, inbox in zip(blocks, inboxes)]
    own = [
        pltpu.make_async_copy(source.at[member], inbox.at[member], local_sems.at[index])
        for index, (source, inbox) in enumerate(zip(blocks, inboxes))
    ]
    for copy in own:
        copy.start()
    for exchange in exchanges:
        exchange.start()
    for exchange in exchanges:
        exchange.wait()
    for copy in own:
        copy.wait()
    copies.drain()


def exchange_rows(steps, collective_id):
    amount = len(steps)
    blocks = [step.reshape(8, step.shape[0] // 8, step.shape[1]) for step in steps]
    vmem = pl.BlockSpec(memory_space=pltpu.VMEM)
    return pl.pallas_call(
        functools.partial(exchange_kernel, amount),
        in_specs=[vmem] * amount,
        out_specs=[vmem] * amount,
        out_shape=[struct(block.shape, low) for block in blocks],
        scratch_shapes=[
            pltpu.SemaphoreType.DMA((7 * amount,)),
            pltpu.SemaphoreType.DMA((7 * amount,)),
            pltpu.SemaphoreType.DMA((amount,)),
        ],
        compiler_params=pltpu.CompilerParams(collective_id=collective_id, has_side_effects=True),
        name="exchange_rows",
    )(*blocks)


def apply_kernel(amount, *refs):
    for index in range(amount):
        old, blocks, new_ref, copy_ref = (refs[index + part * amount] for part in range(4))
        step = jnp.concatenate([blocks[place] for place in range(blocks.shape[0])], axis=1)
        new = old[...] - step.astype(f32)
        new_ref[...] = new
        copy_ref[...] = new.astype(low)


def apply_steps(weights, inboxes):
    return pl.pallas_call(
        functools.partial(apply_kernel, len(weights)),
        out_shape=[struct(weight.shape, dtype) for dtype in (f32, low) for weight in weights],
        compiler_params=pltpu.CompilerParams(vmem_limit_bytes=32 * MIB),
        name="apply_steps",
    )(*weights, *inboxes)


def model_kernel(
    member_ref, tall_ref, qkv_rows_ref, proj_tall_ref, proj_rows_ref, big_ref, root_ref, stats_ref, hidden_small_ref, proj_root_ref,
    small_root_ref, proj_ref,
    big_out_ref, stats_out_ref, qkv_grad_ref, qkv_step_ref, proj_grad_ref, proj_new_ref, proj_copy_ref,
    sum_ref, proj_sum_ref,
):
    tile = pl.program_id(0)
    span = qkv_rows_ref.shape[0]
    model_rows = proj_rows_ref.shape[0]
    last = pl.num_programs(0) - 1
    pick = column_pick(member_ref[0], proj_rows_ref.shape)

    @pl.when(tile < last)
    def _():
        big_new, columns = tile_update(
            tall_ref[...], qkv_rows_ref[...], big_ref[...], root_ref[...], pick, sum_ref, tile == 0
        )
        big_out_ref[...] = big_new
        qkv_grad_ref[...] = columns

    @pl.when(tile == last)
    def _():
        qkv_step_ref[...] = dot(small_root_ref[0], sum_ref[:span, :].astype(low), COLS_BY_COLS).astype(low)
        stats_out_ref[0] = 0.5 * stats_ref[0] + 0.5 * sum_ref[span:, :]
        rows = proj_rows_ref[...]
        proj_left, _ = tile_update(
            proj_tall_ref[...], rows, stats_ref[1], proj_root_ref[0], pick, proj_sum_ref, tile == last
        )
        stats_out_ref[1] = proj_left
        stats_out_ref[2] = 0.5 * stats_ref[2] + 0.5 * proj_sum_ref[model_rows:, :]
        stats_out_ref[3] = hidden_small_ref[0]
        stats_out_ref[4] = hidden_small_ref[1]
        new = proj_ref[...] - dot(proj_sum_ref[:model_rows, :].astype(low), small_root_ref[1])
        proj_new_ref[...] = new
        proj_copy_ref[...] = new.astype(low)
        proj_grad_ref[...] = rows.astype(f32)


def model_update(
    member, qkv_sum, proj_sum, stats_qkv, roots_qkv, stats_model, hidden_small, roots_model, small_roots, proj_weight
):
    width = qkv_sum.shape[1]
    span, qkv_width = stats_qkv.shape
    model_rows = stats_model.shape[1]
    tiles = qkv_width // width

    def fixed(shape):
        return pl.BlockSpec(shape, lambda j, m: (0,) * len(shape))

    clamped = pl.BlockSpec((span, width), lambda j, m: (0, jnp.minimum(j, tiles - 1)))
    return pl.pallas_call(
        model_kernel,
        grid_spec=pltpu.PrefetchScalarGridSpec(
            num_scalar_prefetch=1,
            grid=(tiles + 1,),
            in_specs=[
                pl.BlockSpec((width, width), lambda j, m: (jnp.minimum(j, tiles - 1), 0)),
                pl.BlockSpec((span, width), lambda j, m: (m[0], 0)),
                fixed((width, width)),
                pl.BlockSpec((model_rows, width), lambda j, m: (m[0], 0)),
                clamped,
                clamped,
                fixed(stats_model.shape),
                fixed(hidden_small.shape),
                pl.BlockSpec((1, model_rows, width), lambda j, m: (1, 0, 0)),
                pl.BlockSpec((2, width, width), lambda j, m: (0, 0, 0)),
                fixed(proj_weight.shape),
            ],
            out_specs=[
                clamped,
                fixed(stats_model.shape),
                pl.BlockSpec((model_rows, width), lambda j, m: (0, jnp.minimum(j, tiles - 1))),
                fixed((width, span)),
                fixed((model_rows, width)),
                fixed((model_rows, width)),
                fixed((model_rows, width)),
            ],
            scratch_shapes=[
                pltpu.VMEM((span + model_rows, width), f32),
                pltpu.VMEM((2 * model_rows, width), f32),
            ],
        ),
        out_shape=[
            struct(stats_qkv.shape, f32),
            struct(stats_model.shape, f32),
            struct((model_rows, qkv_width), f32),
            struct((width, span), low),
            struct((model_rows, width), f32),
            struct((model_rows, width), f32),
            struct((model_rows, width), low),
        ],
        compiler_params=pltpu.CompilerParams(vmem_limit_bytes=48 * MIB),
        name="model_update",
    )(
        member, qkv_sum, qkv_sum, proj_sum, proj_sum, stats_qkv, roots_qkv, stats_model, hidden_small, roots_model,
        small_roots, proj_weight,
    )


def plain_update(
    sums, stats_model, stats_qkv, stats_hidden, roots_model, roots_qkv, roots_hidden, small_roots, weights
):
    width = sums[0].shape[1]
    member = lax.axis_index("grp")
    model_rows = stats_model.shape[1]
    picked = member * model_rows + jnp.arange(model_rows, dtype=jnp.int32)
    pick = (picked[:, None] == jnp.arange(width, dtype=jnp.int32)[None, :]).astype(low)

    def statistic_update(tall, small_rows, big_rows):
        columns = dot(pick, tall, COLS_BY_COLS)
        small_new = 0.5 * small_rows + 0.5 * dot(columns.astype(low), tall)
        rows = lax.dynamic_slice_in_dim(tall, member * big_rows.shape[0], big_rows.shape[0], 0)
        big_new = 0.5 * big_rows + 0.5 * dot(rows, tall, COLS_BY_COLS)
        return small_new, big_new, columns, rows.astype(f32)

    def product_of(big_root_rows, tall):
        return dot(big_root_rows.astype(low), tall).astype(low)

    qkv, proj, fc1, fc2 = sums
    qkv_left, qkv_right, qkv_gradient, _ = statistic_update(qkv, stats_model[0], stats_qkv)
    proj_right, proj_left, _, proj_gradient = statistic_update(proj, stats_model[2], stats_model[1])
    fc1_left, fc1_right, fc1_gradient, _ = statistic_update(fc1, stats_model[3], stats_hidden[0])
    fc2_right, fc2_left, _, fc2_gradient = statistic_update(fc2, stats_model[4], stats_hidden[1])
    qkv_step = dot(small_roots[0], product_of(roots_qkv, qkv), COLS_BY_COLS).astype(low)
    fc1_step = dot(small_roots[2], product_of(roots_hidden[0], fc1), COLS_BY_COLS).astype(low)
    qkv_weight, proj_weight, fc1_weight, fc2_weight = weights
    qkv_new = qkv_weight - lax.all_to_all(qkv_step, "grp", 0, 1, tiled=True).astype(f32)
    fc1_new = fc1_weight - lax.all_to_all(fc1_step, "grp", 0, 1, tiled=True).astype(f32)
    proj_new = proj_weight - dot(product_of(roots_model[1], proj), small_roots[1])
    fc2_new = fc2_weight - dot(product_of(roots_hidden[1], fc2), small_roots[3])
    new_stats_model = jnp.stack([qkv_left, proj_left, proj_right, fc1_left, fc2_right])
    return (
        (new_stats_model, qkv_right, jnp.stack([fc1_right, fc2_left])),
        (qkv_gradient, proj_gradient, fc1_gradient, fc2_gradient),
        (qkv_new, proj_new, fc1_new, fc2_new),
    )


def shards(
    plain, tokens, cotangent, window_fill, qkv_weight, proj_weight, fc1_weight, fc2_weight, vectors, vector_moments,
    bias_table, table_moments, stats_model, stats_qkv, stats_hidden, roots_model, roots_qkv, roots_hidden,
):
    width = vectors.shape[1]
    head_count = bias_table.shape[1]
    gather = functools.partial(lax.all_gather, axis_name="grp", tiled=True)
    weights = (qkv_weight, proj_weight, fc1_weight, fc2_weight)
    hot = jnp.asarray(diagonal_tables())
    diagonals = lax.dot_general(bias_table, hot, (((0,), (1,)), ((), ())), precision=lax.Precision.HIGHEST)
    if plain:
        fulls = [gather(weight.astype(low)) for weight in weights]
        base = (lax.axis_index(("rep", "grp")) * window_fill.shape[0]).astype(jnp.int32).reshape(1)
        forward = attention_forward(window_fill, base, tokens, *fulls[:2], vectors, diagonals, head_count)
    else:
        forward, fulls = gathered_forward(window_fill, tokens, weights, vectors, diagonals, head_count, 0)
    probs, mixed, normed, context, middle, normed_two = forward
    qkv_full, proj_full, fc1_full, fc2_full = fulls
    if plain:
        fc1_full = jnp.swapaxes(fc1_full.reshape(width, -1, FFN_TILE), 0, 1)[None, None, None]
    roots_low = jnp.stack([roots_model[i] for i in (0, 2, 3, 4)]).astype(low)
    roots_low, normed_two = lax.optimization_barrier((roots_low, normed_two))
    small_roots = gather(roots_low, axis=1)
    ffn_operands = (normed_two, cotangent, middle, fc1_full, fc2_full, vectors)
    ffn = feed_forward(*ffn_operands) if plain else reduced_feed_forward(*ffn_operands, 3)
    layer_output, middle_back, branch_back, fc1_bias_grad, ffn_vec, fc1_term, fc2_term = ffn[:7]
    small_roots, branch_back = lax.optimization_barrier((small_roots, branch_back))
    operands = [branch_back, middle_back, proj_full, context, normed, tokens, qkv_full, vectors, ffn_vec, fc1_bias_grad]
    if plain:
        input_gradient, att_term, small = attention_backward(probs, mixed, operands, head_count)
        small = lax.psum(small, ("rep", "grp"))
        terms = (att_term[: 3 * width], att_term[3 * width :], fc1_term, fc2_term)
        sums = [
            gather(lax.psum(lax.psum_scatter(term, "grp", scatter_dimension=0, tiled=True), "rep")) for term in terms
        ]
    else:
        input_gradient, sums, small = reduced_backward(probs, mixed, operands, head_count, *ffn[5:], 1)
    vector_total = small[: vectors.shape[0]]
    table_total = lax.dot_general(
        hot, small[SMALL_DIAG:], (((0,), (1,)), ((), ())), precision=lax.Precision.HIGHEST
    )
    if plain:
        statistics, gradients, masters = plain_update(
            sums, stats_model, stats_qkv, stats_hidden, roots_model, roots_qkv, roots_hidden, small_roots, weights
        )
        copies = tuple(master.astype(low) for master in masters)
    else:
        member = lax.axis_index("grp").astype(jnp.int32).reshape(1)
        new_stats_hidden, hidden_small, fc1_gradient, fc1_step, fc2_gradient, fc2_new, fc2_copy = hidden_update(
            member, sums[2], stats_hidden, roots_hidden, stats_model, small_roots, fc2_weight
        )
        qkv_right, new_stats_model, qkv_gradient, qkv_step, proj_gradient, proj_new, proj_copy = model_update(
            member, *sums[:2], stats_qkv, roots_qkv, stats_model, hidden_small, roots_model, small_roots, proj_weight
        )
        inboxes = exchange_rows((qkv_step, fc1_step), 2)
        qkv_new, fc1_new, qkv_copy, fc1_copy = apply_steps((qkv_weight, fc1_weight), inboxes)
        statistics = (new_stats_model, qkv_right, new_stats_hidden)
        gradients = (qkv_gradient, proj_gradient, fc1_gradient, fc2_gradient)
        masters = (qkv_new, proj_new, fc1_new, fc2_new)
        copies = (qkv_copy, proj_copy, fc1_copy, fc2_copy)
    total_tokens = tokens.shape[0] * lax.axis_size("rep") * lax.axis_size("grp")
    rate_base = total_tokens ** (-0.5)
    new_vector_moments = 0.9 * vector_moments + 0.1 * vector_total
    new_vectors = vectors - 2.0 * rate_base * new_vector_moments
    new_table_moments = 0.9 * table_moments + 0.1 * table_total
    new_table = bias_table - 8.0 * rate_base * new_table_moments
    return (
        (layer_output, input_gradient)
        + gradients
        + masters
        + copies
        + statistics
        + (new_vectors, new_vector_moments, new_table, new_table_moments)
    )


def solution(mesh):
    tokens, rows, blocks, copied = P(("rep", "grp"), None), P("grp", None), P(None, "grp", None), P()
    plain = (mesh.shape["rep"], mesh.shape["grp"]) != (4, 8)
    return jax.shard_map(
        functools.partial(shards, plain),
        mesh=mesh,
        in_specs=(tokens, tokens, P(("rep", "grp")))
        + (rows,) * 4
        + (copied,) * 4
        + (blocks, rows, blocks) * 2,
        out_specs=(tokens,) * 2 + (rows,) * 12 + (blocks, rows, blocks) + (copied,) * 4,
        check_vma=False,
    )
```

```python
import functools

import jax
import jax.numpy as jnp
import numpy as np
from jax import lax
from jax.experimental import pallas as pl
from jax.experimental.pallas import tpu as pltpu
from jax.sharding import PartitionSpec as P

WT = 144
SIDE = 12
SPAN = 2 * SIDE - 1
LANES = 256
DIAG = 384
ROW_TILE = 144
MIB = 1024 * 1024
low = jnp.bfloat16
f32 = jnp.float32

ROWS_BY_COLS = (((1,), (0,)), ((), ()))
COLS_BY_COLS = (((1,), (1,)), ((), ()))
ROWS_BY_ROWS = (((0,), (0,)), ((), ()))


def dot(left_matrix, right_matrix, dims=ROWS_BY_COLS):
    return lax.dot_general(left_matrix, right_matrix, dims, preferred_element_type=f32)


def standardize(values):
    centred = values - jnp.mean(values, axis=-1, keepdims=True)
    inverse = lax.rsqrt(jnp.mean(centred * centred, axis=-1, keepdims=True) + 1e-05)
    return centred * inverse, inverse


def norm_back(grad, gain, xhat, inverse):
    scaled = grad * gain
    mean_scaled = jnp.mean(scaled, axis=-1, keepdims=True)
    mean_product = jnp.mean(scaled * xhat, axis=-1, keepdims=True)
    return inverse * (scaled - mean_scaled - xhat * mean_product)


def column_sum(values):
    return jnp.sum(values, axis=0, keepdims=True)


def diagonal_tables():
    pair = np.arange(DIAG) - WT
    quotient, rest = pair // SIDE, pair % SIDE
    near = (quotient + SIDE - 1) * SPAN + rest + SIDE - 1
    far = (quotient + SIDE) * SPAN + rest - 1
    near_live = (np.abs(pair) < WT) & (quotient >= 1 - SIDE)
    far_live = (np.abs(pair) < WT) & (rest >= 1) & (quotient < SIDE - 1)
    hot = np.zeros((2, DIAG, SPAN * SPAN), np.float32)
    hot[0, np.arange(DIAG)[near_live], near[near_live]] = 1.0
    hot[1, np.arange(DIAG)[far_live], far[far_live]] = 1.0
    return hot.reshape(2 * DIAG, SPAN * SPAN)


def near_mask(shape, mirrored=False):
    column = lax.rem(lax.broadcasted_iota(jnp.int32, shape, 0), SIDE)
    if mirrored:
        column = SIDE - 1 - column
    rest = lax.rem(lax.broadcasted_iota(jnp.int32, shape, 1), SIDE)
    return column + rest < SIDE


def additive_types(heads):
    slot = np.arange(WT)
    row_high, col_high = slot // SIDE >= SIDE // 2, slot % SIDE >= SIDE // 2
    row_differs = row_high[:, None] != row_high[None, :]
    col_differs = col_high[:, None] != col_high[None, :]
    types = [
        np.where((row_differs & bool(kind // 2)) | (col_differs & bool(kind % 2)), -100.0, 0.0)
        for kind in range(4)
    ]
    return np.tile(np.stack(types), (1, 1, heads)).astype(np.float32)


def stack_mask(heads, head_size):
    lane_head = np.arange(heads * head_size) // head_size
    hot = lane_head[None, None, :] == np.arange(heads)[:, None, None]
    return np.broadcast_to(hot, (heads, WT, heads * head_size)).reshape(heads * WT, -1).astype(low)


def relative_rows(heads, diag_ref, rel_ref):
    mask = near_mask((WT, DIAG))
    for head in range(heads * rel_ref.shape[0]):
        group, place = head // heads, head % heads
        near = diag_ref[head : head + 1, :DIAG]
        far = diag_ref[head : head + 1, DIAG:]
        rolled = pltpu.roll(jnp.where(mask, near, far), DIAG - WT, 1, stride=1, stride_axis=0)
        rel_ref[group, :, place * WT : (place + 1) * WT] = rolled[:, :WT]


def stacked(block, mask_ref, heads):
    return jnp.concatenate([block] * heads, axis=0) * mask_ref[...]


def diagonal_blocks(full, heads, head_size):
    lane_head = lax.broadcasted_iota(jnp.int32, (WT, full.shape[1]), 1) // head_size
    picked = jnp.zeros((WT, full.shape[1]), f32)
    for head in range(heads):
        picked = jnp.where(lane_head == head, full[head * WT : (head + 1) * WT], picked)
    return picked


def for_row_tiles(count, body):
    def step(index, carry):
        body(pl.ds(pl.multiple_of(index * ROW_TILE, ROW_TILE), ROW_TILE))
        return carry

    lax.fori_loop(0, count // ROW_TILE, step, 0)


class Forward:
    def __init__(self, heads, head_size, refs):
        self.heads, self.head_size = heads, head_size
        self.fill, self.tokens, self.vec, self.diag, self.add, self.mask = refs[:6]
        self.probs, self.mixed_out, self.normed, self.context, self.middle, self.normed_two = refs[6:12]
        self.mixed, self.added, self.rel = refs[12:15]
        self.count, self.width = self.tokens.shape
        self.groups = self.width // LANES

    def norm_one(self):
        def body(rows):
            xhat, _ = standardize(self.tokens[rows, :].astype(f32))
            self.normed[rows, :] = (xhat * self.vec[0:1, :] + self.vec[1:2, :]).astype(low)

        for_row_tiles(self.count, body)

    def mix(self, weight_tile):
        for part in range(3):
            for tile in range(self.groups):
                start = part * self.width + tile * LANES
                sums = dot(self.normed[...], weight_tile(start))
                if part != 1:
                    row = 2 if part == 0 else 3
                    sums = sums + self.vec[row : row + 1, tile * LANES : (tile + 1) * LANES]
                self.mixed[:, start : start + LANES] = sums.astype(low)

    def attend(self, window, first_window):
        width, heads = self.width, self.heads
        rows = pl.ds(pl.multiple_of(window * WT, WT), WT)
        self.mixed_out[...] = self.mixed[rows, :]
        kind = lax.rem(first_window + window, 4)
        slot = lax.broadcasted_iota(jnp.int32, self.added.shape, 0)
        self.added[...] = jnp.where(slot < self.fill[window], self.add[kind], -1e30)
        for group in range(self.groups):
            query, key, value = (
                self.mixed[rows, part * width + group * LANES : part * width + (group + 1) * LANES]
                for part in range(3)
            )
            scores = dot(key, stacked(query, self.mask, heads), COLS_BY_COLS) * self.head_size ** (-0.5)
            scores = scores + self.rel[group] + self.added[...]
            exponent = jnp.exp(scores - jnp.max(scores, axis=0, keepdims=True))
            probs = (exponent * (1.0 / jnp.sum(exponent, axis=0, keepdims=True))).astype(low)
            self.probs[group] = probs
            full = dot(probs, value, ROWS_BY_ROWS)
            self.context[rows, group * LANES : (group + 1) * LANES] = diagonal_blocks(
                full, heads, self.head_size
            ).astype(low)

    def finish(self, weight_tile):
        for tile in range(self.groups):
            span = slice(tile * LANES, (tile + 1) * LANES)
            self.middle[:, span] = (
                self.tokens[:, span].astype(f32) + dot(self.context[...], weight_tile(tile * LANES)) + self.vec[4:5, span]
            )

        def body(rows):
            xhat, _ = standardize(self.middle[rows, :])
            self.normed_two[rows, :] = (xhat * self.vec[5:6, :] + self.vec[6:7, :]).astype(low)

        for_row_tiles(self.count, body)


def plain_forward_kernel(heads, head_size, base_ref, qkv_ref, proj_ref, *refs):
    work = Forward(heads, head_size, refs)
    window = pl.program_id(0)

    @pl.when(window == 0)
    def _():
        relative_rows(heads, work.diag, work.rel)
        work.norm_one()
        work.mix(lambda start: qkv_ref[:, start : start + LANES])

    work.attend(window, base_ref[0])

    @pl.when(window == pl.num_programs(0) - 1)
    def _():
        work.finish(lambda start: proj_ref[:, start : start + LANES])


def whole(shape):
    return pl.BlockSpec(shape, lambda *_: (0,) * len(shape), pipeline_mode=pl.Buffered(1))


def struct(shape, dtype):
    return jax.ShapeDtypeStruct(shape, dtype)


HBM = pl.BlockSpec(memory_space=pl.ANY)
SMEM = pl.BlockSpec(memory_space=pltpu.SMEM)


def forward_parts(fill, tokens, vectors, diagonals, head_count):
    count, width = tokens.shape
    windows = fill.shape[0]
    head_size = width // head_count
    heads = LANES // head_size
    groups = width // LANES
    operands = [tokens, vectors, diagonals, jnp.asarray(additive_types(heads)), jnp.asarray(stack_mask(heads, head_size))]
    in_specs = [SMEM] + [whole(operand.shape) for operand in operands]
    out_specs = [
        pl.BlockSpec((groups, WT, heads * WT), lambda w: (w, 0, 0)),
        pl.BlockSpec((WT, 3 * width), lambda w: (w, 0)),
    ] + [whole((count, width))] * 4
    out_shape = [
        struct((windows * groups, WT, heads * WT), low),
        struct((count, 3 * width), low),
        struct((count, width), low),
        struct((count, width), low),
        struct((count, width), f32),
        struct((count, width), low),
    ]
    scratch = [
        pltpu.VMEM((count, 3 * width), low),
        pltpu.VMEM((WT, heads * WT), f32),
        pltpu.VMEM((groups, WT, heads * WT), f32),
    ]
    return (heads, head_size), [fill] + operands, in_specs, out_specs, out_shape, scratch


def attention_forward(fill, base, tokens, qkv_full, proj_full, vectors, diagonals, head_count):
    sizes, operands, in_specs, out_specs, out_shape, scratch = forward_parts(
        fill, tokens, vectors, diagonals, head_count
    )
    return pl.pallas_call(
        functools.partial(plain_forward_kernel, *sizes),
        grid=(fill.shape[0],),
        in_specs=[SMEM, whole(qkv_full.shape), whole(proj_full.shape)] + in_specs,
        out_specs=out_specs,
        out_shape=out_shape,
        scratch_shapes=scratch,
        compiler_params=pltpu.CompilerParams(vmem_limit_bytes=56 * MIB),
        name="attention_forward",
    )(base, qkv_full, proj_full, *operands)


FFN_TILE = 512
FFN_ROWS = 336
FFN_CHUNK = 16


class FeedForward:
    def __init__(self, refs):
        self.normed, self.cot, self.middle, self.fc1, self.fc2, self.bias, self.vec = refs[:7]
        self.out, self.middle_back, self.branch_back, self.bias_grad, self.vec_grad = refs[7:12]
        self.out_sum, self.back_sum, self.hidden, self.active_back, self.active, self.hidden_back = refs[12:18]
        self.count, self.width = self.cot.shape

    def begin(self):
        self.out_sum[...] = jnp.zeros_like(self.out_sum)
        self.back_sum[...] = jnp.zeros_like(self.back_sum)

    def tile(self):
        fc1 = self.fc1[...].reshape(self.width, FFN_TILE)
        fc2 = self.fc2[...]
        spans = [slice(start, start + FFN_ROWS) for start in range(0, self.count, FFN_ROWS)]

        def enter(rows):
            self.hidden[rows, :] = dot(self.normed[rows, :], fc1)
            self.active_back[rows, :] = dot(self.cot[rows, :], fc2, COLS_BY_COLS)

        def bend(rows):
            total = jnp.zeros((8, FFN_TILE), f32)
            for start in range(rows.start, rows.stop, FFN_CHUNK):
                chunk = slice(start, start + FFN_CHUNK)
                hidden = self.hidden[chunk, :] + self.bias[...]
                bell = jnp.exp(hidden * hidden * -0.5)
                below = 0.5 + 0.5 * lax.erf(hidden * (0.5**0.5))
                self.active[chunk, :] = (hidden * below).astype(low)
                slope = below + hidden * bell * ((2.0 * np.pi) ** -0.5)
                back = (self.active_back[chunk, :] * slope).astype(low)
                self.hidden_back[chunk, :] = back
                total = total + jnp.sum(back.astype(f32).reshape(-1, 8, FFN_TILE), axis=0)
            return total

        def leave(rows):
            self.out_sum[rows, :] += dot(self.active[rows, :], fc2)
            self.back_sum[rows, :] += dot(self.hidden_back[rows, :], fc1, COLS_BY_COLS)

        total = jnp.zeros((8, FFN_TILE), f32)
        amount = len(spans)
        for index in range(amount + 2):
            if index < amount:
                enter(spans[index])
            if 0 <= index - 1 < amount:
                total = total + bend(spans[index - 1])
            if 0 <= index - 2 < amount:
                leave(spans[index - 2])
        self.bias_grad[...] = column_sum(total)
        fc1_grad = dot(self.hidden_back[...], self.normed[...], ROWS_BY_ROWS).astype(low)
        fc2_grad = dot(self.active[...], self.cot[...], ROWS_BY_ROWS).astype(low)
        return fc1_grad, fc2_grad

    def finish(self):
        self.vec_grad[...] = jnp.zeros_like(self.vec_grad)

        def body(rows):
            middle = self.middle[rows, :]
            cot = self.cot[rows, :].astype(f32)
            self.out[rows, :] = (middle + self.out_sum[rows, :] + self.vec[7:8, :]).astype(low)
            xhat, inverse = standardize(middle)
            grad = self.back_sum[rows, :]
            middle_back = cot + norm_back(grad, self.vec[5:6, :], xhat, inverse)
            self.middle_back[rows, :] = middle_back
            branch_back = middle_back.astype(low)
            self.branch_back[rows, :] = branch_back
            self.vec_grad[0:1, :] += column_sum(branch_back.astype(f32))
            self.vec_grad[1:2, :] += column_sum(grad * xhat)
            self.vec_grad[2:3, :] += column_sum(grad)
            self.vec_grad[3:4, :] += column_sum(cot)

        for_row_tiles(self.count, body)


def plain_feed_forward_kernel(*refs):
    work = FeedForward(refs[:12] + refs[14:])
    fc1_grad_ref, fc2_grad_ref = refs[12:14]
    step = pl.program_id(0)

    @pl.when(step == 0)
    def _():
        work.begin()

    fc1_grad_ref[...], fc2_grad_ref[...] = work.tile()

    @pl.when(step == pl.num_programs(0) - 1)
    def _():
        work.finish()


def feed_forward_parts(normed, cotangent, middle, fc1_tiles, fc2_full, vectors):
    count, width = cotangent.shape
    hidden_width = fc2_full.shape[0]
    tiles = hidden_width // FFN_TILE
    bias = vectors[8:].reshape(1, hidden_width)
    in_specs = (
        [whole(x.shape) for x in (normed, cotangent, middle)]
        + [
            pl.BlockSpec(fc1_tiles.shape[:3] + (1,) + fc1_tiles.shape[4:], lambda f: (0, 0, 0, f, 0, 0)),
            pl.BlockSpec((FFN_TILE, width), lambda f: (f, 0)),
            pl.BlockSpec((1, FFN_TILE), lambda f: (0, f)),
            whole(vectors.shape),
        ]
    )
    out_specs = [whole((count, width))] * 3 + [pl.BlockSpec((1, FFN_TILE), lambda f: (0, f)), whole((8, width))]
    out_shape = [
        struct((count, width), low),
        struct((count, width), f32),
        struct((count, width), low),
        struct((1, hidden_width), f32),
        struct((8, width), f32),
    ]
    scratch = [
        pltpu.VMEM((count, width), f32),
        pltpu.VMEM((count, width), f32),
        pltpu.VMEM((count, FFN_TILE), f32),
        pltpu.VMEM((count, FFN_TILE), f32),
        pltpu.VMEM((count, FFN_TILE), low),
        pltpu.VMEM((count, FFN_TILE), low),
    ]
    operands = [normed, cotangent, middle, fc1_tiles, fc2_full, bias, vectors]
    return operands, in_specs, out_specs, out_shape, scratch, tiles


def feed_forward(normed, cotangent, middle, fc1_tiles, fc2_full, vectors):
    operands, in_specs, out_specs, out_shape, scratch, tiles = feed_forward_parts(
        normed, cotangent, middle, fc1_tiles, fc2_full, vectors
    )
    width = cotangent.shape[1]
    return pl.pallas_call(
        plain_feed_forward_kernel,
        grid=(tiles,),
        in_specs=in_specs,
        out_specs=out_specs + [pl.BlockSpec((FFN_TILE, width), lambda f: (f, 0))] * 2,
        out_shape=out_shape + [struct((tiles * FFN_TILE, width), low)] * 2,
        scratch_shapes=scratch,
        compiler_params=pltpu.CompilerParams(vmem_limit_bytes=56 * MIB),
        name="feed_forward",
    )(*operands)


class Backward:
    def __init__(self, heads, head_size, refs, proj_grad, qkv_grad):
        self.heads, self.head_size = heads, head_size
        self.probs, self.query, self.key, self.value = refs[:4]
        self.branch_back, self.middle_back, self.proj, self.context, self.normed, self.tokens, self.qkv = refs[4:11]
        self.vec, self.mask, self.ffn_grad, self.bias_grad = refs[11:15]
        self.input_grad = refs[15]
        self.context_back, self.mixed_back, self.pairs, self.normed_back, self.small = refs[16:]
        self.proj_grad, self.qkv_grad = proj_grad, qkv_grad
        self.count, self.width = self.tokens.shape
        self.groups = self.width // LANES
        self.windows = self.count // WT

    def begin(self):
        self.pairs[...] = jnp.zeros_like(self.pairs)
        self.small[...] = jnp.zeros_like(self.small)
        for tile in range(self.groups):
            span = slice(tile * LANES, (tile + 1) * LANES)
            self.context_back[:, span] = dot(self.branch_back[...], self.proj[span, :], COLS_BY_COLS).astype(low)

    def begin_grads(self):
        for tile in range(self.groups):
            span = slice(tile * LANES, (tile + 1) * LANES)
            self.proj_grad(tile, dot(self.context[:, span], self.branch_back[...], ROWS_BY_ROWS).astype(low))

    def columns(self, part, group):
        return pl.ds(pl.multiple_of(part * self.width + group * LANES, LANES), LANES)

    def attend(self, group, window):
        heads = self.heads
        score_scale = self.head_size ** (-0.5)
        rows = pl.ds(pl.multiple_of(window * WT, WT), WT)
        query, key, value = self.query[...], self.key[...], self.value[...]
        probs_low = self.probs[0]
        probs = probs_low.astype(f32)
        back_stack = stacked(self.context_back[rows, self.columns(0, group)], self.mask, heads)
        value_back = dot(probs_low, back_stack)
        product = probs * dot(value, back_stack, COLS_BY_COLS)
        scores_back = (product - probs * jnp.sum(product, axis=0, keepdims=True)).astype(low)
        self.pairs[group] += scores_back.astype(f32)
        key_back = dot(scores_back, stacked(query, self.mask, heads)) * score_scale
        full = dot(scores_back, key, ROWS_BY_ROWS)
        query_back = diagonal_blocks(full, heads, self.head_size) * score_scale
        for part, back in enumerate((query_back, key_back, value_back)):
            self.mixed_back[rows, self.columns(part, group)] = back.astype(low)

    def group_grads(self, group):
        for part in range(3):
            block = self.mixed_back[:, self.columns(part, group)]
            self.qkv_grad(part, group, dot(block, self.normed[...], ROWS_BY_ROWS).astype(low))

    def normed_back_step(self):
        for tile in range(self.groups):
            span = slice(tile * LANES, (tile + 1) * LANES)
            self.normed_back[:, span] = dot(self.mixed_back[...], self.qkv[span, :], COLS_BY_COLS)

    def finish(self):
        width = self.width
        for row, part in ((2, 0), (3, 2)):

            def body(rows, row=row, part=part):
                block = self.mixed_back[rows, part * width : (part + 1) * width]
                self.small[row : row + 1, :] += column_sum(block.astype(f32))

            for_row_tiles(self.count, body)

        def body(rows):
            xhat, inverse = standardize(self.tokens[rows, :].astype(f32))
            grad = self.normed_back[rows, :]
            back = self.middle_back[rows, :] + norm_back(grad, self.vec[0:1, :], xhat, inverse)
            self.input_grad[rows, :] = back.astype(low)
            self.small[0:1, :] += column_sum(grad * xhat)
            self.small[1:2, :] += column_sum(grad)

        for_row_tiles(self.count, body)
        self.small[4:8, :] = self.ffn_grad[0:4, :]
        for row in range(self.bias_grad.shape[1] // width):
            self.small[8 + row : 9 + row, :] = self.bias_grad[:, row * width : (row + 1) * width]

    def diagonals(self):
        mask = near_mask((WT, DIAG), mirrored=True)
        order = [lax.broadcasted_iota(jnp.int32, (WT, WT), axis) for axis in range(2)]
        mirror = jnp.where(order[0] + order[1] == WT - 1, 1.0, 0.0).astype(f32)
        for group in range(self.groups):
            self.pairs[group] = lax.dot_general(
                mirror, self.pairs[group], ROWS_BY_COLS, precision=lax.Precision.HIGHEST, preferred_element_type=f32
            )
        for head in range(self.groups * self.heads):
            group, place = head // self.heads, head % self.heads
            block = self.pairs[group, :, place * WT : (place + 1) * WT]
            block = jnp.concatenate([block, jnp.zeros((WT, DIAG - WT), f32)], axis=1)
            rolled = pltpu.roll(block, 1, 1, stride=1, stride_axis=0)
            row = SMALL_DIAG + head
            self.small[row : row + 1, :DIAG] = column_sum(jnp.where(mask, rolled, 0.0))
            self.small[row : row + 1, DIAG : 2 * DIAG] = column_sum(jnp.where(mask, 0.0, rolled))


SMALL_DIAG = 16


def plain_backward_kernel(heads, head_size, *refs):
    weight_grad = refs[16]
    width = weight_grad.shape[1]

    def proj_grad(tile, value):
        weight_grad[3 * width + tile * LANES : 3 * width + (tile + 1) * LANES, :] = value

    def qkv_grad(part, group, value):
        weight_grad[pl.ds(pl.multiple_of(part * width + group * LANES, LANES), LANES), :] = value

    work = Backward(heads, head_size, refs[:16] + refs[18:], proj_grad, qkv_grad)
    step = pl.program_id(0)
    windows = work.windows
    busy = windows * work.groups
    group, window = step // windows, lax.rem(step, windows)

    @pl.when(step == 0)
    def _():
        work.begin()
        work.begin_grads()

    @pl.when(step < busy)
    def _():
        work.attend(group, window)

    @pl.when((step < busy) & (window == windows - 1))
    def _():
        work.group_grads(group)

    @pl.when(step == busy)
    def _():
        work.normed_back_step()
        work.finish()
        work.diagonals()
        refs[17][...] = work.small[...]


def backward_parts(probs, mixed, operands, head_count):
    count, width = operands[0].shape
    windows = count // WT
    head_size = width // head_count
    heads = LANES // head_size
    groups = width // LANES
    last = windows * groups - 1
    mask = jnp.asarray(stack_mask(heads, head_size))
    operands = operands[:8] + [mask] + operands[8:]

    def place(step):
        step = jnp.minimum(step, last)
        return step // windows, lax.rem(step, windows)

    def probs_map(step):
        group, window = place(step)
        return window * groups + group, 0, 0

    def mixed_map(part):
        def index(step):
            group, window = place(step)
            return window, part * groups + group

        return index

    in_specs = (
        [pl.BlockSpec((1, WT, heads * WT), probs_map)]
        + [pl.BlockSpec((WT, LANES), mixed_map(part)) for part in range(3)]
        + [whole(operand.shape) for operand in operands]
    )
    scratch = [
        pltpu.VMEM((count, width), low),
        pltpu.VMEM((count, 3 * width), low),
        pltpu.VMEM((groups, WT, heads * WT), f32),
        pltpu.VMEM((count, width), f32),
        pltpu.VMEM((SMALL_DIAG + head_count, width), f32),
    ]
    return (heads, head_size), [probs, mixed, mixed, mixed] + operands, in_specs, scratch, last + 1


def attention_backward(probs, mixed, operands, head_count):
    sizes, operands, in_specs, scratch, busy = backward_parts(probs, mixed, operands, head_count)
    count, width = operands[4].shape
    small_shape = (SMALL_DIAG + head_count, width)
    return pl.pallas_call(
        functools.partial(plain_backward_kernel, *sizes),
        grid=(busy + 1,),
        in_specs=in_specs,
        out_specs=[whole((count, width)), whole((4 * width, width)), whole(small_shape)],
        out_shape=[struct((count, width), low), struct((4 * width, width), low), struct(small_shape, f32)],
        scratch_shapes=scratch,
        compiler_params=pltpu.CompilerParams(vmem_limit_bytes=60 * MIB),
        name="attention_backward",
    )(*operands)


MESH = pl.DeviceIdType.MESH


class Peers:
    def __init__(self):
        self.z = lax.axis_index("rep")
        place = lax.axis_index("grp")
        self.c = lax.rem(place, 2)
        self.x = lax.rem(place // 2, 2)
        self.y = place // 4
        self.core_peer = (self.z, place + 1 - 2 * self.c)
        self.x_peer = (self.z, place + 2 - 4 * self.x)
        self.y_peer = (self.z, place + 4 - 8 * self.y)
        self.odd = lax.rem(self.z, 2)
        self.even = 1 - self.odd
        to_x, to_y = 2 - 4 * self.x, 4 - 8 * self.y
        self.first_peer = (self.z, place + self.even * to_x + self.odd * to_y)
        self.second_peer = (self.z, place + self.odd * to_x + self.even * to_y)
        self.pair_peer = (self.z + 1 - 2 * self.odd, place)
        self.z_places = [lax.rem(self.z + step, 4) for step in range(1, 4)]
        self.z_peers = [(there, place) for there in self.z_places]

    def plane(self):
        return [self.core_peer, self.x_peer, self.y_peer]

    def everyone(self):
        return self.plane() + self.z_peers


def meet(peers):
    barrier = pltpu.get_barrier_semaphore()
    for peer in peers:
        pl.semaphore_signal(barrier, inc=1, device_id=peer, device_id_type=MESH)
    pl.semaphore_wait(barrier, len(peers))


class Copies:
    def __init__(self, send_sems, recv_sems):
        self.send_sems, self.recv_sems = send_sems, recv_sems
        self.made = []

    def make(self, ends, peer):
        copy = Copy(self, len(self.made), ends, peer)
        self.made.append(copy)
        copy.build().start()
        return copy

    def drain(self):
        for copy in self.made:
            copy.build().wait_send()


class Copy:
    def __init__(self, owner, number, ends, peer):
        self.owner, self.number, self.ends, self.peer = owner, number, ends, peer

    def build(self):
        source, target = self.ends()
        return pltpu.make_async_remote_copy(
            src_ref=source,
            dst_ref=target,
            send_sem=self.owner.send_sems.at[self.number],
            recv_sem=self.owner.recv_sems.at[self.number],
            device_id=self.peer,
            device_id_type=MESH,
        )

    def wait_recv(self):
        self.build().wait_recv()


def same(place):
    return lambda: (place(), place())


class Gather:
    def __init__(self, me, copies, source, out):
        self.me, self.copies, self.source, self.out = me, copies, source, out
        self.half = out.shape[3] // 2
        self.across = []

    def block(self, flip_y, flip_x):
        me = self.me
        return self.out.at[1 - me.y if flip_y else me.y, 1 - me.x if flip_x else me.x, me.c]

    def start(self):
        me = self.me

        def ends():
            return self.source(), self.block(False, False)

        self.by_x = self.copies.make(ends, me.x_peer)
        self.by_y = self.copies.make(ends, me.y_peer)
        self.across.append(self.copies.make(ends, me.core_peer))

    def relay(self):
        me = self.me
        self.by_x.wait_recv()
        to_y = self.copies.make(same(lambda: self.block(False, True).at[pl.ds(0, self.half)]), me.y_peer)
        self.by_y.wait_recv()
        to_x = self.copies.make(same(lambda: self.block(True, False).at[pl.ds(self.half, self.half)]), me.x_peer)
        self.relayed = (to_x, to_y)
        self.across.append(self.copies.make(same(lambda: self.block(False, True)), me.core_peer))
        self.across.append(self.copies.make(same(lambda: self.block(True, False)), me.core_peer))

    def cross(self):
        for copy in self.relayed:
            copy.wait_recv()
        self.across.append(self.copies.make(same(lambda: self.block(True, True)), self.me.core_peer))

    def wait(self):
        for copy in self.across:
            copy.wait_recv()


class PairGather:
    def __init__(self, me, copies, source, out, span):
        self.me, self.copies, self.source, self.out, self.span = me, copies, source, out, span
        self.across = []

    def block(self, flip_y, flip_x):
        me = self.me
        return self.out.at[me.y + flip_y * (1 - 2 * me.y), me.x + flip_x * (1 - 2 * me.x), me.c].at[self.span]

    def give(self, flip_y, flip_x, peer):
        return self.copies.make(same(lambda: self.block(flip_y, flip_x)), peer)

    def start(self):
        me = self.me

        def ends():
            return self.source.at[self.span], self.block(0, 0)

        self.first = self.copies.make(ends, me.first_peer)
        self.across.append(self.copies.make(ends, me.core_peer))

    def relay(self):
        me = self.me
        self.first.wait_recv()
        self.second = self.give(me.odd, me.even, me.second_peer)
        self.third = self.give(me.odd, me.even, me.pair_peer)
        self.across.append(self.give(me.odd, me.even, me.core_peer))

    def cross(self):
        me = self.me
        self.second.wait_recv()
        self.across.append(self.give(1, 1, me.core_peer))
        self.third.wait_recv()
        self.across.append(self.give(me.even, me.odd, me.core_peer))

    def wait(self):
        for copy in self.across:
            copy.wait_recv()


def gathered_forward_kernel(heads, head_size, *refs):
    qkv_shard, proj_shard, fc1_shard, fc2_shard = refs[:4]
    outs = refs[10:20]
    qkv_out, proj_out, fc1_out, fc2_out = outs[6:]
    scratch = refs[20:]
    work = Forward(heads, head_size, refs[4:10] + outs[:6] + scratch[:3])
    qkv_full, proj_full, fc1_low, fc2_low, send_sems, recv_sems, local_sems = scratch[3:]
    me = Peers()
    copies = Copies(send_sems, recv_sems)
    own = (me.y, me.x, me.c)
    qkv = Gather(me, copies, lambda: qkv_full.at[own], qkv_full)
    proj = Gather(me, copies, lambda: proj_full.at[own], proj_full)
    hidden_parts = []
    for source, out in ((fc1_low, fc1_out), (fc2_low, fc2_out)):
        half = out.shape[3] // 2
        hidden_parts += [PairGather(me, copies, source, out, pl.ds(start, half)) for start in (0, half)]

    def local(index):
        source = (fc1_low, fc2_low, qkv_full, proj_full)[index]
        target = (fc1_out, fc2_out, qkv_out, proj_out)[index]
        return pltpu.make_async_copy(source, target.at[own] if index < 2 else target, local_sems.at[index])

    window = pl.program_id(0)
    first_window = (me.z * 8 + me.y * 4 + me.x * 2 + me.c) * pl.num_programs(0)

    def weight_tile(full):
        def tile(start):
            return full[:, :, :, :, start : start + LANES].reshape(-1, LANES)

        return tile

    @pl.when(window == 0)
    def _():
        qkv_full[own] = qkv_shard[...].astype(low)
        proj_full[own] = proj_shard[...].astype(low)
        meet(me.plane() + [me.pair_peer])
        qkv.start()
        proj.start()
        for tile in range(fc1_low.shape[0]):
            fc1_low[tile] = fc1_shard[:, tile * FFN_TILE : (tile + 1) * FFN_TILE].astype(low)
        fc2_low[...] = fc2_shard[...].astype(low)
        work.norm_one()
        relative_rows(heads, work.diag, work.rel)
        qkv.relay()
        proj.relay()
        qkv.cross()
        for part in hidden_parts:
            part.start()
        local(0).start()
        local(1).start()
        qkv.wait()
        local(2).start()
        work.mix(weight_tile(qkv_full))

    for at, steps in (
        (1, (proj.cross, hidden_parts[0].relay)),
        (2, (hidden_parts[1].relay,)),
        (3, (hidden_parts[0].cross,)),
        (4, (hidden_parts[2].relay,)),
        (5, (hidden_parts[1].cross,)),
        (6, (hidden_parts[3].relay,)),
    ):

        @pl.when(window == at)
        def _():
            for advance in steps:
                advance()

    work.attend(window, first_window)

    @pl.when(window == pl.num_programs(0) - 1)
    def _():
        proj.wait()
        local(3).start()
        work.finish(weight_tile(proj_full))
        hidden_parts[2].cross()
        hidden_parts[3].cross()
        for part in hidden_parts:
            part.wait()
        for index in range(4):
            local(index).wait()
        copies.drain()


def gathered_forward(fill, tokens, weights, vectors, diagonals, head_count, collective_id):
    sizes, operands, in_specs, out_specs, out_shape, scratch = forward_parts(
        fill, tokens, vectors, diagonals, head_count
    )
    shapes = [weight.shape for weight in weights]
    shapes[2] = (shapes[2][1] // FFN_TILE, shapes[2][0], FFN_TILE)
    fulls = [(2, 2, 2) + shape for shape in shapes]
    results = pl.pallas_call(
        functools.partial(gathered_forward_kernel, *sizes),
        grid=(fill.shape[0],),
        in_specs=[whole(weight.shape) for weight in weights] + in_specs,
        out_specs=out_specs + [HBM] * 4,
        out_shape=out_shape + [struct(full, low) for full in fulls],
        scratch_shapes=scratch
        + [pltpu.VMEM(fulls[0], low), pltpu.VMEM(fulls[1], low)]
        + [pltpu.VMEM(shape, low) for shape in shapes[2:]]
        + [pltpu.SemaphoreType.DMA((44,)), pltpu.SemaphoreType.DMA((44,)), pltpu.SemaphoreType.DMA((4,))],
        compiler_params=pltpu.CompilerParams(
            collective_id=collective_id, has_side_effects=True, vmem_limit_bytes=58 * MIB
        ),
        name="gathered_forward",
    )(*weights, *operands)
    qkv_full, proj_full, fc1_tiles, fc2_full = results[6:]
    return results[:6], [
        qkv_full.reshape(-1, shapes[0][1]), proj_full.reshape(-1, shapes[1][1]), fc1_tiles,
        fc2_full.reshape(-1, shapes[3][1]),
    ]


PIECE = 16


class Reduction:
    def __init__(self, me, copies, term, mine, out, buffers, load_sems, store_sems):
        self.me, self.copies, self.term, self.mine, self.out = me, copies, term, mine, out
        self.core_in, self.first_in, self.second_in, self.z_in, self.final = buffers
        self.load_sems, self.store_sems = load_sems, store_sems
        self.parts, self.half = buffers[0].shape[1], buffers[0].shape[-1] // 2
        self.kept = None
        self.core, self.first, self.second, self.over_z, self.last_z, self.spread, self.relayed, self.across = (
            {} for _ in range(8)
        )

    def sides(self):
        return pl.ds(0, self.half), pl.ds(self.half, self.half)

    def z_columns(self, z):
        return pl.ds(pl.multiple_of(lax.rem(z, 2) * self.half, self.half), self.half)

    def loop(self, amount, body):
        def step(index, carry):
            body(index)
            return carry

        lax.fori_loop(0, amount, step, 0)

    def load(self, k):
        ref, at = self.mine
        return pltpu.make_async_copy(self.term(k, self.me.c), ref.at[k], self.load_sems.at[k])

    def store(self, k):
        me = self.me
        return pltpu.make_async_copy(
            self.final.at[k], self.out(k, me.c, me.x, me.y, (me.z // 2, slice(None), self.z_columns(me.z))),
            self.store_sems.at[k],
        )

    def start(self, k):
        me = self.me
        self.core[k] = self.copies.make(lambda: (self.term(k, 1 - me.c), self.core_in.at[k]), me.core_peer)
        if self.load_sems is not None:
            self.load(k).start()

    def finish_core(self, k):
        me = self.me
        ref, at = self.mine
        if self.load_sems is not None:
            self.load(k).wait()
        self.core[k].wait_recv()

        def add(step):
            part, x, y, row = step // 8, lax.rem(step // 4, 2), lax.rem(step // 2, 2), lax.rem(step, 2)
            place = at(k, part, x, y, row)
            ref[place] = ref[place] + self.core_in[k, part, x, y, row]

        self.loop(8 * self.parts, add)
        every = slice(None)
        self.first[k] = (
            self.copies.make(
                lambda: (
                    ref.at[at(k, every, 1 - me.x, every, every) + (every, self.sides()[0])], self.first_in.at[k, 0],
                ),
                me.x_peer,
            ),
            self.copies.make(
                lambda: (
                    ref.at[at(k, every, every, 1 - me.y, every) + (every, self.sides()[1])], self.first_in.at[k, 1],
                ),
                me.y_peer,
            ),
        )

    def finish_first(self, k):
        me = self.me
        ref, at = self.mine
        for copy in self.first[k]:
            copy.wait_recv()
        half = self.half

        def add(step):
            part, other, row = step // 4, lax.rem(step // 2, 2), lax.rem(step, 2)
            place = at(k, part, me.x, other, row) + (slice(None), slice(0, half))
            ref[place] = ref[place] + self.first_in[k, 0, part, other, row]
            place = at(k, part, other, me.y, row) + (slice(None), slice(half, 2 * half))
            ref[place] = ref[place] + self.first_in[k, 1, part, other, row]

        self.loop(4 * self.parts, add)
        every = slice(None)
        self.second[k] = (
            self.copies.make(
                lambda: (
                    ref.at[at(k, every, me.x, 1 - me.y, every) + (every, self.sides()[0])], self.second_in.at[k, 0],
                ),
                me.y_peer,
            ),
            self.copies.make(
                lambda: (
                    ref.at[at(k, every, 1 - me.x, me.y, every) + (every, self.sides()[1])], self.second_in.at[k, 1],
                ),
                me.x_peer,
            ),
        )

    def add_second(self, k):
        me = self.me
        ref, at = self.mine
        for copy in self.second[k]:
            copy.wait_recv()
        half = self.half

        def add(step):
            part, row = step // 2, lax.rem(step, 2)
            for side, span in enumerate((slice(0, half), slice(half, 2 * half))):
                place = at(k, part, me.x, me.y, row) + (slice(None), span)
                ref[place] = ref[place] + self.second_in[k, side, part, row]

        self.loop(2 * self.parts, add)

    def store_piece(self, k, target):
        ref, at = self.mine
        every = slice(None)
        source = ref.at[at(k, every, self.me.x, self.me.y, every)]
        return pltpu.make_async_copy(source, target.at[k], self.store_sems.at[k])

    def keep_piece(self, k, source):
        return pltpu.make_async_copy(
            source.at[k, :, self.me.z // 2, :, self.z_columns(self.me.z)], self.z_in.at[k, self.me.z], self.load_sems.at[k]
        )

    def start_z(self, k, source):
        self.kept = source
        self.over_z[k] = [
            self.copies.make(
                lambda there=there: (
                    source.at[k, :, there // 2, :, self.z_columns(there)], self.z_in.at[k, self.me.z],
                ),
                peer,
            )
            for there, peer in zip(self.me.z_places, self.me.z_peers)
        ]
        self.keep_piece(k, source).start()

    def finish_second(self, k):
        me = self.me
        ref, at = self.mine
        self.add_second(k)

        def piece(part, z):
            return at(k, part, me.x, me.y, z // 2) + (slice(None), self.z_columns(z))

        self.over_z[k] = [
            self.copies.make(lambda there=there: (ref.at[piece(slice(None), there)], self.z_in.at[k, me.z]), peer)
            for there, peer in zip(me.z_places, me.z_peers)
        ]

        def keep(part):
            self.z_in[k, me.z, part] = ref[piece(part, me.z)]

        self.loop(self.parts, keep)

    def finish_z(self, k):
        me = self.me
        for copy in self.over_z[k]:
            copy.wait_recv()
        if self.kept is not None:
            self.keep_piece(k, self.kept).wait()

        def add(part):
            total = self.z_in[k, 0, part].astype(f32)
            for place in range(1, 4):
                total = total + self.z_in[k, place, part].astype(f32)
            self.final[k, part] = total.astype(low)

        self.loop(self.parts, add)
        self.last_z[k] = [
            self.copies.make(
                lambda: (
                    self.final.at[k],
                    self.out(k, me.c, me.x, me.y, (me.z // 2, slice(None), self.z_columns(me.z))),
                ),
                peer,
            )
            for peer in me.z_peers
        ]
        self.store(k).start()

    def finish_last_z(self, k):
        me = self.me
        for copy in self.last_z[k]:
            copy.wait_recv()
        self.store(k).wait()
        own = same(lambda: self.out(k, me.c, me.x, me.y, ()))
        self.spread[k] = [self.copies.make(own, peer) for peer in (me.x_peer, me.y_peer)]
        self.across[k] = [self.copies.make(own, me.core_peer)]

    def finish_spread(self, k):
        me = self.me
        by_x, by_y = self.spread[k]
        every = slice(None)
        by_y.wait_recv()
        to_x = self.copies.make(
            same(lambda: self.out(k, me.c, me.x, 1 - me.y, (every, every, self.sides()[0]))), me.x_peer
        )
        by_x.wait_recv()
        to_y = self.copies.make(
            same(lambda: self.out(k, me.c, 1 - me.x, me.y, (every, every, self.sides()[1]))), me.y_peer
        )
        self.relayed[k] = (to_x, to_y)
        self.across[k].append(self.copies.make(same(lambda: self.out(k, me.c, 1 - me.x, me.y, ())), me.core_peer))
        self.across[k].append(self.copies.make(same(lambda: self.out(k, me.c, me.x, 1 - me.y, ())), me.core_peer))

    def finish_relay(self, k):
        me = self.me
        for copy in self.relayed[k]:
            copy.wait_recv()
        self.across[k].append(self.copies.make(same(lambda: self.out(k, me.c, 1 - me.x, 1 - me.y, ())), me.core_peer))

    def wait(self, k):
        for copy in self.across[k]:
            copy.wait_recv()

    def stage(self, number, k):
        stages = (
            self.finish_core, self.finish_first, self.finish_second, self.finish_z, self.finish_last_z,
            self.finish_spread, self.finish_relay,
        )
        stages[number](k)


STAGES = 7


def reduction_buffers(amount, parts, width):
    half = width // 2
    return [
        pltpu.VMEM((amount, parts, 2, 2, 2, PIECE, width), low),
        pltpu.VMEM((amount, 2, parts, 2, 2, PIECE, half), low),
        pltpu.VMEM((amount, 2, parts, 2, PIECE, half), low),
        pltpu.VMEM((amount, 4, parts, PIECE, half), low),
        pltpu.VMEM((amount, parts, PIECE, half), low),
    ]


def reduced_feed_forward_kernel(*refs):
    later_fc1, later_fc2, piece_out = refs[12:15]
    term, core_in, first_in, second_in, send_sems, recv_sems, store_sems = refs[21:]
    work = FeedForward(refs[:12] + refs[15:21])
    me = Peers()
    copies = Copies(send_sems, recv_sems)
    per_tile = FFN_TILE // LANES
    early = term.shape[1] // per_tile
    tile_shape = (per_tile,) + term.shape[2:]
    buffers = (core_in, first_in, second_in, None, None)
    first_half = Reduction(
        me, copies, lambda k, c: term.at[k, :, c], (term, lambda k, part, *place: (k, part, me.c) + place), None, buffers,
        None, store_sems,
    )
    step = pl.program_id(0)
    last = pl.num_programs(0) - 1

    @pl.when(step == 0)
    def _():
        work.begin()
        meet(me.plane())

    fc1_grad, fc2_grad = work.tile()

    @pl.when(step < early)
    def _():
        term[0, pl.ds(step * per_tile, per_tile)] = fc1_grad.reshape(tile_shape)
        term[1, pl.ds(step * per_tile, per_tile)] = fc2_grad.reshape(tile_shape)

    @pl.when(step >= early)
    def _():
        later_fc1[...] = fc1_grad
        later_fc2[...] = fc2_grad

    @pl.when(step == early - 1)
    def _():
        for k in range(2):
            first_half.start(k)

    @pl.when(step == early)
    def _():
        for k in range(2):
            first_half.finish_core(k)

    @pl.when(step == last)
    def _():
        for k in range(2):
            first_half.finish_first(k)
        work.finish()
        for k in range(2):
            first_half.add_second(k)
            first_half.store_piece(k, piece_out).start()
        for k in range(2):
            first_half.store_piece(k, piece_out).wait()
        copies.drain()


def reduced_feed_forward(normed, cotangent, middle, fc1_tiles, fc2_full, vectors, collective_id):
    operands, in_specs, out_specs, out_shape, scratch, tiles = feed_forward_parts(
        normed, cotangent, middle, fc1_tiles, fc2_full, vectors
    )
    width = cotangent.shape[1]
    early = tiles // 2
    tile_shape = (2, 2, 2, 2, PIECE, width)
    parts = early * FFN_TILE // LANES
    later = pl.BlockSpec((FFN_TILE, width), lambda f: (jnp.maximum(f - early, 0), 0))
    return pl.pallas_call(
        reduced_feed_forward_kernel,
        grid=(tiles,),
        in_specs=in_specs,
        out_specs=out_specs + [later] * 2 + [HBM],
        out_shape=out_shape
        + [struct(((tiles - early) * FFN_TILE, width), low)] * 2
        + [struct((2, parts, 2, PIECE, width), low)],
        scratch_shapes=scratch
        + [pltpu.VMEM((2, parts) + tile_shape, low)]
        + reduction_buffers(2, parts, width)[:3]
        + [pltpu.SemaphoreType.DMA((10,)), pltpu.SemaphoreType.DMA((10,)), pltpu.SemaphoreType.DMA((2,))],
        compiler_params=pltpu.CompilerParams(
            collective_id=collective_id, has_side_effects=True, vmem_limit_bytes=58 * MIB,
            fuse_transposed_lhs_in_matmul=True,
        ),
        name="reduced_feed_forward",
    )(*operands)


class SmallSum:
    def __init__(self, me, copies, small, inbox):
        self.me, self.copies, self.small, self.inbox, self.made = me, copies, small, inbox, []

    def step(self, number):
        peers = self.me.plane()
        z = self.me.z
        if number > 0:
            self.made[number - 1].wait_recv()
            self.small[...] += self.inbox[number - 1]
        if number < 3:
            self.inbox[3 + number] = self.small[...]
            self.made.append(
                self.copies.make(lambda: (self.inbox.at[3 + number], self.inbox.at[number]), peers[number])
            )
        else:
            self.inbox[6 + z] = self.small[...]
            for peer in self.me.z_peers:
                self.made.append(self.copies.make(same(lambda: self.inbox.at[6 + z]), peer))

    def finish(self):
        for copy in self.made[3:]:
            copy.wait_recv()
        self.small[...] = (self.inbox[6] + self.inbox[7]) + (self.inbox[8] + self.inbox[9])


def column_pick(member, shape):
    row, column = (lax.broadcasted_iota(jnp.int32, shape, axis) for axis in range(2))
    return jnp.where(column == row + member * shape[0], 1.0, 0.0).astype(low)


def exchange_places(me):
    member = me.y * 4 + me.x * 2 + me.c
    return member, [lax.rem(member + step, 8) for step in range(1, 8)]


class Exchange:
    def __init__(self, me, copies, blocks, inbox):
        self.me, self.copies, self.blocks, self.inbox = me, copies, blocks, inbox
        self.member, self.others = exchange_places(me)

    def start(self):
        self.made = [
            self.copies.make(lambda there=there: (self.blocks.at[there], self.inbox.at[self.member]), (self.me.z, there))
            for there in self.others
        ]

    def wait(self):
        for copy in self.made:
            copy.wait_recv()


class HiddenUpdate:
    TILES = 4

    def __init__(self, me, total, stats, roots, small_stats, small_roots, outs, scratch):
        self.me, self.total, self.stats, self.roots = me, total, stats, roots
        self.small_stats, self.small_roots = small_stats, small_roots
        self.stats_out, self.small_out, self.columns, self.fc2_step = outs
        self.tall, self.big, self.root, self.fresh, self.rows, self.sum, self.small_root, self.small_in = scratch[:8]
        self.blocks, self.load_sems, self.store_sems, self.other_sems = scratch[8:]
        self.span, self.width = self.root.shape[1:]

    def columns_of(self, t):
        tile = t % self.TILES
        return pl.ds(tile * self.width, self.width)

    def loads(self, t):
        matrix, tile = divmod(t, self.TILES)
        slot = t % 2
        half, part = divmod(3 * tile, 6)
        copies = [
            pltpu.make_async_copy(
                self.total.at[matrix, half, part + index],
                self.tall.at[slot, pl.ds(2 * index, 2)],
                self.load_sems.at[slot, index],
            )
            for index in range(3)
        ]
        return copies + [
            pltpu.make_async_copy(
                self.stats.at[matrix, :, self.columns_of(t)],
                self.big.at[pl.ds(slot * self.span, self.span)],
                self.load_sems.at[slot, 3],
            ),
            pltpu.make_async_copy(
                self.roots.at[matrix, :, self.columns_of(t)], self.root.at[slot], self.load_sems.at[slot, 4]
            ),
        ]

    def matrix_loads(self, matrix):
        member = self.me.y * 4 + self.me.x * 2 + self.me.c
        copies = []
        for index in range(3):
            unit = 3 * member + index
            place = self.total.at[matrix, unit // 12, lax.rem(unit, 12) // 2, lax.rem(unit, 2)]
            copies.append(pltpu.make_async_copy(place, self.rows.at[index], self.other_sems.at[index]))
        return copies + [
            pltpu.make_async_copy(self.small_roots.at[2 + matrix], self.small_root, self.other_sems.at[3]),
            pltpu.make_async_copy(self.small_stats.at[3 + matrix], self.small_in, self.other_sems.at[4]),
        ]

    def store(self, t):
        return pltpu.make_async_copy(
            self.fresh.at[t % 2], self.stats_out.at[t // self.TILES, :, self.columns_of(t)], self.store_sems.at[t % 2]
        )

    def begin(self):
        for copy in self.matrix_loads(0) + self.loads(0):
            copy.start()

    def tile(self, t):
        matrix, tile = divmod(t, self.TILES)
        slot = t % 2
        if t + 1 < 2 * self.TILES:
            for copy in self.loads(t + 1):
                copy.start()
        if tile == 0:
            for copy in self.matrix_loads(matrix):
                copy.wait()
        for copy in self.loads(t):
            copy.wait()
        if t >= 2:
            self.store(t - 2).wait()
        member = self.me.y * 4 + self.me.x * 2 + self.me.c
        model_rows = self.small_in.shape[0]
        tall = self.tall[slot].reshape(self.width, self.width)
        rows = self.rows[...].reshape(self.span, self.width)
        across = dot(
            jnp.concatenate([rows, column_pick(member, (model_rows, self.width))], axis=0), tall, COLS_BY_COLS
        )
        columns = across[self.span :].astype(low)
        term = dot(jnp.concatenate([self.root[slot].astype(low), columns], axis=0), tall)
        self.sum[...] = term if tile == 0 else self.sum[...] + term
        self.fresh[slot] = 0.5 * self.big[slot * self.span : (slot + 1) * self.span, :] + 0.5 * across[: self.span]
        self.store(t).start()
        if matrix == 0:
            self.columns[:, tile * self.width : (tile + 1) * self.width] = columns
        if tile == self.TILES - 1:
            self.small_out[matrix] = 0.5 * self.small_in[...] + 0.5 * self.sum[self.span :, :]
            product = self.sum[: self.span, :].astype(low)
            if matrix == 0:
                step = dot(self.small_root[...], product, COLS_BY_COLS).astype(low)
                self.blocks[...] = step.reshape(self.blocks.shape)
                for copy in self.matrix_loads(1):
                    copy.start()
            else:
                self.fc2_step[...] = dot(product, self.small_root[...]).astype(low)

    def finish(self):
        for t in (2 * self.TILES - 2, 2 * self.TILES - 1):
            self.store(t).wait()


def reduced_backward_kernel(heads, head_size, *refs):
    fc1_term, fc2_term, piece = refs[15:18]
    stats_hidden, roots_hidden, stats_model, small_roots = refs[18:22]
    input_grad, fc_out, qkv_out, proj_out, small_out = refs[22:27]
    stats_out, hidden_small, fc1_columns, fc1_inbox, fc2_step = refs[27:32]
    work_refs = refs[32:37]
    att, fc_mine = refs[37:39]
    fc_buffers, att_buffers, early_buffers = refs[39:44], refs[44:49], refs[49:51]
    inbox, send_sems, recv_sems, load_sems, early_load_sems, fc_store_sems, early_store_sems, att_store_sems = refs[51:59]
    hidden_scratch = refs[59:]
    groups = att.shape[0] - 1
    tile_shape = (2, 2, 2, 2, PIECE, att.shape[-1])

    def proj_grad(tile, value):
        att[groups, tile] = value.reshape(tile_shape)

    def qkv_grad(part, group, value):
        att[group, part] = value.reshape(tile_shape)

    work = Backward(heads, head_size, refs[:15] + (input_grad,) + work_refs, proj_grad, qkv_grad)
    me = Peers()
    copies = Copies(send_sems, recv_sems)

    def fc_place(half):
        return lambda k, c, x, y, rest: fc_out.at[(k, half, slice(None), c, x, y) + rest]

    def att_place(k, c, x, y, rest):
        if k == groups:
            return proj_out.at[(slice(None), c, x, y) + rest]
        return qkv_out.at[(slice(None), k, c, x, y) + rest]

    early = Reduction(
        me, copies, None, None, fc_place(0), (fc_buffers[0], None, None) + early_buffers, early_load_sems,
        early_store_sems,
    )
    fc = Reduction(
        me, copies, lambda k, c: (fc1_term, fc2_term)[k].at[:, c], (fc_mine, lambda *place: place), fc_place(1),
        fc_buffers, load_sems, fc_store_sems,
    )
    att_sum = Reduction(
        me, copies, lambda k, c: att.at[k, :, c], (att, lambda k, part, *place: (k, part, me.c) + place), att_place,
        att_buffers, None, att_store_sems,
    )
    small = SmallSum(me, copies, work.small, inbox)
    hidden = HiddenUpdate(
        me, fc_out, stats_hidden, roots_hidden, stats_model, small_roots,
        (stats_out, hidden_small, fc1_columns, fc2_step),
        (fc_buffers[0], work.normed_back) + hidden_scratch,
    )
    exchange = Exchange(me, copies, hidden.blocks, fc1_inbox)
    others = exchange_places(me)[1]

    def own_blocks():
        return pltpu.make_async_copy(
            hidden.blocks.at[exchange.member], fc1_inbox.at[exchange.member], hidden.other_sems.at[5]
        )

    order = [(early, 0, -3), (early, 1, -3), (fc, 0, 0), (fc, 1, 1), (att_sum, groups, 2)]
    order += [(att_sum, k, 3 + k) for k in range(groups)]
    waves = 2 + groups + STAGES
    done = [0]

    def wave():
        number = done[0]
        done[0] += 1
        for which, k, first in reversed(order):
            if 0 <= number - first < STAGES:
                which.stage(number - first, k)

    step = pl.program_id(0)
    windows = work.windows
    busy = windows * groups
    group, window = step // windows, lax.rem(step, windows)

    @pl.when(step == 0)
    def _():
        meet([(me.z, there) for there in others] + me.z_peers)
        for k in range(2):
            early.start_z(k, piece)
            fc.start(k)
        work.begin_grads()
        att_sum.start(groups)
        work.begin()

    @pl.when(step < busy)
    def _():
        work.attend(group, window)

    for number in range(groups):

        @pl.when(step == (number + 1) * windows - 1)
        def _():
            work.group_grads(number)
            att_sum.start(number)

    for at in (2, 5, 8, 11, 15, 20):

        @pl.when(step == at)
        def _():
            wave()

    @pl.when(step == busy)
    def _():
        work.normed_back_step()
        wave()
        work.finish()
        wave()
        work.diagonals()
        small.step(0)
        for number in range(1, 5):
            wave()
            if number == 1:
                for which, k, _ in order[:4]:
                    which.wait(k)
                hidden.begin()
            if number < 4:
                small.step(number)
            else:
                small.finish()
            for t in range(2 * number - 2, 2 * number):
                hidden.tile(t)
            if number == 2:
                exchange.start()
                own_blocks().start()
        small_out[...] = work.small[...]
        while done[0] < waves:
            wave()
        for which, k, _ in order[4:]:
            which.wait(k)
        hidden.finish()
        exchange.wait()
        own_blocks().wait()
        copies.drain()


def reduced_backward(probs, mixed, operands, head_count, fc1_term, fc2_term, piece, update_operands, collective_id):
    sizes, operands, in_specs, scratch, busy = backward_parts(probs, mixed, operands, head_count)
    count, width = operands[4].shape
    groups = width // LANES
    tile_shape = (2, 2, 2, 2, PIECE, width)
    parts = fc1_term.shape[0] // LANES
    small_shape = (SMALL_DIAG + head_count, width)
    copies = 14 * 2 + 19 * (2 + groups + 1) + 6 + 7
    stats_hidden, _, stats_model, _ = update_operands
    _, span, hidden_width = stats_hidden.shape
    model_rows = stats_model.shape[1]
    blocks = (8, model_rows, span)
    vmem = pl.BlockSpec(memory_space=pltpu.VMEM)
    buffers = reduction_buffers(2, parts, width)
    input_grad, fc_sum, qkv_sum, proj_sum, small, *update = pl.pallas_call(
        functools.partial(reduced_backward_kernel, *sizes),
        grid=(busy + 1,),
        in_specs=in_specs + [HBM] * 7,
        out_specs=[whole((count, width))] + [HBM] * 3 + [whole(small_shape)] + [HBM] + [vmem] * 2 + [HBM] + [vmem],
        out_shape=[
            struct((count, width), low),
            struct((2, 2, parts) + tile_shape, low),
            struct((3, groups) + tile_shape, low),
            struct((groups,) + tile_shape, low),
            struct(small_shape, f32),
            struct(stats_hidden.shape, f32),
            struct((2, model_rows, width), f32),
            struct((model_rows, hidden_width), low),
            struct(blocks, low),
            struct((span, width), low),
        ],
        scratch_shapes=scratch
        + [pltpu.VMEM((groups + 1, 3) + tile_shape, low), pltpu.VMEM((2, parts) + tile_shape[1:], low)]
        + buffers
        + reduction_buffers(groups + 1, 3, width)
        + buffers[3:]
        + [
            pltpu.VMEM((10,) + small_shape, f32),
            pltpu.SemaphoreType.DMA((copies,)),
            pltpu.SemaphoreType.DMA((copies,)),
        ]
        + [pltpu.SemaphoreType.DMA((2,))] * 4
        + [pltpu.SemaphoreType.DMA((groups + 1,))]
        + [
            pltpu.VMEM((2, span, width), f32),
            pltpu.VMEM((2, span, width), f32),
            pltpu.VMEM((3,) + tile_shape[1:], low),
            pltpu.VMEM((span + model_rows, width), f32),
            pltpu.VMEM((width, width), low),
            pltpu.VMEM((model_rows, width), f32),
            pltpu.VMEM(blocks, low),
            pltpu.SemaphoreType.DMA((2, 5)),
            pltpu.SemaphoreType.DMA((2,)),
            pltpu.SemaphoreType.DMA((6,)),
        ],
        compiler_params=pltpu.CompilerParams(
            collective_id=collective_id, has_side_effects=True, vmem_limit_bytes=62 * MIB
        ),
        name="reduced_backward",
    )(*operands, fc1_term.reshape((parts,) + tile_shape), fc2_term.reshape((parts,) + tile_shape), piece, *update_operands)
    sums = [part.reshape(-1, width) for part in (qkv_sum, proj_sum, fc_sum)]
    return input_grad, sums, small, update


def tile_update(tall, rows, big, root, pick, sum_ref, fresh):
    span = rows.shape[0]
    across = dot(jnp.concatenate([rows, pick], axis=0), tall, COLS_BY_COLS)
    columns = across[span:]
    term = dot(jnp.concatenate([root.astype(low), columns.astype(low)], axis=0), tall)

    @pl.when(fresh)
    def _():
        sum_ref[...] = term

    @pl.when(jnp.logical_not(fresh))
    def _():
        sum_ref[...] += term

    return 0.5 * big + 0.5 * across[:span], columns


def exchange_kernel(amount, *refs):
    blocks, inboxes = refs[:amount], refs[amount : 2 * amount]
    send_sems, recv_sems, local_sems = refs[2 * amount :]
    me = Peers()
    copies = Copies(send_sems, recv_sems)
    member, others = exchange_places(me)
    meet([(me.z, there) for there in others])
    exchanges = [Exchange(me, copies, source, inbox) for source, inbox in zip(blocks, inboxes)]
    own = [
        pltpu.make_async_copy(source.at[member], inbox.at[member], local_sems.at[index])
        for index, (source, inbox) in enumerate(zip(blocks, inboxes))
    ]
    for copy in own:
        copy.start()
    for exchange in exchanges:
        exchange.start()
    for exchange in exchanges:
        exchange.wait()
    for copy in own:
        copy.wait()
    copies.drain()


def exchange_rows(steps, collective_id):
    amount = len(steps)
    blocks = [step.reshape(8, step.shape[0] // 8, step.shape[1]) for step in steps]
    vmem = pl.BlockSpec(memory_space=pltpu.VMEM)
    return pl.pallas_call(
        functools.partial(exchange_kernel, amount),
        in_specs=[vmem] * amount,
        out_specs=[vmem] * amount,
        out_shape=[struct(block.shape, low) for block in blocks],
        scratch_shapes=[
            pltpu.SemaphoreType.DMA((7 * amount,)),
            pltpu.SemaphoreType.DMA((7 * amount,)),
            pltpu.SemaphoreType.DMA((amount,)),
        ],
        compiler_params=pltpu.CompilerParams(collective_id=collective_id, has_side_effects=True),
        name="exchange_rows",
    )(*blocks)


def apply_kernel(
    member_ref, qkv_ref, fc1_ref, fc2_ref, qkv_blocks, fc1_blocks, fc2_step, columns_ref, rows_ref,
    qkv_new, fc1_new, fc2_new, qkv_copy, fc1_copy, fc2_copy, fc1_grad, fc2_grad,
):
    def side_by_side(blocks):
        return jnp.concatenate([blocks[place] for place in range(blocks.shape[0])], axis=1)

    for old, step, new_ref, copy_ref in (
        (qkv_ref, side_by_side(qkv_blocks), qkv_new, qkv_copy),
        (fc1_ref, side_by_side(fc1_blocks), fc1_new, fc1_copy),
        (fc2_ref, fc2_step[...], fc2_new, fc2_copy),
    ):
        new = old[...] - step.astype(f32)
        new_ref[...] = new
        copy_ref[...] = new.astype(low)
    fc1_grad[...] = columns_ref[...].astype(f32)
    fc2_grad[...] = rows_ref[...].astype(f32)


def apply_steps(member, weights, steps, fc1_columns, fc_sum):
    qkv_weight, fc1_weight, fc2_weight = weights
    span = fc2_weight.shape[0]
    skip = fc1_weight.shape[1] // span

    def fixed(operand):
        return pl.BlockSpec(operand.shape, lambda step, m: (0,) * operand.ndim)

    operands = list(weights) + list(steps) + [fc1_columns]
    results = [struct(weight.shape, dtype) for dtype in (f32, low) for weight in weights]
    results += [struct(fc1_weight.shape, f32), struct(fc2_weight.shape, f32)]
    return pl.pallas_call(
        apply_kernel,
        grid_spec=pltpu.PrefetchScalarGridSpec(
            num_scalar_prefetch=1,
            grid=(1,),
            in_specs=[fixed(operand) for operand in operands]
            + [pl.BlockSpec((span, fc_sum.shape[1]), lambda step, m: (skip + m[0], 0))],
            out_specs=[fixed(result) for result in results],
        ),
        out_shape=results,
        compiler_params=pltpu.CompilerParams(vmem_limit_bytes=48 * MIB),
        name="apply_steps",
    )(member, *operands, fc_sum)


def model_kernel(
    member_ref, tall_ref, qkv_rows_ref, proj_tall_ref, proj_rows_ref, big_ref, root_ref, stats_ref, hidden_small_ref, proj_root_ref,
    small_root_ref, proj_ref,
    big_out_ref, stats_out_ref, qkv_grad_ref, qkv_step_ref, proj_grad_ref, proj_new_ref, proj_copy_ref,
    sum_ref, proj_sum_ref,
):
    tile = pl.program_id(0)
    span = qkv_rows_ref.shape[0]
    model_rows = proj_rows_ref.shape[0]
    last = pl.num_programs(0) - 1
    pick = column_pick(member_ref[0], proj_rows_ref.shape)

    @pl.when(tile < last)
    def _():
        big_new, columns = tile_update(
            tall_ref[...], qkv_rows_ref[...], big_ref[...], root_ref[...], pick, sum_ref, tile == 0
        )
        big_out_ref[...] = big_new
        qkv_grad_ref[...] = columns

    @pl.when(tile == last)
    def _():
        qkv_step_ref[...] = dot(small_root_ref[0], sum_ref[:span, :].astype(low), COLS_BY_COLS).astype(low)
        stats_out_ref[0] = 0.5 * stats_ref[0] + 0.5 * sum_ref[span:, :]
        rows = proj_rows_ref[...]
        proj_left, _ = tile_update(
            proj_tall_ref[...], rows, stats_ref[1], proj_root_ref[0], pick, proj_sum_ref, tile == last
        )
        stats_out_ref[1] = proj_left
        stats_out_ref[2] = 0.5 * stats_ref[2] + 0.5 * proj_sum_ref[model_rows:, :]
        stats_out_ref[3] = hidden_small_ref[0]
        stats_out_ref[4] = hidden_small_ref[1]
        new = proj_ref[...] - dot(proj_sum_ref[:model_rows, :].astype(low), small_root_ref[1])
        proj_new_ref[...] = new
        proj_copy_ref[...] = new.astype(low)
        proj_grad_ref[...] = rows.astype(f32)


def model_update(
    member, qkv_sum, proj_sum, stats_qkv, roots_qkv, stats_model, hidden_small, roots_model, small_roots, proj_weight
):
    width = qkv_sum.shape[1]
    span, qkv_width = stats_qkv.shape
    model_rows = stats_model.shape[1]
    tiles = qkv_width // width

    def fixed(shape):
        return pl.BlockSpec(shape, lambda j, m: (0,) * len(shape))

    clamped = pl.BlockSpec((span, width), lambda j, m: (0, jnp.minimum(j, tiles - 1)))
    return pl.pallas_call(
        model_kernel,
        grid_spec=pltpu.PrefetchScalarGridSpec(
            num_scalar_prefetch=1,
            grid=(tiles + 1,),
            in_specs=[
                pl.BlockSpec((width, width), lambda j, m: (jnp.minimum(j, tiles - 1), 0)),
                pl.BlockSpec((span, width), lambda j, m: (m[0], 0)),
                fixed((width, width)),
                pl.BlockSpec((model_rows, width), lambda j, m: (m[0], 0)),
                clamped,
                clamped,
                fixed(stats_model.shape),
                fixed(hidden_small.shape),
                pl.BlockSpec((1, model_rows, width), lambda j, m: (1, 0, 0)),
                pl.BlockSpec((2, width, width), lambda j, m: (0, 0, 0)),
                fixed(proj_weight.shape),
            ],
            out_specs=[
                clamped,
                fixed(stats_model.shape),
                pl.BlockSpec((model_rows, width), lambda j, m: (0, jnp.minimum(j, tiles - 1))),
                fixed((width, span)),
                fixed((model_rows, width)),
                fixed((model_rows, width)),
                fixed((model_rows, width)),
            ],
            scratch_shapes=[
                pltpu.VMEM((span + model_rows, width), f32),
                pltpu.VMEM((2 * model_rows, width), f32),
            ],
        ),
        out_shape=[
            struct(stats_qkv.shape, f32),
            struct(stats_model.shape, f32),
            struct((model_rows, qkv_width), f32),
            struct((width, span), low),
            struct((model_rows, width), f32),
            struct((model_rows, width), f32),
            struct((model_rows, width), low),
        ],
        compiler_params=pltpu.CompilerParams(vmem_limit_bytes=48 * MIB),
        name="model_update",
    )(
        member, qkv_sum, qkv_sum, proj_sum, proj_sum, stats_qkv, roots_qkv, stats_model, hidden_small, roots_model,
        small_roots, proj_weight,
    )


def plain_update(
    sums, stats_model, stats_qkv, stats_hidden, roots_model, roots_qkv, roots_hidden, small_roots, weights
):
    width = sums[0].shape[1]
    member = lax.axis_index("grp")
    model_rows = stats_model.shape[1]
    picked = member * model_rows + jnp.arange(model_rows, dtype=jnp.int32)
    pick = (picked[:, None] == jnp.arange(width, dtype=jnp.int32)[None, :]).astype(low)

    def statistic_update(tall, small_rows, big_rows):
        columns = dot(pick, tall, COLS_BY_COLS)
        small_new = 0.5 * small_rows + 0.5 * dot(columns.astype(low), tall)
        rows = lax.dynamic_slice_in_dim(tall, member * big_rows.shape[0], big_rows.shape[0], 0)
        big_new = 0.5 * big_rows + 0.5 * dot(rows, tall, COLS_BY_COLS)
        return small_new, big_new, columns, rows.astype(f32)

    def product_of(big_root_rows, tall):
        return dot(big_root_rows.astype(low), tall).astype(low)

    qkv, proj, fc1, fc2 = sums
    qkv_left, qkv_right, qkv_gradient, _ = statistic_update(qkv, stats_model[0], stats_qkv)
    proj_right, proj_left, _, proj_gradient = statistic_update(proj, stats_model[2], stats_model[1])
    fc1_left, fc1_right, fc1_gradient, _ = statistic_update(fc1, stats_model[3], stats_hidden[0])
    fc2_right, fc2_left, _, fc2_gradient = statistic_update(fc2, stats_model[4], stats_hidden[1])
    qkv_step = dot(small_roots[0], product_of(roots_qkv, qkv), COLS_BY_COLS).astype(low)
    fc1_step = dot(small_roots[2], product_of(roots_hidden[0], fc1), COLS_BY_COLS).astype(low)
    qkv_weight, proj_weight, fc1_weight, fc2_weight = weights
    qkv_new = qkv_weight - lax.all_to_all(qkv_step, "grp", 0, 1, tiled=True).astype(f32)
    fc1_new = fc1_weight - lax.all_to_all(fc1_step, "grp", 0, 1, tiled=True).astype(f32)
    proj_new = proj_weight - dot(product_of(roots_model[1], proj), small_roots[1])
    fc2_new = fc2_weight - dot(product_of(roots_hidden[1], fc2), small_roots[3])
    new_stats_model = jnp.stack([qkv_left, proj_left, proj_right, fc1_left, fc2_right])
    return (
        (new_stats_model, qkv_right, jnp.stack([fc1_right, fc2_left])),
        (qkv_gradient, proj_gradient, fc1_gradient, fc2_gradient),
        (qkv_new, proj_new, fc1_new, fc2_new),
    )


def shards(
    plain, tokens, cotangent, window_fill, qkv_weight, proj_weight, fc1_weight, fc2_weight, vectors, vector_moments,
    bias_table, table_moments, stats_model, stats_qkv, stats_hidden, roots_model, roots_qkv, roots_hidden,
):
    width = vectors.shape[1]
    head_count = bias_table.shape[1]
    gather = functools.partial(lax.all_gather, axis_name="grp", tiled=True)
    weights = (qkv_weight, proj_weight, fc1_weight, fc2_weight)
    hot = jnp.asarray(diagonal_tables())
    diagonals = lax.dot_general(bias_table, hot, (((0,), (1,)), ((), ())), precision=lax.Precision.HIGHEST)
    if plain:
        fulls = [gather(weight.astype(low)) for weight in weights]
        base = (lax.axis_index(("rep", "grp")) * window_fill.shape[0]).astype(jnp.int32).reshape(1)
        forward = attention_forward(window_fill, base, tokens, *fulls[:2], vectors, diagonals, head_count)
    else:
        forward, fulls = gathered_forward(window_fill, tokens, weights, vectors, diagonals, head_count, 0)
    probs, mixed, normed, context, middle, normed_two = forward
    qkv_full, proj_full, fc1_full, fc2_full = fulls
    if plain:
        fc1_full = jnp.swapaxes(fc1_full.reshape(width, -1, FFN_TILE), 0, 1)[None, None, None]
    roots_low = jnp.stack([roots_model[i] for i in (0, 2, 3, 4)]).astype(low)
    roots_low, normed_two = lax.optimization_barrier((roots_low, normed_two))
    small_roots = gather(roots_low, axis=1)
    ffn_operands = (normed_two, cotangent, middle, fc1_full, fc2_full, vectors)
    ffn = feed_forward(*ffn_operands) if plain else reduced_feed_forward(*ffn_operands, 3)
    layer_output, middle_back, branch_back, fc1_bias_grad, ffn_vec, fc1_term, fc2_term = ffn[:7]
    small_roots, branch_back = lax.optimization_barrier((small_roots, branch_back))
    operands = [branch_back, middle_back, proj_full, context, normed, tokens, qkv_full, vectors, ffn_vec, fc1_bias_grad]
    if plain:
        input_gradient, att_term, small = attention_backward(probs, mixed, operands, head_count)
        small = lax.psum(small, ("rep", "grp"))
        terms = (att_term[: 3 * width], att_term[3 * width :], fc1_term, fc2_term)
        sums = [
            gather(lax.psum(lax.psum_scatter(term, "grp", scatter_dimension=0, tiled=True), "rep")) for term in terms
        ]
    else:
        update_operands = (stats_hidden, roots_hidden, stats_model, small_roots)
        input_gradient, sums, small, update = reduced_backward(
            probs, mixed, operands, head_count, *ffn[5:], update_operands, 1
        )
    vector_total = small[: vectors.shape[0]]
    table_total = lax.dot_general(
        hot, small[SMALL_DIAG:], (((0,), (1,)), ((), ())), precision=lax.Precision.HIGHEST
    )
    if plain:
        statistics, gradients, masters = plain_update(
            sums, stats_model, stats_qkv, stats_hidden, roots_model, roots_qkv, roots_hidden, small_roots, weights
        )
        copies = tuple(master.astype(low) for master in masters)
    else:
        member = lax.axis_index("grp").astype(jnp.int32).reshape(1)
        new_stats_hidden, hidden_small, fc1_columns, fc1_blocks, fc2_step = update
        qkv_right, new_stats_model, qkv_gradient, qkv_step, proj_gradient, proj_new, proj_copy = model_update(
            member, *sums[:2], stats_qkv, roots_qkv, stats_model, hidden_small, roots_model, small_roots, proj_weight
        )
        (qkv_blocks,) = exchange_rows((qkv_step,), 2)
        qkv_new, fc1_new, fc2_new, qkv_copy, fc1_copy, fc2_copy, fc1_gradient, fc2_gradient = apply_steps(
            member, (qkv_weight, fc1_weight, fc2_weight), (qkv_blocks, fc1_blocks, fc2_step), fc1_columns, sums[2]
        )
        statistics = (new_stats_model, qkv_right, new_stats_hidden)
        gradients = (qkv_gradient, proj_gradient, fc1_gradient, fc2_gradient)
        masters = (qkv_new, proj_new, fc1_new, fc2_new)
        copies = (qkv_copy, proj_copy, fc1_copy, fc2_copy)
    total_tokens = tokens.shape[0] * lax.axis_size("rep") * lax.axis_size("grp")
    rate_base = total_tokens ** (-0.5)
    new_vector_moments = 0.9 * vector_moments + 0.1 * vector_total
    new_vectors = vectors - 2.0 * rate_base * new_vector_moments
    new_table_moments = 0.9 * table_moments + 0.1 * table_total
    new_table = bias_table - 8.0 * rate_base * new_table_moments
    return (
        (layer_output, input_gradient)
        + gradients
        + masters
        + copies
        + statistics
        + (new_vectors, new_vector_moments, new_table, new_table_moments)
    )


def solution(mesh):
    tokens, rows, blocks, copied = P(("rep", "grp"), None), P("grp", None), P(None, "grp", None), P()
    plain = (mesh.shape["rep"], mesh.shape["grp"]) != (4, 8)
    return jax.shard_map(
        functools.partial(shards, plain),
        mesh=mesh,
        in_specs=(tokens, tokens, P(("rep", "grp")))
        + (rows,) * 4
        + (copied,) * 4
        + (blocks, rows, blocks) * 2,
        out_specs=(tokens,) * 2 + (rows,) * 12 + (blocks, rows, blocks) + (copied,) * 4,
        check_vma=False,
    )
```
